32 devices in a mesh: head: 4 (over x, core), seq: 4 (over z), dp: 2 (over y).
Axes of the slice: x: 2, y: 2, z: 4, core: 2. Of those that a mesh axis runs over, the one named last changes fastest.
Arguments:
- tokens: bfloat16 [16, 1024, 768], P('dp', 'seq'), may hold values from -6 to 6
- lengths: int32 [16], P('dp'), may hold values from 129 to 1024, as said below
- expert_ids: int32 [16, 1024, 1], P('dp', 'seq'), may hold values from 0 to 15; in each aligned block of 256 rows (0 to 255, 256 to 511, ..., all dimensions but the last counted through in order) at most 20 rows name the same one
- attention_gain: bfloat16 [768], P(('seq', 'dp')), may hold values from 0.5 to 1.5
- query_weight: bfloat16 [768, 768], P(('seq', 'dp'), 'head'), may hold values from -0.0390625 to 0.0390625
- key_weight: bfloat16 [768, 768], P(('seq', 'dp'), 'head'), may hold values from -0.21875 to 0.21875
- value_weight: bfloat16 [768, 768], P(('seq', 'dp'), 'head'), may hold values from -0.21875 to 0.21875
- output_weight: bfloat16 [768, 768], P('head', ('seq', 'dp')), may hold values from -1.75 to 1.75
- position_bias: bfloat16 [32, 12], P(None, 'head'), may hold values from -1 to 1
- feedforward_gain: bfloat16 [768], P(('seq', 'dp')), may hold values from 0.5 to 1.5
- router_weight: bfloat16 [768, 16], P(('seq', 'dp')), may hold values from -0.109375 to 0.109375
- expert_up: bfloat16 [16, 768, 3072], P(('seq', 'dp'), None, 'head'), may hold values from -0.21875 to 0.21875
- expert_down: bfloat16 [16, 3072, 768], P(('seq', 'dp'), 'head'), may hold values from -6 to 6
- cotangent: bfloat16 [16, 1024, 768], P('dp', 'seq'), may hold values from -6 to 6
Outputs:
- output: bfloat16 [16, 1024, 768], P('dp', 'seq')
- tokens_grad: bfloat16 [16, 1024, 768], P('dp', 'seq')
- attention_gain_grad: float32 [768], P(('seq', 'dp'))
- query_weight_grad: float32 [768, 768], P(('seq', 'dp'), 'head')
- key_weight_grad: float32 [768, 768], P(('seq', 'dp'), 'head')
- value_weight_grad: float32 [768, 768], P(('seq', 'dp'), 'head')
- output_weight_grad: float32 [768, 768], P('head', ('seq', 'dp'))
- position_bias_grad: float32 [32, 12], P(None, 'head')
- feedforward_gain_grad: float32 [768], P(('seq', 'dp'))
- router_weight_grad: float32 [768, 16], P(('seq', 'dp'))
- expert_up_grad: float32 [16, 768, 3072], P(('seq', 'dp'), None, 'head')
- expert_down_grad: float32 [16, 3072, 768], P(('seq', 'dp'), 'head')
The draws below stay inside these ranges and needn't reach their ends.
Inputs may be any that keep to these rules, and one draw needn't show every extreme that they name: `lengths`: each group of 8 sequences on one index of dp holds one sequence of full length 1024. `expert_ids`: in each aligned block of 256 positions of one sequence, no expert is named more than 20 times.
All inputs are finite; a program needn't handle non-finite values.
Results may differ from the reference program's by a relative error of at most 0.018.
Values may be sent and summed in bfloat16 or wider, within the bound.
A program may use at most 256 MiB of HBM per device.

```python
import math
import jax
import jax.numpy as jnp
import numpy as np
from jax import lax

D = 768
HEADS = 12
HEAD_DIM = 64
FF = 3072
NBUCKET = 32
SPAN = 256
SEQ_DEV = 8
LEN = 1024
SEQS = 16
EXPERTS = 16
MOST = 20
EXP_ROWS = 1280
N_HEAD = 4
N_SEQ = 4
N_DP = 2


def draw_lengths(key, part):
    key = jax.random.fold_in(key, 11)
    first_key, second_key = jax.random.split(key)
    groups = SEQS // SEQ_DEV
    drawn = jax.random.randint(first_key, (groups, SEQ_DEV), LEN // 8 + 1, LEN + 1)
    chosen = jax.random.randint(second_key, (groups, 1), 0, SEQ_DEV)
    full_one = jnp.arange(SEQ_DEV)[None, :] == chosen
    return jnp.where(full_one, LEN, drawn).reshape(SEQS).astype(jnp.int32)


def block_levels(stream_key, extent, shards, low, top_value):
    loudness, own = 1.0, jax.random.fold_in(stream_key, 6)
    for axis_at, shards_of in shards:
        heights = jnp.exp(jax.random.uniform(jax.random.fold_in(own, axis_at), (shards_of,), jnp.float32, low / len(shards), top_value / len(shards)))
        loudness = loudness * jnp.repeat(heights, extent[axis_at] // shards_of).reshape([-1 if axis == axis_at else 1 for axis in range(len(extent))])
    return loudness


def assign_block(stream_key, own, number, rows, number_of, top, reach, skew):
    ranking = jax.random.permutation(stream_key, number_of)
    heavy_load, common = portions_of(number_of, rows * top, reach, skew, True), portions_of(number_of, rows * top, reach, skew, False)
    places = jnp.arange(number_of)

    def named(tallies, offset_by):
        used = int((tallies > 0).sum())
        fixed = max(1, used // 4)
        moved = fixed + (places - fixed + offset_by * (used - fixed)) % max(1, number_of - fixed)
        return jnp.zeros((number_of,), jnp.int32).at[ranking[jnp.where(places < fixed, places, moved)]].set(jnp.asarray(tallies, jnp.int32))

    tallies = jnp.where(number % 4 == 0, named(heavy_load, number // 4), named(common, number - number // 4 - 1))
    mixed = jax.random.permutation(jax.random.fold_in(own, 3), number_of)
    donor, sink = mixed[0:number_of // 2 * 2:2], mixed[1:number_of // 2 * 2:2]
    margin = jnp.minimum(tallies[donor] - 1, reach - tallies[sink]) // 2
    margin = jnp.where((donor == ranking[0]) | (sink == ranking[0]) | (tallies[sink] == 0), 0, jnp.maximum(margin, 0))
    moved = jax.random.randint(jax.random.fold_in(own, 4), (number_of // 2,), 0, 1 << 20) % (margin + 1)
    tallies = tallies.at[donor].add(-moved).at[sink].add(moved)
    members = jnp.searchsorted(jnp.cumsum(tallies), jnp.arange(rows * top), side="right").astype(jnp.int32)
    table = members.reshape(top, rows).T
    table = table[jax.random.permutation(jax.random.fold_in(own, 1), rows)]
    offset_by = jax.random.randint(jax.random.fold_in(own, 2), (rows, 1), 0, top)
    return jnp.take_along_axis(table, (jnp.arange(top)[None, :] + offset_by) % top, axis=1)


def portions_of(amount, total, reach, slope, full):
    portions = [(1 << 20) // math.isqrt(grade ** slope) + 1 for grade in range(1, amount + 1)]
    largest = reach if full else min(reach, max(-(-total // amount), total * portions[0] // sum(portions)))
    least = 1 if total - largest >= amount - 1 else 0
    given, spare = [largest] + [least] * (amount - 1), total - largest - least * (amount - 1)
    while spare > 0:
        free = [i for i in range(1, amount) if given[i] < largest] or [i for i in range(1, amount) if given[i] < reach]
        mass, left = sum([portions[i] for i in free]), spare
        for i in free:
            extra = min(reach - given[i], max(1, left * portions[i] // mass), spare)
            given[i] = given[i] + extra
            spare = spare - extra
    return np.array(given)


def scatter_about(key, shape, deviation, most, cuts=(), kind=jnp.bfloat16):
    gain = block_levels(key, shape, cuts, -0.22, 0.18) if cuts else 1.0
    values = jax.random.normal(key, shape, jnp.float32) * deviation * gain
    return jnp.minimum(jnp.maximum(values, -most), most).astype(kind)


def setup_inputs(seed: int = 0) -> dict:
    splits = jax.random.split(jax.random.key(seed), 15)
    tokens = scatter_about(splits[0], (SEQS, LEN, D), 1.0, 6.0, ((0, 2), (1, 4)))
    lengths = draw_lengths(jax.random.fold_in(splits[14], 71), 0)
    expert_ids_keys = jax.random.split(jax.random.fold_in(splits[2], 1), SEQS * LEN // SPAN)
    expert_ids_turns = jax.random.permutation(jax.random.fold_in(splits[2], 3), SEQS * LEN // SPAN)
    expert_ids = jax.vmap(lambda own, number: assign_block(jax.random.fold_in(splits[2], 2), own, number, SPAN, EXPERTS, 1, MOST, 2))(expert_ids_keys, expert_ids_turns).reshape((SEQS, LEN, 1))
    attention_gain = jnp.clip(1.0 + 0.1 * jax.random.normal(splits[3], (D,), jnp.float32), 0.5, 1.5).astype(jnp.bfloat16)
    query_weight = scatter_about(splits[4], (D, HEADS * HEAD_DIM), (D * HEAD_DIM // 2) ** -0.5, 0.0390625, ((0, 8), (1, 4)))
    key_weight = scatter_about(splits[5], (D, HEADS * HEAD_DIM), D ** -0.5, 0.21875, ((0, 8), (1, 4)))
    value_weight = scatter_about(splits[6], (D, HEADS * HEAD_DIM), D ** -0.5, 0.21875, ((0, 8), (1, 4)))
    output_weight = scatter_about(splits[7], (HEADS * HEAD_DIM, D), HEADS ** -0.5, 1.75, ((0, 4), (1, 8)))
    position_bias = jnp.clip(jax.random.uniform(splits[8], (NBUCKET, HEADS), jnp.float32, -1.0, 1.0) * block_levels(splits[8], (NBUCKET, HEADS), ((1, 4),), -0.4, 0.0), -1.0, 1.0).astype(jnp.bfloat16)
    feedforward_gain = jnp.clip(1.0 + 0.1 * jax.random.normal(splits[9], (D,), jnp.float32), 0.5, 1.5).astype(jnp.bfloat16)
    router_weight = scatter_about(splits[10], (D, EXPERTS), (4 * D) ** -0.5, 0.109375, ((0, 8),))
    expert_up = scatter_about(splits[11], (EXPERTS, D, FF), D ** -0.5, 0.21875, ((0, 8), (2, 4)))
    expert_down = scatter_about(splits[12], (EXPERTS, FF, D), (2.0 * EXPERTS * FF ** -0.5), 6.0, ((0, 8), (1, 4)))
    cotangent = scatter_about(splits[13], (SEQS, LEN, D), 1.0, 6.0, ((0, 2), (1, 4)))
    return {"tokens": tokens, "lengths": lengths, "expert_ids": expert_ids, "attention_gain": attention_gain, "query_weight": query_weight, "key_weight": key_weight, "value_weight": value_weight, "output_weight": output_weight, "position_bias": position_bias, "feedforward_gain": feedforward_gain, "router_weight": router_weight, "expert_up": expert_up, "expert_down": expert_down, "cotangent": cotangent}


@jax.custom_vjp
def low(v):
    return lax.optimization_barrier(v.astype(jnp.bfloat16)).astype(jnp.float32)

@jax.custom_vjp
def low_back(v):
    return v

def low_keep(v):
    return (low(v), None)

def low_pass(kept, grad):
    return (grad,)

def back_keep(v):
    return (v, None)

def back_low(kept, grad):
    return (low(grad),)
low.defvjp(low_keep, low_pass)
low_back.defvjp(back_keep, back_low)
EPS = 1e-06
bucket_edges = np.array([1, 2, 3, 4, 5, 6, 7, 8, 12, 16, 23, 32, 46, 64, 91], np.int32)

def normalize(vector, scales):
    return vector * lax.rsqrt(lax.optimization_barrier(jnp.mean(vector * vector, axis=-1, keepdims=True)) + EPS) * scales

def buckets(query_pos, key_pos):
    offset = key_pos[None, :] - query_pos[:, None]
    distance = jnp.abs(offset)
    edges = jnp.asarray(bucket_edges)
    magnitude = lax.optimization_barrier(jnp.sum((distance[..., None] >= edges).astype(jnp.int32), axis=-1))
    return magnitude + NBUCKET // 2 * (offset > 0).astype(jnp.int32)

def reference(tokens, lengths, expert_ids, attention_gain, query_weight, key_weight, value_weight, output_weight, position_bias, feedforward_gain, router_weight, expert_up, expert_down, cotangent):
    highest = lax.Precision.HIGHEST
    routed = expert_ids[..., 0]
    blocked = routed.reshape(SEQS, N_SEQ, SPAN)
    routed_hot = (blocked[..., None] == jnp.arange(EXPERTS, dtype=jnp.int32)).astype(jnp.int32)
    slot_index = lax.optimization_barrier(jnp.sum((jnp.cumsum(routed_hot, axis=2) - routed_hot) * routed_hot, axis=-1))
    seq_index = jnp.arange(SEQS, dtype=jnp.int32)[:, None, None]
    block_index = jnp.arange(N_SEQ, dtype=jnp.int32)[None, :, None]
    row_index = ((block_index * N_DP + seq_index // SEQ_DEV) * SEQ_DEV + seq_index % SEQ_DEV) * MOST + slot_index
    row_index = row_index.reshape(SEQS * LEN).astype(jnp.int32)
    expert_flat = routed.reshape(SEQS * LEN).astype(jnp.int32)
    positions = jnp.arange(LEN, dtype=jnp.int32)
    bucket = buckets(positions, positions)
    key_valid = positions[None, :] < lengths[:, None]
    block_width = FF // N_HEAD

    def grouped(array):
        return array.reshape((SEQS // SEQ_DEV, SEQ_DEV) + array.shape[1:])

    def block_forward(inputs, gain_one, query_w, key_w, value_w, output_w, bias_table, gain_two, router_w, up_w, down_w):
        attn_input = low(normalize(inputs, gain_one))

        def project(weight):
            made = jnp.einsum('nld,df->nlf', attn_input, weight, precision=highest)
            return low_back(low(made)).reshape(SEQS, LEN, HEADS, HEAD_DIM)
        queries = project(query_w)
        key_rows = project(key_w)
        value_rows = project(value_w)
        bias_terms = jnp.transpose(bias_table[bucket], (2, 0, 1))

        def attend(group):
            query_part, key_part, value_part, valid_part = group
            dotted = low_back(jnp.einsum('gqhd,gkhd->ghqk', query_part, key_part, precision=highest))
            scores = jnp.where(valid_part[:, None, None, :], dotted + bias_terms[None], -1e+30)
            weights = jax.nn.softmax(scores, axis=-1)
            mixed = jnp.einsum('ghqk,gkhd->gqhd', low(weights), value_part, precision=highest)
            return low_back(low(mixed))
        heads_out = lax.map(jax.checkpoint(attend), (grouped(queries), grouped(key_rows), grouped(value_rows), grouped(key_valid)))
        heads_out = heads_out.reshape(SEQS, LEN, HEADS * HEAD_DIM)
        attention = low_back(jnp.einsum('nlk,kd->nld', heads_out, output_w, precision=highest))
        hidden = inputs + attention
        ffn_input = low(normalize(hidden, gain_two))
        logits = low_back(jnp.einsum('nld,de->nle', ffn_input, router_w, precision=highest))
        router_probs = jax.nn.softmax(logits, axis=-1)
        gate_values = jnp.take_along_axis(router_probs, expert_ids, axis=-1)
        flat_input = ffn_input.reshape(SEQS * LEN, D)
        expert_rows = jnp.zeros((EXPERTS, EXP_ROWS, D), jnp.float32).at[expert_flat, row_index].set(flat_input)
        summed = jnp.zeros((EXPERTS, EXP_ROWS, D), jnp.float32)
        for column in range(N_HEAD):
            first_column = column * block_width
            routed_rows = low_back(expert_rows)
            up_block = lax.slice_in_dim(up_w, first_column, first_column + block_width, axis=2)
            down_block = lax.slice_in_dim(down_w, first_column, first_column + block_width, axis=1)
            hidden_pre = low_back(jnp.einsum('erd,edf->erf', routed_rows, up_block, precision=highest))
            activated = low(jax.nn.gelu(hidden_pre))
            summed = summed + low(jnp.einsum('erf,efd->erd', activated, down_block, precision=highest))
        expert_out = low_back(summed)
        token_out = expert_out[expert_flat, row_index].reshape(SEQS, LEN, D)
        return hidden + gate_values * token_out
    floats = (tokens, attention_gain, query_weight, key_weight, value_weight, output_weight, position_bias, feedforward_gain, router_weight, expert_up, expert_down)
    floats = tuple((item.astype(jnp.float32) for item in floats))
    result, pullback = jax.vjp(block_forward, *floats)
    grads = pullback(cotangent.astype(jnp.float32))
    return (result.astype(jnp.bfloat16), grads[0].astype(jnp.bfloat16), grads[1], grads[2], grads[3], grads[4], grads[5], grads[6], grads[7], grads[8], grads[9], grads[10])
```

```python
import functools

import jax
import jax.numpy as jnp
import numpy as np
from jax import lax
from jax.experimental import pallas as pl
from jax.experimental.pallas import tpu as pltpu
from jax.sharding import PartitionSpec as P

HEAD_DIM = 64
EPS = 1e-06
bucket_edges = np.array([1, 2, 3, 4, 5, 6, 7, 8, 12, 16, 23, 32, 46, 64, 91], np.int32)
ANY = pl.BlockSpec(memory_space=pl.ANY)
VMEM = pl.BlockSpec(memory_space=pltpu.VMEM)
MESH = pl.DeviceIdType.MESH
DMA = pltpu.SemaphoreType.DMA
F32 = jnp.float32
BF16 = jnp.bfloat16


def normalize(vector, scales):
    return vector * lax.rsqrt(jnp.mean(vector * vector, axis=-1, keepdims=True) + EPS) * scales


def gelu_tanh(vector):
    return jax.nn.gelu(vector)


def bucket_of(offset, bucket_count):
    distance = jnp.abs(offset)
    magnitude = jnp.zeros_like(offset)
    for edge in bucket_edges:
        magnitude = magnitude + (distance >= int(edge)).astype(jnp.int32)
    return magnitude + bucket_count // 2 * (offset > 0).astype(jnp.int32)


def send(src, dst, send_sem, recv_sem, **device):
    copy = pltpu.make_async_remote_copy(
        src_ref=src,
        dst_ref=dst,
        send_sem=send_sem,
        recv_sem=recv_sem,
        device_id=device,
        device_id_type=MESH,
    )
    copy.start()
    return copy


def arrived(ref, recv_sem):
    pltpu.make_async_copy(ref, ref, recv_sem).wait()


def greet(devices):
    barrier = pltpu.get_barrier_semaphore()
    for device in devices:
        pl.semaphore_signal(barrier, inc=1, device_id=device, device_id_type=MESH)
    pl.semaphore_wait(barrier, len(devices))


def mod(value, size):
    return lax.rem(value + 2 * size, size)


class Place:
    def __init__(self, seqs, dps):
        self.h, self.s, self.d = lax.axis_index("head"), lax.axis_index("seq"), lax.axis_index("dp")
        self.seqs, self.dps = seqs, dps
        self.near = lax.rem(self.h, 2) * -2 + self.h + 1
        self.across = mod(self.h + 2, 4)
        self.near_across = lax.rem(self.across, 2) * -2 + self.across + 1

    def seq_peers(self):
        return [{"seq": mod(self.s + i, self.seqs)} for i in range(1, self.seqs)]

    def dp_peers(self):
        return [{"dp": mod(self.d + i, self.dps)} for i in range(1, self.dps)]

    def head_pair(self):
        return [{"head": self.near}, {"head": self.across}]

    def group_peers(self):
        return [
            {"seq": mod(self.s + i, self.seqs), "dp": mod(self.d + j, self.dps)}
            for i in range(self.seqs)
            for j in range(self.dps)
            if i or j
        ]

    def block(self, j, h=None):
        return mod((self.h if h is None else h) + 2 * j, 4)


def params(**more):
    return pltpu.CompilerParams(has_side_effects=True, vmem_limit_bytes=56 * 2**20, **more)


def line_gather(me, own, whole, sems, slot):
    (hop_send, hop_recv, dp_send, dp_recv) = sems
    s, d, count = me.s, me.d, me.seqs

    def spread(src, source):
        for i in range(1, me.dps):
            send(
                src,
                whole.at[source, d],
                dp_send.at[i - 1, source],
                dp_recv.at[i - 1, source],
                dp=mod(d + i, me.dps),
            )

    def spread_wait(source):
        for i in range(1, me.dps):
            here = whole.at[source, mod(d - i, me.dps)]
            arrived(here, dp_recv.at[i - 1, source])
            pltpu.make_async_copy(here, here, dp_send.at[i - 1, source]).wait()

    def start():
        @pl.when(s < count - 1)
        def _():
            send(own, whole.at[s, d], hop_send.at[0, s], hop_recv.at[s], seq=s + 1)

        @pl.when(s > 0)
        def _():
            send(own, whole.at[s, d], hop_send.at[1, s], hop_recv.at[s], seq=s - 1)

        spread(own, s)

    def step(t):
        @pl.when(s - t >= 0)
        def _():
            source = s - t
            here = whole.at[source, d]
            arrived(here, hop_recv.at[source])

            @pl.when(s < count - 1)
            def _():
                send(here, here, hop_send.at[0, source], hop_recv.at[source], seq=s + 1)

            spread(here, source)

        @pl.when(s + t < count)
        def _():
            source = s + t
            here = whole.at[source, d]
            arrived(here, hop_recv.at[source])

            @pl.when(s > 0)
            def _():
                send(here, here, hop_send.at[1, source], hop_recv.at[source], seq=s - 1)

            spread(here, source)

    def finish():
        for source in range(count):
            spread_wait(source)
            here = whole.at[source, d]

            @pl.when((s < count - 1) & (source <= s))
            def _():
                pltpu.make_async_copy(here, here, hop_send.at[0, source]).wait()

            @pl.when((s > 0) & (source >= s))
            def _():
                pltpu.make_async_copy(here, here, hop_send.at[1, source]).wait()

    return start, step, finish


def line_sems(seqs, dps):
    return [
        DMA((2, seqs)),
        DMA((seqs,)),
        DMA((max(1, dps - 1), seqs)),
        DMA((max(1, dps - 1), seqs)),
    ]


CHUNKS = 2


def gather_kernel(
    seqs, dps, tok, pack, ids, tok_all, pack_all, ids_all, ls, z_send, z_recv, h_send, h_recv, i_send, i_recv, *sems
):
    me = Place(seqs, dps)
    h, s, d = me.h, me.s, me.d
    per = tok.shape[0] // seqs
    rows = tok.shape[1] // CHUNKS
    own_copies = [pltpu.make_async_copy(tok.at[per * s + j], tok_all.at[j, s], ls.at[j]) for j in range(per)]
    own_copies.append(pltpu.make_async_copy(pack, pack_all.at[s, d], ls.at[per]))
    own_copies.append(pltpu.make_async_copy(ids, ids_all.at[s], ls.at[per + 1]))
    for copy in own_copies:
        copy.start()
    greet(me.seq_peers() + me.dp_peers() + me.head_pair())
    start, step, finish = line_gather(me, pack, pack_all, sems, 0)
    start()
    turn = mod(h - s, 4)
    mine = lax.rem(turn, 2) == 0
    which = lax.div(turn, 2)
    for i in range(1, seqs):
        to = mod(s + i, seqs)
        send(ids, ids_all.at[s], i_send.at[i - 1], i_recv.at[i - 1], seq=to)

    @pl.when(mine)
    def _():
        for c in range(CHUNKS):
            for i in range(1, seqs):
                to = mod(s + i, seqs)
                part = pl.ds(c * rows, rows)
                send(
                    tok.at[per * to + which, part],
                    tok_all.at[which, s, part],
                    z_send.at[i - 1, c],
                    z_recv.at[which, c],
                    seq=to,
                )

    def at(j, c, head):
        return tok_all.at[j, me.block(j, head), pl.ds(c * rows, rows)]

    for t in range(1, seqs):
        step(t)
    for c in range(CHUNKS):
        for j in range(per):
            here = at(j, c, h)

            @pl.when(me.block(j) != s)
            def _():
                arrived(here, z_recv.at[j, c])
                send(here, here, h_send.at[0, j, c], h_recv.at[0, j, c], head=me.across)
                send(here, here, h_send.at[1, j, c], h_recv.at[1, j, c], head=me.near)

    for c in range(CHUNKS):
        for j in range(per):
            there = at(j, c, me.across)

            @pl.when(me.block(j, me.across) != s)
            def _():
                arrived(there, h_recv.at[0, j, c])
                send(there, there, h_send.at[2, j, c], h_recv.at[2, j, c], head=me.near)

    for c in range(CHUNKS):
        for j in range(per):
            here = at(j, c, h)

            @pl.when(me.block(j) != s)
            def _():
                for k in range(2):
                    pltpu.make_async_copy(here, here, h_send.at[k, j, c]).wait()

            @pl.when(me.block(j, me.across) != s)
            def _():
                pltpu.make_async_copy(here, here, h_send.at[2, j, c]).wait()

            @pl.when(me.block(j, me.near) != s)
            def _():
                arrived(at(j, c, me.near), h_recv.at[1, j, c])

            @pl.when(me.block(j, me.near_across) != s)
            def _():
                arrived(at(j, c, me.near_across), h_recv.at[2, j, c])

    for i in range(1, seqs):
        arrived(ids_all.at[mod(s - i, seqs)], i_recv.at[i - 1])
        pltpu.make_async_copy(ids, ids, i_send.at[i - 1]).wait()

    @pl.when(mine)
    def _():
        for c in range(CHUNKS):
            for i in range(1, seqs):
                part = tok.at[0, pl.ds(c * rows, rows)]
                pltpu.make_async_copy(part, part, z_send.at[i - 1, c]).wait()

    finish()
    for copy in own_copies:
        copy.wait()


def gather_inputs(tokens, pack, ids, seqs, dps):
    seq_local, span, width = tokens.shape
    per = seq_local // seqs
    return pl.pallas_call(
        functools.partial(gather_kernel, seqs, dps),
        out_shape=(
            jax.ShapeDtypeStruct((per, seqs, span, width), BF16),
            jax.ShapeDtypeStruct((seqs, dps) + pack.shape, BF16),
            jax.ShapeDtypeStruct((seqs,) + ids.shape, jnp.int32),
        ),
        in_specs=[ANY] * 3,
        out_specs=[ANY] * 3,
        scratch_shapes=[
            DMA((per + 2,)),
            DMA((seqs - 1, CHUNKS)),
            DMA((per, CHUNKS)),
            DMA((3, per, CHUNKS)),
            DMA((3, per, CHUNKS)),
            DMA((seqs - 1,)),
            DMA((seqs - 1,)),
        ]
        + line_sems(seqs, dps),
        compiler_params=params(collective_id=0),
        name="gather_inputs",
    )(tokens, pack, ids)


def heads_kernel(
    seqs, dps, out, cot, pack, out_all, cot_own, pack_all, weight_all, ls, z_send, z_recv, a_send, a_recv, w_send, w_recv, *sems
):
    me = Place(seqs, dps)
    h, s, d = me.h, me.s, me.d
    per = cot_own.shape[0]
    greet(me.seq_peers() + me.dp_peers() + [{"head": mod(h + i, 4)} for i in range(1, 4)])
    start, step, finish = line_gather(me, pack, pack_all, sems, 0)
    copies = []
    for i in range(1, 4):
        to = mod(h + i, 4)
        for j in range(per):
            copies.append(
                send(
                    out.at[j, me.block(j, to)],
                    out_all.at[h, j],
                    a_send.at[i - 1, j],
                    a_recv.at[i - 1, j],
                    head=to,
                )
            )
    own_copies = [pltpu.make_async_copy(out.at[j, me.block(j)], out_all.at[h, j], ls.at[j]) for j in range(per)]
    own_copies.append(pltpu.make_async_copy(pack, pack_all.at[s, d], ls.at[per]))
    for copy in own_copies:
        copy.start()
    start()
    turn = mod(h - s, 4)
    mine = lax.rem(turn, 2) == 0
    which = lax.div(turn, 2)

    @pl.when(mine)
    def _():
        for i in range(1, seqs):
            to = mod(s + i, seqs)
            send(cot.at[per * to + which], cot_own.at[which], z_send.at[i - 1], z_recv.at[which], seq=to)
        own = pltpu.make_async_copy(cot.at[per * s + which], cot_own.at[which], ls.at[per + 1])
        own.start()
        own.wait()

    for t in range(1, seqs):
        step(t)
    for copy in own_copies:
        copy.wait()
    finish()
    lanes = weight_all.shape[-1]
    gone = []
    for i in range(1, 4):
        gone.append(
            send(
                pack_all.at[:, :, :, pl.ds(0, lanes)],
                weight_all.at[h],
                w_send.at[i - 1],
                w_recv.at[i - 1],
                head=mod(h + i, 4),
            )
        )
    own = pltpu.make_async_copy(pack_all.at[:, :, :, pl.ds(0, lanes)], weight_all.at[h], ls.at[0])
    own.start()
    own.wait()
    for j in range(per):

        @pl.when(me.block(j) != s)
        def _():
            arrived(cot_own.at[j], z_recv.at[j])

    @pl.when(mine)
    def _():
        for i in range(1, seqs):
            pltpu.make_async_copy(cot.at[0], cot.at[0], z_send.at[i - 1]).wait()

    for copy in copies + gone:
        copy.wait_send()
    for i in range(1, 4):
        source = mod(h - i, 4)
        for j in range(per):
            arrived(out_all.at[source, j], a_recv.at[i - 1, j])
        arrived(weight_all.at[source], w_recv.at[i - 1])


def gather_heads(out, cot, pack, seqs, dps, lanes):
    per, _, span, width = out.shape
    return pl.pallas_call(
        functools.partial(heads_kernel, seqs, dps),
        out_shape=(
            jax.ShapeDtypeStruct((4, per, span, width), BF16),
            jax.ShapeDtypeStruct((per,) + cot.shape[1:], BF16),
            jax.ShapeDtypeStruct((seqs, dps) + pack.shape, BF16),
            jax.ShapeDtypeStruct((4, seqs, dps, pack.shape[0], lanes), BF16),
        ),
        in_specs=[ANY] * 3,
        out_specs=[ANY] * 4,
        scratch_shapes=[
            DMA((per + 2,)),
            DMA((seqs - 1,)),
            DMA((per,)),
            DMA((3, per)),
            DMA((3, per)),
            DMA((3,)),
            DMA((3,)),
        ]
        + line_sems(seqs, dps),
        compiler_params=params(collective_id=1),
        name="gather_heads",
    )(out, cot, pack)


def dispatch_kernel(seqs, dps, rows, taken, ls, g_send, g_recv, h_send, h_recv):
    me = Place(seqs, dps)
    h, s, d = me.h, me.s, me.d
    groups, parts = seqs * dps, rows.shape[0]
    me_group = s * dps + d
    greet(me.group_peers() + me.head_pair())
    others = [(i, j) for i in range(seqs) for j in range(dps) if i or j]
    for part in range(parts):
        pltpu.make_async_copy(rows.at[part, me_group], taken.at[h, part, me_group], ls.at[part]).start()
        for n, (i, j) in enumerate(others):
            to_s, to_d = mod(s + i, seqs), mod(d + j, dps)
            send(
                rows.at[part, to_s * dps + to_d],
                taken.at[h, part, me_group],
                g_send.at[part, n],
                g_recv.at[part, n],
                seq=to_s,
                dp=to_d,
            )

    def from_of(n):
        i, j = others[n]
        return mod(s - i, seqs) * dps + mod(d - j, dps)

    for part in range(parts):
        for n in range(-1, len(others)):
            source = me_group if n < 0 else from_of(n)
            here = taken.at[h, part, source]
            if n < 0:
                pltpu.make_async_copy(here, here, ls.at[part]).wait()
            else:
                arrived(here, g_recv.at[part, n])
            send(here, here, h_send.at[0, part, n + 1], h_recv.at[0, part, n + 1], head=me.across)
            send(here, here, h_send.at[1, part, n + 1], h_recv.at[1, part, n + 1], head=me.near)
    for part in range(parts):
        for n in range(-1, len(others)):
            source = me_group if n < 0 else from_of(n)
            there = taken.at[me.across, part, source]
            arrived(there, h_recv.at[0, part, n + 1])
            send(there, there, h_send.at[2, part, n + 1], h_recv.at[2, part, n + 1], head=me.near)
    for part in range(parts):
        for n in range(-1, len(others)):
            source = me_group if n < 0 else from_of(n)
            here = taken.at[h, part, source]
            for k in range(3):
                pltpu.make_async_copy(here, here, h_send.at[k, part, n + 1]).wait()
            if n >= 0:
                pltpu.make_async_copy(here, here, g_send.at[part, n]).wait()
            arrived(taken.at[me.near, part, source], h_recv.at[1, part, n + 1])
            arrived(taken.at[me.near_across, part, source], h_recv.at[2, part, n + 1])


def dispatch(rows, seqs, dps):
    parts, groups = rows.shape[:2]
    return pl.pallas_call(
        functools.partial(dispatch_kernel, seqs, dps),
        out_shape=jax.ShapeDtypeStruct((4,) + rows.shape, BF16),
        in_specs=[ANY],
        out_specs=ANY,
        scratch_shapes=[
            DMA((parts,)),
            DMA((parts, groups)),
            DMA((parts, groups)),
            DMA((3, parts, groups)),
            DMA((3, parts, groups)),
        ],
        compiler_params=params(collective_id=2),
        name="dispatch",
    )(rows)


def combine_kernel(
    seqs, dps, partial, summed, own, near, far_out, far_in, total, ls, n_send, n_recv, x_send, x_recv, g_send, g_recv
):
    me = Place(seqs, dps)
    h, s, d = me.h, me.s, me.d
    groups, parts = seqs * dps, summed.shape[0]
    me_group = s * dps + d
    greet(me.group_peers() + me.head_pair())
    others = [(i, j) for i in range(seqs) for j in range(dps) if i or j] + [(0, 0)]
    order = [(part, n) for part in range(parts) for n in range(groups)]

    def group_of(n):
        i, j = others[n]
        return mod(s + i, seqs), mod(d + j, dps)

    for part, n in order:
        to_s, to_d = group_of(n)
        group = to_s * dps + to_d
        for k, head in enumerate((me.near_across, me.near)):
            send(
                partial.at[head, part, group],
                near.at[k, part, n],
                n_send.at[k, part, n],
                n_recv.at[k, part, n],
                head=me.near,
            )
        for k, head in enumerate((me.across, h)):
            pltpu.make_async_copy(partial.at[head, part, group], own.at[k, part, n], ls.at[k, part, n]).start()
    for part, n in order:
        arrived(near.at[0, part, n], n_recv.at[0, part, n])
        pltpu.make_async_copy(own.at[0, part, n], own.at[0, part, n], ls.at[0, part, n]).wait()
        both = own[0, part, n].astype(F32) + near[0, part, n].astype(F32)
        far_out[part, n] = both.astype(BF16)
        send(far_out.at[part, n], far_in.at[part, n], x_send.at[part, n], x_recv.at[part, n], head=me.across)
    for part, n in order:
        to_s, to_d = group_of(n)
        arrived(near.at[1, part, n], n_recv.at[1, part, n])
        pltpu.make_async_copy(own.at[1, part, n], own.at[1, part, n], ls.at[1, part, n]).wait()
        arrived(far_in.at[part, n], x_recv.at[part, n])
        both = own[1, part, n].astype(F32) + near[1, part, n].astype(F32) + far_in[part, n].astype(F32)
        total[part, n] = both.astype(BF16)
        if n < groups - 1:
            send(
                total.at[part, n],
                summed.at[part, me_group],
                g_send.at[part, n],
                g_recv.at[part, n],
                seq=to_s,
                dp=to_d,
            )
        else:
            pltpu.make_async_copy(total.at[part, n], summed.at[part, me_group], g_send.at[part, n]).start()
    for part, n in order:
        i, j = others[n]
        for k in range(2):
            pltpu.make_async_copy(near.at[k, part, n], near.at[k, part, n], n_send.at[k, part, n]).wait()
        pltpu.make_async_copy(far_out.at[part, n], far_out.at[part, n], x_send.at[part, n]).wait()
        pltpu.make_async_copy(total.at[part, n], total.at[part, n], g_send.at[part, n]).wait()
        if n < groups - 1:
            source = mod(s - i, seqs) * dps + mod(d - j, dps)
            arrived(summed.at[part, source], g_recv.at[part, n])


def combine(partial, seqs, dps):
    _, parts, groups, rows, width = partial.shape
    block = (parts, groups, rows, width)
    return pl.pallas_call(
        functools.partial(combine_kernel, seqs, dps),
        out_shape=jax.ShapeDtypeStruct(block, BF16),
        in_specs=[ANY],
        out_specs=ANY,
        scratch_shapes=[
            pltpu.VMEM((2,) + block, BF16),
            pltpu.VMEM((2,) + block, BF16),
            pltpu.VMEM(block, BF16),
            pltpu.VMEM(block, BF16),
            pltpu.VMEM(block, BF16),
        ]
        + [DMA((2, parts, groups))] * 3
        + [DMA((parts, groups))] * 4,
        compiler_params=params(collective_id=3),
        name="combine",
    )(partial)


def send_home(me, own, home, ls, z_send, z_recv, h_send, h_recv):
    h, s, seqs = me.h, me.s, me.seqs
    per = own.shape[0]
    turn = mod(s - h, 4)
    mine = lax.rem(turn, 2) == 0
    which = lax.div(turn, 2)

    def start():
        for j in range(per):
            to = me.block(j)

            @pl.when(to != s)
            def _():
                send(own.at[j], home.at[per * s + j], z_send.at[j], z_recv.at[s], seq=to)

            @pl.when(to == s)
            def _():
                pltpu.make_async_copy(own.at[j], home.at[per * s + j], ls).start()

    def forward():
        @pl.when(mine)
        def _():
            for i in range(seqs):
                source = mod(s + i, seqs)
                here = home.at[per * source + which]
                if i == 0:
                    pltpu.make_async_copy(here, here, ls).wait()
                else:
                    arrived(here, z_recv.at[source])
                send(here, here, h_send.at[0, source], h_recv.at[0, source], head=me.across)
                send(here, here, h_send.at[1, source], h_recv.at[1, source], head=me.near)
            for i in range(seqs):
                source = mod(s + i, seqs)
                there = home.at[per * source + 1 - which]
                arrived(there, h_recv.at[0, source])
                send(there, there, h_send.at[2, source], h_recv.at[2, source], head=me.near)

    def finish():
        for j in range(per):

            @pl.when(me.block(j) != s)
            def _():
                pltpu.make_async_copy(own.at[j], own.at[j], z_send.at[j]).wait()

        @pl.when(mine)
        def _():
            for source in range(seqs):
                for k in range(3):
                    here = home.at[per * source]
                    pltpu.make_async_copy(here, here, h_send.at[k, source]).wait()

        @pl.when(jnp.logical_not(mine))
        def _():
            for source in range(seqs):
                arrived(home.at[per * source], h_recv.at[1, source])
                arrived(home.at[per * source + 1], h_recv.at[2, source])

    return start, forward, finish


def home_sems(per, seqs):
    return [DMA(()), DMA((per,)), DMA((seqs,)), DMA((3, seqs)), DMA((3, seqs))]


def grads_kernel(seqs, dps, grad, result, grad_all, home, ls, a_send, a_recv, *sems):
    me = Place(seqs, dps)
    h = me.h
    per = result.shape[0]
    start, forward, finish = send_home(me, result, home, *sems)
    greet(me.seq_peers() + [{"head": mod(h + i, 4)} for i in range(1, 4)])
    copies = []
    for i in range(1, 4):
        to = mod(h + i, 4)
        for j in range(per):
            copies.append(
                send(
                    grad.at[to, j],
                    grad_all.at[j, me.block(j)],
                    a_send.at[i - 1, j],
                    a_recv.at[i - 1, j],
                    head=to,
                )
            )
    own_copies = [pltpu.make_async_copy(grad.at[h, j], grad_all.at[j, me.block(j)], ls.at[j]) for j in range(per)]
    for copy in own_copies:
        copy.start()
    start()
    forward()
    finish()
    for copy in own_copies:
        copy.wait()
    for copy in copies:
        copy.wait_send()
    for i in range(1, 4):
        source = mod(h - i, 4)
        for j in range(per):
            arrived(grad_all.at[j, me.block(j, source)], a_recv.at[i - 1, j])


def gather_grads(grad, result, seqs, dps):
    _, per, span, width = grad.shape
    return pl.pallas_call(
        functools.partial(grads_kernel, seqs, dps),
        out_shape=(
            jax.ShapeDtypeStruct((per, seqs, span, width), BF16),
            jax.ShapeDtypeStruct((per * seqs,) + result.shape[1:], BF16),
        ),
        in_specs=[ANY] * 2,
        out_specs=[ANY] * 2,
        scratch_shapes=[DMA((per,)), DMA((3, per)), DMA((3, per))] + home_sems(per, seqs),
        compiler_params=params(collective_id=4),
        name="gather_grads",
    )(grad, result)


def input_kernel(
    seqs, dps, partial, weight, total, weight_out, own, near, far_out, far_in, wown, wnear, wfar_out, wfar_in,
    ls, n_send, n_recv, x_send, x_recv, wls, wn_send, wn_recv, wx_send, wx_recv
):
    me = Place(seqs, dps)
    h = me.h
    per = total.shape[0]
    greet(me.head_pair())
    for j in range(per):
        for k, head in enumerate((me.near_across, me.near)):
            send(partial.at[j, me.block(j, head)], near.at[k, j], n_send.at[k, j], n_recv.at[k, j], head=me.near)
        for k, head in enumerate((me.across, h)):
            pltpu.make_async_copy(partial.at[j, me.block(j, head)], own.at[k, j], ls.at[k, j]).start()
    for k, head in enumerate((me.near_across, me.near)):
        send(weight.at[head], wnear.at[k], wn_send.at[k], wn_recv.at[k], head=me.near)
    for k, head in enumerate((me.across, h)):
        pltpu.make_async_copy(weight.at[head], wown.at[k], wls.at[k]).start()
    for j in range(per):
        arrived(near.at[0, j], n_recv.at[0, j])
        pltpu.make_async_copy(own.at[0, j], own.at[0, j], ls.at[0, j]).wait()
        far_out[j] = (own[0, j].astype(F32) + near[0, j].astype(F32)).astype(BF16)
        send(far_out.at[j], far_in.at[j], x_send.at[j], x_recv.at[j], head=me.across)
    arrived(wnear.at[0], wn_recv.at[0])
    pltpu.make_async_copy(wown.at[0], wown.at[0], wls.at[0]).wait()
    wfar_out[...] = (wown[0].astype(F32) + wnear[0].astype(F32)).astype(BF16)
    send(wfar_out, wfar_in, wx_send, wx_recv, head=me.across)
    for j in range(per):
        arrived(near.at[1, j], n_recv.at[1, j])
        pltpu.make_async_copy(own.at[1, j], own.at[1, j], ls.at[1, j]).wait()
        arrived(far_in.at[j], x_recv.at[j])
        total[j] = own[1, j].astype(F32) + near[1, j].astype(F32) + far_in[j].astype(F32)
    arrived(wnear.at[1], wn_recv.at[1])
    pltpu.make_async_copy(wown.at[1], wown.at[1], wls.at[1]).wait()
    arrived(wfar_in, wx_recv)
    weight_out[...] = wown[1].astype(F32) + wnear[1].astype(F32) + wfar_in[...].astype(F32)
    for j in range(per):
        for k in range(2):
            pltpu.make_async_copy(near.at[k, j], near.at[k, j], n_send.at[k, j]).wait()
        pltpu.make_async_copy(far_out.at[j], far_out.at[j], x_send.at[j]).wait()
    for k in range(2):
        pltpu.make_async_copy(wnear.at[k], wnear.at[k], wn_send.at[k]).wait()
    pltpu.make_async_copy(wfar_out, wfar_out, wx_send).wait()


def add_heads(partial, weight, seqs, dps):
    per, _, span, width = partial.shape
    block = (per, span, width)
    wblock = weight.shape[1:]
    return pl.pallas_call(
        functools.partial(input_kernel, seqs, dps),
        out_shape=(jax.ShapeDtypeStruct(block, F32), jax.ShapeDtypeStruct(wblock, F32)),
        in_specs=[ANY] * 2,
        out_specs=[VMEM] * 2,
        scratch_shapes=[
            pltpu.VMEM((2,) + block, BF16),
            pltpu.VMEM((2,) + block, BF16),
            pltpu.VMEM(block, BF16),
            pltpu.VMEM(block, BF16),
            pltpu.VMEM((2,) + wblock, BF16),
            pltpu.VMEM((2,) + wblock, BF16),
            pltpu.VMEM(wblock, BF16),
            pltpu.VMEM(wblock, BF16),
        ]
        + [DMA((2, per))] * 3
        + [DMA((per,))] * 2
        + [DMA((2,))] * 3
        + [DMA(())] * 2,
        compiler_params=params(collective_id=5),
        name="add_heads",
    )(partial, weight)


def last_kernel(
    seqs, dps, grad, weights, bias, home, weights_sum, bias_sum, wsum, wtake, ytake, btake, small,
    ls, y_send, y_recv, w_send, w_recv, b_send, b_recv, s_send, s_recv, *sems
):
    me = Place(seqs, dps)
    h, s, d = me.h, me.s, me.d
    start, forward, finish = send_home(me, grad, home, *sems)
    others = [(i, j) for i in range(seqs) for j in range(dps) if i or j]
    greet(me.group_peers() + [{"head": mod(h + i, 4)} for i in range(1, 4)])
    for i in range(1, dps):
        to = mod(d + i, dps)
        send(weights.at[to], ytake.at[i - 1], y_send.at[i - 1], y_recv.at[i - 1], dp=to)
    mine_y = pltpu.make_async_copy(weights.at[d], wsum, ls)
    mine_y.start()
    for n, (i, j) in enumerate(others):
        send(bias, btake.at[n], b_send.at[n], b_recv.at[n], seq=mod(s + i, seqs), dp=mod(d + j, dps))
    start()
    mine_y.wait()
    for i in range(1, dps):
        arrived(ytake.at[i - 1], y_recv.at[i - 1])
    for t in range(seqs):
        acc = wsum[t].astype(F32)
        for i in range(1, dps):
            acc = acc + ytake[i - 1, t].astype(F32)
        wsum[t] = acc.astype(BF16)
    for i in range(1, seqs):
        to = mod(s + i, seqs)
        send(wsum.at[to], wtake.at[i - 1], w_send.at[i - 1], w_recv.at[i - 1], seq=to)
    forward()
    acc = wsum[s].astype(F32)
    for i in range(1, seqs):
        arrived(wtake.at[i - 1], w_recv.at[i - 1])
        acc = acc + wtake[i - 1].astype(F32)
    weights_sum[...] = acc
    lanes = small.shape[-1]
    small[0] = acc[:, acc.shape[-1] - lanes :]
    for i in range(1, 4):
        send(small.at[0], small.at[i], s_send.at[i - 1], s_recv.at[i - 1], head=mod(h + i, 4))
    total = bias[...]
    for n in range(len(others)):
        arrived(btake.at[n], b_recv.at[n])
        total = total + btake[n]
    bias_sum[...] = total
    tail = small[0]
    for i in range(1, 4):
        arrived(small.at[i], s_recv.at[i - 1])
        tail = tail + small[i]
    weights_sum[:, acc.shape[-1] - lanes :] = tail
    for i in range(1, 4):
        pltpu.make_async_copy(small.at[0], small.at[0], s_send.at[i - 1]).wait()
    for i in range(1, dps):
        pltpu.make_async_copy(ytake.at[0], ytake.at[0], y_send.at[i - 1]).wait()
    for i in range(1, seqs):
        pltpu.make_async_copy(wsum.at[0], wsum.at[0], w_send.at[i - 1]).wait()
    for n in range(len(others)):
        pltpu.make_async_copy(btake.at[0], btake.at[0], b_send.at[n]).wait()
    finish()


def finish_grads(grad, weights, bias, seqs, dps, small):
    per, span, width = grad.shape
    _, _, rows, lanes = weights.shape
    groups = seqs * dps
    return pl.pallas_call(
        functools.partial(last_kernel, seqs, dps),
        out_shape=(
            jax.ShapeDtypeStruct((per * seqs, span, width), BF16),
            jax.ShapeDtypeStruct((rows, lanes), F32),
            jax.ShapeDtypeStruct(bias.shape, F32),
        ),
        in_specs=[ANY, ANY, VMEM],
        out_specs=[ANY, VMEM, VMEM],
        scratch_shapes=[
            pltpu.VMEM((seqs, rows, lanes), BF16),
            pltpu.VMEM((seqs - 1, rows, lanes), BF16),
            pltpu.VMEM((max(1, dps - 1), seqs, rows, lanes), BF16),
            pltpu.VMEM((groups - 1,) + bias.shape, F32),
            pltpu.VMEM((4, rows, small), F32),
            DMA(()),
            DMA((max(1, dps - 1),)),
            DMA((max(1, dps - 1),)),
            DMA((seqs - 1,)),
            DMA((seqs - 1,)),
            DMA((groups - 1,)),
            DMA((groups - 1,)),
            DMA((3,)),
            DMA((3,)),
        ]
        + home_sems(per, seqs),
        compiler_params=params(collective_id=6),
        name="finish_grads",
    )(grad, weights, bias)


def bias_block(band, far, head, q_block, k_block, span):
    step = k_block - q_block
    if abs(step) <= 1:
        return band[head, :, (step + 1) * span : (step + 2) * span]
    return far[head, 0 if step < 0 else 1]


def attend_kernel(heads, blocks, span, q_ref, k_ref, v_ref, band, far, mask, out_ref, prob_ref):
    for head in range(heads):
        cols = slice(head * HEAD_DIM, (head + 1) * HEAD_DIM)
        key = k_ref[0, :, cols]
        value = v_ref[0, :, cols]
        for q_block in range(blocks):
            rows = slice(q_block * span, (q_block + 1) * span)
            query = q_ref[0, rows, cols]
            scores = lax.dot_general(query, key, (((1,), (1,)), ((), ())), preferred_element_type=F32)
            parts = []
            for k_block in range(blocks):
                part = scores[:, k_block * span : (k_block + 1) * span]
                valid = mask[0, :, k_block * span : (k_block + 1) * span]
                term = bias_block(band, far, head, q_block, k_block, span)
                parts.append(jnp.where(valid > 0, part + term, -1e30))
            scores = jnp.concatenate(parts, axis=1)
            top = jnp.max(scores, axis=-1, keepdims=True)
            grown = jnp.exp(scores - top)
            total = jnp.sum(grown, axis=-1, keepdims=True)
            weights = (grown * (1.0 / total)).astype(BF16)
            prob_ref[0, head, rows, :] = weights
            mixed = jnp.dot(weights, value, preferred_element_type=F32)
            out_ref[0, rows, cols] = mixed.astype(BF16)


def attend(queries, keys, values, band, far, mask, heads, blocks, span):
    per, length, width = queries.shape
    whole = pl.BlockSpec((1, length, width), lambda j: (j, 0, 0))
    return pl.pallas_call(
        functools.partial(attend_kernel, heads, blocks, span),
        grid=(per,),
        out_shape=(
            jax.ShapeDtypeStruct((per, length, width), BF16),
            jax.ShapeDtypeStruct((per, heads, length, length), BF16),
        ),
        in_specs=[
            whole,
            whole,
            whole,
            pl.BlockSpec(band.shape, lambda j: (0, 0, 0)),
            pl.BlockSpec(memory_space=pltpu.SMEM),
            pl.BlockSpec((1, 1, length), lambda j: (j, 0, 0)),
        ],
        out_specs=[whole, pl.BlockSpec((1, heads, length, length), lambda j: (j, 0, 0, 0))],
        compiler_params=pltpu.CompilerParams(vmem_limit_bytes=56 * 2**20),
        name="attend",
    )(queries, keys, values, band, far, mask)


def attend_back_kernel(
    heads, blocks, span, q_ref, k_ref, v_ref, g_ref, p_ref, dq_ref, dk_ref, dv_ref, band_ref, far_ref, dk_sum, dv_sum
):
    first = pl.program_id(0) == 0
    for head in range(heads):
        cols = slice(head * HEAD_DIM, (head + 1) * HEAD_DIM)
        key = k_ref[0, :, cols]
        value = v_ref[0, :, cols]
        for q_block in range(blocks):
            rows = slice(q_block * span, (q_block + 1) * span)
            query = q_ref[0, rows, cols]
            grad = g_ref[0, rows, cols]
            weights = p_ref[0, head, rows, :]
            prob_grad = lax.dot_general(grad, value, (((1,), (1,)), ((), ())), preferred_element_type=F32)
            wide = weights.astype(F32)
            delta = jnp.sum(wide * prob_grad, axis=-1, keepdims=True)
            score_grad = wide * (prob_grad - delta)
            for k_block in range(blocks):
                part = score_grad[:, k_block * span : (k_block + 1) * span]
                step = k_block - q_block
                if abs(step) <= 1:
                    where = (head, slice(None), slice((step + 1) * span, (step + 2) * span))
                    begin = first & (q_block == (1 if step < 0 else 0))
                    old = band_ref[where]
                    band_ref[where] = jnp.where(begin, 0.0, old) + part
                else:
                    side = 0 if step < 0 else 1
                    begin = first & ((q_block, k_block) == ((2, 0) if side == 0 else (0, 2)))
                    flat = jnp.sum(part.reshape(span // 8, 8, span), axis=0)
                    old = far_ref[head, side]
                    far_ref[head, side] = jnp.where(begin, 0.0, old) + flat
            low = score_grad.astype(BF16)
            dq_ref[0, rows, cols] = jnp.dot(low, key, preferred_element_type=F32).astype(BF16)
            dk = lax.dot_general(low, query, (((0,), (0,)), ((), ())), preferred_element_type=F32)
            dv = lax.dot_general(weights, grad, (((0,), (0,)), ((), ())), preferred_element_type=F32)
            if q_block == 0:
                dk_sum[...] = dk
                dv_sum[...] = dv
            else:
                dk_sum[...] += dk
                dv_sum[...] += dv
        dk_ref[0, :, cols] = dk_sum[...].astype(BF16)
        dv_ref[0, :, cols] = dv_sum[...].astype(BF16)


def attend_back(queries, keys, values, grads, probs, heads, blocks, span):
    per, length, width = queries.shape
    whole = pl.BlockSpec((1, length, width), lambda j: (j, 0, 0))
    return pl.pallas_call(
        functools.partial(attend_back_kernel, heads, blocks, span),
        grid=(per,),
        out_shape=(
            jax.ShapeDtypeStruct((per, length, width), BF16),
            jax.ShapeDtypeStruct((per, length, width), BF16),
            jax.ShapeDtypeStruct((per, length, width), BF16),
            jax.ShapeDtypeStruct((heads, span, 3 * span), F32),
            jax.ShapeDtypeStruct((heads, 2, 8, span), F32),
        ),
        in_specs=[whole] * 4 + [pl.BlockSpec((1, heads, length, length), lambda j: (j, 0, 0, 0))],
        out_specs=[whole] * 3
        + [
            pl.BlockSpec((heads, span, 3 * span), lambda j: (0, 0, 0)),
            pl.BlockSpec((heads, 2, 8, span), lambda j: (0, 0, 0, 0)),
        ],
        scratch_shapes=[pltpu.VMEM((length, HEAD_DIM), F32)] * 2,
        compiler_params=pltpu.CompilerParams(vmem_limit_bytes=56 * 2**20),
        name="attend_back",
    )(queries, keys, values, grads, probs)


def up_to(value, unit):
    return -(-value // unit) * unit


def body(
    tokens,
    lengths,
    expert_ids,
    attention_gain,
    query_weight,
    key_weight,
    value_weight,
    output_weight,
    position_bias,
    feedforward_gain,
    router_weight,
    expert_up,
    expert_down,
    cotangent,
):
    seqs, dps = lax.axis_size("seq"), lax.axis_size("dp")
    groups = seqs * dps
    seq_local, span, width = tokens.shape
    per = seq_local // seqs
    length = seqs * span
    count = per * length
    own_rows = per * span
    local_width = query_weight.shape[1]
    bucket_count, heads = position_bias.shape
    experts = router_weight.shape[1]
    exp_local = expert_up.shape[0]
    shard = query_weight.shape[0]
    head_at, seq_at = lax.axis_index("head"), lax.axis_index("seq")

    first_width = up_to(3 * local_width + 1, 128)
    first_pack = jnp.concatenate(
        [
            query_weight,
            key_weight,
            value_weight,
            attention_gain[:, None],
            jnp.zeros((shard, first_width - 3 * local_width - 1), BF16),
        ],
        axis=1,
    )
    lanes = up_to(local_width, 128)
    small = up_to(experts + 1, 128)
    second_pack = jnp.concatenate(
        [
            output_weight.T,
            jnp.zeros((shard, lanes - local_width), BF16),
            router_weight,
            feedforward_gain[:, None],
            jnp.zeros((shard, small - experts - 1), BF16),
        ],
        axis=1,
    )
    ids = expert_ids.reshape(seq_local, span)
    tok_all, first_all, ids_all = gather_inputs(tokens, first_pack, ids, seqs, dps)
    first_all = first_all.reshape(width, first_width)
    project_weight = first_all[:, : 3 * local_width]
    gain_one = first_all[:, 3 * local_width].astype(F32)

    inputs = tok_all.reshape(count, width).astype(F32)
    attn_input = normalize(inputs, gain_one).astype(BF16)
    made = jnp.dot(attn_input, project_weight, preferred_element_type=F32).astype(BF16)
    queries, keys, values = (
        made[:, i * local_width : (i + 1) * local_width].reshape(per, length, local_width) for i in range(3)
    )
    offset = jnp.arange(3 * span, dtype=jnp.int32)[None, :] - span - jnp.arange(span, dtype=jnp.int32)[:, None]
    bucket = bucket_of(offset, bucket_count)
    table = position_bias.astype(F32)
    band = jnp.zeros((heads, span, 3 * span), F32)
    for b in range(bucket_count):
        band = jnp.where((bucket == b)[None], table[b][:, None, None], band)
    far = jnp.stack([table[bucket_count // 2 - 1], table[bucket_count - 1]], axis=1)
    own_lengths = lax.dynamic_slice_in_dim(lengths, per * seq_at, per)
    mask = (jnp.arange(length, dtype=jnp.int32)[None, None, :] < own_lengths[:, None, None]).astype(F32)
    heads_out, probs = attend(queries, keys, values, band, far, mask, heads, seqs, span)

    heads_all, cot_own, second_all, out_weight = gather_heads(
        heads_out.reshape(per, seqs, span, local_width), cotangent, second_pack, seqs, dps, lanes
    )
    second_all = second_all.reshape(width, lanes + small)
    router_full = second_all[:, lanes : lanes + experts]
    gain_two = second_all[:, lanes + experts].astype(F32)
    out_weight = out_weight.reshape(4, width, lanes)[:, :, :local_width]
    heads_all = heads_all.reshape(4, own_rows, local_width)
    own_blocks = [lax.rem(head_at + 2 * j, 4) for j in range(per)]
    own_inputs = jnp.stack([lax.dynamic_index_in_dim(tok_all[j], own_blocks[j], 0, False) for j in range(per)])
    own_inputs = own_inputs.reshape(own_rows, width).astype(F32)
    attention = jnp.einsum("htk,hdk->td", heads_all, out_weight, preferred_element_type=F32)
    hidden = own_inputs + attention
    ffn_input = normalize(hidden, gain_two).astype(BF16)
    logits = jnp.dot(ffn_input, router_full, preferred_element_type=F32)
    router_probs = jax.nn.softmax(logits, axis=-1)

    capacity = max(2, (5 * span + 4 * experts - 1) // (4 * experts))
    own_ids = jnp.stack(
        [
            lax.dynamic_index_in_dim(lax.dynamic_index_in_dim(ids_all, own_blocks[j], 0, False), per * seq_at + j, 0, False)
            for j in range(per)
        ]
    )
    earlier = jnp.arange(span)[None, :] < jnp.arange(span)[:, None]
    same = (own_ids[:, :, None] == own_ids[:, None, :]) & earlier[None]
    slot = jnp.sum(same.astype(jnp.int32), axis=-1)
    rows_used = exp_local * per * capacity
    rows_pad = up_to(rows_used, 16)
    place = (
        own_ids // exp_local * rows_pad
        + (own_ids % exp_local * per + jnp.arange(per, dtype=jnp.int32)[:, None]) * capacity
        + slot
    ).reshape(own_rows)
    spots = groups * rows_pad
    place_hot = (jnp.arange(spots, dtype=jnp.int32)[:, None] == place[None, :]).astype(BF16)
    hot = (own_ids.reshape(own_rows, 1) == jnp.arange(experts, dtype=jnp.int32)).astype(F32)
    gate = jnp.sum(router_probs * hot, axis=-1)
    grad_out = cot_own.reshape(own_rows, width).astype(F32)
    sent_grad = (gate[:, None] * grad_out).astype(BF16)
    to_send = jnp.stack([ffn_input, sent_grad])
    rows = jnp.einsum("rt,ptd->prd", place_hot, to_send, preferred_element_type=F32).astype(BF16)
    taken = dispatch(rows.reshape(2, groups, rows_pad, width), seqs, dps)

    def by_expert(part):
        part = taken[:, part, :, :rows_used].reshape(4 * groups, exp_local, per * capacity, width)
        return jnp.swapaxes(part, 0, 1).reshape(exp_local, 4 * groups * per * capacity, width)

    def by_group(part):
        part = jnp.swapaxes(part.reshape(exp_local, 4 * groups, per * capacity, width), 0, 1)
        part = part.reshape(4, groups, rows_used, width)
        return jnp.pad(part, ((0, 0), (0, 0), (0, rows_pad - rows_used), (0, 0)))

    received, grad_rows = by_expert(0), by_expert(1)
    hidden_pre = jnp.einsum("xrd,xdf->xrf", received, expert_up, preferred_element_type=F32)
    activated = gelu_tanh(hidden_pre).astype(BF16)
    partial_out = jnp.einsum("xrf,xfd->xrd", activated, expert_down, preferred_element_type=F32).astype(BF16)
    act_grad = jnp.einsum("xrd,xfd->xrf", grad_rows, expert_down, preferred_element_type=F32)
    _, gelu_pull = jax.vjp(gelu_tanh, hidden_pre)
    pre_grad = gelu_pull(act_grad)[0].astype(BF16)
    input_part = jnp.einsum("xrf,xdf->xrd", pre_grad, expert_up, preferred_element_type=F32).astype(BF16)
    summed = combine(jnp.stack([by_group(partial_out), by_group(input_part)], axis=1), seqs, dps)
    down_grad = jnp.einsum("xrf,xrd->xfd", activated, grad_rows, preferred_element_type=F32)
    up_grad = jnp.einsum("xrd,xrf->xdf", received, pre_grad, preferred_element_type=F32)

    back = jnp.einsum("rt,prd->ptd", place_hot, summed.reshape(2, spots, width), preferred_element_type=F32)
    token_out, expert_input_grad = back[0], back[1]
    result = (hidden + gate[:, None] * token_out).astype(BF16)
    gate_grad = jnp.sum(grad_out * token_out, axis=-1)
    logit_grad = router_probs * (gate_grad[:, None] * hot - (gate_grad * gate)[:, None])
    logit_low = logit_grad.astype(BF16)
    router_grad = jnp.einsum("td,te->de", ffn_input, logit_low, preferred_element_type=F32)
    ffn_input_grad = expert_input_grad + jnp.einsum("te,de->td", logit_low, router_full, preferred_element_type=F32)
    _, norm_pull = jax.vjp(normalize, hidden, gain_two)
    hidden_norm_grad, gain_two_grad = norm_pull(ffn_input_grad)
    hidden_grad = grad_out + hidden_norm_grad
    attn_grad = hidden_grad.astype(BF16)
    heads_grad = jnp.einsum("td,hdk->htk", attn_grad, out_weight, preferred_element_type=F32).astype(BF16)
    grad_all, output = gather_grads(
        heads_grad.reshape(4, per, span, local_width), result.reshape(per, span, width), seqs, dps
    )
    out_w_part = jnp.einsum("td,htk->hdk", attn_grad, heads_all, preferred_element_type=F32).astype(BF16)

    query_grad, key_grad, value_grad, band_grad, far_grad = attend_back(
        queries, keys, values, grad_all.reshape(per, length, local_width), probs, heads, seqs, span
    )
    bias_grad = jnp.stack(
        [jnp.sum(jnp.where((bucket == b)[None], band_grad, 0.0), axis=(1, 2)) for b in range(bucket_count)]
    )
    far_sum = jnp.sum(far_grad, axis=(2, 3))
    bias_grad = bias_grad.at[bucket_count // 2 - 1].add(far_sum[:, 0]).at[bucket_count - 1].add(far_sum[:, 1])
    made_grad = jnp.concatenate([query_grad, key_grad, value_grad], axis=-1).reshape(count, 3 * local_width)
    project_grad = jnp.einsum("td,tk->dk", attn_input, made_grad, preferred_element_type=F32).astype(BF16)
    input_part = jnp.einsum("tk,dk->td", made_grad, project_weight, preferred_element_type=F32).astype(BF16)
    attn_input_grad, out_w_sum = add_heads(input_part.reshape(per, seqs, span, width), out_w_part, seqs, dps)
    _, first_pull = jax.vjp(normalize, own_inputs, gain_one)
    input_norm_grad, gain_one_grad = first_pull(attn_input_grad.reshape(own_rows, width))
    tokens_grad = (hidden_grad + input_norm_grad).astype(BF16).reshape(per, span, width)

    tail = jnp.concatenate(
        [
            router_grad,
            gain_one_grad[:, None],
            gain_two_grad[:, None],
            jnp.zeros((width, up_to(experts + 2, 128) - experts - 2), F32),
        ],
        axis=1,
    ).astype(BF16)
    weights = jnp.concatenate([project_grad, out_w_sum.astype(BF16), tail], axis=1)
    weights = jnp.swapaxes(weights.reshape(seqs, dps, shard, weights.shape[-1]), 0, 1)
    bias_pad = jnp.pad(bias_grad, ((0, 0), (0, 128 - heads)))
    tokens_grad, weights_sum, bias_sum = finish_grads(tokens_grad, weights, bias_pad, seqs, dps, tail.shape[1])
    at = 4 * local_width
    return (
        output,
        tokens_grad,
        weights_sum[:, at + experts],
        weights_sum[:, :local_width],
        weights_sum[:, local_width : 2 * local_width],
        weights_sum[:, 2 * local_width : 3 * local_width],
        weights_sum[:, 3 * local_width : at].T,
        bias_sum[:, :heads],
        weights_sum[:, at + experts + 1],
        weights_sum[:, at : at + experts],
        up_grad,
        down_grad,
    )


def solution(mesh):
    placed = (
        P("dp", "seq", None),
        P("dp"),
        P("dp", "seq", None),
        P(("seq", "dp")),
        P(("seq", "dp"), "head"),
        P(("seq", "dp"), "head"),
        P(("seq", "dp"), "head"),
        P("head", ("seq", "dp")),
        P(None, "head"),
        P(("seq", "dp")),
        P(("seq", "dp"), None),
        P(("seq", "dp"), None, "head"),
        P(("seq", "dp"), "head", None),
        P("dp", "seq", None),
    )
    return jax.shard_map(
        body,
        mesh=mesh,
        in_specs=placed,
        out_specs=(
            P("dp", "seq", None),
            P("dp", "seq", None),
            P(("seq", "dp")),
            P(("seq", "dp"), "head"),
            P(("seq", "dp"), "head"),
            P(("seq", "dp"), "head"),
            P("head", ("seq", "dp")),
            P(None, "head"),
            P(("seq", "dp")),
            P(("seq", "dp"), None),
            P(("seq", "dp"), None, "head"),
            P(("seq", "dp"), "head", None),
        ),
        check_vma=False,
    )
```

```python
import functools

import jax
import jax.numpy as jnp
import numpy as np
from jax import lax
from jax.experimental import pallas as pl
from jax.experimental.pallas import tpu as pltpu
from jax.sharding import PartitionSpec as P

HEAD_DIM = 64
EPS = 1e-06
bucket_edges = np.array([1, 2, 3, 4, 5, 6, 7, 8, 12, 16, 23, 32, 46, 64, 91], np.int32)
ANY = pl.BlockSpec(memory_space=pl.ANY)
VMEM = pl.BlockSpec(memory_space=pltpu.VMEM)
MESH = pl.DeviceIdType.MESH
DMA = pltpu.SemaphoreType.DMA
F32 = jnp.float32
BF16 = jnp.bfloat16


def normalize(vector, scales):
    return vector * lax.rsqrt(jnp.mean(vector * vector, axis=-1, keepdims=True) + EPS) * scales


def gelu_tanh(vector):
    return jax.nn.gelu(vector)


def bucket_of(offset, bucket_count):
    distance = jnp.abs(offset)
    magnitude = jnp.zeros_like(offset)
    for edge in bucket_edges:
        magnitude = magnitude + (distance >= int(edge)).astype(jnp.int32)
    return magnitude + bucket_count // 2 * (offset > 0).astype(jnp.int32)


def send(src, dst, send_sem, recv_sem, **device):
    copy = pltpu.make_async_remote_copy(
        src_ref=src,
        dst_ref=dst,
        send_sem=send_sem,
        recv_sem=recv_sem,
        device_id=device,
        device_id_type=MESH,
    )
    copy.start()
    return copy


def arrived(ref, recv_sem):
    pltpu.make_async_copy(ref, ref, recv_sem).wait()


def greet(devices):
    barrier = pltpu.get_barrier_semaphore()
    for device in devices:
        pl.semaphore_signal(barrier, inc=1, device_id=device, device_id_type=MESH)
    pl.semaphore_wait(barrier, len(devices))


def mod(value, size):
    return lax.rem(value + 2 * size, size)


class Place:
    def __init__(self, seqs, dps):
        self.h, self.s, self.d = lax.axis_index("head"), lax.axis_index("seq"), lax.axis_index("dp")
        self.seqs, self.dps = seqs, dps
        self.near = lax.rem(self.h, 2) * -2 + self.h + 1
        self.across = mod(self.h + 2, 4)
        self.near_across = lax.rem(self.across, 2) * -2 + self.across + 1

    def seq_peers(self):
        return [{"seq": mod(self.s + i, self.seqs)} for i in range(1, self.seqs)]

    def dp_peers(self):
        return [{"dp": mod(self.d + i, self.dps)} for i in range(1, self.dps)]

    def head_pair(self):
        return [{"head": self.near}, {"head": self.across}]

    def group_peers(self):
        return [
            {"seq": mod(self.s + i, self.seqs), "dp": mod(self.d + j, self.dps)}
            for i in range(self.seqs)
            for j in range(self.dps)
            if i or j
        ]

    def block(self, j, h=None):
        return mod((self.h if h is None else h) + 2 * j, 4)


def params(**more):
    return pltpu.CompilerParams(has_side_effects=True, vmem_limit_bytes=56 * 2**20, **more)


def line_gather(me, own, whole, sems, slot):
    (hop_send, hop_recv, dp_send, dp_recv) = sems
    s, d, count = me.s, me.d, me.seqs

    def spread(src, source):
        for i in range(1, me.dps):
            send(
                src,
                whole.at[source, d],
                dp_send.at[i - 1, source],
                dp_recv.at[i - 1, source],
                dp=mod(d + i, me.dps),
            )

    def spread_wait(source):
        for i in range(1, me.dps):
            here = whole.at[source, mod(d - i, me.dps)]
            arrived(here, dp_recv.at[i - 1, source])
            pltpu.make_async_copy(here, here, dp_send.at[i - 1, source]).wait()

    def start():
        @pl.when(s < count - 1)
        def _():
            send(own, whole.at[s, d], hop_send.at[0, s], hop_recv.at[s], seq=s + 1)

        @pl.when(s > 0)
        def _():
            send(own, whole.at[s, d], hop_send.at[1, s], hop_recv.at[s], seq=s - 1)

        spread(own, s)

    def step(t):
        @pl.when(s - t >= 0)
        def _():
            source = s - t
            here = whole.at[source, d]
            arrived(here, hop_recv.at[source])

            @pl.when(s < count - 1)
            def _():
                send(here, here, hop_send.at[0, source], hop_recv.at[source], seq=s + 1)

            spread(here, source)

        @pl.when(s + t < count)
        def _():
            source = s + t
            here = whole.at[source, d]
            arrived(here, hop_recv.at[source])

            @pl.when(s > 0)
            def _():
                send(here, here, hop_send.at[1, source], hop_recv.at[source], seq=s - 1)

            spread(here, source)

    def finish():
        for source in range(count):
            spread_wait(source)
            here = whole.at[source, d]

            @pl.when((s < count - 1) & (source <= s))
            def _():
                pltpu.make_async_copy(here, here, hop_send.at[0, source]).wait()

            @pl.when((s > 0) & (source >= s))
            def _():
                pltpu.make_async_copy(here, here, hop_send.at[1, source]).wait()

    return start, step, finish


def line_sems(seqs, dps):
    return [
        DMA((2, seqs)),
        DMA((seqs,)),
        DMA((max(1, dps - 1), seqs)),
        DMA((max(1, dps - 1), seqs)),
    ]


def spread_hot(at, shard, width):
    row = lax.broadcasted_iota(jnp.int32, (128, width), 0)
    column = lax.broadcasted_iota(jnp.int32, (128, width), 1)
    return ((column == row + at) & (row < shard)).astype(BF16)


def squeeze_hot(shard, padded, rows, count):
    row = lax.broadcasted_iota(jnp.int32, (rows, count * padded), 0)
    column = lax.broadcasted_iota(jnp.int32, (rows, count * padded), 1)
    inside = lax.rem(column, padded)
    return ((lax.div(column, padded) * shard + inside == row) & (inside < shard)).astype(BF16)


CHUNKS = 4


def front_kernel(
    seqs, dps, heads,
    tok, cot, wq, wk, wv, wo, router, gain_a, gain_f, ids, table, lengths,
    attn_input, weights, split_out, probs, heads_all, own_tok, cot_own, wo_all, gains, ids_all,
    tok_all, pack, pack_all, wo_pad, wo_parts, tile, tile_all, split, ext, slot, out,
    p_sem, ls, z_send, z_recv, h_send, h_recv, c_send, c_recv, a_send, a_recv, w_send, w_recv, i_send, i_recv, *line
):
    me = Place(seqs, dps)
    h, s, d = me.h, me.s, me.d
    per, blocks, span, width = tok_all.shape
    length = blocks * span
    shard, local = wq.shape
    groups = seqs * dps
    experts = router.shape[1]
    part_rows = span // CHUNKS
    half = CHUNKS // 2
    pack[...] = jnp.zeros_like(pack)
    for n, ref in enumerate((wq, wk, wv)):
        pack[:shard, n * local : (n + 1) * local] = ref[...]
    pack[:shard, 3 * local : 3 * local + experts] = router[...]
    wo_pad[...] = jnp.zeros_like(wo_pad)
    wo_pad[:, :shard] = wo[...]
    tile[...] = jnp.zeros_like(tile)
    tile[0:1, :shard] = gain_a[...].astype(F32)
    tile[1:2, :shard] = gain_f[...].astype(F32)
    greet(
        me.seq_peers()
        + [{"head": me.near} | peer for peer in me.seq_peers()]
        + me.dp_peers()
        + [{"head": mod(h + i, 4)} for i in range(1, 4)]
    )
    lines = [
        line_gather(me, pack, pack_all, line[0:4], 0),
        line_gather(me, tile, tile_all, line[4:8], 0),
        line_gather(me, wo_pad, wo_parts, line[8:12], 0),
    ]
    own_copies = [
        pltpu.make_async_copy(pack, pack_all.at[s, d], ls.at[0]),
        pltpu.make_async_copy(tile, tile_all.at[s, d], ls.at[1]),
        pltpu.make_async_copy(wo_pad, wo_parts.at[s, d], ls.at[2]),
        pltpu.make_async_copy(ids, ids_all.at[s], ls.at[3]),
    ]
    for j in range(per):
        own_copies.append(pltpu.make_async_copy(tok.at[per * s + j], tok_all.at[j, s], ls.at[4 + j]))
    for copy in own_copies:
        copy.start()
    for start, _, _ in lines:
        start()
    for i in range(1, seqs):
        send(ids, ids_all.at[s], i_send.at[i - 1], i_recv.at[i - 1], seq=mod(s + i, seqs))

    owns = lax.rem(mod(h - s, 4), 2) == 0
    target = jnp.where(owns, h, me.near)
    which = lax.div(mod(target - s, 4), 2)
    first = jnp.where(owns, 0, half)

    def chunk(c):
        return pl.ds(pl.multiple_of(c * part_rows, part_rows), part_rows)

    for c in range(half):
        for i in range(1, seqs):
            to = mod(s + i, seqs)
            rows = chunk(first + c)
            send(
                tok.at[per * to + which, rows],
                tok_all.at[which, s, rows],
                z_send.at[i - 1, c],
                z_recv.at[which, first + c],
                head=target,
                seq=to,
            )
        for _, step, _ in lines:
            step(c + 1)

    def build_bias(head):
        turn = lax.broadcasted_iota(jnp.int32, (8, 4 * span), 1)
        bucket = bucket_of(jnp.where(turn < 3 * span, turn, turn - 4 * span) - span, table.shape[0])
        row = jnp.zeros((8, 4 * span), F32)
        for b in range(table.shape[0]):
            row = jnp.where(bucket == b, table[b, head], row)
        rolled = pltpu.roll(jnp.broadcast_to(row[0:1], (span, 4 * span)), 0, 1, stride=1, stride_axis=0)
        ext[head, :, 2 * span : 5 * span] = rolled[:, : 3 * span]
        ext[head, :, : 2 * span] = jnp.broadcast_to(row[0:1, 0:1], (span, 2 * span))
        ext[head, :, 5 * span :] = jnp.broadcast_to(row[0:1, 3 * span - 1 : 3 * span], (span, 2 * span))

    build_bias(0)
    for _, step, _ in lines:
        for t in range(half + 1, seqs):
            step(t)
    for head in range(1, heads):
        build_bias(head)

    def at(j, c, head):
        return tok_all.at[j, me.block(j, head), chunk(c)]

    for c in range(half):
        for part in range(2):
            for j in range(per):
                k = part * half + c
                here = at(j, k, h)

                @pl.when(me.block(j) != s)
                def _():
                    arrived(here, z_recv.at[j, k])
                    send(here, here, h_send.at[0, j, k], h_recv.at[0, j, k], head=me.across)
                    send(here, here, h_send.at[1, j, k], h_recv.at[1, j, k], head=me.near)

    for copy in own_copies:
        copy.wait()
    for _, _, finish in lines:
        finish()
    if shard % 16:
        whole = pack_all[...].reshape(groups * pack.shape[0], pack.shape[1])
        hot = squeeze_hot(shard, pack.shape[0], width, groups)
        weights[...] = jnp.dot(hot, whole, preferred_element_type=F32).astype(BF16)
    else:
        weights[...] = pack_all[...].reshape(width, pack.shape[1])
    row = jnp.zeros((8, width), F32)
    for g in range(groups):
        piece = tile_all[g // dps, g % dps].astype(BF16)
        row = row + jnp.dot(piece, spread_hot(g * shard, shard, width), preferred_element_type=F32)
    gains[...] = row

    def project(j, block):
        rows = pl.ds(pl.multiple_of(block * span, span), span)
        x = tok_all[j, block].astype(F32)
        normed = (x * lax.rsqrt(jnp.mean(x * x, axis=-1, keepdims=True) + EPS) * gains[0:1, :]).astype(BF16)
        attn_input[j, rows, :] = normed
        parts = jnp.dot(normed, weights[...], preferred_element_type=F32).astype(BF16)
        for n in range(3 * heads):
            split[j, n, rows, :] = parts[:, n * HEAD_DIM : (n + 1) * HEAD_DIM]

    for c in range(half):
        for part in range(2):
            for j in range(per):
                k = part * half + c
                there = at(j, k, me.across)

                @pl.when(me.block(j, me.across) != s)
                def _():
                    arrived(there, h_recv.at[0, j, k])
                    send(there, there, h_send.at[2, j, k], h_recv.at[2, j, k], head=me.near)

    @pl.loop(0, 4 * per)
    def _(n):
        hop, j = lax.div(n, per), lax.rem(n, per)
        source = jnp.where(hop == 0, h, jnp.where(hop == 1, me.across, jnp.where(hop == 2, me.near, me.near_across)))
        block = mod(source + 2 * j, 4)

        @pl.when((hop >= 2) & (block != s))
        def _():
            for k in range(CHUNKS):
                arrived(tok_all.at[j, block, chunk(k)], h_recv.at[hop - 1, j, k])

        project(j, block)

    out_split = pltpu.make_async_copy(split, split_out, ls.at[4 + per])
    out_split.start()
    own_tokens = [pltpu.make_async_copy(tok_all.at[j, me.block(j)], own_tok.at[j], ls.at[4 + j]) for j in range(per)]
    for copy in own_tokens:
        copy.start()
    total = jnp.zeros((local, width), F32)
    for g in range(groups):
        total = total + jnp.dot(
            wo_parts[g // dps, g % dps], spread_hot(g * shard, shard, width), preferred_element_type=F32
        )
    wo_all[h] = total.astype(BF16)
    send(wo_all.at[h], wo_all.at[h], w_send.at[0], w_recv.at[0], head=me.across)
    send(wo_all.at[h], wo_all.at[h], w_send.at[1], w_recv.at[1], head=me.near)

    @pl.loop(0, per * blocks)
    def _(unit):
        j, block = lax.div(unit, blocks), lax.rem(unit, blocks)
        rows = pl.ds(pl.multiple_of(block * span, span), span)
        turn = lax.rem(unit, 2)

        @pl.when(unit >= 2)
        def _():
            pltpu.make_async_copy(slot.at[turn], slot.at[turn], p_sem.at[turn]).wait()

        window = pl.ds(pl.multiple_of((blocks - 1 - block) * span, span), length)
        valid = lax.broadcasted_iota(jnp.int32, (1, length), 1) < lengths[per * s + j]
        for head in range(heads):
            query, key, value = split[j, head, rows, :], split[j, heads + head], split[j, 2 * heads + head]
            scores = lax.dot_general(query, key, (((1,), (1,)), ((), ())), preferred_element_type=F32)
            scores = jnp.where(valid, scores + ext[head, :, window], -1e30)
            top = jnp.max(scores, axis=-1, keepdims=True)
            grown = jnp.exp(scores - top)
            total = jnp.sum(grown, axis=-1, keepdims=True)
            part = (grown * (1.0 / total)).astype(BF16)
            slot[turn, head] = part
            mixed = jnp.dot(part, value, preferred_element_type=F32)
            out[unit, :, head * HEAD_DIM : (head + 1) * HEAD_DIM] = mixed.astype(BF16)
        pltpu.make_async_copy(slot.at[turn], probs.at[j, :, rows, :], p_sem.at[turn]).start()
        owner = mod(block - 2 * j, 4)
        away = mod(owner - h, 4)

        @pl.when(away == 0)
        def _():
            pltpu.make_async_copy(out.at[unit], heads_all.at[h, j], ls.at[j]).start()

        @pl.when(away > 0)
        def _():
            send(out.at[unit], heads_all.at[h, j], a_send.at[away - 1, j], a_recv.at[away - 1, j], head=owner)

        for i in range(1, seqs):

            @pl.when(unit == i - 1)
            def _():
                to = mod(s + i, seqs)
                half_rows = pl.ds(pl.multiple_of(first * part_rows, part_rows), half * part_rows)
                send(
                    cot.at[per * to + which, half_rows],
                    cot_own.at[which, half_rows],
                    c_send.at[i - 1],
                    c_recv.at[which, lax.div(first, half)],
                    head=target,
                    seq=to,
                )

        @pl.when(unit == seqs)
        def _():
            there = wo_all.at[me.across]
            arrived(there, w_recv.at[0])
            send(there, there, w_send.at[2], w_recv.at[2], head=me.near)

    out_split.wait()
    for copy in own_tokens:
        copy.wait()
    for turn in range(2):
        pltpu.make_async_copy(slot.at[turn], slot.at[turn], p_sem.at[turn]).wait()
    for j in range(per):
        block = me.block(j)

        @pl.when(block == s)
        def _():
            own = pltpu.make_async_copy(cot.at[per * s + j], cot_own.at[j], ls.at[2 + j])
            own.start()
            own.wait()

        @pl.when(block != s)
        def _():
            for part in range(2):
                arrived(cot_own.at[j, pl.ds(part * half * part_rows, half * part_rows)], c_recv.at[j, part])

        pltpu.make_async_copy(out.at[0], heads_all.at[h, j], ls.at[j]).wait()
        for i in range(1, 4):
            pltpu.make_async_copy(out.at[0], out.at[0], a_send.at[i - 1, j]).wait()
            arrived(heads_all.at[mod(h - i, 4), j], a_recv.at[i - 1, j])
        for k in range(CHUNKS):
            here = at(j, k, h)

            @pl.when(me.block(j) != s)
            def _():
                for n in range(2):
                    pltpu.make_async_copy(here, here, h_send.at[n, j, k]).wait()

            @pl.when(me.block(j, me.across) != s)
            def _():
                pltpu.make_async_copy(here, here, h_send.at[2, j, k]).wait()

    for i in range(1, seqs):
        for c in range(half):
            rows = tok.at[0, pl.ds(0, part_rows)]
            pltpu.make_async_copy(rows, rows, z_send.at[i - 1, c]).wait()
        rows = cot.at[0, pl.ds(0, half * part_rows)]
        pltpu.make_async_copy(rows, rows, c_send.at[i - 1]).wait()
        pltpu.make_async_copy(ids, ids, i_send.at[i - 1]).wait()
        arrived(ids_all.at[mod(s - i, seqs)], i_recv.at[i - 1])
    for k in range(3):
        pltpu.make_async_copy(wo_all.at[h], wo_all.at[h], w_send.at[k]).wait()
    arrived(wo_all.at[me.near], w_recv.at[1])
    arrived(wo_all.at[me.near_across], w_recv.at[2])


def front(tokens, cot, wq, wk, wv, wo, router, gain_a, gain_f, ids, table, lengths, seqs, dps):
    seq_local, span, width = tokens.shape
    per = seq_local // seqs
    length = seqs * span
    shard, local = wq.shape
    heads = local // HEAD_DIM
    lanes = up_to(3 * local + router.shape[1], 128)
    padded = up_to(shard, 16)
    smem = pl.BlockSpec(memory_space=pltpu.SMEM)
    return pl.pallas_call(
        functools.partial(front_kernel, seqs, dps, heads),
        out_shape=(
            jax.ShapeDtypeStruct((per, length, width), BF16),
            jax.ShapeDtypeStruct((width, lanes), BF16),
            jax.ShapeDtypeStruct((per, 3 * heads, length, HEAD_DIM), BF16),
            jax.ShapeDtypeStruct((per, heads, length, length), BF16),
            jax.ShapeDtypeStruct((4, per, span, local), BF16),
            jax.ShapeDtypeStruct((per, span, width), BF16),
            jax.ShapeDtypeStruct((per, span, width), BF16),
            jax.ShapeDtypeStruct((4, local, width), BF16),
            jax.ShapeDtypeStruct((8, width), F32),
            jax.ShapeDtypeStruct((seqs,) + ids.shape, jnp.int32),
        ),
        in_specs=[ANY] * 2 + [VMEM] * 7 + [ANY, smem, smem],
        out_specs=[VMEM] * 2 + [ANY] * 5 + [VMEM] * 2 + [ANY],
        scratch_shapes=[
            pltpu.VMEM((per, seqs, span, width), BF16),
            pltpu.VMEM((padded, lanes), BF16),
            pltpu.VMEM((seqs, dps, padded, lanes), BF16),
            pltpu.VMEM((local, 128), BF16),
            pltpu.VMEM((seqs, dps, local, 128), BF16),
            pltpu.VMEM((8, 128), F32),
            pltpu.VMEM((seqs, dps, 8, 128), F32),
            pltpu.VMEM((per, 3 * heads, length, HEAD_DIM), BF16),
            pltpu.VMEM((heads, span, 7 * span), F32),
            pltpu.VMEM((2, heads, span, length), BF16),
            pltpu.VMEM((per * seqs, span, local), BF16),
            DMA((2,)),
            DMA((5 + per,)),
            DMA((seqs - 1, CHUNKS // 2)),
            DMA((per, CHUNKS)),
            DMA((3, per, CHUNKS)),
            DMA((3, per, CHUNKS)),
            DMA((seqs - 1,)),
            DMA((per, 2)),
            DMA((3, per)),
            DMA((3, per)),
            DMA((3,)),
            DMA((3,)),
            DMA((seqs - 1,)),
            DMA((seqs - 1,)),
        ]
        + line_sems(seqs, dps) * 3,
        compiler_params=params(collective_id=0),
        name="front",
    )(tokens, cot, wq, wk, wv, wo, router, gain_a, gain_f, ids, table, lengths)


def expert_windows(exp_local, per_expert):
    return [(e * per_expert // 16 * 16, up_to((e + 1) * per_expert, 16)) for e in range(exp_local)]


def contract(a, b, over_a, over_b):
    return lax.dot_general(a, b, (((over_a,), (over_b,)), ((), ())), preferred_element_type=F32)


GELU_A, GELU_B = float(np.sqrt(2.0 / np.pi)), 0.044715


def experts_kernel(
    seqs, dps, per_expert, rows, up, down, summed, up_grad, down_grad, taken, near, far,
    ls, g_send, g_recv, h_send, h_recv, n_send, n_recv, x_send, x_recv, r_send, r_recv
):
    me = Place(seqs, dps)
    h, s, d = me.h, me.s, me.d
    groups, _, height, width = rows.shape
    exp_local = up.shape[0]
    windows = expert_windows(exp_local, per_expert)
    me_group = s * dps + d

    def away(n):
        i, j = lax.div(n, dps), lax.rem(n, dps)
        return jnp.where(i == 2, 3, jnp.where(i == 3, 2, i)), j

    def ahead(n):
        i, j = away(n)
        return mod(s + i, seqs), mod(d + j, dps)

    def behind(n):
        i, j = away(n)
        return mod(s - i, seqs), mod(d - j, dps)

    up_grad[...] = jnp.zeros_like(up_grad)
    down_grad[...] = jnp.zeros_like(down_grad)
    greet(me.group_peers() + me.head_pair())
    pltpu.make_async_copy(rows.at[me_group], taken.at[h, 0], ls.at[0]).start()

    @pl.loop(1, groups)
    def _(n):
        to_s, to_d = ahead(n)
        send(rows.at[to_s * dps + to_d], taken.at[h, n], g_send.at[n], g_recv.at[n], seq=to_s, dp=to_d)

    def gather_own(n):
        here = taken.at[h, n]

        @pl.when(n == 0)
        def _():
            pltpu.make_async_copy(here, here, ls.at[0]).wait()

        @pl.when(n > 0)
        def _():
            arrived(here, g_recv.at[n])

        send(here, here, h_send.at[0, n], h_recv.at[0, n], head=me.across)
        send(here, here, h_send.at[1, n], h_recv.at[1, n], head=me.near)

    def gather_across(n):
        there = taken.at[me.across, n]
        arrived(there, h_recv.at[0, n])
        send(there, there, h_send.at[2, n], h_recv.at[2, n], head=me.near)

    def compute(n):
        arrived(taken.at[me.near, n], h_recv.at[1, n])
        arrived(taken.at[me.near_across, n], h_recv.at[2, n])
        for k in range(3):
            pltpu.make_async_copy(taken.at[h, n], taken.at[h, n], h_send.at[k, n]).wait()
        kept = []
        for e, (low, high) in enumerate(windows):
            size = high - low
            at = lax.broadcasted_iota(jnp.int32, (4 * size, width), 0)
            slot = lax.rem(at, size) + low
            inside = (slot >= e * per_expert) & (slot < (e + 1) * per_expert)

            def mine(part):
                block = jnp.concatenate([taken[q, n, part, low:high, :] for q in range(4)], axis=0)
                return jnp.where(inside, block.astype(F32), 0.0).astype(BF16)

            x, g = mine(0), mine(1)
            pre = jnp.dot(x, up[e], preferred_element_type=F32)
            square = pre * pre
            bent = jnp.tanh(GELU_A * pre * (1.0 + GELU_B * square))
            act = (0.5 * pre * (1.0 + bent)).astype(BF16)
            slope = 0.5 * (1.0 + bent) + 0.5 * pre * (1.0 - bent * bent) * (GELU_A * (1.0 + 3.0 * GELU_B * square))
            out = jnp.dot(act, down[e], preferred_element_type=F32).astype(BF16)
            act_grad = contract(g, down[e], 1, 1)
            pre_grad = (act_grad * slope).astype(BF16)
            back = contract(pre_grad, up[e], 1, 1).astype(BF16)
            kept.append((x, g, act, pre_grad, out, back))
        for q in range(4):
            for part in range(2):
                for tile in range(0, height, 16):
                    total = None
                    for (low, high), made in zip(windows, kept):
                        if low <= tile < high:
                            begin = q * (high - low) + tile - low
                            piece = made[4 + part][begin : begin + 16, :]
                            total = piece if total is None else total + piece
                    if total is not None:
                        taken[q, n, part, tile : tile + 16, :] = total
        send(taken.at[me.near_across, n], near.at[0, n], n_send.at[0, n], n_recv.at[0, n], head=me.near)
        send(taken.at[me.near, n], near.at[1, n], n_send.at[1, n], n_recv.at[1, n], head=me.near)
        for e in range(exp_local):
            x, g, act, pre_grad, _, _ = kept[e]
            up_grad[e] += contract(x, pre_grad, 0, 0)
            down_grad[e] += contract(act, g, 0, 0)

    def add_near(n):
        arrived(near.at[0, n], n_recv.at[0, n])
        both = taken[me.across, n].astype(F32) + near[0, n].astype(F32)
        taken[me.across, n] = both.astype(BF16)
        send(taken.at[me.across, n], far.at[n], x_send.at[n], x_recv.at[n], head=me.across)

    def send_back(n):
        arrived(near.at[1, n], n_recv.at[1, n])
        arrived(far.at[n], x_recv.at[n])
        total = taken[h, n].astype(F32) + near[1, n].astype(F32) + far[n].astype(F32)
        taken[h, n] = total.astype(BF16)
        to_s, to_d = behind(n)

        @pl.when(n == 0)
        def _():
            pltpu.make_async_copy(taken.at[h, n], summed.at[me_group], r_send.at[n]).start()

        @pl.when(n > 0)
        def _():
            send(taken.at[h, n], summed.at[me_group], r_send.at[n], r_recv.at[n], seq=to_s, dp=to_d)

    stages = (send_back, add_near, compute, gather_across, gather_own)

    @pl.loop(0, groups + len(stages) - 1)
    def _(step):
        for k, stage in enumerate(stages):
            n = step - (len(stages) - 1 - k)

            @pl.when((n >= 0) & (n < groups))
            def _():
                stage(n)

    @pl.loop(0, groups)
    def _(n):
        here = taken.at[h, n]
        for k in range(2):
            pltpu.make_async_copy(here, here, n_send.at[k, n]).wait()
        pltpu.make_async_copy(here, here, x_send.at[n]).wait()
        pltpu.make_async_copy(here, here, r_send.at[n]).wait()

        @pl.when(n > 0)
        def _():
            pltpu.make_async_copy(here, here, g_send.at[n]).wait()
            from_s, from_d = ahead(n)
            arrived(summed.at[from_s * dps + from_d], r_recv.at[n])


def run_experts(rows, up, down, seqs, dps, per_expert):
    groups, parts, height, width = rows.shape
    return pl.pallas_call(
        functools.partial(experts_kernel, seqs, dps, per_expert),
        out_shape=(
            jax.ShapeDtypeStruct(rows.shape, BF16),
            jax.ShapeDtypeStruct(up.shape, F32),
            jax.ShapeDtypeStruct(down.shape, F32),
        ),
        in_specs=[ANY, VMEM, VMEM],
        out_specs=[ANY, VMEM, VMEM],
        scratch_shapes=[
            pltpu.VMEM((4,) + rows.shape, BF16),
            pltpu.VMEM((2,) + rows.shape, BF16),
            pltpu.VMEM(rows.shape, BF16),
            DMA((1,)),
            DMA((groups,)),
            DMA((groups,)),
            DMA((3, groups)),
            DMA((3, groups)),
            DMA((2, groups)),
            DMA((2, groups)),
            DMA((groups,)),
            DMA((groups,)),
            DMA((groups,)),
            DMA((groups,)),
        ],
        compiler_params=params(collective_id=2),
        name="experts",
    )(rows, up, down)


def send_home(me, own, home, ls, z_send, z_recv, h_send, h_recv):
    h, s, seqs = me.h, me.s, me.seqs
    per = own.shape[0]
    turn = mod(s - h, 4)
    mine = lax.rem(turn, 2) == 0
    which = lax.div(turn, 2)

    def start():
        for j in range(per):
            to = me.block(j)

            @pl.when(to != s)
            def _():
                send(own.at[j], home.at[per * s + j], z_send.at[j], z_recv.at[s], seq=to)

            @pl.when(to == s)
            def _():
                pltpu.make_async_copy(own.at[j], home.at[per * s + j], ls).start()

    def forward():
        @pl.when(mine)
        def _():
            for i in range(seqs):
                source = mod(s + i, seqs)
                here = home.at[per * source + which]
                if i == 0:
                    pltpu.make_async_copy(here, here, ls).wait()
                else:
                    arrived(here, z_recv.at[source])
                send(here, here, h_send.at[0, source], h_recv.at[0, source], head=me.across)
                send(here, here, h_send.at[1, source], h_recv.at[1, source], head=me.near)
            for i in range(seqs):
                source = mod(s + i, seqs)
                there = home.at[per * source + 1 - which]
                arrived(there, h_recv.at[0, source])
                send(there, there, h_send.at[2, source], h_recv.at[2, source], head=me.near)

    def finish():
        for j in range(per):

            @pl.when(me.block(j) != s)
            def _():
                pltpu.make_async_copy(own.at[j], own.at[j], z_send.at[j]).wait()

        @pl.when(mine)
        def _():
            for source in range(seqs):
                for k in range(3):
                    here = home.at[per * source]
                    pltpu.make_async_copy(here, here, h_send.at[k, source]).wait()

        @pl.when(jnp.logical_not(mine))
        def _():
            for source in range(seqs):
                arrived(home.at[per * source], h_recv.at[1, source])
                arrived(home.at[per * source + 1], h_recv.at[2, source])

    return start, forward, finish


def home_sems(per, seqs):
    return [DMA(()), DMA((per,)), DMA((seqs,)), DMA((3, seqs)), DMA((3, seqs))]


def grads_kernel(seqs, dps, grad, result, grad_all, home, ls, a_send, a_recv, *sems):
    me = Place(seqs, dps)
    h = me.h
    per = result.shape[0]
    start, forward, finish = send_home(me, result, home, *sems)
    greet(me.seq_peers() + [{"head": mod(h + i, 4)} for i in range(1, 4)])
    copies = []
    for i in range(1, 4):
        to = mod(h + i, 4)
        for j in range(per):
            copies.append(
                send(
                    grad.at[to, j],
                    grad_all.at[j, me.block(j)],
                    a_send.at[i - 1, j],
                    a_recv.at[i - 1, j],
                    head=to,
                )
            )
    own_copies = [pltpu.make_async_copy(grad.at[h, j], grad_all.at[j, me.block(j)], ls.at[j]) for j in range(per)]
    for copy in own_copies:
        copy.start()
    start()
    forward()
    finish()
    for copy in own_copies:
        copy.wait()
    for copy in copies:
        copy.wait_send()
    for i in range(1, 4):
        source = mod(h - i, 4)
        for j in range(per):
            arrived(grad_all.at[j, me.block(j, source)], a_recv.at[i - 1, j])


def gather_grads(grad, result, seqs, dps):
    _, per, span, width = grad.shape
    return pl.pallas_call(
        functools.partial(grads_kernel, seqs, dps),
        out_shape=(
            jax.ShapeDtypeStruct((per, seqs, span, width), BF16),
            jax.ShapeDtypeStruct((per * seqs,) + result.shape[1:], BF16),
        ),
        in_specs=[ANY] * 2,
        out_specs=[ANY] * 2,
        scratch_shapes=[DMA((per,)), DMA((3, per)), DMA((3, per))] + home_sems(per, seqs),
        compiler_params=params(collective_id=4),
        name="gather_grads",
    )(grad, result)


def input_kernel(
    seqs, dps, partial, weight, total, weight_out, own, near, far_out, far_in, wown, wnear, wfar_out, wfar_in,
    ls, n_send, n_recv, x_send, x_recv, wls, wn_send, wn_recv, wx_send, wx_recv
):
    me = Place(seqs, dps)
    h = me.h
    per = total.shape[0]
    greet(me.head_pair())
    for j in range(per):
        for k, head in enumerate((me.near_across, me.near)):
            send(partial.at[j, me.block(j, head)], near.at[k, j], n_send.at[k, j], n_recv.at[k, j], head=me.near)
        for k, head in enumerate((me.across, h)):
            pltpu.make_async_copy(partial.at[j, me.block(j, head)], own.at[k, j], ls.at[k, j]).start()
    for k, head in enumerate((me.near_across, me.near)):
        send(weight.at[head], wnear.at[k], wn_send.at[k], wn_recv.at[k], head=me.near)
    for k, head in enumerate((me.across, h)):
        pltpu.make_async_copy(weight.at[head], wown.at[k], wls.at[k]).start()
    for j in range(per):
        arrived(near.at[0, j], n_recv.at[0, j])
        pltpu.make_async_copy(own.at[0, j], own.at[0, j], ls.at[0, j]).wait()
        far_out[j] = (own[0, j].astype(F32) + near[0, j].astype(F32)).astype(BF16)
        send(far_out.at[j], far_in.at[j], x_send.at[j], x_recv.at[j], head=me.across)
    arrived(wnear.at[0], wn_recv.at[0])
    pltpu.make_async_copy(wown.at[0], wown.at[0], wls.at[0]).wait()
    wfar_out[...] = (wown[0].astype(F32) + wnear[0].astype(F32)).astype(BF16)
    send(wfar_out, wfar_in, wx_send, wx_recv, head=me.across)
    for j in range(per):
        arrived(near.at[1, j], n_recv.at[1, j])
        pltpu.make_async_copy(own.at[1, j], own.at[1, j], ls.at[1, j]).wait()
        arrived(far_in.at[j], x_recv.at[j])
        total[j] = own[1, j].astype(F32) + near[1, j].astype(F32) + far_in[j].astype(F32)
    arrived(wnear.at[1], wn_recv.at[1])
    pltpu.make_async_copy(wown.at[1], wown.at[1], wls.at[1]).wait()
    arrived(wfar_in, wx_recv)
    weight_out[...] = wown[1].astype(F32) + wnear[1].astype(F32) + wfar_in[...].astype(F32)
    for j in range(per):
        for k in range(2):
            pltpu.make_async_copy(near.at[k, j], near.at[k, j], n_send.at[k, j]).wait()
        pltpu.make_async_copy(far_out.at[j], far_out.at[j], x_send.at[j]).wait()
    for k in range(2):
        pltpu.make_async_copy(wnear.at[k], wnear.at[k], wn_send.at[k]).wait()
    pltpu.make_async_copy(wfar_out, wfar_out, wx_send).wait()


def add_heads(partial, weight, seqs, dps):
    per, _, span, width = partial.shape
    block = (per, span, width)
    wblock = weight.shape[1:]
    return pl.pallas_call(
        functools.partial(input_kernel, seqs, dps),
        out_shape=(jax.ShapeDtypeStruct(block, F32), jax.ShapeDtypeStruct(wblock, F32)),
        in_specs=[ANY] * 2,
        out_specs=[VMEM] * 2,
        scratch_shapes=[
            pltpu.VMEM((2,) + block, BF16),
            pltpu.VMEM((2,) + block, BF16),
            pltpu.VMEM(block, BF16),
            pltpu.VMEM(block, BF16),
            pltpu.VMEM((2,) + wblock, BF16),
            pltpu.VMEM((2,) + wblock, BF16),
            pltpu.VMEM(wblock, BF16),
            pltpu.VMEM(wblock, BF16),
        ]
        + [DMA((2, per))] * 3
        + [DMA((per,))] * 2
        + [DMA((2,))] * 3
        + [DMA(())] * 2,
        compiler_params=params(collective_id=5),
        name="add_heads",
    )(partial, weight)


def last_kernel(
    seqs, dps, grad, weights, bias, home, weights_sum, bias_sum, wsum, wtake, ytake, btake, small,
    ls, y_send, y_recv, w_send, w_recv, b_send, b_recv, s_send, s_recv, *sems
):
    me = Place(seqs, dps)
    h, s, d = me.h, me.s, me.d
    start, forward, finish = send_home(me, grad, home, *sems)
    others = [(i, j) for i in range(seqs) for j in range(dps) if i or j]
    greet(me.group_peers() + [{"head": mod(h + i, 4)} for i in range(1, 4)])
    for i in range(1, dps):
        to = mod(d + i, dps)
        send(weights.at[to], ytake.at[i - 1], y_send.at[i - 1], y_recv.at[i - 1], dp=to)
    mine_y = pltpu.make_async_copy(weights.at[d], wsum, ls)
    mine_y.start()
    for n, (i, j) in enumerate(others):
        send(bias, btake.at[n], b_send.at[n], b_recv.at[n], seq=mod(s + i, seqs), dp=mod(d + j, dps))
    start()
    mine_y.wait()
    for i in range(1, dps):
        arrived(ytake.at[i - 1], y_recv.at[i - 1])
    for t in range(seqs):
        acc = wsum[t].astype(F32)
        for i in range(1, dps):
            acc = acc + ytake[i - 1, t].astype(F32)
        wsum[t] = acc.astype(BF16)
    for i in range(1, seqs):
        to = mod(s + i, seqs)
        send(wsum.at[to], wtake.at[i - 1], w_send.at[i - 1], w_recv.at[i - 1], seq=to)
    forward()
    acc = wsum[s].astype(F32)
    for i in range(1, seqs):
        arrived(wtake.at[i - 1], w_recv.at[i - 1])
        acc = acc + wtake[i - 1].astype(F32)
    weights_sum[...] = acc
    lanes = small.shape[-1]
    small[0] = acc[:, acc.shape[-1] - lanes :]
    for i in range(1, 4):
        send(small.at[0], small.at[i], s_send.at[i - 1], s_recv.at[i - 1], head=mod(h + i, 4))
    total = bias[...]
    for n in range(len(others)):
        arrived(btake.at[n], b_recv.at[n])
        total = total + btake[n]
    bias_sum[...] = total
    tail = small[0]
    for i in range(1, 4):
        arrived(small.at[i], s_recv.at[i - 1])
        tail = tail + small[i]
    weights_sum[:, acc.shape[-1] - lanes :] = tail
    for i in range(1, 4):
        pltpu.make_async_copy(small.at[0], small.at[0], s_send.at[i - 1]).wait()
    for i in range(1, dps):
        pltpu.make_async_copy(ytake.at[0], ytake.at[0], y_send.at[i - 1]).wait()
    for i in range(1, seqs):
        pltpu.make_async_copy(wsum.at[0], wsum.at[0], w_send.at[i - 1]).wait()
    for n in range(len(others)):
        pltpu.make_async_copy(btake.at[0], btake.at[0], b_send.at[n]).wait()
    finish()


def finish_grads(grad, weights, bias, seqs, dps, small):
    per, span, width = grad.shape
    _, _, rows, lanes = weights.shape
    groups = seqs * dps
    return pl.pallas_call(
        functools.partial(last_kernel, seqs, dps),
        out_shape=(
            jax.ShapeDtypeStruct((per * seqs, span, width), BF16),
            jax.ShapeDtypeStruct((rows, lanes), F32),
            jax.ShapeDtypeStruct(bias.shape, F32),
        ),
        in_specs=[ANY, ANY, VMEM],
        out_specs=[ANY, VMEM, VMEM],
        scratch_shapes=[
            pltpu.VMEM((seqs, rows, lanes), BF16),
            pltpu.VMEM((seqs - 1, rows, lanes), BF16),
            pltpu.VMEM((max(1, dps - 1), seqs, rows, lanes), BF16),
            pltpu.VMEM((groups - 1,) + bias.shape, F32),
            pltpu.VMEM((4, rows, small), F32),
            DMA(()),
            DMA((max(1, dps - 1),)),
            DMA((max(1, dps - 1),)),
            DMA((seqs - 1,)),
            DMA((seqs - 1,)),
            DMA((groups - 1,)),
            DMA((groups - 1,)),
            DMA((3,)),
            DMA((3,)),
        ]
        + home_sems(per, seqs),
        compiler_params=params(collective_id=6),
        name="finish_grads",
    )(grad, weights, bias)


def attend_back_kernel(
    heads, blocks, span, s_ref, g_ref, p_ref, dq_ref, dk_ref, dv_ref, band_ref, far_ref, dk_sum, dv_sum
):
    first = pl.program_id(0) == 0
    for head in range(heads):
        cols = slice(head * HEAD_DIM, (head + 1) * HEAD_DIM)
        key = s_ref[0, heads + head]
        value = s_ref[0, 2 * heads + head]
        for q_block in range(blocks):
            rows = slice(q_block * span, (q_block + 1) * span)
            query = s_ref[0, head, rows, :]
            grad = g_ref[0, rows, cols]
            weights = p_ref[0, head, rows, :]
            prob_grad = lax.dot_general(grad, value, (((1,), (1,)), ((), ())), preferred_element_type=F32)
            wide = weights.astype(F32)
            delta = jnp.sum(wide * prob_grad, axis=-1, keepdims=True)
            score_grad = wide * (prob_grad - delta)
            for k_block in range(blocks):
                part = score_grad[:, k_block * span : (k_block + 1) * span]
                step = k_block - q_block
                if abs(step) <= 1:
                    where = (head, slice(None), slice((step + 1) * span, (step + 2) * span))
                    begin = first & (q_block == (1 if step < 0 else 0))
                    old = band_ref[where]
                    band_ref[where] = jnp.where(begin, 0.0, old) + part
                else:
                    side = 0 if step < 0 else 1
                    begin = first & ((q_block, k_block) == ((2, 0) if side == 0 else (0, 2)))
                    flat = jnp.sum(part.reshape(span // 8, 8, span), axis=0)
                    old = far_ref[head, side]
                    far_ref[head, side] = jnp.where(begin, 0.0, old) + flat
            low = score_grad.astype(BF16)
            dq_ref[0, rows, cols] = jnp.dot(low, key, preferred_element_type=F32).astype(BF16)
            dk = lax.dot_general(low, query, (((0,), (0,)), ((), ())), preferred_element_type=F32)
            dv = lax.dot_general(weights, grad, (((0,), (0,)), ((), ())), preferred_element_type=F32)
            if q_block == 0:
                dk_sum[...] = dk
                dv_sum[...] = dv
            else:
                dk_sum[...] += dk
                dv_sum[...] += dv
        dk_ref[0, :, cols] = dk_sum[...].astype(BF16)
        dv_ref[0, :, cols] = dv_sum[...].astype(BF16)


def attend_back(split, grads, probs, heads, blocks, span):
    per, length, width = grads.shape
    whole = pl.BlockSpec((1, length, width), lambda j: (j, 0, 0))
    return pl.pallas_call(
        functools.partial(attend_back_kernel, heads, blocks, span),
        grid=(per,),
        out_shape=(
            jax.ShapeDtypeStruct((per, length, width), BF16),
            jax.ShapeDtypeStruct((per, length, width), BF16),
            jax.ShapeDtypeStruct((per, length, width), BF16),
            jax.ShapeDtypeStruct((heads, span, 3 * span), F32),
            jax.ShapeDtypeStruct((heads, 2, 8, span), F32),
        ),
        in_specs=[pl.BlockSpec((1,) + split.shape[1:], lambda j: (j, 0, 0, 0)), whole]
        + [pl.BlockSpec((1, heads, length, length), lambda j: (j, 0, 0, 0))],
        out_specs=[whole] * 3
        + [
            pl.BlockSpec((heads, span, 3 * span), lambda j: (0, 0, 0)),
            pl.BlockSpec((heads, 2, 8, span), lambda j: (0, 0, 0, 0)),
        ],
        scratch_shapes=[pltpu.VMEM((length, HEAD_DIM), F32)] * 2,
        compiler_params=pltpu.CompilerParams(vmem_limit_bytes=56 * 2**20),
        name="attend_back",
    )(split, grads, probs)


def up_to(value, unit):
    return -(-value // unit) * unit


def body(
    tokens,
    lengths,
    expert_ids,
    attention_gain,
    query_weight,
    key_weight,
    value_weight,
    output_weight,
    position_bias,
    feedforward_gain,
    router_weight,
    expert_up,
    expert_down,
    cotangent,
):
    seqs, dps = lax.axis_size("seq"), lax.axis_size("dp")
    groups = seqs * dps
    seq_local, span, width = tokens.shape
    per = seq_local // seqs
    length = seqs * span
    count = per * length
    own_rows = per * span
    local_width = query_weight.shape[1]
    bucket_count, heads = position_bias.shape
    experts = router_weight.shape[1]
    exp_local = expert_up.shape[0]
    shard = query_weight.shape[0]
    head_at, seq_at = lax.axis_index("head"), lax.axis_index("seq")

    ids = expert_ids.reshape(seq_local, span)
    attn_input, weights, split, probs, heads_all, own_tok, cot_own, out_weight, gains, ids_all = front(
        tokens,
        cotangent,
        query_weight,
        key_weight,
        value_weight,
        output_weight,
        router_weight,
        attention_gain[None, :],
        feedforward_gain[None, :],
        ids,
        position_bias.astype(F32),
        lengths,
        seqs,
        dps,
    )
    project_weight = weights[:, : 3 * local_width]
    router_full = weights[:, 3 * local_width : 3 * local_width + experts]
    gain_one, gain_two = gains[0], gains[1]
    attn_input = attn_input.reshape(count, width)
    offset = jnp.arange(3 * span, dtype=jnp.int32)[None, :] - span - jnp.arange(span, dtype=jnp.int32)[:, None]
    bucket = bucket_of(offset, bucket_count)
    heads_all = heads_all.reshape(4, own_rows, local_width)
    own_blocks = [lax.rem(head_at + 2 * j, 4) for j in range(per)]
    own_inputs = own_tok.reshape(own_rows, width).astype(F32)
    attention = jnp.einsum("htk,hkd->td", heads_all, out_weight, preferred_element_type=F32)
    hidden = own_inputs + attention
    ffn_input = normalize(hidden, gain_two).astype(BF16)
    logits = jnp.dot(ffn_input, router_full, preferred_element_type=F32)
    router_probs = jax.nn.softmax(logits, axis=-1)

    capacity = max(2, (5 * span + 4 * experts - 1) // (4 * experts))
    own_ids = jnp.stack(
        [
            lax.dynamic_index_in_dim(lax.dynamic_index_in_dim(ids_all, own_blocks[j], 0, False), per * seq_at + j, 0, False)
            for j in range(per)
        ]
    )
    earlier = jnp.arange(span)[None, :] < jnp.arange(span)[:, None]
    same = (own_ids[:, :, None] == own_ids[:, None, :]) & earlier[None]
    slot = jnp.sum(same.astype(jnp.int32), axis=-1)
    rows_used = exp_local * per * capacity
    rows_pad = up_to(rows_used, 16)
    place = (
        own_ids // exp_local * rows_pad
        + (own_ids % exp_local * per + jnp.arange(per, dtype=jnp.int32)[:, None]) * capacity
        + slot
    ).reshape(own_rows)
    spots = groups * rows_pad
    place_hot = (jnp.arange(spots, dtype=jnp.int32)[:, None] == place[None, :]).astype(BF16)
    hot = (own_ids.reshape(own_rows, 1) == jnp.arange(experts, dtype=jnp.int32)).astype(F32)
    gate = jnp.sum(router_probs * hot, axis=-1)
    grad_out = cot_own.reshape(own_rows, width).astype(F32)
    sent_grad = (gate[:, None] * grad_out).astype(BF16)
    to_send = jnp.concatenate([ffn_input, sent_grad], axis=1)
    rows = jnp.dot(place_hot, to_send, preferred_element_type=F32).astype(BF16)
    rows = jnp.swapaxes(rows.reshape(groups, rows_pad, 2, width), 1, 2)
    summed, up_grad, down_grad = run_experts(rows, expert_up, expert_down, seqs, dps, per * capacity)
    summed = jnp.swapaxes(summed, 1, 2).reshape(spots, 2 * width)
    back = jnp.einsum("rt,rd->td", place_hot, summed, preferred_element_type=F32)
    back = (back[:, :width], back[:, width:])
    token_out, expert_input_grad = back[0], back[1]
    result = (hidden + gate[:, None] * token_out).astype(BF16)
    gate_grad = jnp.sum(grad_out * token_out, axis=-1)
    logit_grad = router_probs * (gate_grad[:, None] * hot - (gate_grad * gate)[:, None])
    logit_low = logit_grad.astype(BF16)
    router_grad = jnp.einsum("td,te->de", ffn_input, logit_low, preferred_element_type=F32)
    ffn_input_grad = expert_input_grad + jnp.einsum("te,de->td", logit_low, router_full, preferred_element_type=F32)
    _, norm_pull = jax.vjp(normalize, hidden, gain_two)
    hidden_norm_grad, gain_two_grad = norm_pull(ffn_input_grad)
    hidden_grad = grad_out + hidden_norm_grad
    attn_grad = hidden_grad.astype(BF16)
    heads_grad = jnp.einsum("td,hkd->htk", attn_grad, out_weight, preferred_element_type=F32).astype(BF16)
    grad_all, output = gather_grads(
        heads_grad.reshape(4, per, span, local_width), result.reshape(per, span, width), seqs, dps
    )
    out_w_part = jnp.einsum("td,htk->hdk", attn_grad, heads_all, preferred_element_type=F32).astype(BF16)

    query_grad, key_grad, value_grad, band_grad, far_grad = attend_back(
        split, grad_all.reshape(per, length, local_width), probs, heads, seqs, span
    )
    bias_grad = jnp.stack(
        [jnp.sum(jnp.where((bucket == b)[None], band_grad, 0.0), axis=(1, 2)) for b in range(bucket_count)]
    )
    far_sum = jnp.sum(far_grad, axis=(2, 3))
    bias_grad = bias_grad.at[bucket_count // 2 - 1].add(far_sum[:, 0]).at[bucket_count - 1].add(far_sum[:, 1])
    made_grad = jnp.concatenate([query_grad, key_grad, value_grad], axis=-1).reshape(count, 3 * local_width)
    project_grad = jnp.einsum("td,tk->dk", attn_input, made_grad, preferred_element_type=F32).astype(BF16)
    input_part = jnp.einsum("tk,dk->td", made_grad, project_weight, preferred_element_type=F32).astype(BF16)
    attn_input_grad, out_w_sum = add_heads(input_part.reshape(per, seqs, span, width), out_w_part, seqs, dps)
    _, first_pull = jax.vjp(normalize, own_inputs, gain_one)
    input_norm_grad, gain_one_grad = first_pull(attn_input_grad.reshape(own_rows, width))
    tokens_grad = (hidden_grad + input_norm_grad).astype(BF16).reshape(per, span, width)

    tail = jnp.concatenate(
        [
            router_grad,
            gain_one_grad[:, None],
            gain_two_grad[:, None],
            jnp.zeros((width, up_to(experts + 2, 128) - experts - 2), F32),
        ],
        axis=1,
    ).astype(BF16)
    weights = jnp.concatenate([project_grad, out_w_sum.astype(BF16), tail], axis=1)
    weights = jnp.swapaxes(weights.reshape(seqs, dps, shard, weights.shape[-1]), 0, 1)
    bias_pad = jnp.pad(bias_grad, ((0, 0), (0, 128 - heads)))
    tokens_grad, weights_sum, bias_sum = finish_grads(tokens_grad, weights, bias_pad, seqs, dps, tail.shape[1])
    at = 4 * local_width
    return (
        output,
        tokens_grad,
        weights_sum[:, at + experts],
        weights_sum[:, :local_width],
        weights_sum[:, local_width : 2 * local_width],
        weights_sum[:, 2 * local_width : 3 * local_width],
        weights_sum[:, 3 * local_width : at].T,
        bias_sum[:, :heads],
        weights_sum[:, at + experts + 1],
        weights_sum[:, at : at + experts],
        up_grad,
        down_grad,
    )


def solution(mesh):
    placed = (
        P("dp", "seq", None),
        P("dp"),
        P("dp", "seq", None),
        P(("seq", "dp")),
        P(("seq", "dp"), "head"),
        P(("seq", "dp"), "head"),
        P(("seq", "dp"), "head"),
        P("head", ("seq", "dp")),
        P(None, "head"),
        P(("seq", "dp")),
        P(("seq", "dp"), None),
        P(("seq", "dp"), None, "head"),
        P(("seq", "dp"), "head", None),
        P("dp", "seq", None),
    )
    return jax.shard_map(
        body,
        mesh=mesh,
        in_specs=placed,
        out_specs=(
            P("dp", "seq", None),
            P("dp", "seq", None),
            P(("seq", "dp")),
            P(("seq", "dp"), "head"),
            P(("seq", "dp"), "head"),
            P(("seq", "dp"), "head"),
            P("head", ("seq", "dp")),
            P(None, "head"),
            P(("seq", "dp")),
            P(("seq", "dp"), None),
            P(("seq", "dp"), None, "head"),
            P(("seq", "dp"), "head", None),
        ),
        check_vma=False,
    )
```

```python
import functools

import jax
import jax.numpy as jnp
import numpy as np
from jax import lax
from jax.experimental import pallas as pl
from jax.experimental.pallas import tpu as pltpu
from jax.sharding import PartitionSpec as P

HEAD_DIM = 64
EPS = 1e-06
bucket_edges = np.array([1, 2, 3, 4, 5, 6, 7, 8, 12, 16, 23, 32, 46, 64, 91], np.int32)
ANY = pl.BlockSpec(memory_space=pl.ANY)
VMEM = pl.BlockSpec(memory_space=pltpu.VMEM)
MESH = pl.DeviceIdType.MESH
DMA = pltpu.SemaphoreType.DMA
F32 = jnp.float32
BF16 = jnp.bfloat16


def normalize(vector, scales):
    return vector * lax.rsqrt(jnp.mean(vector * vector, axis=-1, keepdims=True) + EPS) * scales


def gelu_tanh(vector):
    return jax.nn.gelu(vector)


def bucket_of(offset, bucket_count):
    distance = jnp.abs(offset)
    magnitude = jnp.zeros_like(offset)
    for edge in bucket_edges:
        magnitude = magnitude + (distance >= int(edge)).astype(jnp.int32)
    return magnitude + bucket_count // 2 * (offset > 0).astype(jnp.int32)


def send(src, dst, send_sem, recv_sem, **device):
    copy = pltpu.make_async_remote_copy(
        src_ref=src,
        dst_ref=dst,
        send_sem=send_sem,
        recv_sem=recv_sem,
        device_id=device,
        device_id_type=MESH,
    )
    copy.start()
    return copy


def arrived(ref, recv_sem):
    pltpu.make_async_copy(ref, ref, recv_sem).wait()


def greet(devices):
    barrier = pltpu.get_barrier_semaphore()
    for device in devices:
        pl.semaphore_signal(barrier, inc=1, device_id=device, device_id_type=MESH)
    pl.semaphore_wait(barrier, len(devices))


def mod(value, size):
    return lax.rem(value + 4 * size, size)


class Place:
    def __init__(self, seqs, dps):
        self.h, self.s, self.d = lax.axis_index("head"), lax.axis_index("seq"), lax.axis_index("dp")
        self.seqs, self.dps = seqs, dps
        self.near = lax.rem(self.h, 2) * -2 + self.h + 1
        self.across = mod(self.h + 2, 4)
        self.near_across = lax.rem(self.across, 2) * -2 + self.across + 1

    def seq_peers(self):
        return [{"seq": mod(self.s + i, self.seqs)} for i in range(1, self.seqs)]

    def dp_peers(self):
        return [{"dp": mod(self.d + i, self.dps)} for i in range(1, self.dps)]

    def head_pair(self):
        return [{"head": self.near}, {"head": self.across}]

    def group_peers(self):
        return [
            {"seq": mod(self.s + i, self.seqs), "dp": mod(self.d + j, self.dps)}
            for i in range(self.seqs)
            for j in range(self.dps)
            if i or j
        ]

    def block(self, j, h=None):
        return mod((self.h if h is None else h) + 2 * (j + self.s), 4)


def params(**more):
    return pltpu.CompilerParams(has_side_effects=True, vmem_limit_bytes=60 * 2**20, **more)


def line_gather(me, own, whole, sems, slot):
    (hop_send, hop_recv, dp_send, dp_recv) = sems
    s, d, count = me.s, me.d, me.seqs

    def spread(src, source):
        for i in range(1, me.dps):
            send(
                src,
                whole.at[source, d],
                dp_send.at[i - 1, source],
                dp_recv.at[i - 1, source],
                dp=mod(d + i, me.dps),
            )

    def spread_wait(source):
        for i in range(1, me.dps):
            here = whole.at[source, mod(d - i, me.dps)]
            arrived(here, dp_recv.at[i - 1, source])
            pltpu.make_async_copy(here, here, dp_send.at[i - 1, source]).wait()

    def start():
        @pl.when(s < count - 1)
        def _():
            send(own, whole.at[s, d], hop_send.at[0, s], hop_recv.at[s], seq=s + 1)

        @pl.when(s > 0)
        def _():
            send(own, whole.at[s, d], hop_send.at[1, s], hop_recv.at[s], seq=s - 1)

        spread(own, s)

    def step(t):
        @pl.when(s - t >= 0)
        def _():
            source = s - t
            here = whole.at[source, d]
            arrived(here, hop_recv.at[source])

            @pl.when(s < count - 1)
            def _():
                send(here, here, hop_send.at[0, source], hop_recv.at[source], seq=s + 1)

            spread(here, source)

        @pl.when(s + t < count)
        def _():
            source = s + t
            here = whole.at[source, d]
            arrived(here, hop_recv.at[source])

            @pl.when(s > 0)
            def _():
                send(here, here, hop_send.at[1, source], hop_recv.at[source], seq=s - 1)

            spread(here, source)

    def finish():
        for source in range(count):
            spread_wait(source)
            here = whole.at[source, d]

            @pl.when((s < count - 1) & (source <= s))
            def _():
                pltpu.make_async_copy(here, here, hop_send.at[0, source]).wait()

            @pl.when((s > 0) & (source >= s))
            def _():
                pltpu.make_async_copy(here, here, hop_send.at[1, source]).wait()

    return start, step, finish


def line_sems(seqs, dps):
    return [
        DMA((2, seqs)),
        DMA((seqs,)),
        DMA((max(1, dps - 1), seqs)),
        DMA((max(1, dps - 1), seqs)),
    ]


def spread_hot(at, shard, width):
    row = lax.broadcasted_iota(jnp.int32, (128, width), 0)
    column = lax.broadcasted_iota(jnp.int32, (128, width), 1)
    return ((column == row + at) & (row < shard)).astype(BF16)


def squeeze_hot(shard, padded, rows, count):
    row = lax.broadcasted_iota(jnp.int32, (rows, count * padded), 0)
    column = lax.broadcasted_iota(jnp.int32, (rows, count * padded), 1)
    inside = lax.rem(column, padded)
    return ((lax.div(column, padded) * shard + inside == row) & (inside < shard)).astype(BF16)


CHUNKS = 4


def front_kernel(
    seqs, dps, heads,
    tok, cot, wq, wk, wv, wo, router, gain_a, gain_f, ids, table, lengths,
    attn_input, weights, split_out, probs, heads_all, own_tok, cot_own, wo_all, gains, ids_all,
    tok_all, pack, pack_all, wo_pad, wo_parts, tile, tile_all, split, ext, slot, out,
    p_sem, ls, z_send, z_recv, h_send, h_recv, c_send, c_recv, a_send, a_recv, w_send, w_recv, i_send, i_recv, *line
):
    me = Place(seqs, dps)
    h, s, d = me.h, me.s, me.d
    per, blocks, span, width = tok_all.shape
    length = blocks * span
    shard, local = wq.shape
    groups = seqs * dps
    experts = router.shape[1]
    part_rows = span // CHUNKS
    half = CHUNKS // 2
    pack[...] = jnp.zeros_like(pack)
    for n, ref in enumerate((wq, wk, wv)):
        pack[:shard, n * local : (n + 1) * local] = ref[...]
    pack[:shard, 3 * local : 3 * local + experts] = router[...]
    wo_pad[...] = jnp.zeros_like(wo_pad)
    wo_pad[:, :shard] = wo[...]
    tile[...] = jnp.zeros_like(tile)
    tile[0:1, :shard] = gain_a[...].astype(F32)
    tile[1:2, :shard] = gain_f[...].astype(F32)
    greet(
        me.seq_peers()
        + [{"head": me.near} | peer for peer in me.seq_peers()]
        + me.dp_peers()
        + [{"head": mod(h + i, 4)} for i in range(1, 4)]
    )
    lines = [
        line_gather(me, pack, pack_all, line[0:4], 0),
        line_gather(me, tile, tile_all, line[4:8], 0),
        line_gather(me, wo_pad, wo_parts, line[8:12], 0),
    ]
    own_copies = [
        pltpu.make_async_copy(pack, pack_all.at[s, d], ls.at[0]),
        pltpu.make_async_copy(tile, tile_all.at[s, d], ls.at[1]),
        pltpu.make_async_copy(wo_pad, wo_parts.at[s, d], ls.at[2]),
        pltpu.make_async_copy(ids, ids_all.at[s], ls.at[3]),
    ]
    for j in range(per):
        own_copies.append(pltpu.make_async_copy(tok.at[per * s + j], tok_all.at[j, s], ls.at[4 + j]))
    for copy in own_copies:
        copy.start()
    for start, _, _ in lines:
        start()
    for i in range(1, seqs):
        send(ids, ids_all.at[s], i_send.at[i - 1], i_recv.at[i - 1], seq=mod(s + i, seqs))

    owns = lax.rem(mod(h - s, 4), 2) == 0
    target = jnp.where(owns, h, me.near)
    turned = lax.div(mod(s - target, 4), 2)
    first = jnp.where(owns, 0, half)

    def chunk(c):
        return pl.ds(pl.multiple_of(c * part_rows, part_rows), part_rows)

    for c in range(half):
        for i in range(1, seqs):
            to = mod(s + i, seqs)
            rows = chunk(first + c)
            which = lax.rem(turned + to, 2)
            send(
                tok.at[per * to + which, rows],
                tok_all.at[which, s, rows],
                z_send.at[i - 1, c],
                z_recv.at[which, first + c],
                head=target,
                seq=to,
            )
        for _, step, _ in lines:
            step(c + 1)

    def build_bias(head):
        turn = lax.broadcasted_iota(jnp.int32, (8, 4 * span), 1)
        bucket = bucket_of(jnp.where(turn < 3 * span, turn, turn - 4 * span) - span, table.shape[0])
        row = jnp.zeros((8, 4 * span), F32)
        for b in range(table.shape[0]):
            row = jnp.where(bucket == b, table[b, head], row)
        rolled = pltpu.roll(jnp.broadcast_to(row[0:1], (span, 4 * span)), 0, 1, stride=1, stride_axis=0)
        ext[head, :, 2 * span : 5 * span] = rolled[:, : 3 * span]
        ext[head, :, : 2 * span] = jnp.broadcast_to(row[0:1, 0:1], (span, 2 * span))
        ext[head, :, 5 * span :] = jnp.broadcast_to(row[0:1, 3 * span - 1 : 3 * span], (span, 2 * span))

    build_bias(0)
    for _, step, _ in lines:
        for t in range(half + 1, seqs):
            step(t)
    for head in range(1, heads):
        build_bias(head)

    def at(j, c, head):
        return tok_all.at[j, me.block(j, head), chunk(c)]

    for c in range(half):
        for part in range(2):
            for j in range(per):
                k = part * half + c
                here = at(j, k, h)

                @pl.when(me.block(j) != s)
                def _():
                    arrived(here, z_recv.at[j, k])
                    send(here, here, h_send.at[0, j, k], h_recv.at[0, j, k], head=me.across)
                    send(here, here, h_send.at[1, j, k], h_recv.at[1, j, k], head=me.near)

    for copy in own_copies:
        copy.wait()
    for _, _, finish in lines:
        finish()
    if shard % 16:
        whole = pack_all[...].reshape(groups * pack.shape[0], pack.shape[1])
        hot = squeeze_hot(shard, pack.shape[0], width, groups)
        weights[...] = jnp.dot(hot, whole, preferred_element_type=F32).astype(BF16)
    else:
        weights[...] = pack_all[...].reshape(width, pack.shape[1])
    row = jnp.zeros((8, width), F32)
    for g in range(groups):
        piece = tile_all[g // dps, g % dps].astype(BF16)
        row = row + jnp.dot(piece, spread_hot(g * shard, shard, width), preferred_element_type=F32)
    gains[...] = row

    def project(j, block):
        rows = pl.ds(pl.multiple_of(block * span, span), span)
        x = tok_all[j, block].astype(F32)
        normed = (x * lax.rsqrt(jnp.mean(x * x, axis=-1, keepdims=True) + EPS) * gains[0:1, :]).astype(BF16)
        attn_input[j, rows, :] = normed
        parts = jnp.dot(normed, weights[...], preferred_element_type=F32).astype(BF16)
        for n in range(3 * heads):
            split[j, n, rows, :] = parts[:, n * HEAD_DIM : (n + 1) * HEAD_DIM]

    for c in range(half):
        for part in range(2):
            for j in range(per):
                k = part * half + c
                there = at(j, k, me.across)

                @pl.when(me.block(j, me.across) != s)
                def _():
                    arrived(there, h_recv.at[0, j, k])
                    send(there, there, h_send.at[2, j, k], h_recv.at[2, j, k], head=me.near)

    @pl.loop(0, 4 * per)
    def _(n):
        hop, j = lax.div(n, per), lax.rem(n, per)
        source = jnp.where(hop == 0, h, jnp.where(hop == 1, me.across, jnp.where(hop == 2, me.near, me.near_across)))
        block = me.block(j, source)

        @pl.when((hop >= 2) & (block != s))
        def _():
            for k in range(CHUNKS):
                arrived(tok_all.at[j, block, chunk(k)], h_recv.at[hop - 1, j, k])

        project(j, block)

    out_split = pltpu.make_async_copy(split, split_out, ls.at[4 + per])
    out_split.start()
    own_tokens = [pltpu.make_async_copy(tok_all.at[j, me.block(j)], own_tok.at[j], ls.at[4 + j]) for j in range(per)]
    for copy in own_tokens:
        copy.start()
    total = jnp.zeros((local, width), F32)
    for g in range(groups):
        total = total + jnp.dot(
            wo_parts[g // dps, g % dps], spread_hot(g * shard, shard, width), preferred_element_type=F32
        )
    wo_all[h] = total.astype(BF16)
    send(wo_all.at[h], wo_all.at[h], w_send.at[0], w_recv.at[0], head=me.across)
    send(wo_all.at[h], wo_all.at[h], w_send.at[1], w_recv.at[1], head=me.near)

    @pl.loop(0, per * blocks)
    def _(unit):
        j, block = lax.div(unit, blocks), lax.rem(unit, blocks)
        rows = pl.ds(pl.multiple_of(block * span, span), span)
        turn = lax.rem(unit, 2)

        @pl.when(unit >= 2)
        def _():
            pltpu.make_async_copy(slot.at[turn], slot.at[turn], p_sem.at[turn]).wait()

        window = pl.ds(pl.multiple_of((blocks - 1 - block) * span, span), length)
        valid = lax.broadcasted_iota(jnp.int32, (1, length), 1) < lengths[per * s + j]
        for head in range(heads):
            query, key, value = split[j, head, rows, :], split[j, heads + head], split[j, 2 * heads + head]
            scores = lax.dot_general(query, key, (((1,), (1,)), ((), ())), preferred_element_type=F32)
            scores = jnp.where(valid, scores + ext[head, :, window], -1e30)
            top = jnp.max(scores, axis=-1, keepdims=True)
            grown = jnp.exp(scores - top)
            total = jnp.sum(grown, axis=-1, keepdims=True)
            part = (grown * (1.0 / total)).astype(BF16)
            slot[turn, head] = part
            mixed = jnp.dot(part, value, preferred_element_type=F32)
            out[unit, :, head * HEAD_DIM : (head + 1) * HEAD_DIM] = mixed.astype(BF16)
        pltpu.make_async_copy(slot.at[turn], probs.at[j, :, rows, :], p_sem.at[turn]).start()
        owner = mod(block - 2 * (j + s), 4)
        away = mod(owner - h, 4)

        @pl.when(away == 0)
        def _():
            pltpu.make_async_copy(out.at[unit], heads_all.at[h, j], ls.at[j]).start()

        @pl.when(away > 0)
        def _():
            send(out.at[unit], heads_all.at[h, j], a_send.at[away - 1, j], a_recv.at[away - 1, j], head=owner)

        for i in range(1, seqs):

            @pl.when(unit == i - 1)
            def _():
                to = mod(s + i, seqs)
                which = lax.rem(turned + to, 2)
                half_rows = pl.ds(pl.multiple_of(first * part_rows, part_rows), half * part_rows)
                send(
                    cot.at[per * to + which, half_rows],
                    cot_own.at[which, half_rows],
                    c_send.at[i - 1],
                    c_recv.at[which, lax.div(first, half)],
                    head=target,
                    seq=to,
                )

        @pl.when(unit == seqs)
        def _():
            there = wo_all.at[me.across]
            arrived(there, w_recv.at[0])
            send(there, there, w_send.at[2], w_recv.at[2], head=me.near)

    out_split.wait()
    for copy in own_tokens:
        copy.wait()
    for turn in range(2):
        pltpu.make_async_copy(slot.at[turn], slot.at[turn], p_sem.at[turn]).wait()
    for j in range(per):
        block = me.block(j)

        @pl.when(block == s)
        def _():
            own = pltpu.make_async_copy(cot.at[per * s + j], cot_own.at[j], ls.at[2 + j])
            own.start()
            own.wait()

        @pl.when(block != s)
        def _():
            for part in range(2):
                arrived(cot_own.at[j, pl.ds(part * half * part_rows, half * part_rows)], c_recv.at[j, part])

        pltpu.make_async_copy(out.at[0], heads_all.at[h, j], ls.at[j]).wait()
        for i in range(1, 4):
            pltpu.make_async_copy(out.at[0], out.at[0], a_send.at[i - 1, j]).wait()
            arrived(heads_all.at[mod(h - i, 4), j], a_recv.at[i - 1, j])
        for k in range(CHUNKS):
            here = at(j, k, h)

            @pl.when(me.block(j) != s)
            def _():
                for n in range(2):
                    pltpu.make_async_copy(here, here, h_send.at[n, j, k]).wait()

            @pl.when(me.block(j, me.across) != s)
            def _():
                pltpu.make_async_copy(here, here, h_send.at[2, j, k]).wait()

    for i in range(1, seqs):
        for c in range(half):
            rows = tok.at[0, pl.ds(0, part_rows)]
            pltpu.make_async_copy(rows, rows, z_send.at[i - 1, c]).wait()
        rows = cot.at[0, pl.ds(0, half * part_rows)]
        pltpu.make_async_copy(rows, rows, c_send.at[i - 1]).wait()
        pltpu.make_async_copy(ids, ids, i_send.at[i - 1]).wait()
        arrived(ids_all.at[mod(s - i, seqs)], i_recv.at[i - 1])
    for k in range(3):
        pltpu.make_async_copy(wo_all.at[h], wo_all.at[h], w_send.at[k]).wait()
    arrived(wo_all.at[me.near], w_recv.at[1])
    arrived(wo_all.at[me.near_across], w_recv.at[2])


def front(tokens, cot, wq, wk, wv, wo, router, gain_a, gain_f, ids, table, lengths, seqs, dps):
    seq_local, span, width = tokens.shape
    per = seq_local // seqs
    length = seqs * span
    shard, local = wq.shape
    heads = local // HEAD_DIM
    lanes = up_to(3 * local + router.shape[1], 128)
    padded = up_to(shard, 16)
    smem = pl.BlockSpec(memory_space=pltpu.SMEM)
    return pl.pallas_call(
        functools.partial(front_kernel, seqs, dps, heads),
        out_shape=(
            jax.ShapeDtypeStruct((per, length, width), BF16),
            jax.ShapeDtypeStruct((width, lanes), BF16),
            jax.ShapeDtypeStruct((per, 3 * heads, length, HEAD_DIM), BF16),
            jax.ShapeDtypeStruct((per, heads, length, length), BF16),
            jax.ShapeDtypeStruct((4, per, span, local), BF16),
            jax.ShapeDtypeStruct((per, span, width), BF16),
            jax.ShapeDtypeStruct((per, span, width), BF16),
            jax.ShapeDtypeStruct((4, local, width), BF16),
            jax.ShapeDtypeStruct((8, width), F32),
            jax.ShapeDtypeStruct((seqs,) + ids.shape, jnp.int32),
        ),
        in_specs=[ANY] * 2 + [VMEM] * 7 + [ANY, smem, smem],
        out_specs=[VMEM] * 2 + [ANY] * 5 + [VMEM] * 2 + [ANY],
        scratch_shapes=[
            pltpu.VMEM((per, seqs, span, width), BF16),
            pltpu.VMEM((padded, lanes), BF16),
            pltpu.VMEM((seqs, dps, padded, lanes), BF16),
            pltpu.VMEM((local, 128), BF16),
            pltpu.VMEM((seqs, dps, local, 128), BF16),
            pltpu.VMEM((8, 128), F32),
            pltpu.VMEM((seqs, dps, 8, 128), F32),
            pltpu.VMEM((per, 3 * heads, length, HEAD_DIM), BF16),
            pltpu.VMEM((heads, span, 7 * span), F32),
            pltpu.VMEM((2, heads, span, length), BF16),
            pltpu.VMEM((per * seqs, span, local), BF16),
            DMA((2,)),
            DMA((5 + per,)),
            DMA((seqs - 1, CHUNKS // 2)),
            DMA((per, CHUNKS)),
            DMA((3, per, CHUNKS)),
            DMA((3, per, CHUNKS)),
            DMA((seqs - 1,)),
            DMA((per, 2)),
            DMA((3, per)),
            DMA((3, per)),
            DMA((3,)),
            DMA((3,)),
            DMA((seqs - 1,)),
            DMA((seqs - 1,)),
        ]
        + line_sems(seqs, dps) * 3,
        compiler_params=params(collective_id=0),
        name="front",
    )(tokens, cot, wq, wk, wv, wo, router, gain_a, gain_f, ids, table, lengths)


def expert_windows(exp_local, per_expert):
    return [(e * per_expert // 16 * 16, up_to((e + 1) * per_expert, 16)) for e in range(exp_local)]


def contract(a, b, over_a, over_b):
    return lax.dot_general(a, b, (((over_a,), (over_b,)), ((), ())), preferred_element_type=F32)


GELU_A, GELU_B = float(np.sqrt(2.0 / np.pi)), 0.044715


def experts_kernel(
    seqs, dps, per_expert, rows, up, down, summed, up_grad, down_grad, taken, near, far,
    ls, g_send, g_recv, h_send, h_recv, n_send, n_recv, x_send, x_recv, r_send, r_recv
):
    me = Place(seqs, dps)
    h, s, d = me.h, me.s, me.d
    groups, _, height, width = rows.shape
    exp_local = up.shape[0]
    windows = expert_windows(exp_local, per_expert)
    me_group = s * dps + d

    def away(n):
        i, j = lax.div(n, dps), lax.rem(n, dps)
        return jnp.where(i == 2, 3, jnp.where(i == 3, 2, i)), j

    def ahead(n):
        i, j = away(n)
        return mod(s + i, seqs), mod(d + j, dps)

    def behind(n):
        i, j = away(n)
        return mod(s - i, seqs), mod(d - j, dps)

    up_grad[...] = jnp.zeros_like(up_grad)
    down_grad[...] = jnp.zeros_like(down_grad)
    greet(me.group_peers() + me.head_pair())
    pltpu.make_async_copy(rows.at[me_group], taken.at[h, 0], ls.at[0]).start()

    @pl.loop(1, groups)
    def _(n):
        to_s, to_d = ahead(n)
        send(rows.at[to_s * dps + to_d], taken.at[h, n], g_send.at[n], g_recv.at[n], seq=to_s, dp=to_d)

    def gather_own(n):
        here = taken.at[h, n]

        @pl.when(n == 0)
        def _():
            pltpu.make_async_copy(here, here, ls.at[0]).wait()

        @pl.when(n > 0)
        def _():
            arrived(here, g_recv.at[n])

        send(here, here, h_send.at[0, n], h_recv.at[0, n], head=me.across)
        send(here, here, h_send.at[1, n], h_recv.at[1, n], head=me.near)

    def gather_across(n):
        there = taken.at[me.across, n]
        arrived(there, h_recv.at[0, n])
        send(there, there, h_send.at[2, n], h_recv.at[2, n], head=me.near)

    def compute(n):
        arrived(taken.at[me.near, n], h_recv.at[1, n])
        arrived(taken.at[me.near_across, n], h_recv.at[2, n])
        for k in range(3):
            pltpu.make_async_copy(taken.at[h, n], taken.at[h, n], h_send.at[k, n]).wait()
        kept = []
        for e, (low, high) in enumerate(windows):
            size = high - low
            at = lax.broadcasted_iota(jnp.int32, (4 * size, width), 0)
            slot = lax.rem(at, size) + low
            inside = (slot >= e * per_expert) & (slot < (e + 1) * per_expert)

            def mine(part):
                block = jnp.concatenate([taken[q, n, part, low:high, :] for q in range(4)], axis=0)
                return jnp.where(inside, block.astype(F32), 0.0).astype(BF16)

            x, g = mine(0), mine(1)
            pre = jnp.dot(x, up[e], preferred_element_type=F32)
            square = pre * pre
            bent = jnp.tanh(GELU_A * pre * (1.0 + GELU_B * square))
            act = (0.5 * pre * (1.0 + bent)).astype(BF16)
            slope = 0.5 * (1.0 + bent) + 0.5 * pre * (1.0 - bent * bent) * (GELU_A * (1.0 + 3.0 * GELU_B * square))
            out = jnp.dot(act, down[e], preferred_element_type=F32).astype(BF16)
            act_grad = contract(g, down[e], 1, 1)
            pre_grad = (act_grad * slope).astype(BF16)
            back = contract(pre_grad, up[e], 1, 1).astype(BF16)
            kept.append((x, g, act, pre_grad, out, back))
        for q in range(4):
            for part in range(2):
                for tile in range(0, height, 16):
                    total = None
                    for (low, high), made in zip(windows, kept):
                        if low <= tile < high:
                            begin = q * (high - low) + tile - low
                            piece = made[4 + part][begin : begin + 16, :]
                            total = piece if total is None else total + piece
                    if total is not None:
                        taken[q, n, part, tile : tile + 16, :] = total
        send(taken.at[me.near_across, n], near.at[0, n], n_send.at[0, n], n_recv.at[0, n], head=me.near)
        send(taken.at[me.near, n], near.at[1, n], n_send.at[1, n], n_recv.at[1, n], head=me.near)
        for e in range(exp_local):
            x, g, act, pre_grad, _, _ = kept[e]
            up_grad[e] += contract(x, pre_grad, 0, 0)
            down_grad[e] += contract(act, g, 0, 0)

    def add_near(n):
        arrived(near.at[0, n], n_recv.at[0, n])
        both = taken[me.across, n].astype(F32) + near[0, n].astype(F32)
        taken[me.across, n] = both.astype(BF16)
        send(taken.at[me.across, n], far.at[n], x_send.at[n], x_recv.at[n], head=me.across)

    def send_back(n):
        arrived(near.at[1, n], n_recv.at[1, n])
        arrived(far.at[n], x_recv.at[n])
        total = taken[h, n].astype(F32) + near[1, n].astype(F32) + far[n].astype(F32)
        taken[h, n] = total.astype(BF16)
        to_s, to_d = behind(n)

        @pl.when(n == 0)
        def _():
            pltpu.make_async_copy(taken.at[h, n], summed.at[me_group], r_send.at[n]).start()

        @pl.when(n > 0)
        def _():
            send(taken.at[h, n], summed.at[me_group], r_send.at[n], r_recv.at[n], seq=to_s, dp=to_d)

    stages = (send_back, add_near, compute, gather_across, gather_own)

    @pl.loop(0, groups + len(stages) - 1)
    def _(step):
        for k, stage in enumerate(stages):
            n = step - (len(stages) - 1 - k)

            @pl.when((n >= 0) & (n < groups))
            def _():
                stage(n)

    @pl.loop(0, groups)
    def _(n):
        here = taken.at[h, n]
        for k in range(2):
            pltpu.make_async_copy(here, here, n_send.at[k, n]).wait()
        pltpu.make_async_copy(here, here, x_send.at[n]).wait()
        pltpu.make_async_copy(here, here, r_send.at[n]).wait()

        @pl.when(n > 0)
        def _():
            pltpu.make_async_copy(here, here, g_send.at[n]).wait()
            from_s, from_d = ahead(n)
            arrived(summed.at[from_s * dps + from_d], r_recv.at[n])


def run_experts(rows, up, down, seqs, dps, per_expert):
    groups, parts, height, width = rows.shape
    return pl.pallas_call(
        functools.partial(experts_kernel, seqs, dps, per_expert),
        out_shape=(
            jax.ShapeDtypeStruct(rows.shape, BF16),
            jax.ShapeDtypeStruct(up.shape, F32),
            jax.ShapeDtypeStruct(down.shape, F32),
        ),
        in_specs=[ANY, VMEM, VMEM],
        out_specs=[ANY, VMEM, VMEM],
        scratch_shapes=[
            pltpu.VMEM((4,) + rows.shape, BF16),
            pltpu.VMEM((2,) + rows.shape, BF16),
            pltpu.VMEM(rows.shape, BF16),
            DMA((1,)),
            DMA((groups,)),
            DMA((groups,)),
            DMA((3, groups)),
            DMA((3, groups)),
            DMA((2, groups)),
            DMA((2, groups)),
            DMA((groups,)),
            DMA((groups,)),
            DMA((groups,)),
            DMA((groups,)),
        ],
        compiler_params=params(collective_id=2),
        name="experts",
    )(rows, up, down)


def send_home(me, own, home, ls, z_send, z_recv, h_send, h_recv):
    h, s, seqs = me.h, me.s, me.seqs
    per = own.shape[0]
    turn = mod(s - h, 4)
    mine = lax.rem(turn, 2) == 0
    turned = lax.div(turn, 2)

    def sources(j, across):
        return [lax.rem(turned + j + across, 2) + 2 * k for k in range(seqs // 2)]

    def start(j):
        to = me.block(j)

        @pl.when(to != s)
        def _():
            send(own.at[j], home.at[per * s + j], z_send.at[j], z_recv.at[s], seq=to)

        @pl.when(to == s)
        def _():
            pltpu.make_async_copy(own.at[j], home.at[per * s + j], ls).start()

    def pass_on(j):
        @pl.when(mine)
        def _():
            for source in sources(j, 0):
                here = home.at[per * source + j]

                @pl.when(source == s)
                def _():
                    pltpu.make_async_copy(here, here, ls).wait()

                @pl.when(source != s)
                def _():
                    arrived(here, z_recv.at[source])

                send(here, here, h_send.at[0, source], h_recv.at[0, source], head=me.across)
                send(here, here, h_send.at[1, source], h_recv.at[1, source], head=me.near)

    def pass_near(j):
        @pl.when(mine)
        def _():
            for source in sources(j, 1):
                there = home.at[per * source + j]
                arrived(there, h_recv.at[0, source])
                send(there, there, h_send.at[2, source], h_recv.at[2, source], head=me.near)

    def finish():
        for j in range(per):

            @pl.when(me.block(j) != s)
            def _():
                pltpu.make_async_copy(own.at[j], own.at[j], z_send.at[j]).wait()

        @pl.when(mine)
        def _():
            for source in range(seqs):
                for k in range(3):
                    here = home.at[per * source]
                    pltpu.make_async_copy(here, here, h_send.at[k, source]).wait()

        @pl.when(jnp.logical_not(mine))
        def _():
            for source in range(seqs):
                arrived(home.at[per * source], h_recv.at[1, source])
                arrived(home.at[per * source + 1], h_recv.at[2, source])

    return start, pass_on, pass_near, finish


def home_sems(per, seqs):
    return [DMA(()), DMA((per,)), DMA((seqs,)), DMA((3, seqs)), DMA((3, seqs))]


def add_groups(me, parts, dp_take, seq_take, result, dp_send, dp_recv, seq_send, seq_recv):
    s, d, seqs, dps = me.s, me.d, me.seqs, me.dps

    def start():
        for i in range(1, dps):
            to = mod(d + i, dps)
            send(parts.at[to], dp_take.at[i - 1], dp_send.at[i - 1], dp_recv.at[i - 1], dp=to)

    def middle():
        for i in range(1, dps):
            arrived(dp_take.at[i - 1], dp_recv.at[i - 1])
        for n in range(seqs):
            to = mod(s + n, seqs)
            total = parts[d, to].astype(F32)
            for i in range(1, dps):
                total = total + dp_take[i - 1, to].astype(F32)
            parts[d, to] = total.astype(parts.dtype)
            if n:
                send(parts.at[d, to], seq_take.at[n - 1], seq_send.at[n - 1], seq_recv.at[n - 1], seq=to)

    def end():
        total = parts[d, s].astype(F32)
        for n in range(1, seqs):
            arrived(seq_take.at[n - 1], seq_recv.at[n - 1])
            total = total + seq_take[n - 1].astype(F32)
        result[...] = total
        for i in range(1, dps):
            pltpu.make_async_copy(dp_take.at[0], dp_take.at[0], dp_send.at[i - 1]).wait()
        for n in range(1, seqs):
            pltpu.make_async_copy(seq_take.at[0], seq_take.at[0], seq_send.at[n - 1]).wait()

    return start, middle, end


def group_scratch(seqs, dps, shape, dtype):
    return [
        pltpu.VMEM((dps, seqs) + shape, dtype),
        pltpu.VMEM((max(1, dps - 1), seqs) + shape, dtype),
        pltpu.VMEM((seqs - 1,) + shape, dtype),
    ]


def group_sems(seqs, dps):
    return [DMA((max(1, dps - 1),))] * 2 + [DMA((seqs - 1,))] * 2


def back_kernel(
    seqs, dps, heads,
    attn_grad, result, hidden_grad, own_tok, heads_all, wo_all, split, probs, attn_input, weights, gains, router, gain_f,
    output, tokens_home, w_sum, small_sum, wo_sum, gain_sum, bias_sum,
    hsend, grad_all, slot, ext, made, dk_sum, dv_sum, w_acc, x_out, x_near, x_far, tg, wo_part, wo_near, wo_far,
    w_parts, w_dp, w_seq, wo_parts, wo_dp, wo_seq, g_parts, g_dp, g_seq, g_acc, bias, bias_take, small, gsmall,
    p_sem, a_send, a_recv, n_send, n_recv, f_send, f_recv, on_send, on_recv, of_send, of_recv,
    b_send, b_recv, s_send, s_recv, t_send, t_recv, *sems
):
    me = Place(seqs, dps)
    h, s, d = me.h, me.s, me.d
    per, span, width = attn_grad.shape
    blocks = seqs
    length = blocks * span
    local = heads * HEAD_DIM
    groups = seqs * dps
    shard = width // groups
    padded = w_sum.shape[0]
    lanes = weights.shape[1]
    experts = router.shape[1]
    buckets = 32
    others = [(i, j) for i in range(seqs) for j in range(dps) if i or j]
    order = (h, me.near, me.across, me.near_across)
    greet(me.group_peers() + [{"head": mod(h + i, 4)} for i in range(1, 4)])
    out_home = send_home(me, result, output, *sems[0:5])
    grad_home = send_home(me, tg, tokens_home, *sems[5:10])
    w_group = add_groups(me, w_parts, w_dp, w_seq, w_sum, *sems[10:14])
    wo_group = add_groups(me, wo_parts, wo_dp, wo_seq, wo_sum, *sems[14:18])
    g_group = add_groups(me, g_parts, g_dp, g_seq, gain_sum, *sems[18:22])

    def fetch(j, n):
        q = jnp.where(n == 0, h, jnp.where(n == 1, me.near, jnp.where(n == 2, me.across, me.near_across)))
        block = me.block(j, q)
        rows = pl.ds(pl.multiple_of(block * span, span), span)
        turn = lax.rem(n, 2)
        return q, block, rows, turn, pltpu.make_async_copy(probs.at[j, :, rows, :], slot.at[turn], p_sem.at[turn])

    fetch(0, 0)[4].start()
    for j in range(per):
        for i in (1, 2, 3, 0):
            to = mod(h + i, 4)
            grad = contract(attn_grad[j], wo_all[to], 1, 1).astype(BF16)
            if i:
                hsend[j, i - 1] = grad
                send(
                    hsend.at[j, i - 1],
                    grad_all.at[j, me.block(j)],
                    a_send.at[i - 1, j],
                    a_recv.at[i - 1, j],
                    head=to,
                )
            else:
                grad_all[j, me.block(j)] = grad
    for k, q in enumerate((me.near_across, me.near, me.across, h)):
        total = jnp.zeros((local, width), F32)
        for j in range(per):
            total = total + contract(heads_all[q, j], attn_grad[j], 0, 0)
        wo_part[k] = total.astype(BF16)
        if k < 2:
            send(wo_part.at[k], wo_near.at[k], on_send.at[k], on_recv.at[k], head=me.near)
    for j in range(per):
        out_home[0](j)
    ext[...] = jnp.zeros_like(ext)
    made[...] = jnp.zeros_like(made)

    def wo_across():
        arrived(wo_near.at[0], on_recv.at[0])
        wo_part[2] = (wo_part[2].astype(F32) + wo_near[0].astype(F32)).astype(BF16)
        send(wo_part.at[2], wo_far, of_send, of_recv, head=me.across)

    def wo_total():
        arrived(wo_near.at[1], on_recv.at[1])
        arrived(wo_far, of_recv)
        total = (wo_part[3].astype(F32) + wo_near[1].astype(F32) + wo_far[...].astype(F32)).astype(BF16)
        for g in range(groups):
            hot = spread_hot(g * shard, shard, width)
            wo_parts[g % dps, g // dps] = contract(total, hot, 1, 1).astype(BF16)
        wo_group[0]()

    def x_partial(j):
        for k, q in enumerate((me.near_across, me.near, me.across, h)):
            rows = pl.ds(pl.multiple_of(me.block(j, q) * span, span), span)
            x_out[j, k] = contract(made[j, rows, :], weights[...], 1, 1).astype(BF16)
            if k < 2:
                send(x_out.at[j, k], x_near.at[j, k], n_send.at[j, k], n_recv.at[j, k], head=me.near)

    def x_across(j):
        arrived(x_near.at[j, 0], n_recv.at[j, 0])
        x_out[j, 2] = (x_out[j, 2].astype(F32) + x_near[j, 0].astype(F32)).astype(BF16)
        send(x_out.at[j, 2], x_far.at[j], f_send.at[j], f_recv.at[j], head=me.across)

    def x_total(j):
        arrived(x_near.at[j, 1], n_recv.at[j, 1])
        arrived(x_far.at[j], f_recv.at[j])
        grad = x_out[j, 3].astype(F32) + x_near[j, 1].astype(F32) + x_far[j].astype(F32)
        v = own_tok[j].astype(F32)
        inverse = lax.rsqrt(jnp.mean(v * v, axis=-1, keepdims=True) + EPS)
        r = v * inverse
        u = grad * gains[0:1, :]
        back = (u - r * jnp.mean(u * r, axis=-1, keepdims=True)) * inverse
        tg[j] = (hidden_grad[j] + back).astype(BF16)
        grad_home[0](j)
        g_acc[0:1, :] += jnp.sum(grad * r, axis=0, keepdims=True)

    def attention(j, service):
        @pl.loop(0, blocks)
        def _(n):
            q, block, rows, turn, copy = fetch(j, n)
            away = mod(h - q, 4)

            @pl.when(away > 0)
            def _():
                arrived(grad_all.at[j, block], a_recv.at[away - 1, j])

            copy.wait()

            @pl.when(n < blocks - 1)
            def _():
                fetch(j, n + 1)[4].start()

            if j < per - 1:

                @pl.when(n == blocks - 1)
                def _():
                    fetch(j + 1, 0)[4].start()

            window = pl.ds(pl.multiple_of((blocks - 1 - block) * span, span), length)
            for head in range(heads):
                cols = slice(head * HEAD_DIM, (head + 1) * HEAD_DIM)
                query = split[j, head, rows, :]
                key, value = split[j, heads + head], split[j, 2 * heads + head]
                grad = grad_all[j, block, :, cols]
                part = slot[turn, head]
                prob_grad = contract(grad, value, 1, 1)
                wide = part.astype(F32)
                delta = jnp.sum(wide * prob_grad, axis=-1, keepdims=True)
                score_grad = wide * (prob_grad - delta)
                ext[head, :, window] += score_grad
                low = score_grad.astype(BF16)
                made[j, rows, cols] = jnp.dot(low, key, preferred_element_type=F32).astype(BF16)
                dk = contract(low, query, 0, 0)
                dv = contract(part, grad, 0, 0)

                @pl.when(n == 0)
                def _():
                    dk_sum[head] = dk
                    dv_sum[head] = dv

                @pl.when(n > 0)
                def _():
                    dk_sum[head] += dk
                    dv_sum[head] += dv

            for k, call in enumerate(service):

                @pl.when(n == k)
                def _():
                    for act in call:
                        act()

        for head in range(heads):
            cols = slice(local + head * HEAD_DIM, local + (head + 1) * HEAD_DIM)
            made[j, :, cols] = dk_sum[head].astype(BF16)
            cols = slice(2 * local + head * HEAD_DIM, 2 * local + (head + 1) * HEAD_DIM)
            made[j, :, cols] = dv_sum[head].astype(BF16)
        x_partial(j)
        total = contract(attn_input[j], made[j], 0, 0)
        if j == 0:
            w_acc[...] = total
        else:
            w_acc[...] += total

    g_acc[...] = jnp.zeros_like(g_acc)
    g_acc[1:2, :] = gain_f[...]
    attention(
        0,
        (
            (wo_across,),
            (lambda: out_home[1](0),),
            (wo_total, lambda: out_home[1](1)),
            (lambda: out_home[2](0), lambda: out_home[2](1)),
        ),
    )
    attention(
        1,
        (
            (lambda: x_across(0), wo_group[1]),
            (lambda: x_total(0),),
            (lambda: grad_home[1](0),),
            (lambda: grad_home[2](0),),
        ),
    )
    x_across(1)
    w_acc[:, 3 * local : 3 * local + experts] = router[...]
    low = w_acc[...].astype(BF16)
    if shard % 16:
        low = contract(squeeze_hot(shard, padded, width, groups), low, 0, 0).astype(BF16)
    for g in range(groups):
        w_parts[g % dps, g // dps] = low[g * padded : (g + 1) * padded, :]
    w_group[0]()
    turn = lax.broadcasted_iota(jnp.int32, (4 * span, 128), 0)
    bucket = bucket_of(jnp.where(turn < 3 * span, turn, turn - 4 * span) - span, buckets)
    hot = (bucket == lax.broadcasted_iota(jnp.int32, (4 * span, 128), 1)).astype(F32)
    lane = lax.broadcasted_iota(jnp.int32, (1, 128), 1)
    head_row = lax.broadcasted_iota(jnp.int32, (8, 4 * span), 0)
    diagonals = jnp.zeros((8, 4 * span), F32)
    far_row = lax.broadcasted_iota(jnp.int32, (8, 128), 0)
    far = jnp.zeros((8, 128), F32)
    for head in range(heads):
        eight = jnp.zeros((8, 4 * span), F32)
        for group in range(span // 8):
            piece = ext[head, group * 8 : (group + 1) * 8, 2 * span : 5 * span]
            piece = jnp.concatenate([piece, jnp.zeros((8, span), F32)], axis=1)
            eight = eight + pltpu.roll(piece, (4 * span - 8 * group) % (4 * span), 1)
        one = jnp.zeros((8, 4 * span), F32)
        for i in range(8):
            line = jnp.broadcast_to(eight[i : i + 1, :], (8, 4 * span))
            one = one + pltpu.roll(line, (4 * span - i) % (4 * span), 1)
        diagonals = jnp.where(head_row == head, one, diagonals)
        left, right = jnp.sum(ext[head, :, : 2 * span]), jnp.sum(ext[head, :, 5 * span :])
        sides = jnp.where(lane == buckets // 2 - 1, left, jnp.where(lane == buckets - 1, right, 0.0))
        far = jnp.where(far_row == head, sides, far)
    bias[...] = far + jnp.dot(diagonals, hot, preferred_element_type=F32, precision=lax.Precision.HIGHEST)
    for n, (i, j) in enumerate(others):
        send(bias, bias_take.at[n], b_send.at[n], b_recv.at[n], seq=mod(s + i, seqs), dp=mod(d + j, dps))
    w_group[1]()
    x_total(1)
    g_rows = g_acc[...].astype(BF16)
    for g in range(groups):
        g_parts[g % dps, g // dps] = contract(g_rows, spread_hot(g * shard, shard, width), 1, 1)
    g_group[0]()
    g_group[1]()
    w_group[2]()
    small[0] = w_sum[:, lanes - small.shape[-1] :]
    for i in range(1, 4):
        send(small.at[0], small.at[i], s_send.at[i - 1], s_recv.at[i - 1], head=mod(h + i, 4))
    grad_home[1](1)
    g_group[2]()
    gsmall[0] = gain_sum[...]
    for i in range(1, 4):
        send(gsmall.at[0], gsmall.at[i], t_send.at[i - 1], t_recv.at[i - 1], head=mod(h + i, 4))
    grad_home[2](1)
    wo_group[2]()
    total = bias[...]
    for n in range(len(others)):
        arrived(bias_take.at[n], b_recv.at[n])
        total = total + bias_take[n]
    bias_sum[...] = total
    total, gain_total = small[0], gsmall[0]
    for i in range(1, 4):
        arrived(small.at[i], s_recv.at[i - 1])
        arrived(gsmall.at[i], t_recv.at[i - 1])
        total = total + small[i]
        gain_total = gain_total + gsmall[i]
    small_sum[...] = total
    gain_sum[...] = gain_total
    out_home[3]()
    grad_home[3]()
    for j in range(per):
        for i in range(3):
            pltpu.make_async_copy(hsend.at[0, 0], hsend.at[0, 0], a_send.at[i, j]).wait()
        for k in range(2):
            pltpu.make_async_copy(x_near.at[0, 0], x_near.at[0, 0], n_send.at[j, k]).wait()
        pltpu.make_async_copy(x_near.at[0, 0], x_near.at[0, 0], f_send.at[j]).wait()
    for k in range(2):
        pltpu.make_async_copy(wo_far, wo_far, on_send.at[k]).wait()
    pltpu.make_async_copy(wo_far, wo_far, of_send).wait()
    for i in range(3):
        pltpu.make_async_copy(small.at[0], small.at[0], s_send.at[i]).wait()
        pltpu.make_async_copy(gsmall.at[0], gsmall.at[0], t_send.at[i]).wait()
    for n in range(len(others)):
        pltpu.make_async_copy(bias, bias, b_send.at[n]).wait()


def back_pass(
    attn_grad, result, hidden_grad, own_tok, heads_all, wo_all, split, probs, attn_input, weights, gains, router, gain_f,
    seqs, dps
):
    per, span, width = attn_grad.shape
    length = seqs * span
    heads = probs.shape[1]
    local = heads * HEAD_DIM
    groups = seqs * dps
    shard = width // groups
    padded = up_to(shard, 16)
    lanes = weights.shape[1]
    block = (span, width)
    return pl.pallas_call(
        functools.partial(back_kernel, seqs, dps, heads),
        out_shape=(
            jax.ShapeDtypeStruct((per * seqs,) + block, BF16),
            jax.ShapeDtypeStruct((per * seqs,) + block, BF16),
            jax.ShapeDtypeStruct((padded, lanes), F32),
            jax.ShapeDtypeStruct((padded, 128 * (lanes // 128 - 3 * local // 128)), F32),
            jax.ShapeDtypeStruct((local, 128), F32),
            jax.ShapeDtypeStruct((8, 128), F32),
            jax.ShapeDtypeStruct((8, 128), F32),
        ),
        in_specs=[VMEM, ANY] + [VMEM] * 5 + [ANY] + [VMEM] * 5,
        out_specs=[ANY] * 2 + [VMEM] * 5,
        scratch_shapes=[
            pltpu.VMEM((per, 3, span, local), BF16),
            pltpu.VMEM((per, seqs, span, local), BF16),
            pltpu.VMEM((2, heads, span, length), BF16),
            pltpu.VMEM((heads, span, 7 * span), F32),
            pltpu.VMEM((per, length, lanes), BF16),
            pltpu.VMEM((heads, length, HEAD_DIM), F32),
            pltpu.VMEM((heads, length, HEAD_DIM), F32),
            pltpu.VMEM((width, lanes), F32),
            pltpu.VMEM((per, 4) + block, BF16),
            pltpu.VMEM((per, 2) + block, BF16),
            pltpu.VMEM((per,) + block, BF16),
            pltpu.VMEM((per,) + block, BF16),
            pltpu.VMEM((4, local, width), BF16),
            pltpu.VMEM((2, local, width), BF16),
            pltpu.VMEM((local, width), BF16),
        ]
        + group_scratch(seqs, dps, (padded, lanes), BF16)
        + group_scratch(seqs, dps, (local, 128), BF16)
        + group_scratch(seqs, dps, (8, 128), F32)
        + [
            pltpu.VMEM((8, width), F32),
            pltpu.VMEM((8, 128), F32),
            pltpu.VMEM((groups - 1, 8, 128), F32),
            pltpu.VMEM((4, padded, 128 * (lanes // 128 - 3 * local // 128)), F32),
            pltpu.VMEM((4, 8, 128), F32),
            DMA((2,)),
            DMA((3, per)),
            DMA((3, per)),
            DMA((per, 2)),
            DMA((per, 2)),
            DMA((per,)),
            DMA((per,)),
            DMA((2,)),
            DMA((2,)),
            DMA(()),
            DMA(()),
            DMA((groups - 1,)),
            DMA((groups - 1,)),
            DMA((3,)),
            DMA((3,)),
            DMA((3,)),
            DMA((3,)),
        ]
        + home_sems(per, seqs) * 2
        + group_sems(seqs, dps) * 3,
        compiler_params=params(collective_id=4),
        name="back",
    )(attn_grad, result, hidden_grad, own_tok, heads_all, wo_all, split, probs, attn_input, weights, gains, router, gain_f)


def up_to(value, unit):
    return -(-value // unit) * unit


def body(
    tokens,
    lengths,
    expert_ids,
    attention_gain,
    query_weight,
    key_weight,
    value_weight,
    output_weight,
    position_bias,
    feedforward_gain,
    router_weight,
    expert_up,
    expert_down,
    cotangent,
):
    seqs, dps = lax.axis_size("seq"), lax.axis_size("dp")
    groups = seqs * dps
    seq_local, span, width = tokens.shape
    per = seq_local // seqs
    length = seqs * span
    count = per * length
    own_rows = per * span
    local_width = query_weight.shape[1]
    bucket_count, heads = position_bias.shape
    experts = router_weight.shape[1]
    exp_local = expert_up.shape[0]
    shard = query_weight.shape[0]
    head_at, seq_at = lax.axis_index("head"), lax.axis_index("seq")

    ids = expert_ids.reshape(seq_local, span)
    attn_input, weights, split, probs, heads_all, own_tok, cot_own, out_weight, gains, ids_all = front(
        tokens,
        cotangent,
        query_weight,
        key_weight,
        value_weight,
        output_weight,
        router_weight,
        attention_gain[None, :],
        feedforward_gain[None, :],
        ids,
        position_bias.astype(F32),
        lengths,
        seqs,
        dps,
    )
    router_full = weights[:, 3 * local_width : 3 * local_width + experts]
    gain_two = gains[1]
    heads_all = heads_all.reshape(4, own_rows, local_width)
    own_blocks = [lax.rem(head_at + 2 * (j + seq_at), 4) for j in range(per)]
    own_inputs = own_tok.reshape(own_rows, width).astype(F32)
    attention = jnp.einsum("htk,hkd->td", heads_all, out_weight, preferred_element_type=F32)
    hidden = own_inputs + attention
    ffn_input = normalize(hidden, gain_two).astype(BF16)
    logits = jnp.dot(ffn_input, router_full, preferred_element_type=F32)
    router_probs = jax.nn.softmax(logits, axis=-1)

    capacity = max(2, (5 * span + 4 * experts - 1) // (4 * experts))
    own_ids = jnp.stack(
        [
            lax.dynamic_index_in_dim(lax.dynamic_index_in_dim(ids_all, own_blocks[j], 0, False), per * seq_at + j, 0, False)
            for j in range(per)
        ]
    )
    earlier = jnp.arange(span)[None, :] < jnp.arange(span)[:, None]
    same = (own_ids[:, :, None] == own_ids[:, None, :]) & earlier[None]
    slot = jnp.sum(same.astype(jnp.int32), axis=-1)
    rows_used = exp_local * per * capacity
    rows_pad = up_to(rows_used, 16)
    place = (
        own_ids // exp_local * rows_pad
        + (own_ids % exp_local * per + jnp.arange(per, dtype=jnp.int32)[:, None]) * capacity
        + slot
    ).reshape(own_rows)
    spots = groups * rows_pad
    place_hot = (jnp.arange(spots, dtype=jnp.int32)[:, None] == place[None, :]).astype(BF16)
    hot = (own_ids.reshape(own_rows, 1) == jnp.arange(experts, dtype=jnp.int32)).astype(F32)
    gate = jnp.sum(router_probs * hot, axis=-1)
    grad_out = cot_own.reshape(own_rows, width).astype(F32)
    sent_grad = (gate[:, None] * grad_out).astype(BF16)
    to_send = jnp.concatenate([ffn_input, sent_grad], axis=1)
    rows = jnp.dot(place_hot, to_send, preferred_element_type=F32).astype(BF16)
    rows = jnp.swapaxes(rows.reshape(groups, rows_pad, 2, width), 1, 2)
    summed, up_grad, down_grad = run_experts(rows, expert_up, expert_down, seqs, dps, per * capacity)
    summed = jnp.swapaxes(summed, 1, 2).reshape(spots, 2 * width)
    back = jnp.einsum("rt,rd->td", place_hot, summed, preferred_element_type=F32)
    back = (back[:, :width], back[:, width:])
    token_out, expert_input_grad = back[0], back[1]
    result = (hidden + gate[:, None] * token_out).astype(BF16)
    gate_grad = jnp.sum(grad_out * token_out, axis=-1)
    logit_grad = router_probs * (gate_grad[:, None] * hot - (gate_grad * gate)[:, None])
    logit_low = logit_grad.astype(BF16)
    router_grad = jnp.einsum("td,te->de", ffn_input, logit_low, preferred_element_type=F32)
    ffn_input_grad = expert_input_grad + jnp.einsum("te,de->td", logit_low, router_full, preferred_element_type=F32)
    _, norm_pull = jax.vjp(normalize, hidden, gain_two)
    hidden_norm_grad, gain_two_grad = norm_pull(ffn_input_grad)
    hidden_grad = grad_out + hidden_norm_grad
    attn_grad = hidden_grad.astype(BF16)
    output, tokens_grad, w_sum, small_sum, wo_sum, gain_sum, bias_sum = back_pass(
        attn_grad.reshape(per, span, width),
        result.reshape(per, span, width),
        hidden_grad.reshape(per, span, width),
        own_tok,
        heads_all.reshape(4, per, span, local_width),
        out_weight,
        split,
        probs,
        attn_input,
        weights,
        gains,
        router_grad,
        gain_two_grad[None, :],
        seqs,
        dps,
    )
    at = 3 * local_width - (w_sum.shape[1] - small_sum.shape[1])
    return (
        output,
        tokens_grad,
        gain_sum[0, :shard],
        w_sum[:shard, :local_width],
        w_sum[:shard, local_width : 2 * local_width],
        w_sum[:shard, 2 * local_width : 3 * local_width],
        wo_sum[:, :shard],
        bias_sum[:heads, :bucket_count].T,
        gain_sum[1, :shard],
        small_sum[:shard, at : at + experts],
        up_grad,
        down_grad,
    )


def solution(mesh):
    placed = (
        P("dp", "seq", None),
        P("dp"),
        P("dp", "seq", None),
        P(("seq", "dp")),
        P(("seq", "dp"), "head"),
        P(("seq", "dp"), "head"),
        P(("seq", "dp"), "head"),
        P("head", ("seq", "dp")),
        P(None, "head"),
        P(("seq", "dp")),
        P(("seq", "dp"), None),
        P(("seq", "dp"), None, "head"),
        P(("seq", "dp"), "head", None),
        P("dp", "seq", None),
    )
    return jax.shard_map(
        body,
        mesh=mesh,
        in_specs=placed,
        out_specs=(
            P("dp", "seq", None),
            P("dp", "seq", None),
            P(("seq", "dp")),
            P(("seq", "dp"), "head"),
            P(("seq", "dp"), "head"),
            P(("seq", "dp"), "head"),
            P("head", ("seq", "dp")),
            P(None, "head"),
            P(("seq", "dp")),
            P(("seq", "dp"), None),
            P(("seq", "dp"), None, "head"),
            P(("seq", "dp"), "head", None),
        ),
        check_vma=False,
    )
```

```python
import functools

import jax
import jax.numpy as jnp
import numpy as np
from jax import lax
from jax.experimental import pallas as pl
from jax.experimental.pallas import tpu as pltpu
from jax.sharding import PartitionSpec as P

HEAD_DIM = 64
EPS = 1e-06
bucket_edges = np.array([1, 2, 3, 4, 5, 6, 7, 8, 12, 16, 23, 32, 46, 64, 91], np.int32)
ANY = pl.BlockSpec(memory_space=pl.ANY)
VMEM = pl.BlockSpec(memory_space=pltpu.VMEM)
MESH = pl.DeviceIdType.MESH
DMA = pltpu.SemaphoreType.DMA
F32 = jnp.float32
BF16 = jnp.bfloat16


def bucket_of(offset, bucket_count):
    distance = jnp.abs(offset)
    magnitude = jnp.zeros_like(offset)
    for edge in bucket_edges:
        magnitude = magnitude + (distance >= int(edge)).astype(jnp.int32)
    return magnitude + bucket_count // 2 * (offset > 0).astype(jnp.int32)


def send(src, dst, send_sem, recv_sem, **device):
    copy = pltpu.make_async_remote_copy(
        src_ref=src,
        dst_ref=dst,
        send_sem=send_sem,
        recv_sem=recv_sem,
        device_id=device,
        device_id_type=MESH,
    )
    copy.start()
    return copy


def arrived(ref, recv_sem):
    pltpu.make_async_copy(ref, ref, recv_sem).wait()


def greet(devices):
    barrier = pltpu.get_barrier_semaphore()
    for device in devices:
        pl.semaphore_signal(barrier, inc=1, device_id=device, device_id_type=MESH)
    pl.semaphore_wait(barrier, len(devices))


def mod(value, size):
    return lax.rem(value + 4 * size, size)


class Place:
    def __init__(self, seqs, dps):
        self.h, self.s, self.d = lax.axis_index("head"), lax.axis_index("seq"), lax.axis_index("dp")
        self.seqs, self.dps = seqs, dps
        self.near = lax.rem(self.h, 2) * -2 + self.h + 1
        self.across = mod(self.h + 2, 4)
        self.near_across = lax.rem(self.across, 2) * -2 + self.across + 1

    def seq_peers(self):
        return [{"seq": mod(self.s + i, self.seqs)} for i in range(1, self.seqs)]

    def dp_peers(self):
        return [{"dp": mod(self.d + i, self.dps)} for i in range(1, self.dps)]

    def head_pair(self):
        return [{"head": self.near}, {"head": self.across}]

    def group_peers(self):
        return [
            {"seq": mod(self.s + i, self.seqs), "dp": mod(self.d + j, self.dps)}
            for i in range(self.seqs)
            for j in range(self.dps)
            if i or j
        ]

    def block(self, j, h=None):
        return mod((self.h if h is None else h) + 2 * (j + self.s), 4)


def params(**more):
    return pltpu.CompilerParams(has_side_effects=True, vmem_limit_bytes=60 * 2**20, **more)


def gather_groups(me, own, whole, z_send, z_recv, dp_send, dp_recv):
    s, d, seqs, dps = me.s, me.d, me.seqs, me.dps

    def spread(src, source):
        for i in range(1, dps):
            send(
                src,
                whole.at[source, d],
                dp_send.at[i - 1, source],
                dp_recv.at[i - 1, source],
                dp=mod(d + i, dps),
            )

    def start():
        for i in range(1, seqs):
            send(own, whole.at[s, d], z_send.at[i - 1], z_recv.at[i - 1], seq=mod(s + i, seqs))
        spread(own, s)

    def relay(i):
        source = mod(s - i, seqs)
        here = whole.at[source, d]
        arrived(here, z_recv.at[i - 1])
        spread(here, source)

    def finish():
        for i in range(1, dps):
            for source in range(seqs):
                arrived(whole.at[source, mod(d - i, dps)], dp_recv.at[i - 1, source])
                pltpu.make_async_copy(own, own, dp_send.at[i - 1, source]).wait()
        for i in range(1, seqs):
            pltpu.make_async_copy(own, own, z_send.at[i - 1]).wait()

    return start, relay, finish


def gather_sems(seqs, dps):
    return [
        DMA((seqs - 1,)),
        DMA((seqs - 1,)),
        DMA((max(1, dps - 1), seqs)),
        DMA((max(1, dps - 1), seqs)),
    ]


def spread_hot(at, shard, width):
    row = lax.broadcasted_iota(jnp.int32, (128, width), 0)
    column = lax.broadcasted_iota(jnp.int32, (128, width), 1)
    return ((column == row + at) & (row < shard)).astype(BF16)


def squeeze_hot(shard, padded, rows, count):
    row = lax.broadcasted_iota(jnp.int32, (rows, count * padded), 0)
    column = lax.broadcasted_iota(jnp.int32, (rows, count * padded), 1)
    inside = lax.rem(column, padded)
    return ((lax.div(column, padded) * shard + inside == row) & (inside < shard)).astype(BF16)


CHUNKS = 8


def front_kernel(
    seqs, dps, heads,
    tok, cot, wq, wk, wv, wo, router, gain_a, gain_f, ids, table, lengths,
    attn_input, weights, split, probs, heads_all, own_tok, cot_own, wo_all, gains, ids_all,
    tok_all, pack, pack_all, wo_pad, wo_parts, tile, tile_all, ext, slot, out,
    p_sem, ls, z_send, z_recv, h_send, h_recv, c_send, c_recv, a_send, a_recv, w_send, w_recv, i_send, i_recv, *line
):
    me = Place(seqs, dps)
    h, s, d = me.h, me.s, me.d
    per, blocks, span, width = tok_all.shape
    length = blocks * span
    shard, local = wq.shape
    groups = seqs * dps
    experts = router.shape[0]
    part_rows = span // CHUNKS
    half = CHUNKS // 2
    pack[...] = jnp.zeros_like(pack)
    split[...] = jnp.zeros_like(split)
    for n, ref in enumerate((wq, wk, wv)):
        pack[:shard, n * local : (n + 1) * local] = ref[...]
    same = lax.broadcasted_iota(jnp.int32, (experts, experts), 0) == lax.broadcasted_iota(jnp.int32, (experts, experts), 1)
    pack[:shard, 3 * local : 3 * local + experts] = contract(router[...], same.astype(BF16), 0, 0).astype(BF16)
    wo_pad[...] = jnp.zeros_like(wo_pad)
    wo_pad[:, :shard] = wo[...]
    tile[...] = jnp.zeros_like(tile)
    tile[0:1, :shard] = gain_a[...].astype(F32)
    tile[1:2, :shard] = gain_f[...].astype(F32)
    greet(
        me.seq_peers()
        + [{"head": me.near} | peer for peer in me.seq_peers()]
        + me.dp_peers()
        + [{"head": mod(h + i, 4)} for i in range(1, 4)]
    )
    gathers = [
        gather_groups(me, pack, pack_all, *line[0:4]),
        gather_groups(me, tile, tile_all, *line[4:8]),
        gather_groups(me, wo_pad, wo_parts, *line[8:12]),
    ]
    own_copies = [
        pltpu.make_async_copy(pack, pack_all.at[s, d], ls.at[0]),
        pltpu.make_async_copy(tile, tile_all.at[s, d], ls.at[1]),
        pltpu.make_async_copy(wo_pad, wo_parts.at[s, d], ls.at[2]),
        pltpu.make_async_copy(ids, ids_all.at[s], ls.at[3]),
    ]
    for j in range(per):
        own_copies.append(pltpu.make_async_copy(tok.at[per * s + j], tok_all.at[j, s], ls.at[4 + j]))
    for copy in own_copies:
        copy.start()
    for j in range(per):

        @pl.when(me.block(j) == s)
        def _():
            pltpu.make_async_copy(cot.at[per * s + j], cot_own.at[j], ls.at[4 + per + j]).start()

    for start, _, _ in gathers[:2]:
        start()
    for i in range(1, seqs):
        send(ids, ids_all.at[s], i_send.at[i - 1], i_recv.at[i - 1], seq=mod(s + i, seqs))

    owns = lax.rem(mod(h - s, 4), 2) == 0
    target = jnp.where(owns, h, me.near)
    turned = lax.div(mod(s - target, 4), 2)
    first = jnp.where(owns, 0, half)

    def chunk(c):
        return pl.ds(pl.multiple_of(c * part_rows, part_rows), part_rows)

    def send_round(c):
        for i in range(1, seqs):
            to = mod(s + i, seqs)
            rows = chunk(first + c)
            which = lax.rem(turned + to, 2)
            send(
                tok.at[per * to + which, rows],
                tok_all.at[which, s, rows],
                z_send.at[i - 1, c],
                z_recv.at[which, first + c],
                head=target,
                seq=to,
            )

    def send_later():
        gathers[2][0]()
        for i in range(1, seqs):
            to = mod(s + i, seqs)
            which = lax.rem(turned + to, 2)
            half_rows = pl.ds(pl.multiple_of(first * part_rows, part_rows), half * part_rows)
            send(
                cot.at[per * to + which, half_rows],
                cot_own.at[which, half_rows],
                c_send.at[i - 1],
                c_recv.at[which, lax.div(first, half)],
                head=target,
                seq=to,
            )

    send_round(0)
    send_round(1)

    buckets = table.shape[1]
    turn = lax.broadcasted_iota(jnp.int32, (buckets, 4 * span), 1)
    bucket = bucket_of(jnp.where(turn < 3 * span, turn, turn - 4 * span) - span, buckets)
    hot = (bucket == lax.broadcasted_iota(jnp.int32, (buckets, 4 * span), 0)).astype(BF16)
    bias_rows = jnp.dot(table[...], hot, preferred_element_type=F32)

    def build_bias(head):
        row = bias_rows[head : head + 1]
        rolled = pltpu.roll(jnp.broadcast_to(row, (span, 4 * span)), 0, 1, stride=1, stride_axis=0)
        ext[head, :, 2 * span : 5 * span] = rolled[:, : 3 * span]
        ext[head, :, : 2 * span] = jnp.broadcast_to(row[0:1, 0:1], (span, 2 * span))
        ext[head, :, 5 * span :] = jnp.broadcast_to(row[0:1, 3 * span - 1 : 3 * span], (span, 2 * span))

    for head in range(heads):
        build_bias(head)
    for i in range(1, seqs):
        for _, relay, _ in gathers[:2]:
            relay(i)
    send_round(2)

    def at(j, c, head):
        return tok_all.at[j, me.block(j, head), chunk(c)]

    items = [(j, part * half + c) for c in range(half) for part in range(2) for j in range(per)]

    def pass_own(j, k):
        here = at(j, k, h)

        @pl.when(me.block(j) != s)
        def _():
            arrived(here, z_recv.at[j, k])
            send(here, here, h_send.at[0, j, k], h_recv.at[0, j, k], head=me.across)
            send(here, here, h_send.at[1, j, k], h_recv.at[1, j, k], head=me.near)

    def pass_across(j, k):
        there = at(j, k, me.across)

        @pl.when(me.block(j, me.across) != s)
        def _():
            arrived(there, h_recv.at[0, j, k])
            send(there, there, h_send.at[2, j, k], h_recv.at[2, j, k], head=me.near)

    def project(j, block):
        rows = pl.ds(pl.multiple_of(block * span, span), span)
        x = tok_all[j, block].astype(F32)
        normed = (x * lax.rsqrt(jnp.mean(x * x, axis=-1, keepdims=True) + EPS) * gains[0:1, :]).astype(BF16)
        attn_input[j, rows, :] = normed
        parts = jnp.dot(normed, weights[...], preferred_element_type=F32).astype(BF16)
        for n in range(3 * heads):
            split[j, n, rows, :HEAD_DIM] = parts[:, n * HEAD_DIM : (n + 1) * HEAD_DIM]

    def assemble():
        if shard % 16:
            whole = pack_all[...].reshape(groups * pack.shape[0], pack.shape[1])
            hot = squeeze_hot(shard, pack.shape[0], width, groups)
            weights[...] = jnp.dot(hot, whole, preferred_element_type=F32).astype(BF16)
        else:
            weights[...] = pack_all[...].reshape(width, pack.shape[1])
        row = jnp.zeros((8, width), F32)
        for g in range(groups):
            piece = tile_all[g // dps, g % dps].astype(BF16)
            row = row + jnp.dot(piece, spread_hot(g * shard, shard, width), preferred_element_type=F32)
        gains[...] = row

    for n, item in enumerate(items):
        pass_own(*item)
        if (n + 1) % (2 * per) == 0:
            done_round = n // (2 * per)
            if done_round + 3 < half:
                send_round(done_round + 3)
            if done_round == half - 2:
                send_later()
        if n == 2 * per:
            for copy in own_copies:
                copy.wait()
            for _, _, finish in gathers[:2]:
                finish()
            assemble()
            for j in range(per):
                project(j, s)
        if n >= 2 * per:
            pass_across(*items[n - 2 * per])

    def project_from(hop):
        @pl.loop(0, per)
        def _(j):
            block = me.block(j, (h, me.across, me.near, me.near_across)[hop])

            @pl.when(block != s)
            def _():
                if hop >= 2:
                    for k in range(CHUNKS):
                        arrived(tok_all.at[j, block, chunk(k)], h_recv.at[hop - 1, j, k])
                project(j, block)

    project_from(0)
    for item in items[-2 * per :]:
        pass_across(*item)
    project_from(2)
    project_from(1)
    project_from(3)
    for j in range(per):
        own_tok[j] = tok_all[j, me.block(j)]
    for i in range(1, seqs):
        gathers[2][1](i)

    @pl.loop(0, per * blocks)
    def _(unit):
        j, block = lax.div(unit, blocks), lax.rem(unit, blocks)
        rows = pl.ds(pl.multiple_of(block * span, span), span)
        turn = lax.rem(unit, 2)

        @pl.when(unit >= 2)
        def _():
            pltpu.make_async_copy(slot.at[turn], slot.at[turn], p_sem.at[turn]).wait()

        window = pl.ds(pl.multiple_of((blocks - 1 - block) * span, span), length)
        valid = lax.broadcasted_iota(jnp.int32, (1, length), 1) < lengths[per * s + j]
        for head in range(heads):
            query = split[j, head, rows, :HEAD_DIM]
            key, value = split[j, heads + head, :, :HEAD_DIM], split[j, 2 * heads + head, :, :HEAD_DIM]
            scores = lax.dot_general(query, key, (((1,), (1,)), ((), ())), preferred_element_type=F32)
            scores = jnp.where(valid, scores + ext[head, :, window], -1e30)
            top = jnp.max(scores, axis=-1, keepdims=True)
            grown = jnp.exp(scores - top)
            total = jnp.sum(grown, axis=-1, keepdims=True)
            part = (grown * (1.0 / total)).astype(BF16)
            slot[turn, head] = part
            mixed = jnp.dot(part, value, preferred_element_type=F32)
            out[unit, :, head * HEAD_DIM : (head + 1) * HEAD_DIM] = mixed.astype(BF16)
        pltpu.make_async_copy(slot.at[turn], probs.at[j, :, rows, :], p_sem.at[turn]).start()
        owner = mod(block - 2 * (j + s), 4)
        away = mod(owner - h, 4)

        @pl.when(away == 0)
        def _():
            pltpu.make_async_copy(out.at[unit], heads_all.at[h, j], ls.at[j]).start()

        @pl.when(away > 0)
        def _():
            send(out.at[unit], heads_all.at[h, j], a_send.at[away - 1, j], a_recv.at[away - 1, j], head=owner)

        @pl.when(unit == 1)
        def _():
            gathers[2][2]()
            total = jnp.zeros((local, width), F32)
            for g in range(groups):
                total = total + jnp.dot(
                    wo_parts[g // dps, g % dps], spread_hot(g * shard, shard, width), preferred_element_type=F32
                )
            wo_all[h] = total.astype(BF16)
            send(wo_all.at[h], wo_all.at[h], w_send.at[0], w_recv.at[0], head=me.across)
            send(wo_all.at[h], wo_all.at[h], w_send.at[1], w_recv.at[1], head=me.near)

        @pl.when(unit == seqs)
        def _():
            there = wo_all.at[me.across]
            arrived(there, w_recv.at[0])
            send(there, there, w_send.at[2], w_recv.at[2], head=me.near)

    for turn in range(2):
        pltpu.make_async_copy(slot.at[turn], slot.at[turn], p_sem.at[turn]).wait()
    for j in range(per):
        block = me.block(j)

        @pl.when(block == s)
        def _():
            pltpu.make_async_copy(cot_own.at[j], cot_own.at[j], ls.at[4 + per + j]).wait()

        @pl.when(block != s)
        def _():
            for part in range(2):
                arrived(cot_own.at[j, pl.ds(part * half * part_rows, half * part_rows)], c_recv.at[j, part])

        pltpu.make_async_copy(out.at[0], heads_all.at[h, j], ls.at[j]).wait()
        for i in range(1, 4):
            pltpu.make_async_copy(out.at[0], out.at[0], a_send.at[i - 1, j]).wait()
            arrived(heads_all.at[mod(h - i, 4), j], a_recv.at[i - 1, j])
        for k in range(CHUNKS):
            here = at(j, k, h)

            @pl.when(me.block(j) != s)
            def _():
                for n in range(2):
                    pltpu.make_async_copy(here, here, h_send.at[n, j, k]).wait()

            @pl.when(me.block(j, me.across) != s)
            def _():
                pltpu.make_async_copy(here, here, h_send.at[2, j, k]).wait()

    for i in range(1, seqs):
        for c in range(half):
            rows = tok.at[0, pl.ds(0, part_rows)]
            pltpu.make_async_copy(rows, rows, z_send.at[i - 1, c]).wait()
        rows = cot.at[0, pl.ds(0, half * part_rows)]
        pltpu.make_async_copy(rows, rows, c_send.at[i - 1]).wait()
        pltpu.make_async_copy(ids, ids, i_send.at[i - 1]).wait()
        arrived(ids_all.at[mod(s - i, seqs)], i_recv.at[i - 1])
    for k in range(3):
        pltpu.make_async_copy(wo_all.at[h], wo_all.at[h], w_send.at[k]).wait()
    arrived(wo_all.at[me.near], w_recv.at[1])
    arrived(wo_all.at[me.near_across], w_recv.at[2])


def front(tokens, cot, wq, wk, wv, wo, router, gain_a, gain_f, ids, table, lengths, seqs, dps):
    seq_local, span, width = tokens.shape
    per = seq_local // seqs
    length = seqs * span
    shard, local = wq.shape
    heads = local // HEAD_DIM
    lanes = up_to(3 * local + router.shape[0], 128)
    padded = up_to(shard, 16)
    smem = pl.BlockSpec(memory_space=pltpu.SMEM)
    return pl.pallas_call(
        functools.partial(front_kernel, seqs, dps, heads),
        out_shape=(
            jax.ShapeDtypeStruct((per, length, width), BF16),
            jax.ShapeDtypeStruct((width, lanes), BF16),
            jax.ShapeDtypeStruct((per, 3 * heads, length, 128), BF16),
            jax.ShapeDtypeStruct((per, heads, length, length), BF16),
            jax.ShapeDtypeStruct((4, per, span, local), BF16),
            jax.ShapeDtypeStruct((per, span, width), BF16),
            jax.ShapeDtypeStruct((per, span, width), BF16),
            jax.ShapeDtypeStruct((4, local, width), BF16),
            jax.ShapeDtypeStruct((8, width), F32),
            jax.ShapeDtypeStruct((seqs,) + ids.shape, jnp.int32),
        ),
        in_specs=[ANY] * 2 + [VMEM] * 7 + [ANY, VMEM, smem],
        out_specs=[VMEM] * 3 + [ANY] * 2 + [VMEM, ANY] + [VMEM] * 2 + [ANY],
        scratch_shapes=[
            pltpu.VMEM((per, seqs, span, width), BF16),
            pltpu.VMEM((padded, lanes), BF16),
            pltpu.VMEM((seqs, dps, padded, lanes), BF16),
            pltpu.VMEM((local, 128), BF16),
            pltpu.VMEM((seqs, dps, local, 128), BF16),
            pltpu.VMEM((8, 128), F32),
            pltpu.VMEM((seqs, dps, 8, 128), F32),
            pltpu.VMEM((heads, span, 7 * span), F32),
            pltpu.VMEM((2, heads, span, length), BF16),
            pltpu.VMEM((per * seqs, span, local), BF16),
            DMA((2,)),
            DMA((4 + 2 * per,)),
            DMA((seqs - 1, CHUNKS // 2)),
            DMA((per, CHUNKS)),
            DMA((3, per, CHUNKS)),
            DMA((3, per, CHUNKS)),
            DMA((seqs - 1,)),
            DMA((per, 2)),
            DMA((3, per)),
            DMA((3, per)),
            DMA((3,)),
            DMA((3,)),
            DMA((seqs - 1,)),
            DMA((seqs - 1,)),
        ]
        + gather_sems(seqs, dps) * 3,
        compiler_params=params(collective_id=0),
        name="front",
    )(tokens, cot, wq, wk, wv, wo, router, gain_a, gain_f, ids, table, lengths)


def expert_windows(exp_local, per_expert):
    return [(e * per_expert // 16 * 16, up_to((e + 1) * per_expert, 16)) for e in range(exp_local)]


def contract(a, b, over_a, over_b):
    return lax.dot_general(a, b, (((over_a,), (over_b,)), ((), ())), preferred_element_type=F32)


AHEAD = 2
GELU_A, GELU_B = float(np.sqrt(2.0 / np.pi)), 0.044715


def experts_kernel(
    seqs, dps, per_expert, capacity, local,
    heads_all, own_tok, wo_all, weights, gains, cot_own, ids_all, up, down,
    result, hidden_grad, router_grad, gain_grad, up_grad, down_grad,
    rows, summed, place_hot, hidden_ref, ffn_ref, router_ref, gate_ref, hot_ref, taken, near, far,
    ls, g_send, g_recv, h_send, h_recv, n_send, n_recv, x_send, x_recv, r_send, r_recv
):
    me = Place(seqs, dps)
    h, s, d = me.h, me.s, me.d
    groups, _, height, width = rows.shape
    exp_local = up.shape[0]
    windows = expert_windows(exp_local, per_expert)
    me_group = s * dps + d

    def away(n):
        return lax.div(n, dps), lax.rem(n, dps)

    def ahead(n):
        i, j = away(n)
        return mod(s + i, seqs), mod(d + j, dps)

    def behind(n):
        i, j = away(n)
        return mod(s - i, seqs), mod(d - j, dps)

    per, span, _ = own_tok.shape
    spots = groups * height
    first_lane = 3 * local // 128 * 128
    spread = weights.shape[1] - first_lane
    shift = 3 * local - first_lane
    experts = groups * exp_local
    router = weights[:, first_lane:]
    earlier = lax.broadcasted_iota(jnp.int32, (span, span), 0) < lax.broadcasted_iota(jnp.int32, (span, span), 1)
    earlier = earlier.astype(BF16)
    lane = lax.broadcasted_iota(jnp.int32, (span, spread), 1)
    is_expert = (lane >= shift) & (lane < shift + experts)

    def tokens_in(j):
        total = own_tok[j].astype(F32)
        for q in range(4):
            total = total + jnp.dot(heads_all[q, j], wo_all[q], preferred_element_type=F32)
        hidden_ref[j] = total
        inverse = lax.rsqrt(jnp.mean(total * total, axis=-1, keepdims=True) + EPS)
        ffn = (total * inverse * gains[1:2, :]).astype(BF16)
        ffn_ref[j] = ffn
        logits = jnp.where(is_expert, jnp.dot(ffn, router, preferred_element_type=F32), -1e30)
        grown = jnp.exp(logits - jnp.max(logits, axis=-1, keepdims=True))
        router_probs = grown / jnp.sum(grown, axis=-1, keepdims=True)
        router_ref[j] = router_probs
        ids = ids_all[me.block(j), pl.ds(per * s + j, 1), :]
        own = lax.broadcasted_iota(jnp.int32, (spread, span), 0) == ids + shift
        own_low = own.astype(BF16)
        before = jnp.dot(own_low, earlier, preferred_element_type=F32)
        slot = jnp.sum(jnp.where(own, before, 0.0), axis=0, keepdims=True).astype(jnp.int32)
        same = lax.broadcasted_iota(jnp.int32, (spread, spread), 0) == lax.broadcasted_iota(jnp.int32, (spread, spread), 1)
        hot = contract(own_low, same.astype(BF16), 0, 0)
        hot_ref[j] = hot
        gate = jnp.sum(router_probs * hot, axis=-1, keepdims=True)
        gate_ref[j] = gate
        group = lax.div(ids, exp_local)
        place = group * height + ((ids - group * exp_local) * per + j) * capacity + slot
        spot = lax.broadcasted_iota(jnp.int32, (spots, span), 0)
        place_hot[j] = (spot == place).astype(BF16)
        return ffn, (gate * cot_own[j].astype(F32)).astype(BF16)

    made = [tokens_in(j) for j in range(per)]
    for part in range(2):
        total = jnp.zeros((spots, width), F32)
        for j in range(per):
            total = total + jnp.dot(place_hot[j], made[j][part], preferred_element_type=F32)
        total = total.astype(BF16)
        for g in range(groups):
            rows[g, part] = total[g * height : (g + 1) * height, :]
    up_grad[...] = jnp.zeros_like(up_grad)
    down_grad[...] = jnp.zeros_like(down_grad)
    greet(me.group_peers() + me.head_pair())
    pltpu.make_async_copy(rows.at[me_group], taken.at[h, 0], ls.at[0]).start()

    def send_out(n):
        to_s, to_d = ahead(n)
        send(rows.at[to_s * dps + to_d], taken.at[h, n], g_send.at[n], g_recv.at[n], seq=to_s, dp=to_d)

    for n in range(1, min(AHEAD, groups)):
        send_out(n)

    def gather_own(n):
        here = taken.at[h, n]

        @pl.when(n == 0)
        def _():
            pltpu.make_async_copy(here, here, ls.at[0]).wait()

        @pl.when(n > 0)
        def _():
            arrived(here, g_recv.at[n])

        send(here, here, h_send.at[0, n], h_recv.at[0, n], head=me.across)
        send(here, here, h_send.at[1, n], h_recv.at[1, n], head=me.near)

    def gather_across(n):
        there = taken.at[me.across, n]
        arrived(there, h_recv.at[0, n])
        send(there, there, h_send.at[2, n], h_recv.at[2, n], head=me.near)

    def compute(n):
        arrived(taken.at[me.near, n], h_recv.at[1, n])
        arrived(taken.at[me.near_across, n], h_recv.at[2, n])
        for k in range(3):
            pltpu.make_async_copy(taken.at[h, n], taken.at[h, n], h_send.at[k, n]).wait()
        kept = []
        for e, (low, high) in enumerate(windows):
            size = high - low
            at = lax.broadcasted_iota(jnp.int32, (4 * size, width), 0)
            slot = lax.rem(at, size) + low
            inside = (slot >= e * per_expert) & (slot < (e + 1) * per_expert)

            def mine(part):
                block = jnp.concatenate([taken[q, n, part, low:high, :] for q in range(4)], axis=0)
                return jnp.where(inside, block.astype(F32), 0.0).astype(BF16)

            x, g = mine(0), mine(1)
            pre = jnp.dot(x, up[e], preferred_element_type=F32)
            square = pre * pre
            bent = jnp.tanh(GELU_A * pre * (1.0 + GELU_B * square))
            act = (0.5 * pre * (1.0 + bent)).astype(BF16)
            slope = 0.5 * (1.0 + bent) + 0.5 * pre * (1.0 - bent * bent) * (GELU_A * (1.0 + 3.0 * GELU_B * square))
            out = jnp.dot(act, down[e], preferred_element_type=F32).astype(BF16)
            act_grad = contract(g, down[e], 1, 1)
            pre_grad = (act_grad * slope).astype(BF16)
            back = contract(pre_grad, up[e], 1, 1).astype(BF16)
            kept.append((x, g, act, pre_grad, out, back))
        for q in range(4):
            for part in range(2):
                for tile in range(0, height, 16):
                    total = None
                    for (low, high), made in zip(windows, kept):
                        if low <= tile < high:
                            begin = q * (high - low) + tile - low
                            piece = made[4 + part][begin : begin + 16, :]
                            total = piece if total is None else total + piece
                    if total is not None:
                        taken[q, n, part, tile : tile + 16, :] = total
        send(taken.at[me.near_across, n], near.at[0, n], n_send.at[0, n], n_recv.at[0, n], head=me.near)
        send(taken.at[me.near, n], near.at[1, n], n_send.at[1, n], n_recv.at[1, n], head=me.near)
        for e in range(exp_local):
            x, g, act, pre_grad, _, _ = kept[e]
            up_grad[e] += contract(x, pre_grad, 0, 0)
            down_grad[e] += contract(act, g, 0, 0)

    def add_near(n):
        arrived(near.at[0, n], n_recv.at[0, n])
        both = taken[me.across, n].astype(F32) + near[0, n].astype(F32)
        taken[me.across, n] = both.astype(BF16)
        send(taken.at[me.across, n], far.at[n], x_send.at[n], x_recv.at[n], head=me.across)

    def send_back(n):
        arrived(near.at[1, n], n_recv.at[1, n])
        arrived(far.at[n], x_recv.at[n])
        total = taken[h, n].astype(F32) + near[1, n].astype(F32) + far[n].astype(F32)
        taken[h, n] = total.astype(BF16)
        to_s, to_d = behind(n)

        @pl.when(n == 0)
        def _():
            pltpu.make_async_copy(taken.at[h, n], summed.at[:, me_group], r_send.at[n]).start()

        @pl.when(n > 0)
        def _():
            send(taken.at[h, n], summed.at[:, me_group], r_send.at[n], r_recv.at[n], seq=to_s, dp=to_d)

    stages = (send_back, add_near, compute, gather_across, gather_own)

    @pl.loop(0, groups + len(stages) - 1)
    def _(step):
        @pl.when(step + AHEAD < groups)
        def _():
            send_out(step + AHEAD)

        for k, stage in enumerate(stages):
            n = step - (len(stages) - 1 - k)

            @pl.when((n >= 0) & (n < groups))
            def _():
                stage(n)

    @pl.loop(0, groups)
    def _(n):
        here = taken.at[h, n]
        for k in range(2):
            pltpu.make_async_copy(here, here, n_send.at[k, n]).wait()
        pltpu.make_async_copy(here, here, x_send.at[n]).wait()
        pltpu.make_async_copy(here, here, r_send.at[n]).wait()

        @pl.when(n > 0)
        def _():
            pltpu.make_async_copy(here, here, g_send.at[n]).wait()
            from_s, from_d = ahead(n)
            arrived(summed.at[:, from_s * dps + from_d], r_recv.at[n])

    def tokens_out(j):
        hidden, gate, router_probs, hot = hidden_ref[j], gate_ref[j], router_ref[j], hot_ref[j]
        grad = cot_own[j].astype(F32)
        token_out = contract(place_hot[j], summed[0].reshape(spots, width), 0, 0)
        input_grad = contract(place_hot[j], summed[1].reshape(spots, width), 0, 0)
        result[j] = (hidden + gate * token_out).astype(BF16)
        gate_grad = jnp.sum(grad * token_out, axis=-1, keepdims=True)
        logit_low = (router_probs * (gate_grad * hot - gate_grad * gate)).astype(BF16)
        router_part = contract(ffn_ref[j], logit_low, 0, 0)
        input_grad = input_grad + contract(logit_low, router, 1, 1)
        inverse = lax.rsqrt(jnp.mean(hidden * hidden, axis=-1, keepdims=True) + EPS)
        r = hidden * inverse
        u = input_grad * gains[1:2, :]
        hidden_grad[j] = grad + (u - r * jnp.mean(u * r, axis=-1, keepdims=True)) * inverse
        gain_part = jnp.sum(input_grad * r, axis=0, keepdims=True)
        if j == 0:
            router_grad[...] = router_part
            gain_grad[...] = gain_part
        else:
            router_grad[...] += router_part
            gain_grad[...] += gain_part

    for j in range(per):
        tokens_out(j)


def run_experts(
    heads_all, own_tok, wo_all, weights, gains, cot_own, ids_all, up, down, seqs, dps, per_expert, capacity
):
    per, span, width = own_tok.shape
    local = wo_all.shape[1]
    groups = seqs * dps
    height = up_to(up.shape[0] * per_expert, 16)
    spread = weights.shape[1] - 3 * local // 128 * 128
    rows = (groups, 2, height, width)
    return pl.pallas_call(
        functools.partial(experts_kernel, seqs, dps, per_expert, capacity, local),
        out_shape=(
            jax.ShapeDtypeStruct((per, span, width), BF16),
            jax.ShapeDtypeStruct((per, span, width), F32),
            jax.ShapeDtypeStruct((width, spread), F32),
            jax.ShapeDtypeStruct((1, width), F32),
            jax.ShapeDtypeStruct(up.shape, F32),
            jax.ShapeDtypeStruct(down.shape, F32),
        ),
        in_specs=[VMEM] * 9,
        out_specs=[VMEM] * 6,
        scratch_shapes=[
            pltpu.VMEM(rows, BF16),
            pltpu.VMEM((2, groups, height, width), BF16),
            pltpu.VMEM((per, groups * height, span), BF16),
            pltpu.VMEM((per, span, width), F32),
            pltpu.VMEM((per, span, width), BF16),
            pltpu.VMEM((per, span, spread), F32),
            pltpu.VMEM((per, span, 1), F32),
            pltpu.VMEM((per, span, spread), F32),
            pltpu.VMEM((4,) + rows, BF16),
            pltpu.VMEM((2,) + rows, BF16),
            pltpu.VMEM(rows, BF16),
            DMA((1,)),
            DMA((groups,)),
            DMA((groups,)),
            DMA((3, groups)),
            DMA((3, groups)),
            DMA((2, groups)),
            DMA((2, groups)),
            DMA((groups,)),
            DMA((groups,)),
            DMA((groups,)),
            DMA((groups,)),
        ],
        compiler_params=params(collective_id=2),
        name="experts",
    )(heads_all, own_tok, wo_all, weights, gains, cot_own, ids_all, up, down)


def send_home(me, own, home, ls, z_send, z_recv, h_send, h_recv):
    h, s, seqs = me.h, me.s, me.seqs
    per = own.shape[0]
    turn = mod(s - h, 4)
    mine = lax.rem(turn, 2) == 0
    turned = lax.div(turn, 2)

    def sources(j, across):
        return [lax.rem(turned + j + across, 2) + 2 * k for k in range(seqs // 2)]

    def start(j):
        to = me.block(j)

        @pl.when(to != s)
        def _():
            send(own.at[j], home.at[per * s + j], z_send.at[j], z_recv.at[s], seq=to)

        @pl.when(to == s)
        def _():
            pltpu.make_async_copy(own.at[j], home.at[per * s + j], ls).start()

    def pass_on(j):
        @pl.when(mine)
        def _():
            for source in sources(j, 0):
                here = home.at[per * source + j]

                @pl.when(source == s)
                def _():
                    pltpu.make_async_copy(here, here, ls).wait()

                @pl.when(source != s)
                def _():
                    arrived(here, z_recv.at[source])

                send(here, here, h_send.at[0, source], h_recv.at[0, source], head=me.across)
                send(here, here, h_send.at[1, source], h_recv.at[1, source], head=me.near)

    def pass_near(j):
        @pl.when(mine)
        def _():
            for source in sources(j, 1):
                there = home.at[per * source + j]
                arrived(there, h_recv.at[0, source])
                send(there, there, h_send.at[2, source], h_recv.at[2, source], head=me.near)

    def finish():
        for j in range(per):

            @pl.when(me.block(j) != s)
            def _():
                pltpu.make_async_copy(own.at[j], own.at[j], z_send.at[j]).wait()

        @pl.when(mine)
        def _():
            for source in range(seqs):
                for k in range(3):
                    here = home.at[per * source]
                    pltpu.make_async_copy(here, here, h_send.at[k, source]).wait()

        @pl.when(jnp.logical_not(mine))
        def _():
            for source in range(seqs):
                arrived(home.at[per * source], h_recv.at[1, source])
                arrived(home.at[per * source + 1], h_recv.at[2, source])

    return start, pass_on, pass_near, finish


def home_sems(per, seqs):
    return [DMA(()), DMA((per,)), DMA((seqs,)), DMA((3, seqs)), DMA((3, seqs))]


def add_groups(me, parts, dp_take, seq_take, result, dp_send, dp_recv, seq_send, seq_recv):
    s, d, seqs, dps = me.s, me.d, me.seqs, me.dps

    def start():
        for i in range(1, dps):
            to = mod(d + i, dps)
            send(parts.at[to], dp_take.at[i - 1], dp_send.at[i - 1], dp_recv.at[i - 1], dp=to)

    def middle():
        for i in range(1, dps):
            arrived(dp_take.at[i - 1], dp_recv.at[i - 1])
        for n in range(seqs):
            to = mod(s + n, seqs)
            total = parts[d, to].astype(F32)
            for i in range(1, dps):
                total = total + dp_take[i - 1, to].astype(F32)
            parts[d, to] = total.astype(parts.dtype)
            if n:
                send(parts.at[d, to], seq_take.at[n - 1], seq_send.at[n - 1], seq_recv.at[n - 1], seq=to)

    def end():
        total = parts[d, s].astype(F32)
        for n in range(1, seqs):
            arrived(seq_take.at[n - 1], seq_recv.at[n - 1])
            total = total + seq_take[n - 1].astype(F32)
        result[...] = total
        for i in range(1, dps):
            pltpu.make_async_copy(dp_take.at[0], dp_take.at[0], dp_send.at[i - 1]).wait()
        for n in range(1, seqs):
            pltpu.make_async_copy(seq_take.at[0], seq_take.at[0], seq_send.at[n - 1]).wait()

    return start, middle, end


def group_scratch(seqs, dps, shape, dtype):
    return [
        pltpu.VMEM((dps, seqs) + shape, dtype),
        pltpu.VMEM((max(1, dps - 1), seqs) + shape, dtype),
        pltpu.VMEM((seqs - 1,) + shape, dtype),
    ]


def group_sems(seqs, dps):
    return [DMA((max(1, dps - 1),))] * 2 + [DMA((seqs - 1,))] * 2


def back_kernel(
    seqs, dps, heads,
    result, hidden_grad, own_tok, heads_all, wo_all, split, probs, attn_input, weights, gains, router, gain_f,
    output, tokens_home, w_sum, small_sum, wo_sum, gain_sum, bias_sum,
    attn_grad, hsend, grad_all, slot, ext, made, dk_sum, dv_sum, w_acc, x_out, x_near, x_far, tg, wo_part, wo_near, wo_far,
    w_parts, w_dp, w_seq, wo_parts, wo_dp, wo_seq, g_parts, g_dp, g_seq, g_acc, bias, bias_take, small, gsmall,
    p_sem, a_send, a_recv, n_send, n_recv, f_send, f_recv, on_send, on_recv, of_send, of_recv,
    b_send, b_recv, s_send, s_recv, t_send, t_recv, *sems
):
    me = Place(seqs, dps)
    h, s, d = me.h, me.s, me.d
    per, span, width = hidden_grad.shape
    blocks = seqs
    length = blocks * span
    local = heads * HEAD_DIM
    groups = seqs * dps
    shard = width // groups
    padded = w_sum.shape[0]
    lanes = weights.shape[1]
    buckets = 32
    others = [(i, j) for i in range(seqs) for j in range(dps) if i or j]
    order = (h, me.near, me.across, me.near_across)
    greet(me.group_peers() + [{"head": mod(h + i, 4)} for i in range(1, 4)])
    out_home = send_home(me, result, output, *sems[0:5])
    grad_home = send_home(me, tg, tokens_home, *sems[5:10])
    w_group = add_groups(me, w_parts, w_dp, w_seq, w_sum, *sems[10:14])
    wo_group = add_groups(me, wo_parts, wo_dp, wo_seq, wo_sum, *sems[14:18])
    g_group = add_groups(me, g_parts, g_dp, g_seq, gain_sum, *sems[18:22])

    def fetch(j, n):
        q = jnp.where(n == 0, h, jnp.where(n == 1, me.near, jnp.where(n == 2, me.across, me.near_across)))
        block = me.block(j, q)
        rows = pl.ds(pl.multiple_of(block * span, span), span)
        turn = lax.rem(n, 2)
        return q, block, rows, turn, pltpu.make_async_copy(probs.at[j, :, rows, :], slot.at[turn], p_sem.at[turn])

    fetch(0, 0)[4].start()
    attn_grad[...] = hidden_grad[...].astype(BF16)
    for j in range(per):
        for i in (1, 2, 3, 0):
            to = mod(h + i, 4)
            grad = contract(attn_grad[j], wo_all[to], 1, 1).astype(BF16)
            if i:
                hsend[j, i - 1, :, :local] = grad[: span // 2]
                hsend[j, i - 1, :, local:] = grad[span // 2 :]
                send(
                    hsend.at[j, i - 1],
                    grad_all.at[j, me.block(j)],
                    a_send.at[i - 1, j],
                    a_recv.at[i - 1, j],
                    head=to,
                )
            else:
                grad_all[j, me.block(j), :, :local] = grad[: span // 2]
                grad_all[j, me.block(j), :, local:] = grad[span // 2 :]
    for k, q in enumerate((me.near_across, me.near, me.across, h)):
        total = jnp.zeros((local, width), F32)
        for j in range(per):
            total = total + contract(heads_all[q, j], attn_grad[j], 0, 0)
        wo_part[k] = total.astype(BF16)
        if k < 2:
            send(wo_part.at[k], wo_near.at[k], on_send.at[k], on_recv.at[k], head=me.near)
    out_home[0](0)
    ext[...] = jnp.zeros_like(ext)
    made[...] = jnp.zeros_like(made)

    def wo_across():
        arrived(wo_near.at[0], on_recv.at[0])
        wo_part[2] = (wo_part[2].astype(F32) + wo_near[0].astype(F32)).astype(BF16)
        send(wo_part.at[2], wo_far, of_send, of_recv, head=me.across)

    def wo_total():
        arrived(wo_near.at[1], on_recv.at[1])
        arrived(wo_far, of_recv)
        total = (wo_part[3].astype(F32) + wo_near[1].astype(F32) + wo_far[...].astype(F32)).astype(BF16)
        for g in range(groups):
            hot = spread_hot(g * shard, shard, width)
            wo_parts[g % dps, g // dps] = contract(total, hot, 1, 1).astype(BF16)
        wo_group[0]()

    def x_partial(j):
        for k, q in enumerate((me.near_across, me.near, me.across, h)):
            rows = pl.ds(pl.multiple_of(me.block(j, q) * span, span), span)
            x_out[j, k] = contract(made[j, rows, :], weights[...], 1, 1).astype(BF16)
            if k < 2:
                send(x_out.at[j, k], x_near.at[j, k], n_send.at[j, k], n_recv.at[j, k], head=me.near)

    def x_across(j):
        arrived(x_near.at[j, 0], n_recv.at[j, 0])
        x_out[j, 2] = (x_out[j, 2].astype(F32) + x_near[j, 0].astype(F32)).astype(BF16)
        send(x_out.at[j, 2], x_far.at[j], f_send.at[j], f_recv.at[j], head=me.across)

    def x_total(j):
        arrived(x_near.at[j, 1], n_recv.at[j, 1])
        arrived(x_far.at[j], f_recv.at[j])
        grad = x_out[j, 3].astype(F32) + x_near[j, 1].astype(F32) + x_far[j].astype(F32)
        v = own_tok[j].astype(F32)
        inverse = lax.rsqrt(jnp.mean(v * v, axis=-1, keepdims=True) + EPS)
        r = v * inverse
        u = grad * gains[0:1, :]
        back = (u - r * jnp.mean(u * r, axis=-1, keepdims=True)) * inverse
        tg[j] = (hidden_grad[j] + back).astype(BF16)
        grad_home[0](j)
        g_acc[0:1, :] += jnp.sum(grad * r, axis=0, keepdims=True)

    def attention(j, service):
        @pl.loop(0, blocks)
        def _(n):
            q, block, rows, turn, copy = fetch(j, n)
            away = mod(h - q, 4)

            @pl.when(away > 0)
            def _():
                arrived(grad_all.at[j, block], a_recv.at[away - 1, j])

            copy.wait()

            @pl.when(n < blocks - 1)
            def _():
                fetch(j, n + 1)[4].start()

            if j < per - 1:

                @pl.when(n == blocks - 1)
                def _():
                    fetch(j + 1, 0)[4].start()

            window = pl.ds(pl.multiple_of((blocks - 1 - block) * span, span), length)
            for head in range(heads):
                cols = slice(head * HEAD_DIM, (head + 1) * HEAD_DIM)
                query = split[j, head, rows, :HEAD_DIM]
                key, value = split[j, heads + head, :, :HEAD_DIM], split[j, 2 * heads + head, :, :HEAD_DIM]
                more = slice(local + head * HEAD_DIM, local + (head + 1) * HEAD_DIM)
                grad = jnp.concatenate([grad_all[j, block, :, cols], grad_all[j, block, :, more]], axis=0)
                part = slot[turn, head]
                prob_grad = contract(grad, value, 1, 1)
                wide = part.astype(F32)
                delta = jnp.sum(wide * prob_grad, axis=-1, keepdims=True)
                score_grad = wide * (prob_grad - delta)
                ext[head, :, window] += score_grad
                low = score_grad.astype(BF16)
                made[j, rows, cols] = jnp.dot(low, key, preferred_element_type=F32).astype(BF16)
                dk = contract(low, query, 0, 0)
                dv = contract(part, grad, 0, 0)

                @pl.when(n == 0)
                def _():
                    dk_sum[head] = dk
                    dv_sum[head] = dv

                @pl.when(n > 0)
                def _():
                    dk_sum[head] += dk
                    dv_sum[head] += dv

            for k, call in enumerate(service):

                @pl.when(n == k)
                def _():
                    for act in call:
                        act()

        for head in range(heads):
            cols = slice(local + head * HEAD_DIM, local + (head + 1) * HEAD_DIM)
            made[j, :, cols] = dk_sum[head].astype(BF16)
            cols = slice(2 * local + head * HEAD_DIM, 2 * local + (head + 1) * HEAD_DIM)
            made[j, :, cols] = dv_sum[head].astype(BF16)
        x_partial(j)
        total = contract(attn_input[j], made[j], 0, 0)
        if j == 0:
            w_acc[...] = total
        else:
            w_acc[...] += total

    g_acc[...] = jnp.zeros_like(g_acc)
    g_acc[1:2, :] = gain_f[...]
    attention(
        0,
        (
            (),
            (wo_across,),
            (lambda: out_home[0](1), lambda: out_home[1](0)),
            (wo_total,),
        ),
    )
    attention(
        1,
        (
            (lambda: x_across(0),),
            (wo_group[1], lambda: out_home[1](1)),
            (lambda: out_home[2](0),),
            (lambda: x_total(0),),
        ),
    )
    x_across(1)
    w_acc[:, lanes - router.shape[1] :] += router[...]
    low = w_acc[...].astype(BF16)
    if shard % 16:
        low = contract(squeeze_hot(shard, padded, width, groups), low, 0, 0).astype(BF16)
    for g in range(groups):
        w_parts[g % dps, g // dps] = low[g * padded : (g + 1) * padded, :]
    w_group[0]()
    turn = lax.broadcasted_iota(jnp.int32, (4 * span, 128), 0)
    bucket = bucket_of(jnp.where(turn < 3 * span, turn, turn - 4 * span) - span, buckets)
    hot = (bucket == lax.broadcasted_iota(jnp.int32, (4 * span, 128), 1)).astype(F32)
    lane = lax.broadcasted_iota(jnp.int32, (1, 128), 1)
    head_row = lax.broadcasted_iota(jnp.int32, (8, 4 * span), 0)
    diagonals = jnp.zeros((8, 4 * span), F32)
    far_row = lax.broadcasted_iota(jnp.int32, (8, 128), 0)
    far = jnp.zeros((8, 128), F32)
    for head in range(heads):
        eight = jnp.zeros((8, 4 * span), F32)
        for group in range(span // 8):
            piece = ext[head, group * 8 : (group + 1) * 8, 2 * span : 5 * span]
            piece = jnp.concatenate([piece, jnp.zeros((8, span), F32)], axis=1)
            eight = eight + pltpu.roll(piece, (4 * span - 8 * group) % (4 * span), 1)
        one = jnp.zeros((8, 4 * span), F32)
        for i in range(8):
            line = jnp.broadcast_to(eight[i : i + 1, :], (8, 4 * span))
            one = one + pltpu.roll(line, (4 * span - i) % (4 * span), 1)
        diagonals = jnp.where(head_row == head, one, diagonals)
        left, right = jnp.sum(ext[head, :, : 2 * span]), jnp.sum(ext[head, :, 5 * span :])
        sides = jnp.where(lane == buckets // 2 - 1, left, jnp.where(lane == buckets - 1, right, 0.0))
        far = jnp.where(far_row == head, sides, far)
    bias[...] = far + jnp.dot(diagonals, hot, preferred_element_type=F32, precision=lax.Precision.HIGHEST)
    for n, (i, j) in enumerate(others):
        send(bias, bias_take.at[n], b_send.at[n], b_recv.at[n], seq=mod(s + i, seqs), dp=mod(d + j, dps))
    out_home[2](1)
    x_total(1)
    grad_home[1](0)
    g_rows = g_acc[...].astype(BF16)
    for g in range(groups):
        g_parts[g % dps, g // dps] = contract(g_rows, spread_hot(g * shard, shard, width), 1, 1)
    g_group[0]()
    grad_home[2](0)
    grad_home[1](1)
    w_group[1]()
    g_group[1]()
    w_group[2]()
    small[0] = w_sum[:, lanes - small.shape[-1] :]
    for i in range(1, 4):
        send(small.at[0], small.at[i], s_send.at[i - 1], s_recv.at[i - 1], head=mod(h + i, 4))
    g_group[2]()
    gsmall[0] = gain_sum[...]
    for i in range(1, 4):
        send(gsmall.at[0], gsmall.at[i], t_send.at[i - 1], t_recv.at[i - 1], head=mod(h + i, 4))
    grad_home[2](1)
    wo_group[2]()
    total = bias[...]
    for n in range(len(others)):
        arrived(bias_take.at[n], b_recv.at[n])
        total = total + bias_take[n]
    bias_sum[...] = total
    total, gain_total = small[0], gsmall[0]
    for i in range(1, 4):
        arrived(small.at[i], s_recv.at[i - 1])
        arrived(gsmall.at[i], t_recv.at[i - 1])
        total = total + small[i]
        gain_total = gain_total + gsmall[i]
    small_sum[...] = total
    gain_sum[...] = gain_total
    out_home[3]()
    grad_home[3]()
    for j in range(per):
        for i in range(3):
            pltpu.make_async_copy(hsend.at[0, 0], hsend.at[0, 0], a_send.at[i, j]).wait()
        for k in range(2):
            pltpu.make_async_copy(x_near.at[0, 0], x_near.at[0, 0], n_send.at[j, k]).wait()
        pltpu.make_async_copy(x_near.at[0, 0], x_near.at[0, 0], f_send.at[j]).wait()
    for k in range(2):
        pltpu.make_async_copy(wo_far, wo_far, on_send.at[k]).wait()
    pltpu.make_async_copy(wo_far, wo_far, of_send).wait()
    for i in range(3):
        pltpu.make_async_copy(small.at[0], small.at[0], s_send.at[i]).wait()
        pltpu.make_async_copy(gsmall.at[0], gsmall.at[0], t_send.at[i]).wait()
    for n in range(len(others)):
        pltpu.make_async_copy(bias, bias, b_send.at[n]).wait()


def back_pass(
    result, hidden_grad, own_tok, heads_all, wo_all, split, probs, attn_input, weights, gains, router, gain_f, seqs, dps
):
    per, span, width = hidden_grad.shape
    length = seqs * span
    heads = probs.shape[1]
    local = heads * HEAD_DIM
    groups = seqs * dps
    shard = width // groups
    padded = up_to(shard, 16)
    lanes = weights.shape[1]
    block = (span, width)
    return pl.pallas_call(
        functools.partial(back_kernel, seqs, dps, heads),
        out_shape=(
            jax.ShapeDtypeStruct((per * seqs,) + block, BF16),
            jax.ShapeDtypeStruct((per * seqs,) + block, BF16),
            jax.ShapeDtypeStruct((padded, lanes), F32),
            jax.ShapeDtypeStruct((padded, 128 * (lanes // 128 - 3 * local // 128)), F32),
            jax.ShapeDtypeStruct((local, 128), F32),
            jax.ShapeDtypeStruct((8, 128), F32),
            jax.ShapeDtypeStruct((8, 128), F32),
        ),
        in_specs=[VMEM] * 6 + [ANY] + [VMEM] * 5,
        out_specs=[ANY] * 2 + [VMEM] * 5,
        scratch_shapes=[
            pltpu.VMEM((per,) + block, BF16),
            pltpu.VMEM((per, 3, span // 2, 2 * local), BF16),
            pltpu.VMEM((per, seqs, span // 2, 2 * local), BF16),
            pltpu.VMEM((2, heads, span, length), BF16),
            pltpu.VMEM((heads, span, 7 * span), F32),
            pltpu.VMEM((per, length, lanes), BF16),
            pltpu.VMEM((heads, length, HEAD_DIM), F32),
            pltpu.VMEM((heads, length, HEAD_DIM), F32),
            pltpu.VMEM((width, lanes), F32),
            pltpu.VMEM((per, 4) + block, BF16),
            pltpu.VMEM((per, 2) + block, BF16),
            pltpu.VMEM((per,) + block, BF16),
            pltpu.VMEM((per,) + block, BF16),
            pltpu.VMEM((4, local, width), BF16),
            pltpu.VMEM((2, local, width), BF16),
            pltpu.VMEM((local, width), BF16),
        ]
        + group_scratch(seqs, dps, (padded, lanes), BF16)
        + group_scratch(seqs, dps, (local, 128), BF16)
        + group_scratch(seqs, dps, (8, 128), F32)
        + [
            pltpu.VMEM((8, width), F32),
            pltpu.VMEM((8, 128), F32),
            pltpu.VMEM((groups - 1, 8, 128), F32),
            pltpu.VMEM((4, padded, 128 * (lanes // 128 - 3 * local // 128)), F32),
            pltpu.VMEM((4, 8, 128), F32),
            DMA((2,)),
            DMA((3, per)),
            DMA((3, per)),
            DMA((per, 2)),
            DMA((per, 2)),
            DMA((per,)),
            DMA((per,)),
            DMA((2,)),
            DMA((2,)),
            DMA(()),
            DMA(()),
            DMA((groups - 1,)),
            DMA((groups - 1,)),
            DMA((3,)),
            DMA((3,)),
            DMA((3,)),
            DMA((3,)),
        ]
        + home_sems(per, seqs) * 2
        + group_sems(seqs, dps) * 3,
        compiler_params=params(collective_id=4),
        name="back",
    )(result, hidden_grad, own_tok, heads_all, wo_all, split, probs, attn_input, weights, gains, router, gain_f)


def up_to(value, unit):
    return -(-value // unit) * unit


def body(
    tokens,
    lengths,
    expert_ids,
    attention_gain,
    query_weight,
    key_weight,
    value_weight,
    output_weight,
    position_bias,
    feedforward_gain,
    router_weight,
    expert_up,
    expert_down,
    cotangent,
):
    seqs, dps = lax.axis_size("seq"), lax.axis_size("dp")
    groups = seqs * dps
    seq_local, span, width = tokens.shape
    per = seq_local // seqs
    local_width = query_weight.shape[1]
    bucket_count, heads = position_bias.shape
    experts = router_weight.shape[1]
    shard = query_weight.shape[0]
    capacity = max(2, (5 * span + 4 * experts - 1) // (4 * experts))
    ids = expert_ids.reshape(seq_local, span)
    attn_input, weights, split, probs, heads_all, own_tok, cot_own, out_weight, gains, ids_all = front(
        tokens,
        cotangent,
        query_weight,
        key_weight,
        value_weight,
        output_weight,
        router_weight.T,
        attention_gain[None, :],
        feedforward_gain[None, :],
        ids,
        position_bias.T,
        lengths,
        seqs,
        dps,
    )
    result, hidden_grad, router_grad, gain_two_grad, up_grad, down_grad = run_experts(
        heads_all,
        own_tok,
        out_weight,
        weights,
        gains,
        cot_own,
        ids_all,
        expert_up,
        expert_down,
        seqs,
        dps,
        per * capacity,
        capacity,
    )
    output, tokens_grad, w_sum, small_sum, wo_sum, gain_sum, bias_sum = back_pass(
        result,
        hidden_grad,
        own_tok,
        heads_all,
        out_weight,
        split,
        probs,
        attn_input,
        weights,
        gains,
        router_grad,
        gain_two_grad,
        seqs,
        dps,
    )
    at = 3 * local_width - (w_sum.shape[1] - small_sum.shape[1])
    return (
        output,
        tokens_grad,
        gain_sum[0, :shard],
        w_sum[:shard, :local_width],
        w_sum[:shard, local_width : 2 * local_width],
        w_sum[:shard, 2 * local_width : 3 * local_width],
        wo_sum[:, :shard],
        bias_sum[:heads, :bucket_count].T,
        gain_sum[1, :shard],
        small_sum[:shard, at : at + experts],
        up_grad,
        down_grad,
    )


def solution(mesh):
    placed = (
        P("dp", "seq", None),
        P("dp"),
        P("dp", "seq", None),
        P(("seq", "dp")),
        P(("seq", "dp"), "head"),
        P(("seq", "dp"), "head"),
        P(("seq", "dp"), "head"),
        P("head", ("seq", "dp")),
        P(None, "head"),
        P(("seq", "dp")),
        P(("seq", "dp"), None),
        P(("seq", "dp"), None, "head"),
        P(("seq", "dp"), "head", None),
        P("dp", "seq", None),
    )
    return jax.shard_map(
        body,
        mesh=mesh,
        in_specs=placed,
        out_specs=(
            P("dp", "seq", None),
            P("dp", "seq", None),
            P(("seq", "dp")),
            P(("seq", "dp"), "head"),
            P(("seq", "dp"), "head"),
            P(("seq", "dp"), "head"),
            P("head", ("seq", "dp")),
            P(None, "head"),
            P(("seq", "dp")),
            P(("seq", "dp"), None),
            P(("seq", "dp"), None, "head"),
            P(("seq", "dp"), "head", None),
        ),
        check_vma=False,
    )
```

```python
import functools

import jax
import jax.numpy as jnp
import numpy as np
from jax import lax
from jax.experimental import pallas as pl
from jax.experimental.pallas import tpu as pltpu
from jax.sharding import PartitionSpec as P

HEAD_DIM = 64
EPS = 1e-06
bucket_edges = np.array([1, 2, 3, 4, 5, 6, 7, 8, 12, 16, 23, 32, 46, 64, 91], np.int32)
ANY = pl.BlockSpec(memory_space=pl.ANY)
VMEM = pl.BlockSpec(memory_space=pltpu.VMEM)
MESH = pl.DeviceIdType.MESH
DMA = pltpu.SemaphoreType.DMA
F32 = jnp.float32
BF16 = jnp.bfloat16


def bucket_of(offset, bucket_count):
    distance = jnp.abs(offset)
    magnitude = jnp.zeros_like(offset)
    for edge in bucket_edges:
        magnitude = magnitude + (distance >= int(edge)).astype(jnp.int32)
    return magnitude + bucket_count // 2 * (offset > 0).astype(jnp.int32)


def send(src, dst, send_sem, recv_sem, **device):
    copy = pltpu.make_async_remote_copy(
        src_ref=src,
        dst_ref=dst,
        send_sem=send_sem,
        recv_sem=recv_sem,
        device_id=device,
        device_id_type=MESH,
    )
    copy.start()
    return copy


def arrived(ref, recv_sem):
    pltpu.make_async_copy(ref, ref, recv_sem).wait()


def greet(devices):
    barrier = pltpu.get_barrier_semaphore()
    for device in devices:
        pl.semaphore_signal(barrier, inc=1, device_id=device, device_id_type=MESH)
    pl.semaphore_wait(barrier, len(devices))


def mod(value, size):
    return lax.rem(value + 4 * size, size)


class Place:
    def __init__(self, seqs, dps):
        self.h, self.s, self.d = lax.axis_index("head"), lax.axis_index("seq"), lax.axis_index("dp")
        self.seqs, self.dps = seqs, dps
        self.x, self.c = lax.div(self.h, 2), lax.rem(self.h, 2)
        self.near = self.h + 1 - 2 * self.c
        self.across = mod(self.h + 2, 4)
        self.near_across = lax.rem(self.across, 2) * -2 + self.across + 1

    def seq_peers(self):
        return [{"seq": mod(self.s + i, self.seqs)} for i in range(1, self.seqs)]

    def dp_peers(self):
        return [{"dp": mod(self.d + i, self.dps)} for i in range(1, self.dps)]

    def head_pair(self):
        return [{"head": self.near}, {"head": self.across}]

    def group_peers(self):
        return [
            {"seq": mod(self.s + i, self.seqs), "dp": mod(self.d + j, self.dps)}
            for i in range(self.seqs)
            for j in range(self.dps)
            if i or j
        ]

    def block(self, j, core=None):
        return lax.rem((self.c if core is None else core) + self.s, 2) + 2 * j


def params(**more):
    return pltpu.CompilerParams(has_side_effects=True, vmem_limit_bytes=60 * 2**20, **more)


def gather_groups(me, own, whole, z_send, z_recv, dp_send, dp_recv, far=None, far_send=None, far_recv=None):
    s, d, seqs, dps = me.s, me.d, me.seqs, me.dps

    def spread(src, source):
        for i in range(1, dps):
            send(
                src,
                whole.at[source, d],
                dp_send.at[i - 1, source],
                dp_recv.at[i - 1, source],
                dp=mod(d + i, dps),
            )

    def onward(src, source, dp):
        if far is not None:
            send(src, far.at[source, dp], far_send.at[source, dp], far_recv.at[source, dp], head=me.across)

    def start():
        for i in range(1, seqs):
            send(own, whole.at[s, d], z_send.at[i - 1], z_recv.at[i - 1], seq=mod(s + i, seqs))
        spread(own, s)
        onward(own, s, d)

    def relay(i):
        source = mod(s - i, seqs)
        here = whole.at[source, d]
        arrived(here, z_recv.at[i - 1])
        spread(here, source)
        onward(here, source, d)

    def finish():
        for i in range(1, dps):
            for source in range(seqs):
                there = mod(d - i, dps)
                arrived(whole.at[source, there], dp_recv.at[i - 1, source])
                onward(whole.at[source, there], source, there)
                pltpu.make_async_copy(own, own, dp_send.at[i - 1, source]).wait()
        for i in range(1, seqs):
            pltpu.make_async_copy(own, own, z_send.at[i - 1]).wait()

    def take_far():
        for source in range(seqs):
            for dp in range(dps):
                arrived(far.at[source, dp], far_recv.at[source, dp])

    def finish_far():
        for source in range(seqs):
            for dp in range(dps):
                pltpu.make_async_copy(own, own, far_send.at[source, dp]).wait()

    return start, relay, finish, take_far, finish_far


def gather_sems(seqs, dps):
    return [
        DMA((seqs - 1,)),
        DMA((seqs - 1,)),
        DMA((max(1, dps - 1), seqs)),
        DMA((max(1, dps - 1), seqs)),
    ]


def spread_hot(at, shard, width):
    row = lax.broadcasted_iota(jnp.int32, (128, width), 0)
    column = lax.broadcasted_iota(jnp.int32, (128, width), 1)
    return ((column == row + at) & (row < shard)).astype(BF16)


def squeeze_hot(shard, padded, rows, count):
    row = lax.broadcasted_iota(jnp.int32, (rows, count * padded), 0)
    column = lax.broadcasted_iota(jnp.int32, (rows, count * padded), 1)
    inside = lax.rem(column, padded)
    return ((lax.div(column, padded) * shard + inside == row) & (inside < shard)).astype(BF16)


def front_kernel(
    seqs, dps, heads,
    tok, cot, wq, wk, wv, wo, router, gain_a, gain_f, ids, table, lengths,
    attn_input_out, weights, weights_far, split_out, probs, heads_all, own_tok, cot_own, wo_all, gains, ids_all,
    attn_input, split, tok_all, pack, pack_all, far_all, wo_pad, wo_parts, tile, tile_all, table_own, table_far,
    ext, slot, out,
    p_sem, ls, os, z_send, z_recv, h_send, h_recv, c_send, c_recv, a_send, a_recv, w_send, w_recv, i_send, i_recv,
    f_send, f_recv, t_sem, *line
):
    me = Place(seqs, dps)
    h, s, d, x, c = me.h, me.s, me.d, me.x, me.c
    blocks, span, width = tok_all.shape
    per = own_tok.shape[0]
    length = blocks * span
    shard, local = wq.shape
    groups = seqs * dps
    experts = router.shape[0]
    half = span // 2
    own_half = pl.ds(pl.multiple_of(c * half, half), half)
    other_half = pl.ds(pl.multiple_of((1 - c) * half, half), half)
    pack[...] = jnp.zeros_like(pack)
    split[...] = jnp.zeros_like(split)
    for n, ref in enumerate((wq, wk, wv)):
        pack[:shard, n * local : (n + 1) * local] = ref[...]
    same = lax.broadcasted_iota(jnp.int32, (experts, experts), 0) == lax.broadcasted_iota(jnp.int32, (experts, experts), 1)
    pack[:shard, 3 * local : 3 * local + experts] = contract(router[...], same.astype(BF16), 0, 0).astype(BF16)
    wo_pad[...] = jnp.zeros_like(wo_pad)
    wo_pad[:, :shard] = wo[...]
    tile[...] = jnp.zeros_like(tile)
    tile[0:1, :shard] = gain_a[...].astype(F32)
    tile[1:2, :shard] = gain_f[...].astype(F32)
    buckets = table.shape[1]
    table_own[...] = jnp.zeros_like(table_own)
    table_own[:heads, :buckets] = table[...].astype(F32)
    own_copies = [
        pltpu.make_async_copy(pack, pack_all.at[s, d], ls.at[0]),
        pltpu.make_async_copy(tile, tile_all.at[s, d], ls.at[1]),
        pltpu.make_async_copy(wo_pad, wo_parts.at[s, d], ls.at[2]),
        pltpu.make_async_copy(ids, ids_all.at[s], ls.at[3]),
        pltpu.make_async_copy(tok.at[per * s + x], tok_all.at[s], ls.at[4]),
    ]
    for copy in own_copies:
        copy.start()

    @pl.when(c == 0)
    def _():
        pltpu.make_async_copy(cot.at[per * s + x], cot_own.at[lax.div(s, 2)], ls.at[5]).start()

    greet(
        me.seq_peers()
        + [{"head": me.near} | peer for peer in me.seq_peers()]
        + me.dp_peers()
        + [{"head": mod(h + i, 4)} for i in range(1, 4)]
    )
    packs = gather_groups(me, pack, pack_all, *line[0:4], far_all, f_send, f_recv)
    tiles = gather_groups(me, tile, tile_all, *line[4:8])
    outs = gather_groups(me, wo_pad, wo_parts, *line[8:12])
    packs[0]()
    tiles[0]()
    to_table = send(table_own, table_far, t_sem.at[0], t_sem.at[1], head=me.across)
    for i in range(1, seqs):
        send(ids, ids_all.at[s], i_send.at[i - 1], i_recv.at[i - 1], seq=mod(s + i, seqs))
    for i in range(1, seqs):
        to = mod(s + i, seqs)
        send(tok.at[per * to + x, own_half], tok_all.at[s, own_half], z_send.at[i - 1], z_recv.at[i - 1], seq=to)

    def send_later():
        outs[0]()
        for i in range(1, seqs):
            to = mod(s + i, seqs)
            target = jnp.where(lax.rem(s + to, 2) == c, h, me.near)
            j = lax.div(s, 2)
            send(
                cot.at[per * to + x, own_half],
                cot_own.at[j, own_half],
                c_send.at[i - 1],
                c_recv.at[j, c],
                head=target,
                seq=to,
            )

    def build_bias(rows):
        turn = lax.broadcasted_iota(jnp.int32, (128, 4 * span), 1)
        bucket = bucket_of(jnp.where(turn < 3 * span, turn, turn - 4 * span) - span, buckets)
        hot = (bucket == lax.broadcasted_iota(jnp.int32, (128, 4 * span), 0)).astype(BF16)
        bias_rows = jnp.dot(rows[...].astype(BF16), hot, preferred_element_type=F32)
        for head in range(heads):
            row = bias_rows[head : head + 1]
            rolled = pltpu.roll(jnp.broadcast_to(row, (span, 4 * span)), 0, 1, stride=1, stride_axis=0)
            ext[head, :, 2 * span : 5 * span] = rolled[:, : 3 * span]
            ext[head, :, : 2 * span] = jnp.broadcast_to(row[:, 0:1], (span, 2 * span))
            ext[head, :, 5 * span :] = jnp.broadcast_to(row[:, 3 * span - 1 : 3 * span], (span, 2 * span))

    def whole_weights(parts, into):
        if shard % 16:
            whole = parts[...].reshape(groups * pack.shape[0], pack.shape[1])
            hot = squeeze_hot(shard, pack.shape[0], width, groups)
            into[...] = jnp.dot(hot, whole, preferred_element_type=F32).astype(BF16)
        else:
            into[...] = parts[...].reshape(width, pack.shape[1])

    def assemble():
        whole_weights(pack_all, weights)
        row = jnp.zeros((8, width), F32)
        for g in range(groups):
            piece = tile_all[g // dps, g % dps].astype(BF16)
            row = row + jnp.dot(piece, spread_hot(g * shard, shard, width), preferred_element_type=F32)
        gains[...] = row

    def project(group, block):
        rows = pl.ds(pl.multiple_of(block * span, span), span)
        if group == 0:
            v = tok_all[block].astype(F32)
            normed = v * lax.rsqrt(jnp.mean(v * v, axis=-1, keepdims=True) + EPS) * gains[0:1, :]
            attn_input[rows, :] = normed.astype(BF16)
        which = weights if group == 0 else weights_far
        parts = jnp.dot(attn_input[rows, :], which[...], preferred_element_type=F32).astype(BF16)
        for n in range(3 * heads):
            split[group, n, rows, :HEAD_DIM] = parts[:, n * HEAD_DIM : (n + 1) * HEAD_DIM]

    build_bias(table_own)
    for i in range(1, seqs):
        packs[1](i)
        tiles[1](i)
    far_first = [i for i in range(1, seqs) if i != 2] + [2]

    def pass_own(i):
        here = tok_all.at[mod(s - i, seqs), own_half]
        arrived(here, z_recv.at[i - 1])
        send(here, here, h_send.at[i - 1], h_recv.at[i - 1], head=me.near)

    for copy in own_copies:
        copy.wait()
    packs[2]()
    tiles[2]()
    assemble()
    project(0, s)
    for i in far_first:
        pass_own(i)
    send_later()
    for i in far_first:
        source = mod(s - i, seqs)
        arrived(tok_all.at[source, other_half], h_recv.at[i - 1])
        project(0, source)
    kept = [
        pltpu.make_async_copy(attn_input, attn_input_out, ls.at[6]),
        pltpu.make_async_copy(split.at[0], split_out.at[0], ls.at[7]),
        pltpu.make_async_copy(split.at[1], split_out.at[1], ls.at[8]),
    ]
    for copy in kept[:2]:
        copy.start()
    for j in range(per):
        own_tok[j] = tok_all[me.block(j)]

    def second_group():
        packs[3]()
        whole_weights(far_all, weights_far)
        arrived(table_far, t_sem.at[1])
        build_bias(table_far)

        @pl.loop(0, blocks)
        def _(block):
            project(1, block)

        kept[2].start()

    @pl.loop(0, 2 * blocks)
    def _(unit):
        group, block = lax.div(unit, blocks), lax.rem(unit, blocks)
        rows = pl.ds(pl.multiple_of(block * span, span), span)
        turn = lax.rem(unit, 2)

        @pl.when(unit == blocks)
        def _():
            second_group()

        @pl.when(unit >= 2)
        def _():
            pltpu.make_async_copy(slot.at[turn], slot.at[turn], p_sem.at[turn]).wait()

        window = pl.ds(pl.multiple_of((blocks - 1 - block) * span, span), length)
        valid = lax.broadcasted_iota(jnp.int32, (1, length), 1) < lengths[per * s + x]
        for head in range(heads):
            query = split[group, head, rows, :HEAD_DIM]
            key, value = split[group, heads + head, :, :HEAD_DIM], split[group, 2 * heads + head, :, :HEAD_DIM]
            scores = lax.dot_general(query, key, (((1,), (1,)), ((), ())), preferred_element_type=F32)
            scores = jnp.where(valid, scores + ext[head, :, window], -1e30)
            top = jnp.max(scores, axis=-1, keepdims=True)
            grown = jnp.exp(scores - top)
            total = jnp.sum(grown, axis=-1, keepdims=True)
            part = (grown * (1.0 / total)).astype(BF16)
            slot[turn, head] = part
            mixed = jnp.dot(part, value, preferred_element_type=F32)
            out[unit, :, head * HEAD_DIM : (head + 1) * HEAD_DIM] = mixed.astype(BF16)
        pltpu.make_async_copy(slot.at[turn], probs.at[group, :, rows, :], p_sem.at[turn]).start()
        source = jnp.where(group == 0, h, me.across)
        j = lax.div(block, 2)

        @pl.when(lax.rem(block + s, 2) == c)
        def _():
            pltpu.make_async_copy(out.at[unit], heads_all.at[source, j], os.at[group, j]).start()

        @pl.when(lax.rem(block + s, 2) != c)
        def _():
            send(out.at[unit], heads_all.at[source, j], a_send.at[group, j], a_recv.at[group, j], head=me.near)

        @pl.when(unit == 2)
        def _():
            for i in range(1, seqs):
                outs[1](i)

        @pl.when(unit == blocks)
        def _():
            outs[2]()
            total = jnp.zeros((local, width), F32)
            for g in range(groups):
                total = total + jnp.dot(
                    wo_parts[g // dps, g % dps], spread_hot(g * shard, shard, width), preferred_element_type=F32
                )
            wo_all[h] = total.astype(BF16)
            send(wo_all.at[h], wo_all.at[h], w_send.at[0], w_recv.at[0], head=me.across)
            send(wo_all.at[h], wo_all.at[h], w_send.at[1], w_recv.at[1], head=me.near)

    there = wo_all.at[me.across]
    arrived(there, w_recv.at[0])
    send(there, there, w_send.at[2], w_recv.at[2], head=me.near)
    for copy in kept:
        copy.wait()
    for turn in range(2):
        pltpu.make_async_copy(slot.at[turn], slot.at[turn], p_sem.at[turn]).wait()
    packs[4]()
    to_table.wait_send()
    for j in range(per):
        block = me.block(j)

        @pl.when(block == s)
        def _():
            pltpu.make_async_copy(cot_own.at[j], cot_own.at[j], ls.at[5]).wait()

        @pl.when(block != s)
        def _():
            for part in range(2):
                arrived(cot_own.at[j, pl.ds(part * half, half)], c_recv.at[j, part])

        for group in range(2):
            pltpu.make_async_copy(out.at[0], heads_all.at[h, j], os.at[group, j]).wait()
            pltpu.make_async_copy(out.at[0], out.at[0], a_send.at[group, j]).wait()
            source = me.near if group == 0 else me.near_across
            arrived(heads_all.at[source, j], a_recv.at[group, j])

    for i in range(1, seqs):
        rows = tok.at[0, pl.ds(0, half)]
        for sem in (z_send, h_send, c_send):
            pltpu.make_async_copy(rows, rows, sem.at[i - 1]).wait()
        pltpu.make_async_copy(ids, ids, i_send.at[i - 1]).wait()
        arrived(ids_all.at[mod(s - i, seqs)], i_recv.at[i - 1])
    for k in range(3):
        pltpu.make_async_copy(wo_all.at[h], wo_all.at[h], w_send.at[k]).wait()
    arrived(wo_all.at[me.near], w_recv.at[1])
    arrived(wo_all.at[me.near_across], w_recv.at[2])


def front(tokens, cot, wq, wk, wv, wo, router, gain_a, gain_f, ids, table, lengths, seqs, dps):
    seq_local, span, width = tokens.shape
    per = seq_local // seqs
    length = seqs * span
    shard, local = wq.shape
    heads = local // HEAD_DIM
    lanes = up_to(3 * local + router.shape[0], 128)
    padded = up_to(shard, 16)
    smem = pl.BlockSpec(memory_space=pltpu.SMEM)
    return pl.pallas_call(
        functools.partial(front_kernel, seqs, dps, heads),
        out_shape=(
            jax.ShapeDtypeStruct((length, width), BF16),
            jax.ShapeDtypeStruct((width, lanes), BF16),
            jax.ShapeDtypeStruct((width, lanes), BF16),
            jax.ShapeDtypeStruct((2, 3 * heads, length, 128), BF16),
            jax.ShapeDtypeStruct((2, heads, length, length), BF16),
            jax.ShapeDtypeStruct((4, per, span, local), BF16),
            jax.ShapeDtypeStruct((per, span, width), BF16),
            jax.ShapeDtypeStruct((per, span, width), BF16),
            jax.ShapeDtypeStruct((4, local, width), BF16),
            jax.ShapeDtypeStruct((8, width), F32),
            jax.ShapeDtypeStruct((seqs,) + ids.shape, jnp.int32),
        ),
        in_specs=[ANY] * 2 + [VMEM] * 7 + [ANY, VMEM, smem],
        out_specs=[ANY, VMEM, VMEM] + [ANY] * 3 + [VMEM, ANY] + [VMEM] * 2 + [ANY],
        scratch_shapes=[
            pltpu.VMEM((length, width), BF16),
            pltpu.VMEM((2, 3 * heads, length, 128), BF16),
            pltpu.VMEM((seqs, span, width), BF16),
            pltpu.VMEM((padded, lanes), BF16),
            pltpu.VMEM((seqs, dps, padded, lanes), BF16),
            pltpu.VMEM((seqs, dps, padded, lanes), BF16),
            pltpu.VMEM((local, 128), BF16),
            pltpu.VMEM((seqs, dps, local, 128), BF16),
            pltpu.VMEM((8, 128), F32),
            pltpu.VMEM((seqs, dps, 8, 128), F32),
            pltpu.VMEM((8, 128), F32),
            pltpu.VMEM((8, 128), F32),
            pltpu.VMEM((heads, span, 7 * span), F32),
            pltpu.VMEM((2, heads, span, length), BF16),
            pltpu.VMEM((2 * seqs, span, local), BF16),
            DMA((2,)),
            DMA((9,)),
            DMA((2, per)),
            DMA((seqs - 1,)),
            DMA((seqs - 1,)),
            DMA((seqs - 1,)),
            DMA((seqs - 1,)),
            DMA((seqs - 1,)),
            DMA((per, 2)),
            DMA((2, per)),
            DMA((2, per)),
            DMA((3,)),
            DMA((3,)),
            DMA((seqs - 1,)),
            DMA((seqs - 1,)),
            DMA((seqs, dps)),
            DMA((seqs, dps)),
            DMA((2,)),
        ]
        + gather_sems(seqs, dps) * 3,
        compiler_params=params(collective_id=0),
        name="front",
    )(tokens, cot, wq, wk, wv, wo, router, gain_a, gain_f, ids, table, lengths)


def expert_windows(exp_local, per_expert):
    return [(e * per_expert // 16 * 16, up_to((e + 1) * per_expert, 16)) for e in range(exp_local)]


def contract(a, b, over_a, over_b):
    return lax.dot_general(a, b, (((over_a,), (over_b,)), ((), ())), preferred_element_type=F32)


AHEAD = 2
GELU_A, GELU_B = float(np.sqrt(2.0 / np.pi)), 0.044715


def experts_kernel(
    seqs, dps, per_expert, capacity, local,
    heads_all, own_tok, wo_all, weights, gains, cot_own, ids_all, up_in, down_in,
    result, hidden_grad, router_grad, gain_grad, up_out, down_out,
    up, down, up_grad, down_grad, rows, summed, place_hot, hidden_ref, ffn_ref, router_ref, gate_ref, hot_ref, taken, near, far,
    ls, g_send, g_recv, h_send, h_recv, n_send, n_recv, x_send, x_recv, r_send, r_recv
):
    me = Place(seqs, dps)
    h, s, d = me.h, me.s, me.d
    groups, _, height, width = rows.shape
    exp_local = up.shape[0]
    windows = expert_windows(exp_local, per_expert)
    me_group = s * dps + d

    def away(n):
        return lax.div(n, dps), lax.rem(n, dps)

    def ahead(n):
        i, j = away(n)
        return mod(s + i, seqs), mod(d + j, dps)

    def behind(n):
        i, j = away(n)
        return mod(s - i, seqs), mod(d - j, dps)

    per, span, _ = own_tok.shape
    loads = [pltpu.make_async_copy(up_in, up, ls.at[1]), pltpu.make_async_copy(down_in, down, ls.at[2])]
    for copy in loads:
        copy.start()
    spots = groups * height
    first_lane = 3 * local // 128 * 128
    spread = weights.shape[1] - first_lane
    shift = 3 * local - first_lane
    experts = groups * exp_local
    router = weights[:, first_lane:]
    earlier = lax.broadcasted_iota(jnp.int32, (span, span), 0) < lax.broadcasted_iota(jnp.int32, (span, span), 1)
    earlier = earlier.astype(BF16)
    lane = lax.broadcasted_iota(jnp.int32, (span, spread), 1)
    is_expert = (lane >= shift) & (lane < shift + experts)

    def tokens_in(j):
        total = own_tok[j].astype(F32)
        for q in range(4):
            total = total + jnp.dot(heads_all[q, j], wo_all[q], preferred_element_type=F32)
        hidden_ref[j] = total
        inverse = lax.rsqrt(jnp.mean(total * total, axis=-1, keepdims=True) + EPS)
        ffn = (total * inverse * gains[1:2, :]).astype(BF16)
        ffn_ref[j] = ffn
        logits = jnp.where(is_expert, jnp.dot(ffn, router, preferred_element_type=F32), -1e30)
        grown = jnp.exp(logits - jnp.max(logits, axis=-1, keepdims=True))
        router_probs = grown / jnp.sum(grown, axis=-1, keepdims=True)
        router_ref[j] = router_probs
        ids = ids_all[me.block(j), pl.ds(per * s + me.x, 1), :]
        own = lax.broadcasted_iota(jnp.int32, (spread, span), 0) == ids + shift
        own_low = own.astype(BF16)
        before = jnp.dot(own_low, earlier, preferred_element_type=F32)
        slot = jnp.sum(jnp.where(own, before, 0.0), axis=0, keepdims=True).astype(jnp.int32)
        same = lax.broadcasted_iota(jnp.int32, (spread, spread), 0) == lax.broadcasted_iota(jnp.int32, (spread, spread), 1)
        hot = contract(own_low, same.astype(BF16), 0, 0)
        hot_ref[j] = hot
        gate = jnp.sum(router_probs * hot, axis=-1, keepdims=True)
        gate_ref[j] = gate
        group = lax.div(ids, exp_local)
        place = group * height + ((ids - group * exp_local) * per + j) * capacity + slot
        spot = lax.broadcasted_iota(jnp.int32, (spots, span), 0)
        place_hot[j] = (spot == place).astype(BF16)
        return ffn, (gate * cot_own[j].astype(F32)).astype(BF16)

    made = [tokens_in(j) for j in range(per)]
    for part in range(2):
        total = jnp.zeros((spots, width), F32)
        for j in range(per):
            total = total + jnp.dot(place_hot[j], made[j][part], preferred_element_type=F32)
        total = total.astype(BF16)
        for g in range(groups):
            rows[g, part] = total[g * height : (g + 1) * height, :]
    up_grad[...] = jnp.zeros_like(up_grad)
    down_grad[...] = jnp.zeros_like(down_grad)
    greet(me.group_peers() + me.head_pair())
    pltpu.make_async_copy(rows.at[me_group], taken.at[h, 0], ls.at[0]).start()
    for copy in loads:
        copy.wait()

    def send_out(n):
        to_s, to_d = ahead(n)
        send(rows.at[to_s * dps + to_d], taken.at[h, n], g_send.at[n], g_recv.at[n], seq=to_s, dp=to_d)

    for n in range(1, min(AHEAD + 1, groups)):
        send_out(n)

    def gather_own(n):
        here = taken.at[h, n]

        @pl.when(n == 0)
        def _():
            pltpu.make_async_copy(here, here, ls.at[0]).wait()

        @pl.when(n > 0)
        def _():
            arrived(here, g_recv.at[n])

        send(here, here, h_send.at[0, n], h_recv.at[0, n], head=me.across)
        send(here, here, h_send.at[1, n], h_recv.at[1, n], head=me.near)

    def gather_across(n):
        there = taken.at[me.across, n]
        arrived(there, h_recv.at[0, n])
        send(there, there, h_send.at[2, n], h_recv.at[2, n], head=me.near)

    def compute(n):
        arrived(taken.at[me.near, n], h_recv.at[1, n])
        arrived(taken.at[me.near_across, n], h_recv.at[2, n])
        for k in range(3):
            pltpu.make_async_copy(taken.at[h, n], taken.at[h, n], h_send.at[k, n]).wait()
        kept = []
        for e, (low, high) in enumerate(windows):
            size = high - low
            at = lax.broadcasted_iota(jnp.int32, (4 * size, width), 0)
            slot = lax.rem(at, size) + low
            inside = (slot >= e * per_expert) & (slot < (e + 1) * per_expert)

            def mine(part):
                block = jnp.concatenate([taken[q, n, part, low:high, :] for q in range(4)], axis=0)
                return jnp.where(inside, block.astype(F32), 0.0).astype(BF16)

            x, g = mine(0), mine(1)
            pre = jnp.dot(x, up[e], preferred_element_type=F32)
            square = pre * pre
            bent = jnp.tanh(GELU_A * pre * (1.0 + GELU_B * square))
            act = (0.5 * pre * (1.0 + bent)).astype(BF16)
            slope = 0.5 * (1.0 + bent) + 0.5 * pre * (1.0 - bent * bent) * (GELU_A * (1.0 + 3.0 * GELU_B * square))
            out = jnp.dot(act, down[e], preferred_element_type=F32).astype(BF16)
            act_grad = contract(g, down[e], 1, 1)
            pre_grad = (act_grad * slope).astype(BF16)
            back = contract(pre_grad, up[e], 1, 1).astype(BF16)
            kept.append((x, g, act, pre_grad, out, back))
        for q in range(4):
            for part in range(2):
                for tile in range(0, height, 16):
                    total = None
                    for (low, high), made in zip(windows, kept):
                        if low <= tile < high:
                            begin = q * (high - low) + tile - low
                            piece = made[4 + part][begin : begin + 16, :]
                            total = piece if total is None else total + piece
                    if total is not None:
                        taken[q, n, part, tile : tile + 16, :] = total
        send(taken.at[me.near_across, n], near.at[0, n], n_send.at[0, n], n_recv.at[0, n], head=me.near)
        send(taken.at[me.near, n], near.at[1, n], n_send.at[1, n], n_recv.at[1, n], head=me.near)
        for e in range(exp_local):
            x, g, act, pre_grad, _, _ = kept[e]
            up_grad[e] += contract(x, pre_grad, 0, 0)
            down_grad[e] += contract(act, g, 0, 0)

    def add_near(n):
        arrived(near.at[0, n], n_recv.at[0, n])
        both = taken[me.across, n].astype(F32) + near[0, n].astype(F32)
        taken[me.across, n] = both.astype(BF16)
        send(taken.at[me.across, n], far.at[n], x_send.at[n], x_recv.at[n], head=me.across)

    def send_back(n):
        arrived(near.at[1, n], n_recv.at[1, n])
        arrived(far.at[n], x_recv.at[n])
        total = taken[h, n].astype(F32) + near[1, n].astype(F32) + far[n].astype(F32)
        taken[h, n] = total.astype(BF16)
        to_s, to_d = behind(n)

        @pl.when(n == 0)
        def _():
            pltpu.make_async_copy(taken.at[h, n], summed.at[:, me_group], r_send.at[n]).start()

        @pl.when(n > 0)
        def _():
            send(taken.at[h, n], summed.at[:, me_group], r_send.at[n], r_recv.at[n], seq=to_s, dp=to_d)

    gather_own(0)
    stages = (send_back, add_near, compute, gather_across, gather_own)

    @pl.loop(0, groups + len(stages) - 1)
    def _(step):
        @pl.when(step + 1 + AHEAD < groups)
        def _():
            send_out(step + 1 + AHEAD)

        for k, stage in enumerate(stages):
            turn = step - (len(stages) - 1 - k)
            last = groups - 1 if stage is gather_own else groups

            @pl.when((turn >= 0) & (turn < last))
            def _():
                stage(lax.rem(turn + 1, groups))

    stores = [
        pltpu.make_async_copy(up_grad, up_out, ls.at[1]),
        pltpu.make_async_copy(down_grad, down_out, ls.at[2]),
    ]
    for copy in stores:
        copy.start()

    @pl.loop(0, groups)
    def _(n):
        here = taken.at[h, n]
        for k in range(2):
            pltpu.make_async_copy(here, here, n_send.at[k, n]).wait()
        pltpu.make_async_copy(here, here, x_send.at[n]).wait()
        pltpu.make_async_copy(here, here, r_send.at[n]).wait()

        @pl.when(n > 0)
        def _():
            pltpu.make_async_copy(here, here, g_send.at[n]).wait()
            from_s, from_d = ahead(n)
            arrived(summed.at[:, from_s * dps + from_d], r_recv.at[n])

    def tokens_out(j):
        hidden, gate, router_probs, hot = hidden_ref[j], gate_ref[j], router_ref[j], hot_ref[j]
        grad = cot_own[j].astype(F32)
        token_out = contract(place_hot[j], summed[0].reshape(spots, width), 0, 0)
        input_grad = contract(place_hot[j], summed[1].reshape(spots, width), 0, 0)
        result[j] = (hidden + gate * token_out).astype(BF16)
        gate_grad = jnp.sum(grad * token_out, axis=-1, keepdims=True)
        logit_low = (router_probs * (gate_grad * hot - gate_grad * gate)).astype(BF16)
        router_part = contract(ffn_ref[j], logit_low, 0, 0)
        input_grad = input_grad + contract(logit_low, router, 1, 1)
        inverse = lax.rsqrt(jnp.mean(hidden * hidden, axis=-1, keepdims=True) + EPS)
        r = hidden * inverse
        u = input_grad * gains[1:2, :]
        hidden_grad[j] = grad + (u - r * jnp.mean(u * r, axis=-1, keepdims=True)) * inverse
        gain_part = jnp.sum(input_grad * r, axis=0, keepdims=True)
        if j == 0:
            router_grad[...] = router_part
            gain_grad[...] = gain_part
        else:
            router_grad[...] += router_part
            gain_grad[...] += gain_part

    for j in range(per):
        tokens_out(j)
    for copy in stores:
        copy.wait()


def run_experts(
    heads_all, own_tok, wo_all, weights, gains, cot_own, ids_all, up, down, seqs, dps, per_expert, capacity
):
    per, span, width = own_tok.shape
    local = wo_all.shape[1]
    groups = seqs * dps
    height = up_to(up.shape[0] * per_expert, 16)
    spread = weights.shape[1] - 3 * local // 128 * 128
    rows = (groups, 2, height, width)
    return pl.pallas_call(
        functools.partial(experts_kernel, seqs, dps, per_expert, capacity, local),
        out_shape=(
            jax.ShapeDtypeStruct((per, span, width), BF16),
            jax.ShapeDtypeStruct((per, span, width), F32),
            jax.ShapeDtypeStruct((width, spread), F32),
            jax.ShapeDtypeStruct((1, width), F32),
            jax.ShapeDtypeStruct(up.shape, F32),
            jax.ShapeDtypeStruct(down.shape, F32),
        ),
        in_specs=[VMEM] * 7 + [ANY] * 2,
        out_specs=[VMEM] * 4 + [ANY] * 2,
        scratch_shapes=[
            pltpu.VMEM(up.shape, BF16),
            pltpu.VMEM(down.shape, BF16),
            pltpu.VMEM(up.shape, F32),
            pltpu.VMEM(down.shape, F32),
            pltpu.VMEM(rows, BF16),
            pltpu.VMEM((2, groups, height, width), BF16),
            pltpu.VMEM((per, groups * height, span), BF16),
            pltpu.VMEM((per, span, width), F32),
            pltpu.VMEM((per, span, width), BF16),
            pltpu.VMEM((per, span, spread), F32),
            pltpu.VMEM((per, span, 1), F32),
            pltpu.VMEM((per, span, spread), F32),
            pltpu.VMEM((4,) + rows, BF16),
            pltpu.VMEM((2,) + rows, BF16),
            pltpu.VMEM(rows, BF16),
            DMA((3,)),
            DMA((groups,)),
            DMA((groups,)),
            DMA((3, groups)),
            DMA((3, groups)),
            DMA((2, groups)),
            DMA((2, groups)),
            DMA((groups,)),
            DMA((groups,)),
            DMA((groups,)),
            DMA((groups,)),
        ],
        compiler_params=params(collective_id=2),
        name="experts",
    )(heads_all, own_tok, wo_all, weights, gains, cot_own, ids_all, up, down)


def send_home(me, own, home, ls, z_send, z_recv, h_send, h_recv):
    s, seqs, x, core = me.s, me.seqs, me.x, me.c
    per, span, _ = own.shape
    rows = span // PIECES
    lands = [(k, lax.rem(s + core, 2) + 2 * k) for k in range(seqs // 2)]

    def part(c):
        return pl.ds(c * rows, rows)

    def start(c):
        for j in range(per):
            to = me.block(j)
            there = home.at[per * s + x, part(c)]

            @pl.when(to != s)
            def _():
                k = lax.div(s, 2)
                send(own.at[j, part(c)], there, z_send.at[j, c], z_recv.at[k, c], seq=to)

            @pl.when(to == s)
            def _():
                pltpu.make_async_copy(own.at[j, part(c)], there, ls.at[c]).start()

    def pass_on(c):
        for k, source in lands:
            here = home.at[per * source + x, part(c)]

            @pl.when(source == s)
            def _():
                pltpu.make_async_copy(here, here, ls.at[c]).wait()

            @pl.when(source != s)
            def _():
                arrived(here, z_recv.at[k, c])

            send(here, here, h_send.at[0, k, c], h_recv.at[0, k, c], head=me.across)
            send(here, here, h_send.at[1, k, c], h_recv.at[1, k, c], head=me.near)

    def pass_near(c):
        for k, source in lands:
            there = home.at[per * source + 1 - x, part(c)]
            arrived(there, h_recv.at[0, k, c])
            send(there, there, h_send.at[2, k, c], h_recv.at[2, k, c], head=me.near)

    def finish():
        some = own.at[0, part(0)]
        for c in range(PIECES):
            for j in range(per):

                @pl.when(me.block(j) != s)
                def _():
                    pltpu.make_async_copy(some, some, z_send.at[j, c]).wait()

            for k in range(seqs // 2):
                source = lax.rem(s + 1 + core, 2) + 2 * k
                arrived(home.at[per * source + x, part(c)], h_recv.at[1, k, c])
                arrived(home.at[per * source + 1 - x, part(c)], h_recv.at[2, k, c])
                for n in range(3):
                    pltpu.make_async_copy(some, some, h_send.at[n, k, c]).wait()

    return start, pass_on, pass_near, finish


def home_sems(per, seqs):
    return [
        DMA((PIECES,)),
        DMA((per, PIECES)),
        DMA((seqs // 2, PIECES)),
        DMA((3, seqs // 2, PIECES)),
        DMA((3, seqs // 2, PIECES)),
    ]


def add_groups(me, parts, dp_take, seq_take, result, dp_send, dp_recv, seq_send, seq_recv):
    s, d, seqs, dps = me.s, me.d, me.seqs, me.dps
    order = [mod(s + n, seqs) for n in list(range(1, seqs)) + [0]]

    def start():
        for to in order:
            for i in range(1, dps):
                there = mod(d + i, dps)
                send(
                    parts.at[there, to], dp_take.at[i - 1, to], dp_send.at[i - 1, to], dp_recv.at[i - 1, to], dp=there
                )

    def middle():
        for n, to in enumerate(order):
            total = parts[d, to].astype(F32)
            for i in range(1, dps):
                arrived(dp_take.at[i - 1, to], dp_recv.at[i - 1, to])
                total = total + dp_take[i - 1, to].astype(F32)
            parts[d, to] = total.astype(parts.dtype)
            if n < seqs - 1:
                send(parts.at[d, to], seq_take.at[n], seq_send.at[n], seq_recv.at[n], seq=to)

    def end():
        total = parts[d, s].astype(F32)
        for n in range(seqs - 1):
            arrived(seq_take.at[n], seq_recv.at[n])
            total = total + seq_take[n].astype(F32)
        result[...] = total
        some = seq_take.at[0]
        for to in range(seqs):
            for i in range(1, dps):
                pltpu.make_async_copy(some, some, dp_send.at[i - 1, to]).wait()
        for n in range(seqs - 1):
            pltpu.make_async_copy(some, some, seq_send.at[n]).wait()

    return start, middle, end


def group_scratch(seqs, dps, shape, dtype):
    return [
        pltpu.VMEM((dps, seqs) + shape, dtype),
        pltpu.VMEM((max(1, dps - 1), seqs) + shape, dtype),
        pltpu.VMEM((seqs - 1,) + shape, dtype),
    ]


def group_sems(seqs, dps):
    return [DMA((max(1, dps - 1), seqs))] * 2 + [DMA((seqs - 1,))] * 2


PIECES = 2


def back_kernel(
    seqs, dps, heads,
    result, hidden_grad, own_tok, heads_all, wo_all, split_in, probs, attn_input_in, weights, weights_far, gains, router,
    gain_f,
    output, tokens_home, w_sum, small_sum, wo_sum, gain_sum, bias_sum,
    split, attn_input, attn_grad, hsend, grad_all, slot, ext, made, dk_sum, dv_sum, x_acc, x_out, x_near, tg,
    wo_part, wo_near, wo_far, w_parts, w_dp, w_seq, far_parts, far_dp, far_seq, far_sum, far_out, far_in,
    wo_parts, wo_dp, wo_seq, g_parts, g_dp, g_seq, r_parts, r_dp, r_seq, r_sum, g_acc,
    bias, bias_out, bias_in, bias_take, small, gsmall,
    ls, p_sem, a_send, a_recv, n_send, n_recv, on_send, on_recv, of_send, of_recv,
    b_send, b_recv, s_send, s_recv, t_send, t_recv, fs, *sems
):
    me = Place(seqs, dps)
    h, s, d = me.h, me.s, me.d
    per, span, width = hidden_grad.shape
    blocks = seqs
    length = blocks * span
    local = heads * HEAD_DIM
    groups = seqs * dps
    shard = width // groups
    padded = w_sum.shape[0]
    buckets = 32
    size = span // PIECES
    others = [(i, j) for i in range(seqs) for j in range(dps) if i or j]
    loads = [pltpu.make_async_copy(split_in, split, ls.at[0]), pltpu.make_async_copy(attn_input_in, attn_input, ls.at[1])]
    for copy in loads:
        copy.start()
    greet(me.group_peers() + [{"head": mod(h + i, 4)} for i in range(1, 4)])
    out_home = send_home(me, result, output, *sems[0:5])
    grad_home = send_home(me, tg, tokens_home, *sems[5:10])
    w_group = add_groups(me, w_parts, w_dp, w_seq, w_sum, *sems[10:14])
    wo_group = add_groups(me, wo_parts, wo_dp, wo_seq, wo_sum, *sems[14:18])
    g_group = add_groups(me, g_parts, g_dp, g_seq, gain_sum, *sems[18:22])
    r_group = add_groups(me, r_parts, r_dp, r_seq, r_sum, *sems[22:26])
    far_group = add_groups(me, far_parts, far_dp, far_seq, far_sum, *sems[26:30])

    def by_group(whole, parts):
        low = whole.astype(BF16)
        if shard % 16:
            low = contract(squeeze_hot(shard, padded, width, groups), low, 0, 0).astype(BF16)
        for g in range(groups):
            parts[g % dps, g // dps] = low[g * padded : (g + 1) * padded, :]

    def fetch(group, n):
        block = jnp.where(n < per, me.block(lax.rem(n, per)), me.block(lax.rem(n, per), 1 - me.c))
        rows = pl.ds(pl.multiple_of(block * span, span), span)
        turn = lax.rem(n, 2)
        return block, rows, turn, pltpu.make_async_copy(probs.at[group, :, rows, :], slot.at[turn], p_sem.at[turn])

    def put(ref, grad):
        ref[:, :local] = grad[: span // 2]
        ref[:, local:] = grad[span // 2 :]

    fetch(1, 0)[3].start()
    attn_grad[...] = hidden_grad[...].astype(BF16)
    for group, (own, other) in ((1, (me.across, me.near_across)), (0, (h, me.near))):
        for j in range(per):
            put(hsend.at[group, j], contract(attn_grad[j], wo_all[other], 1, 1).astype(BF16))
            send(
                hsend.at[group, j],
                grad_all.at[group, me.block(j)],
                a_send.at[group, j],
                a_recv.at[group, j],
                head=me.near,
            )
            put(grad_all.at[group, me.block(j)], contract(attn_grad[j], wo_all[own], 1, 1).astype(BF16))
        if group:
            out_home[0](0)
    for k, q in enumerate((me.near_across, me.near, me.across, h)):
        total = jnp.zeros((local, width), F32)
        for j in range(per):
            total = total + contract(heads_all[q, j], attn_grad[j], 0, 0)
        wo_part[k] = total.astype(BF16)
        if k < 2:
            send(wo_part.at[k], wo_near.at[k], on_send.at[k], on_recv.at[k], head=me.near)
    by_group(router[...], r_parts)
    r_group[0]()
    for copy in loads:
        copy.wait()
    ext[...] = jnp.zeros_like(ext)
    made[...] = jnp.zeros_like(made)

    def wo_across():
        arrived(wo_near.at[0], on_recv.at[0])
        wo_part[2] = (wo_part[2].astype(F32) + wo_near[0].astype(F32)).astype(BF16)
        send(wo_part.at[2], wo_far, of_send, of_recv, head=me.across)

    def wo_total():
        arrived(wo_near.at[1], on_recv.at[1])
        arrived(wo_far, of_recv)
        total = (wo_part[3].astype(F32) + wo_near[1].astype(F32) + wo_far[...].astype(F32)).astype(BF16)
        for g in range(groups):
            hot = spread_hot(g * shard, shard, width)
            wo_parts[g % dps, g // dps] = contract(total, hot, 1, 1).astype(BF16)
        wo_group[0]()

    def cut(c):
        return pl.ds(c * size, size)

    def x_partial():
        for core in (1 - me.c, me.c):
            for c in range(PIECES):
                for j in range(per):
                    rows = pl.ds(pl.multiple_of(me.block(j, core) * span + c * size, size), size)
                    total = x_acc[rows, :] + contract(made[rows, :], weights[...], 1, 1)
                    if core is me.c:
                        x_acc[rows, :] = total
                    else:
                        x_out[j, cut(c)] = total.astype(BF16)
                        send(x_out.at[j, cut(c)], x_near.at[j, cut(c)], n_send.at[j, c], n_recv.at[j, c], head=me.near)

    def x_total(c):
        for j in range(per):
            arrived(x_near.at[j, cut(c)], n_recv.at[j, c])
            rows = pl.ds(pl.multiple_of(me.block(j) * span + c * size, size), size)
            grad = x_acc[rows, :] + x_near[j, cut(c)].astype(F32)
            v = own_tok[j, cut(c)].astype(F32)
            inverse = lax.rsqrt(jnp.mean(v * v, axis=-1, keepdims=True) + EPS)
            r = v * inverse
            u = grad * gains[0:1, :]
            back = (u - r * jnp.mean(u * r, axis=-1, keepdims=True)) * inverse
            tg[j, cut(c)] = (hidden_grad[j, cut(c)] + back).astype(BF16)
            g_acc[0:1, :] += jnp.sum(grad * r, axis=0, keepdims=True)
        grad_home[0](c)

    def attention(group, service):
        @pl.loop(0, blocks)
        def _(n):
            block, rows, turn, copy = fetch(group, n)

            @pl.when(n >= per)
            def _():
                arrived(grad_all.at[group, block], a_recv.at[group, n - per])

            copy.wait()

            @pl.when(n < blocks - 1)
            def _():
                fetch(group, n + 1)[3].start()

            if group:

                @pl.when(n == blocks - 1)
                def _():
                    fetch(0, 0)[3].start()

            window = pl.ds(pl.multiple_of((blocks - 1 - block) * span, span), length)
            for head in range(heads):
                cols = slice(head * HEAD_DIM, (head + 1) * HEAD_DIM)
                query = split[group, head, rows, :HEAD_DIM]
                key, value = split[group, heads + head, :, :HEAD_DIM], split[group, 2 * heads + head, :, :HEAD_DIM]
                more = slice(local + head * HEAD_DIM, local + (head + 1) * HEAD_DIM)
                grad = jnp.concatenate([grad_all[group, block, :, cols], grad_all[group, block, :, more]], axis=0)
                part = slot[turn, head]
                prob_grad = contract(grad, value, 1, 1)
                wide = part.astype(F32)
                delta = jnp.sum(wide * prob_grad, axis=-1, keepdims=True)
                score_grad = wide * (prob_grad - delta)
                ext[head, :, window] += score_grad
                low = score_grad.astype(BF16)
                made[rows, cols] = jnp.dot(low, key, preferred_element_type=F32).astype(BF16)
                dk = contract(low, query, 0, 0)
                dv = contract(part, grad, 0, 0)

                @pl.when(n == 0)
                def _():
                    dk_sum[head] = dk
                    dv_sum[head] = dv

                @pl.when(n > 0)
                def _():
                    dk_sum[head] += dk
                    dv_sum[head] += dv

            for k, call in enumerate(service):

                @pl.when(n == k)
                def _():
                    for act in call:
                        act()

        for head in range(heads):
            cols = slice(local + head * HEAD_DIM, local + (head + 1) * HEAD_DIM)
            made[:, cols] = dk_sum[head].astype(BF16)
            cols = slice(2 * local + head * HEAD_DIM, 2 * local + (head + 1) * HEAD_DIM)
            made[:, cols] = dv_sum[head].astype(BF16)

    def bias_rows(into):
        turn = lax.broadcasted_iota(jnp.int32, (4 * span, 128), 0)
        bucket = bucket_of(jnp.where(turn < 3 * span, turn, turn - 4 * span) - span, buckets)
        hot = (bucket == lax.broadcasted_iota(jnp.int32, (4 * span, 128), 1)).astype(F32)
        lane = lax.broadcasted_iota(jnp.int32, (1, 128), 1)
        head_row = lax.broadcasted_iota(jnp.int32, (8, 4 * span), 0)
        diagonals = jnp.zeros((8, 4 * span), F32)
        far_row = lax.broadcasted_iota(jnp.int32, (8, 128), 0)
        far = jnp.zeros((8, 128), F32)
        for head in range(heads):
            eight = jnp.zeros((8, 4 * span), F32)
            for group in range(span // 8):
                piece = ext[head, group * 8 : (group + 1) * 8, 2 * span : 5 * span]
                piece = jnp.concatenate([piece, jnp.zeros((8, span), F32)], axis=1)
                eight = eight + pltpu.roll(piece, (4 * span - 8 * group) % (4 * span), 1)
            one = jnp.zeros((8, 4 * span), F32)
            for i in range(8):
                line = jnp.broadcast_to(eight[i : i + 1, :], (8, 4 * span))
                one = one + pltpu.roll(line, (4 * span - i) % (4 * span), 1)
            diagonals = jnp.where(head_row == head, one, diagonals)
            left, right = jnp.sum(ext[head, :, : 2 * span]), jnp.sum(ext[head, :, 5 * span :])
            sides = jnp.where(lane == buckets // 2 - 1, left, jnp.where(lane == buckets - 1, right, 0.0))
            far = jnp.where(far_row == head, sides, far)
        into[...] = far + jnp.dot(diagonals, hot, preferred_element_type=F32, precision=lax.Precision.HIGHEST)

    def router_total():
        r_group[2]()
        small[0] = r_sum[...]
        for i in range(1, 4):
            send(small.at[0], small.at[i], s_send.at[i - 1], s_recv.at[i - 1], head=mod(h + i, 4))

    g_acc[...] = jnp.zeros_like(g_acc)
    g_acc[1:2, :] = gain_f[...]
    attention(
        1,
        (
            (wo_across,),
            (functools.partial(out_home[0], 1),),
            (r_group[1], functools.partial(out_home[1], 0)),
            (wo_total,),
        ),
    )
    by_group(contract(attn_input[...], made[...], 0, 0), far_parts)
    far_group[0]()
    x_acc[...] = contract(made[...], weights_far[...], 1, 1)
    bias_rows(bias_out)
    to_bias = send(bias_out, bias_in, fs.at[0], fs.at[1], head=me.across)
    ext[...] = jnp.zeros_like(ext)
    attention(
        0,
        (
            (functools.partial(out_home[1], 1),),
            (wo_group[1], router_total),
            (far_group[1], functools.partial(out_home[2], 0)),
            (),
        ),
    )
    x_partial()
    x_total(0)
    by_group(contract(attn_input[...], made[...], 0, 0), w_parts)
    w_group[0]()
    x_total(1)
    g_rows = g_acc[...].astype(BF16)
    for g in range(groups):
        g_parts[g % dps, g // dps] = contract(g_rows, spread_hot(g * shard, shard, width), 1, 1)
    g_group[0]()
    far_group[2]()
    far_out[...] = far_sum[...].astype(BF16)
    to_far = send(far_out, far_in, fs.at[2], fs.at[3], head=me.across)
    bias_rows(bias)
    arrived(bias_in, fs.at[1])
    bias[...] += bias_in[...]
    for n, (i, j) in enumerate(others):
        send(bias, bias_take.at[n], b_send.at[n], b_recv.at[n], seq=mod(s + i, seqs), dp=mod(d + j, dps))
    out_home[2](1)
    w_group[1]()
    g_group[1]()
    grad_home[1](0)
    grad_home[1](1)
    g_group[2]()
    gsmall[0] = gain_sum[...]
    for i in range(1, 4):
        send(gsmall.at[0], gsmall.at[i], t_send.at[i - 1], t_recv.at[i - 1], head=mod(h + i, 4))
    wo_group[2]()
    total = bias[...]
    for n in range(len(others)):
        arrived(bias_take.at[n], b_recv.at[n])
        total = total + bias_take[n]
    bias_sum[...] = total
    grad_home[2](0)
    arrived(far_in, fs.at[3])
    w_group[2]()
    w_sum[...] += far_in[...].astype(F32)
    total, gain_total = small[0], gsmall[0]
    for i in range(1, 4):
        arrived(small.at[i], s_recv.at[i - 1])
        arrived(gsmall.at[i], t_recv.at[i - 1])
        total = total + small[i]
        gain_total = gain_total + gsmall[i]
    small_sum[...] = total
    gain_sum[...] = gain_total
    grad_home[2](1)
    out_home[3]()
    grad_home[3]()
    to_bias.wait_send()
    to_far.wait_send()
    for j in range(per):
        for group in range(2):
            pltpu.make_async_copy(hsend.at[0, 0], hsend.at[0, 0], a_send.at[group, j]).wait()
        some = x_near.at[0, cut(0)]
        for c in range(PIECES):
            pltpu.make_async_copy(some, some, n_send.at[j, c]).wait()
    for k in range(2):
        pltpu.make_async_copy(wo_far, wo_far, on_send.at[k]).wait()
    pltpu.make_async_copy(wo_far, wo_far, of_send).wait()
    for i in range(3):
        pltpu.make_async_copy(small.at[0], small.at[0], s_send.at[i]).wait()
        pltpu.make_async_copy(gsmall.at[0], gsmall.at[0], t_send.at[i]).wait()
    for n in range(len(others)):
        pltpu.make_async_copy(bias, bias, b_send.at[n]).wait()


def back_pass(
    result, hidden_grad, own_tok, heads_all, wo_all, split, probs, attn_input, weights, weights_far, gains, router, gain_f,
    seqs, dps
):
    per, span, width = hidden_grad.shape
    length = seqs * span
    heads = probs.shape[1]
    local = heads * HEAD_DIM
    groups = seqs * dps
    shard = width // groups
    padded = up_to(shard, 16)
    lanes = weights.shape[1]
    spread = router.shape[1]
    block = (span, width)
    return pl.pallas_call(
        functools.partial(back_kernel, seqs, dps, heads),
        out_shape=(
            jax.ShapeDtypeStruct((per * seqs,) + block, BF16),
            jax.ShapeDtypeStruct((per * seqs,) + block, BF16),
            jax.ShapeDtypeStruct((padded, lanes), F32),
            jax.ShapeDtypeStruct((padded, spread), F32),
            jax.ShapeDtypeStruct((local, 128), F32),
            jax.ShapeDtypeStruct((8, 128), F32),
            jax.ShapeDtypeStruct((8, 128), F32),
        ),
        in_specs=[VMEM] * 5 + [ANY] * 3 + [VMEM] * 5,
        out_specs=[ANY] * 2 + [VMEM] * 5,
        scratch_shapes=[
            pltpu.VMEM(split.shape, BF16),
            pltpu.VMEM(attn_input.shape, BF16),
            pltpu.VMEM((per,) + block, BF16),
            pltpu.VMEM((2, per, span // 2, 2 * local), BF16),
            pltpu.VMEM((2, seqs, span // 2, 2 * local), BF16),
            pltpu.VMEM((2, heads, span, length), BF16),
            pltpu.VMEM((heads, span, 7 * span), F32),
            pltpu.VMEM((length, lanes), BF16),
            pltpu.VMEM((heads, length, HEAD_DIM), F32),
            pltpu.VMEM((heads, length, HEAD_DIM), F32),
            pltpu.VMEM((length, width), F32),
            pltpu.VMEM((per,) + block, BF16),
            pltpu.VMEM((per,) + block, BF16),
            pltpu.VMEM((per,) + block, BF16),
            pltpu.VMEM((4, local, width), BF16),
            pltpu.VMEM((2, local, width), BF16),
            pltpu.VMEM((local, width), BF16),
        ]
        + group_scratch(seqs, dps, (padded, lanes), BF16) * 2
        + [
            pltpu.VMEM((padded, lanes), F32),
            pltpu.VMEM((padded, lanes), BF16),
            pltpu.VMEM((padded, lanes), BF16),
        ]
        + group_scratch(seqs, dps, (local, 128), BF16)
        + group_scratch(seqs, dps, (8, 128), F32)
        + group_scratch(seqs, dps, (padded, spread), BF16)
        + [
            pltpu.VMEM((padded, spread), F32),
            pltpu.VMEM((8, width), F32),
            pltpu.VMEM((8, 128), F32),
            pltpu.VMEM((8, 128), F32),
            pltpu.VMEM((8, 128), F32),
            pltpu.VMEM((groups - 1, 8, 128), F32),
            pltpu.VMEM((4, padded, spread), F32),
            pltpu.VMEM((4, 8, 128), F32),
            DMA((2,)),
            DMA((2,)),
            DMA((2, per)),
            DMA((2, per)),
            DMA((per, PIECES)),
            DMA((per, PIECES)),
            DMA((2,)),
            DMA((2,)),
            DMA(()),
            DMA(()),
            DMA((groups - 1,)),
            DMA((groups - 1,)),
            DMA((3,)),
            DMA((3,)),
            DMA((3,)),
            DMA((3,)),
            DMA((4,)),
        ]
        + home_sems(per, seqs) * 2
        + group_sems(seqs, dps) * 5,
        compiler_params=params(collective_id=4),
        name="back",
    )(
        result, hidden_grad, own_tok, heads_all, wo_all, split, probs, attn_input, weights, weights_far, gains, router, gain_f
    )


def settle_kernel(count, *refs):
    large, (w, router, wo, gain, bias) = refs[:count], refs[count : count + 5]
    refs = refs[count + 5 :]
    large_out, (wq_out, wk_out, wv_out, wo_out, router_out, gain_a, gain_f, bias_out) = refs[:count], refs[count : count + 8]
    refs = refs[count + 8 :]
    held, sems = refs[:count], refs[count]
    copies = []
    for n in range(count):
        half = large[n].shape[0] // 2
        for k in range(2):
            part = pl.ds(k * half, half)
            come = pltpu.make_async_copy(large[n].at[part], held[n].at[part], sems.at[0, n, k])
            go = pltpu.make_async_copy(held[n].at[part], large_out[n].at[part], sems.at[1, n, k])
            come.start()
            copies.append((come, go))
    shard, local = wq_out.shape
    for n, ref in enumerate((wq_out, wk_out, wv_out)):
        ref[...] = w[:shard, n * local : (n + 1) * local]
    wo_out[...] = wo[:, :shard]
    router_out[...] = router[...]
    gain_a[...] = gain[0:1, :shard]
    gain_f[...] = gain[1:2, :shard]
    bias_out[...] = bias[: bias_out.shape[0], : bias_out.shape[1]]
    for come, go in copies:
        come.wait()
        go.start()
    for _, go in copies:
        go.wait()


def settle(large, small, shapes):
    count = len(large)
    return pl.pallas_call(
        functools.partial(settle_kernel, count),
        out_shape=tuple(jax.ShapeDtypeStruct(x.shape, x.dtype) for x in large)
        + tuple(jax.ShapeDtypeStruct(shape, F32) for shape in shapes),
        in_specs=[ANY] * count + [VMEM] * len(small),
        out_specs=[ANY] * count + [VMEM] * len(shapes),
        scratch_shapes=[pltpu.VMEM(x.shape, x.dtype) for x in large] + [DMA((2, count, 2))],
        compiler_params=pltpu.CompilerParams(vmem_limit_bytes=60 * 2**20),
        name="settle",
    )(*large, *small)


def up_to(value, unit):
    return -(-value // unit) * unit


def body(
    tokens,
    lengths,
    expert_ids,
    attention_gain,
    query_weight,
    key_weight,
    value_weight,
    output_weight,
    position_bias,
    feedforward_gain,
    router_weight,
    expert_up,
    expert_down,
    cotangent,
):
    seqs, dps = lax.axis_size("seq"), lax.axis_size("dp")
    groups = seqs * dps
    seq_local, span, width = tokens.shape
    per = seq_local // seqs
    local_width = query_weight.shape[1]
    bucket_count, heads = position_bias.shape
    experts = router_weight.shape[1]
    shard = query_weight.shape[0]
    capacity = max(2, (5 * span + 4 * experts - 1) // (4 * experts))
    ids = expert_ids.reshape(seq_local, span)
    attn_input, weights, weights_far, split, probs, heads_all, own_tok, cot_own, out_weight, gains, ids_all = front(
        tokens,
        cotangent,
        query_weight,
        key_weight,
        value_weight,
        output_weight,
        router_weight.T,
        attention_gain[None, :],
        feedforward_gain[None, :],
        ids,
        position_bias.T,
        lengths,
        seqs,
        dps,
    )
    result, hidden_grad, router_grad, gain_two_grad, up_grad, down_grad = run_experts(
        heads_all,
        own_tok,
        out_weight,
        weights,
        gains,
        cot_own,
        ids_all,
        expert_up,
        expert_down,
        seqs,
        dps,
        per * capacity,
        capacity,
    )
    output, tokens_grad, w_sum, small_sum, wo_sum, gain_sum, bias_sum = back_pass(
        result,
        hidden_grad,
        own_tok,
        heads_all,
        out_weight,
        split,
        probs,
        attn_input,
        weights,
        weights_far,
        gains,
        router_grad,
        gain_two_grad,
        seqs,
        dps,
    )
    at = 3 * local_width % 128
    router_t = small_sum[:shard, at : at + experts].T
    output, tokens_grad, up_grad, down_grad, *small = settle(
        (output, tokens_grad, up_grad, down_grad),
        (w_sum, router_t, wo_sum, gain_sum, bias_sum),
        ((shard, local_width),) * 3
        + ((local_width, shard), (experts, shard), (1, shard), (1, shard), (heads, bucket_count)),
    )
    return (
        output,
        tokens_grad,
        small[5][0],
        small[0],
        small[1],
        small[2],
        small[3],
        small[7].T,
        small[6][0],
        small[4].T,
        up_grad,
        down_grad,
    )


def solution(mesh):
    placed = (
        P("dp", "seq", None),
        P("dp"),
        P("dp", "seq", None),
        P(("seq", "dp")),
        P(("seq", "dp"), "head"),
        P(("seq", "dp"), "head"),
        P(("seq", "dp"), "head"),
        P("head", ("seq", "dp")),
        P(None, "head"),
        P(("seq", "dp")),
        P(("seq", "dp"), None),
        P(("seq", "dp"), None, "head"),
        P(("seq", "dp"), "head", None),
        P("dp", "seq", None),
    )
    return jax.shard_map(
        body,
        mesh=mesh,
        in_specs=placed,
        out_specs=(
            P("dp", "seq", None),
            P("dp", "seq", None),
            P(("seq", "dp")),
            P(("seq", "dp"), "head"),
            P(("seq", "dp"), "head"),
            P(("seq", "dp"), "head"),
            P("head", ("seq", "dp")),
            P(None, "head"),
            P(("seq", "dp")),
            P(("seq", "dp"), None),
            P(("seq", "dp"), None, "head"),
            P(("seq", "dp"), "head", None),
        ),
        check_vma=False,
    )
```

```python
import functools

import jax
import jax.numpy as jnp
import numpy as np
from jax import lax
from jax.experimental import pallas as pl
from jax.experimental.pallas import tpu as pltpu
from jax.sharding import PartitionSpec as P

HEAD_DIM = 64
EPS = 1e-06
bucket_edges = np.array([1, 2, 3, 4, 5, 6, 7, 8, 12, 16, 23, 32, 46, 64, 91], np.int32)
ANY = pl.BlockSpec(memory_space=pl.ANY)
VMEM = pl.BlockSpec(memory_space=pltpu.VMEM)
MESH = pl.DeviceIdType.MESH
DMA = pltpu.SemaphoreType.DMA
F32 = jnp.float32
BF16 = jnp.bfloat16


def bucket_of(offset, bucket_count):
    distance = jnp.abs(offset)
    magnitude = jnp.zeros_like(offset)
    for edge in bucket_edges:
        magnitude = magnitude + (distance >= int(edge)).astype(jnp.int32)
    return magnitude + bucket_count // 2 * (offset > 0).astype(jnp.int32)


def send(src, dst, send_sem, recv_sem, **device):
    copy = pltpu.make_async_remote_copy(
        src_ref=src,
        dst_ref=dst,
        send_sem=send_sem,
        recv_sem=recv_sem,
        device_id=device,
        device_id_type=MESH,
    )
    copy.start()
    return copy


def arrived(ref, recv_sem):
    pltpu.make_async_copy(ref, ref, recv_sem).wait()


def greet(devices):
    barrier = pltpu.get_barrier_semaphore()
    for device in devices:
        pl.semaphore_signal(barrier, inc=1, device_id=device, device_id_type=MESH)
    pl.semaphore_wait(barrier, len(devices))


def mod(value, size):
    return lax.rem(value + 4 * size, size)


class Place:
    def __init__(self, seqs, dps):
        self.h, self.s, self.d = lax.axis_index("head"), lax.axis_index("seq"), lax.axis_index("dp")
        self.seqs, self.dps = seqs, dps
        self.x, self.c = lax.div(self.h, 2), lax.rem(self.h, 2)
        self.near = self.h + 1 - 2 * self.c
        self.across = mod(self.h + 2, 4)
        self.near_across = lax.rem(self.across, 2) * -2 + self.across + 1

    def seq_peers(self):
        return [{"seq": mod(self.s + i, self.seqs)} for i in range(1, self.seqs)]

    def dp_peers(self):
        return [{"dp": mod(self.d + i, self.dps)} for i in range(1, self.dps)]

    def head_pair(self):
        return [{"head": self.near}, {"head": self.across}]

    def group_peers(self):
        return [
            {"seq": mod(self.s + i, self.seqs), "dp": mod(self.d + j, self.dps)}
            for i in range(self.seqs)
            for j in range(self.dps)
            if i or j
        ]

    def block(self, j, core=None):
        return lax.rem((self.c if core is None else core) + self.s, 2) + 2 * j


def params(**more):
    return pltpu.CompilerParams(has_side_effects=True, vmem_limit_bytes=60 * 2**20, **more)


def gather_groups(me, own, whole, z_send, z_recv, dp_send, dp_recv, far=None, far_send=None, far_recv=None):
    s, d, seqs, dps = me.s, me.d, me.seqs, me.dps

    def spread(src, source):
        for i in range(1, dps):
            send(
                src,
                whole.at[source, d],
                dp_send.at[i - 1, source],
                dp_recv.at[i - 1, source],
                dp=mod(d + i, dps),
            )

    def onward(src, source, dp):
        if far is not None:
            send(src, far.at[source, dp], far_send.at[source, dp], far_recv.at[source, dp], head=me.across)

    def start():
        for i in range(1, seqs):
            send(own, whole.at[s, d], z_send.at[i - 1], z_recv.at[i - 1], seq=mod(s + i, seqs))
        spread(own, s)
        onward(own, s, d)

    def relay(i):
        source = mod(s - i, seqs)
        here = whole.at[source, d]
        arrived(here, z_recv.at[i - 1])
        spread(here, source)
        onward(here, source, d)

    def finish():
        for i in range(1, dps):
            for source in range(seqs):
                there = mod(d - i, dps)
                arrived(whole.at[source, there], dp_recv.at[i - 1, source])
                onward(whole.at[source, there], source, there)
                pltpu.make_async_copy(own, own, dp_send.at[i - 1, source]).wait()
        for i in range(1, seqs):
            pltpu.make_async_copy(own, own, z_send.at[i - 1]).wait()

    def take_far():
        for source in range(seqs):
            for dp in range(dps):
                arrived(far.at[source, dp], far_recv.at[source, dp])

    def finish_far():
        for source in range(seqs):
            for dp in range(dps):
                pltpu.make_async_copy(own, own, far_send.at[source, dp]).wait()

    return start, relay, finish, take_far, finish_far


def gather_sems(seqs, dps):
    return [
        DMA((seqs - 1,)),
        DMA((seqs - 1,)),
        DMA((max(1, dps - 1), seqs)),
        DMA((max(1, dps - 1), seqs)),
    ]


def spread_hot(at, shard, width):
    row = lax.broadcasted_iota(jnp.int32, (128, width), 0)
    column = lax.broadcasted_iota(jnp.int32, (128, width), 1)
    return ((column == row + at) & (row < shard)).astype(BF16)


def squeeze_hot(shard, padded, rows, count):
    row = lax.broadcasted_iota(jnp.int32, (rows, count * padded), 0)
    column = lax.broadcasted_iota(jnp.int32, (rows, count * padded), 1)
    inside = lax.rem(column, padded)
    return ((lax.div(column, padded) * shard + inside == row) & (inside < shard)).astype(BF16)


def front_kernel(
    seqs, dps, heads,
    tok, cot, wq, wk, wv, wo, router, gain_a, gain_f, ids_own, table, lengths,
    attn_input_out, weights_out, far_out, split_out, probs, heads_all, own_tok, cot_own, wo_all, gains, ids_all,
    attn_input, weights, weights_far, split, tok_all, pack, pack_all, far_all, wo_pad, wo_parts, tile, tile_all, table_own, table_far,
    ext, slot, out,
    p_sem, ls, os, z_send, z_recv, h_send, h_recv, c_send, c_recv, a_send, a_recv, w_send, w_recv, i_send, i_recv,
    f_send, f_recv, t_sem, *line
):
    me = Place(seqs, dps)
    h, s, d, x, c = me.h, me.s, me.d, me.x, me.c
    blocks, span, width = tok_all.shape
    per = own_tok.shape[0]
    length = blocks * span
    shard, local = wq.shape
    groups = seqs * dps
    experts = router.shape[0]
    half = span // 2
    own_half = pl.ds(pl.multiple_of(c * half, half), half)
    other_half = pl.ds(pl.multiple_of((1 - c) * half, half), half)
    pack[...] = jnp.zeros_like(pack)
    split[...] = jnp.zeros_like(split)
    for n, ref in enumerate((wq, wk, wv)):
        pack[:shard, n * local : (n + 1) * local] = ref[...]
    same = lax.broadcasted_iota(jnp.int32, (experts, experts), 0) == lax.broadcasted_iota(jnp.int32, (experts, experts), 1)
    pack[:shard, 3 * local : 3 * local + experts] = contract(router[...], same.astype(BF16), 0, 0).astype(BF16)
    wo_pad[...] = jnp.zeros_like(wo_pad)
    wo_pad[:, :shard] = wo[...]
    tile[...] = jnp.zeros_like(tile)
    tile[0:1, :shard] = gain_a[...].astype(F32)
    tile[1:2, :shard] = gain_f[...].astype(F32)
    buckets = table.shape[1]
    table_own[...] = jnp.zeros_like(table_own)
    table_own[:heads, :buckets] = table[...].astype(F32)
    own_copies = [
        pltpu.make_async_copy(pack, pack_all.at[s, d], ls.at[0]),
        pltpu.make_async_copy(tile, tile_all.at[s, d], ls.at[1]),
        pltpu.make_async_copy(wo_pad, wo_parts.at[s, d], ls.at[2]),
        pltpu.make_async_copy(ids_own, ids_all.at[s], ls.at[3]),
        pltpu.make_async_copy(tok.at[per * s + x], tok_all.at[s], ls.at[4]),
    ]
    for copy in own_copies:
        copy.start()

    @pl.when(c == 0)
    def _():
        pltpu.make_async_copy(cot.at[per * s + x], cot_own.at[lax.div(s, 2)], ls.at[5]).start()

    greet(
        me.seq_peers()
        + [{"head": me.near} | peer for peer in me.seq_peers()]
        + me.dp_peers()
        + [{"head": mod(h + i, 4)} for i in range(1, 4)]
    )
    packs = gather_groups(me, pack, pack_all, *line[0:4], far_all, f_send, f_recv)
    tiles = gather_groups(me, tile, tile_all, *line[4:8])
    outs = gather_groups(me, wo_pad, wo_parts, *line[8:12])
    packs[0]()
    tiles[0]()
    to_table = send(table_own, table_far, t_sem.at[0], t_sem.at[1], head=me.across)
    for i in range(1, seqs):
        send(ids_own, ids_all.at[s], i_send.at[i - 1], i_recv.at[i - 1], seq=mod(s + i, seqs))
    for i in range(1, seqs):
        to = mod(s + i, seqs)
        send(tok.at[per * to + x, own_half], tok_all.at[s, own_half], z_send.at[i - 1], z_recv.at[i - 1], seq=to)

    def send_cotangent():
        for i in range(1, seqs):
            to = mod(s + i, seqs)
            target = jnp.where(lax.rem(s + to, 2) == c, h, me.near)
            j = lax.div(s, 2)
            send(
                cot.at[per * to + x, own_half],
                cot_own.at[j, own_half],
                c_send.at[i - 1],
                c_recv.at[j, c],
                head=target,
                seq=to,
            )

    def build_bias(rows):
        turn = lax.broadcasted_iota(jnp.int32, (128, 4 * span), 1)
        bucket = bucket_of(jnp.where(turn < 3 * span, turn, turn - 4 * span) - span, buckets)
        hot = (bucket == lax.broadcasted_iota(jnp.int32, (128, 4 * span), 0)).astype(BF16)
        bias_rows = jnp.dot(rows[...].astype(BF16), hot, preferred_element_type=F32)
        for head in range(heads):
            row = bias_rows[head : head + 1]
            rolled = pltpu.roll(jnp.broadcast_to(row, (span, 4 * span)), 0, 1, stride=1, stride_axis=0)
            ext[head, :, 2 * span : 5 * span] = rolled[:, : 3 * span]
            ext[head, :, : 2 * span] = jnp.broadcast_to(row[:, 0:1], (span, 2 * span))
            ext[head, :, 5 * span :] = jnp.broadcast_to(row[:, 3 * span - 1 : 3 * span], (span, 2 * span))

    def whole_weights(parts, into):
        if shard % 16:
            whole = parts[...].reshape(groups * pack.shape[0], pack.shape[1])
            hot = squeeze_hot(shard, pack.shape[0], width, groups)
            into[...] = jnp.dot(hot, whole, preferred_element_type=F32).astype(BF16)
        else:
            into[...] = parts[...].reshape(width, pack.shape[1])

    def assemble():
        whole_weights(pack_all, weights)
        row = jnp.zeros((8, width), F32)
        for g in range(groups):
            piece = tile_all[g // dps, g % dps].astype(BF16)
            row = row + jnp.dot(piece, spread_hot(g * shard, shard, width), preferred_element_type=F32)
        gains[...] = row

    def project(group, block):
        rows = pl.ds(pl.multiple_of(block * span, span), span)
        if group == 0:
            v = tok_all[block].astype(F32)
            normed = v * lax.rsqrt(jnp.mean(v * v, axis=-1, keepdims=True) + EPS) * gains[0:1, :]
            attn_input[rows, :] = normed.astype(BF16)
        which = weights if group == 0 else weights_far
        parts = jnp.dot(attn_input[rows, :], which[...], preferred_element_type=F32).astype(BF16)
        for n in range(3 * heads):
            split[group, n, rows, :HEAD_DIM] = parts[:, n * HEAD_DIM : (n + 1) * HEAD_DIM]

    build_bias(table_own)
    for i in range(1, seqs):
        packs[1](i)
        tiles[1](i)
    far_first = [i for i in range(1, seqs) if i != 2] + [2]

    def pass_own(i):
        here = tok_all.at[mod(s - i, seqs), own_half]
        arrived(here, z_recv.at[i - 1])
        send(here, here, h_send.at[i - 1], h_recv.at[i - 1], head=me.near)

    for copy in own_copies:
        copy.wait()
    packs[2]()
    tiles[2]()
    assemble()
    project(0, s)
    for i in far_first:
        pass_own(i)
    outs[0]()
    for i in far_first:
        source = mod(s - i, seqs)
        arrived(tok_all.at[source, other_half], h_recv.at[i - 1])
        project(0, source)
    kept = [
        pltpu.make_async_copy(attn_input, attn_input_out, ls.at[6]),
        pltpu.make_async_copy(split.at[0], split_out.at[0], ls.at[7]),
        pltpu.make_async_copy(weights, weights_out, ls.at[8]),
    ]
    kept += [pltpu.make_async_copy(tok_all.at[me.block(j)], own_tok.at[j], ls.at[9 + j]) for j in range(per)]
    for copy in kept:
        copy.start()
    late = [
        pltpu.make_async_copy(split.at[1], split_out.at[1], ls.at[9 + per]),
        pltpu.make_async_copy(weights_far, far_out, ls.at[10 + per]),
    ]

    def second_group():
        packs[3]()
        whole_weights(far_all, weights_far)
        arrived(table_far, t_sem.at[1])
        build_bias(table_far)

        @pl.loop(0, blocks)
        def _(block):
            project(1, block)

        for copy in late:
            copy.start()

    @pl.loop(0, 2 * blocks)
    def _(unit):
        group, block = lax.div(unit, blocks), lax.rem(unit, blocks)
        rows = pl.ds(pl.multiple_of(block * span, span), span)
        turn = lax.rem(unit, 2)

        @pl.when(unit == blocks)
        def _():
            second_group()

        @pl.when(unit >= 2)
        def _():
            pltpu.make_async_copy(slot.at[turn], slot.at[turn], p_sem.at[turn]).wait()

        window = pl.ds(pl.multiple_of((blocks - 1 - block) * span, span), length)
        valid = lax.broadcasted_iota(jnp.int32, (1, length), 1) < lengths[per * s + x]
        for head in range(heads):
            query = split[group, head, rows, :HEAD_DIM]
            key, value = split[group, heads + head, :, :HEAD_DIM], split[group, 2 * heads + head, :, :HEAD_DIM]
            scores = lax.dot_general(query, key, (((1,), (1,)), ((), ())), preferred_element_type=F32)
            scores = jnp.where(valid, scores + ext[head, :, window], -1e30)
            top = jnp.max(scores, axis=-1, keepdims=True)
            grown = jnp.exp(scores - top)
            total = jnp.sum(grown, axis=-1, keepdims=True)
            part = (grown * (1.0 / total)).astype(BF16)
            slot[turn, head] = part
            mixed = jnp.dot(part, value, preferred_element_type=F32)
            out[unit, :, head * HEAD_DIM : (head + 1) * HEAD_DIM] = mixed.astype(BF16)
        pltpu.make_async_copy(slot.at[turn], probs.at[group, :, rows, :], p_sem.at[turn]).start()
        source = jnp.where(group == 0, h, me.across)
        j = lax.div(block, 2)

        @pl.when(lax.rem(block + s, 2) == c)
        def _():
            pltpu.make_async_copy(out.at[unit], heads_all.at[source, j], os.at[group, j]).start()

        @pl.when(lax.rem(block + s, 2) != c)
        def _():
            send(out.at[unit], heads_all.at[source, j], a_send.at[group, j], a_recv.at[group, j], head=me.near)

        @pl.when(unit == 0)
        def _():
            for i in range(1, seqs):
                outs[1](i)
            send_cotangent()

        @pl.when(unit == 2)
        def _():
            outs[2]()
            total = jnp.zeros((local, width), F32)
            for g in range(groups):
                total = total + jnp.dot(
                    wo_parts[g // dps, g % dps], spread_hot(g * shard, shard, width), preferred_element_type=F32
                )
            wo_all[h] = total.astype(BF16)
            send(wo_all.at[h], wo_all.at[h], w_send.at[0], w_recv.at[0], head=me.across)
            send(wo_all.at[h], wo_all.at[h], w_send.at[1], w_recv.at[1], head=me.near)

    there = wo_all.at[me.across]
    arrived(there, w_recv.at[0])
    send(there, there, w_send.at[2], w_recv.at[2], head=me.near)
    for copy in kept + late:
        copy.wait()
    for turn in range(2):
        pltpu.make_async_copy(slot.at[turn], slot.at[turn], p_sem.at[turn]).wait()
    packs[4]()
    to_table.wait_send()
    for j in range(per):
        block = me.block(j)

        @pl.when(block == s)
        def _():
            pltpu.make_async_copy(cot_own.at[j], cot_own.at[j], ls.at[5]).wait()

        @pl.when(block != s)
        def _():
            for part in range(2):
                arrived(cot_own.at[j, pl.ds(part * half, half)], c_recv.at[j, part])

        for group in range(2):
            pltpu.make_async_copy(out.at[0], heads_all.at[h, j], os.at[group, j]).wait()
            pltpu.make_async_copy(out.at[0], out.at[0], a_send.at[group, j]).wait()
            source = me.near if group == 0 else me.near_across
            arrived(heads_all.at[source, j], a_recv.at[group, j])

    for i in range(1, seqs):
        rows = tok.at[0, pl.ds(0, half)]
        for sem in (z_send, h_send, c_send):
            pltpu.make_async_copy(rows, rows, sem.at[i - 1]).wait()
        pltpu.make_async_copy(ids_own, ids_own, i_send.at[i - 1]).wait()
        arrived(ids_all.at[mod(s - i, seqs)], i_recv.at[i - 1])
    for k in range(3):
        pltpu.make_async_copy(wo_all.at[h], wo_all.at[h], w_send.at[k]).wait()
    arrived(wo_all.at[me.near], w_recv.at[1])
    arrived(wo_all.at[me.near_across], w_recv.at[2])


def front(tokens, cot, wq, wk, wv, wo, router, gain_a, gain_f, ids, table, lengths, seqs, dps):
    seq_local, span, width = tokens.shape
    per = seq_local // seqs
    length = seqs * span
    shard, local = wq.shape
    heads = local // HEAD_DIM
    lanes = up_to(3 * local + router.shape[0], 128)
    padded = up_to(shard, 16)
    smem = pl.BlockSpec(memory_space=pltpu.SMEM)
    return pl.pallas_call(
        functools.partial(front_kernel, seqs, dps, heads),
        out_shape=(
            jax.ShapeDtypeStruct((length, width), BF16),
            jax.ShapeDtypeStruct((width, lanes), BF16),
            jax.ShapeDtypeStruct((width, lanes), BF16),
            jax.ShapeDtypeStruct((2, 3 * heads, length, 128), BF16),
            jax.ShapeDtypeStruct((2, heads, length, length), BF16),
            jax.ShapeDtypeStruct((4, per, span, local), BF16),
            jax.ShapeDtypeStruct((per, span, width), BF16),
            jax.ShapeDtypeStruct((per, span, width), BF16),
            jax.ShapeDtypeStruct((4, local, width), BF16),
            jax.ShapeDtypeStruct((8, width), F32),
            jax.ShapeDtypeStruct((seqs,) + ids.shape[:2], jnp.int32),
        ),
        in_specs=[ANY] * 2 + [VMEM] * 7 + [ANY, VMEM, smem],
        out_specs=[ANY] * 8 + [VMEM] * 2 + [ANY],
        scratch_shapes=[
            pltpu.VMEM((length, width), BF16),
            pltpu.VMEM((width, lanes), BF16),
            pltpu.VMEM((width, lanes), BF16),
            pltpu.VMEM((2, 3 * heads, length, 128), BF16),
            pltpu.VMEM((seqs, span, width), BF16),
            pltpu.VMEM((padded, lanes), BF16),
            pltpu.VMEM((seqs, dps, padded, lanes), BF16),
            pltpu.VMEM((seqs, dps, padded, lanes), BF16),
            pltpu.VMEM((local, 128), BF16),
            pltpu.VMEM((seqs, dps, local, 128), BF16),
            pltpu.VMEM((8, 128), F32),
            pltpu.VMEM((seqs, dps, 8, 128), F32),
            pltpu.VMEM((8, 128), F32),
            pltpu.VMEM((8, 128), F32),
            pltpu.VMEM((heads, span, 7 * span), F32),
            pltpu.VMEM((2, heads, span, length), BF16),
            pltpu.VMEM((2 * seqs, span, local), BF16),
            DMA((2,)),
            DMA((11 + per,)),
            DMA((2, per)),
            DMA((seqs - 1,)),
            DMA((seqs - 1,)),
            DMA((seqs - 1,)),
            DMA((seqs - 1,)),
            DMA((seqs - 1,)),
            DMA((per, 2)),
            DMA((2, per)),
            DMA((2, per)),
            DMA((3,)),
            DMA((3,)),
            DMA((seqs - 1,)),
            DMA((seqs - 1,)),
            DMA((seqs, dps)),
            DMA((seqs, dps)),
            DMA((2,)),
        ]
        + gather_sems(seqs, dps) * 3,
        compiler_params=params(collective_id=0),
        name="front",
    )(tokens, cot, wq, wk, wv, wo, router, gain_a, gain_f, ids, table, lengths)


def expert_windows(exp_local, per_expert):
    return [(e * per_expert // 16 * 16, up_to((e + 1) * per_expert, 16)) for e in range(exp_local)]


def contract(a, b, over_a, over_b):
    return lax.dot_general(a, b, (((over_a,), (over_b,)), ((), ())), preferred_element_type=F32)


AHEAD = 3
GELU_A, GELU_B = float(np.sqrt(2.0 / np.pi)), 0.044715


def experts_kernel(
    seqs, dps, per_expert, capacity, local,
    heads_all, own_tok, wo_all, weights, gains, cot_own, ids_all, up_in, down_in,
    result, hidden_grad, router_grad, gain_grad, up_out, down_out,
    up, down, up_grad, down_grad, rows, summed, place_hot, place_turned, hidden_ref, ffn_ref, router_ref, gate_ref, hot_ref, taken, near, far,
    ls, g_send, g_recv, h_send, h_recv, n_send, n_recv, x_send, x_recv, r_send, r_recv
):
    me = Place(seqs, dps)
    h, s, d = me.h, me.s, me.d
    groups, _, height, width = rows.shape
    exp_local = up.shape[0]
    windows = expert_windows(exp_local, per_expert)
    me_group = s * dps + d

    def away(n):
        return lax.div(n, dps), lax.rem(n, dps)

    def ahead(n):
        i, j = away(n)
        return mod(s + i, seqs), mod(d + j, dps)

    def behind(n):
        i, j = away(n)
        return mod(s - i, seqs), mod(d - j, dps)

    per, span, _ = own_tok.shape
    loads = [pltpu.make_async_copy(up_in, up, ls.at[1]), pltpu.make_async_copy(down_in, down, ls.at[2])]
    for copy in loads:
        copy.start()
    spots = groups * height
    first_lane = 3 * local // 128 * 128
    spread = weights.shape[1] - first_lane
    shift = 3 * local - first_lane
    experts = groups * exp_local
    router = weights[:, first_lane:]
    earlier = lax.broadcasted_iota(jnp.int32, (span, span), 0) < lax.broadcasted_iota(jnp.int32, (span, span), 1)
    earlier = earlier.astype(BF16)
    lane = lax.broadcasted_iota(jnp.int32, (span, spread), 1)
    is_expert = (lane >= shift) & (lane < shift + experts)

    def tokens_in(j):
        total = own_tok[j].astype(F32)
        for q in range(4):
            total = total + jnp.dot(heads_all[q, j], wo_all[q], preferred_element_type=F32)
        hidden_ref[j] = total
        inverse = lax.rsqrt(jnp.mean(total * total, axis=-1, keepdims=True) + EPS)
        ffn = (total * inverse * gains[1:2, :]).astype(BF16)
        ffn_ref[j] = ffn
        logits = jnp.where(is_expert, jnp.dot(ffn, router, preferred_element_type=F32), -1e30)
        grown = jnp.exp(logits - jnp.max(logits, axis=-1, keepdims=True))
        router_probs = grown / jnp.sum(grown, axis=-1, keepdims=True)
        router_ref[j] = router_probs
        ids = ids_all[me.block(j), pl.ds(per * s + me.x, 1), :]
        own = lax.broadcasted_iota(jnp.int32, (spread, span), 0) == ids + shift
        own_low = own.astype(BF16)
        before = jnp.dot(own_low, earlier, preferred_element_type=F32)
        slot = jnp.sum(jnp.where(own, before, 0.0), axis=0, keepdims=True).astype(jnp.int32)
        same = lax.broadcasted_iota(jnp.int32, (spread, spread), 0) == lax.broadcasted_iota(jnp.int32, (spread, spread), 1)
        hot = contract(own_low, same.astype(BF16), 0, 0)
        hot_ref[j] = hot
        gate = jnp.sum(router_probs * hot, axis=-1, keepdims=True)
        gate_ref[j] = gate
        group = lax.div(ids, exp_local)
        place = group * height + ((ids - group * exp_local) * per + j) * capacity + slot
        spot = lax.broadcasted_iota(jnp.int32, (spots, span), 0)
        place_hot[j] = (spot == place).astype(BF16)
        return ffn, (gate * cot_own[j].astype(F32)).astype(BF16)

    made = [tokens_in(j) for j in range(per)]
    for part in range(2):
        total = jnp.zeros((spots, width), F32)
        for j in range(per):
            total = total + jnp.dot(place_hot[j], made[j][part], preferred_element_type=F32)
        total = total.astype(BF16)
        for g in range(groups):
            rows[g, part] = total[g * height : (g + 1) * height, :]
    up_grad[...] = jnp.zeros_like(up_grad)
    down_grad[...] = jnp.zeros_like(down_grad)
    greet(me.group_peers() + me.head_pair())
    pltpu.make_async_copy(rows.at[me_group], taken.at[h, 0], ls.at[0]).start()

    def send_out(n):
        to_s, to_d = ahead(n)
        send(rows.at[to_s * dps + to_d], taken.at[h, n], g_send.at[n], g_recv.at[n], seq=to_s, dp=to_d)

    for n in range(1, min(AHEAD + 1, groups)):
        send_out(n)

    def gather_own(n):
        here = taken.at[h, n]

        @pl.when(n == 0)
        def _():
            pltpu.make_async_copy(here, here, ls.at[0]).wait()

        @pl.when(n > 0)
        def _():
            arrived(here, g_recv.at[n])

        send(here, here, h_send.at[0, n], h_recv.at[0, n], head=me.across)
        send(here, here, h_send.at[1, n], h_recv.at[1, n], head=me.near)

    def gather_across(n):
        there = taken.at[me.across, n]
        arrived(there, h_recv.at[0, n])
        send(there, there, h_send.at[2, n], h_recv.at[2, n], head=me.near)

    def compute(n):
        @pl.when(n == first_turn)
        def _():
            for copy in loads:
                copy.wait()

        arrived(taken.at[me.near, n], h_recv.at[1, n])
        arrived(taken.at[me.near_across, n], h_recv.at[2, n])
        for k in range(3):
            pltpu.make_async_copy(taken.at[h, n], taken.at[h, n], h_send.at[k, n]).wait()
        kept = []
        for e, (low, high) in enumerate(windows):
            size = high - low
            at = lax.broadcasted_iota(jnp.int32, (4 * size, width), 0)
            slot = lax.rem(at, size) + low
            inside = (slot >= e * per_expert) & (slot < (e + 1) * per_expert)

            def mine(part):
                block = jnp.concatenate([taken[q, n, part, low:high, :] for q in range(4)], axis=0)
                return jnp.where(inside, block.astype(F32), 0.0).astype(BF16)

            x, g = mine(0), mine(1)
            pre = jnp.dot(x, up[e], preferred_element_type=F32)
            square = pre * pre
            bent = jnp.tanh(GELU_A * pre * (1.0 + GELU_B * square))
            act = (0.5 * pre * (1.0 + bent)).astype(BF16)
            slope = 0.5 * (1.0 + bent) + 0.5 * pre * (1.0 - bent * bent) * (GELU_A * (1.0 + 3.0 * GELU_B * square))
            out = jnp.dot(act, down[e], preferred_element_type=F32).astype(BF16)
            act_grad = contract(g, down[e], 1, 1)
            pre_grad = (act_grad * slope).astype(BF16)
            back = contract(pre_grad, up[e], 1, 1).astype(BF16)
            kept.append((x, g, act, pre_grad, out, back))
        for q in range(4):
            for part in range(2):
                for tile in range(0, height, 16):
                    total = None
                    for (low, high), made in zip(windows, kept):
                        if low <= tile < high:
                            begin = q * (high - low) + tile - low
                            piece = made[4 + part][begin : begin + 16, :]
                            total = piece if total is None else total + piece
                    if total is not None:
                        taken[q, n, part, tile : tile + 16, :] = total
        send(taken.at[me.near_across, n], near.at[0, n], n_send.at[0, n], n_recv.at[0, n], head=me.near)
        send(taken.at[me.near, n], near.at[1, n], n_send.at[1, n], n_recv.at[1, n], head=me.near)
        for e in range(exp_local):
            x, g, act, pre_grad, _, _ = kept[e]
            up_grad[e] += contract(x, pre_grad, 0, 0)
            down_grad[e] += contract(act, g, 0, 0)

    def add_near(n):
        arrived(near.at[0, n], n_recv.at[0, n])
        both = taken[me.across, n].astype(F32) + near[0, n].astype(F32)
        taken[me.across, n] = both.astype(BF16)
        send(taken.at[me.across, n], far.at[n], x_send.at[n], x_recv.at[n], head=me.across)

    def send_back(n):
        arrived(near.at[1, n], n_recv.at[1, n])
        arrived(far.at[n], x_recv.at[n])
        total = taken[h, n].astype(F32) + near[1, n].astype(F32) + far[n].astype(F32)
        taken[h, n] = total.astype(BF16)
        to_s, to_d = behind(n)

        @pl.when(n == 0)
        def _():
            pltpu.make_async_copy(taken.at[h, n], summed.at[:, me_group], r_send.at[n]).start()

        @pl.when(n > 0)
        def _():
            send(taken.at[h, n], summed.at[:, me_group], r_send.at[n], r_recv.at[n], seq=to_s, dp=to_d)

    first_turn = 1 % groups
    gather_own(0)
    stages = (send_back, add_near, compute, gather_across, gather_own)

    @pl.loop(0, groups + len(stages) - 1)
    def _(step):
        @pl.when((step > 0) & (step + AHEAD < groups))
        def _():
            send_out(step + AHEAD)

        for j in range(per):

            @pl.when(step == 2 + j)
            def _():
                place_turned[j] = place_hot[j].astype(F32).T.astype(BF16)

        for k, stage in enumerate(stages):
            turn = step - (len(stages) - 1 - k)
            last = groups - 1 if stage is gather_own else groups

            @pl.when((turn >= 0) & (turn < last))
            def _():
                stage(lax.rem(turn + 1, groups))

    up[...] = up_grad[...].astype(BF16)
    down[...] = down_grad[...].astype(BF16)
    stores = [
        pltpu.make_async_copy(up, up_out, ls.at[1]),
        pltpu.make_async_copy(down, down_out, ls.at[2]),
    ]
    for copy in stores:
        copy.start()

    @pl.loop(0, groups)
    def _(n):
        here = taken.at[h, n]
        for k in range(2):
            pltpu.make_async_copy(here, here, n_send.at[k, n]).wait()
        pltpu.make_async_copy(here, here, x_send.at[n]).wait()
        pltpu.make_async_copy(here, here, r_send.at[n]).wait()

        @pl.when(n > 0)
        def _():
            pltpu.make_async_copy(here, here, g_send.at[n]).wait()
            from_s, from_d = ahead(n)
            arrived(summed.at[:, from_s * dps + from_d], r_recv.at[n])

    def tokens_out(j):
        hidden, gate, router_probs, hot = hidden_ref[j], gate_ref[j], router_ref[j], hot_ref[j]
        grad = cot_own[j].astype(F32)
        token_out = jnp.dot(place_turned[j], summed[0].reshape(spots, width), preferred_element_type=F32)
        input_grad = jnp.dot(place_turned[j], summed[1].reshape(spots, width), preferred_element_type=F32)
        result[j] = (hidden + gate * token_out).astype(BF16)
        gate_grad = jnp.sum(grad * token_out, axis=-1, keepdims=True)
        logit_low = (router_probs * (gate_grad * hot - gate_grad * gate)).astype(BF16)
        router_part = contract(logit_low, ffn_ref[j], 0, 0)
        input_grad = input_grad + contract(logit_low, router, 1, 1)
        inverse = lax.rsqrt(jnp.mean(hidden * hidden, axis=-1, keepdims=True) + EPS)
        r = hidden * inverse
        u = input_grad * gains[1:2, :]
        hidden_grad[j] = grad + (u - r * jnp.mean(u * r, axis=-1, keepdims=True)) * inverse
        gain_part = jnp.sum(input_grad * r, axis=0, keepdims=True)
        if j == 0:
            router_grad[...] = router_part
            gain_grad[...] = gain_part
        else:
            router_grad[...] += router_part
            gain_grad[...] += gain_part

    for j in range(per):
        tokens_out(j)
    for copy in stores:
        copy.wait()


def run_experts(
    heads_all, own_tok, wo_all, weights, gains, cot_own, ids_all, up, down, seqs, dps, per_expert, capacity
):
    per, span, width = own_tok.shape
    local = wo_all.shape[1]
    groups = seqs * dps
    height = up_to(up.shape[0] * per_expert, 16)
    spread = weights.shape[1] - 3 * local // 128 * 128
    rows = (groups, 2, height, width)
    return pl.pallas_call(
        functools.partial(experts_kernel, seqs, dps, per_expert, capacity, local),
        out_shape=(
            jax.ShapeDtypeStruct((per, span, width), BF16),
            jax.ShapeDtypeStruct((per, span, width), F32),
            jax.ShapeDtypeStruct((spread, width), F32),
            jax.ShapeDtypeStruct((1, width), F32),
            jax.ShapeDtypeStruct(up.shape, BF16),
            jax.ShapeDtypeStruct(down.shape, BF16),
        ),
        in_specs=[VMEM] * 7 + [ANY] * 2,
        out_specs=[VMEM] * 4 + [ANY] * 2,
        scratch_shapes=[
            pltpu.VMEM(up.shape, BF16),
            pltpu.VMEM(down.shape, BF16),
            pltpu.VMEM(up.shape, F32),
            pltpu.VMEM(down.shape, F32),
            pltpu.VMEM(rows, BF16),
            pltpu.VMEM((2, groups, height, width), BF16),
            pltpu.VMEM((per, groups * height, span), BF16),
            pltpu.VMEM((per, span, groups * height), BF16),
            pltpu.VMEM((per, span, width), F32),
            pltpu.VMEM((per, span, width), BF16),
            pltpu.VMEM((per, span, spread), F32),
            pltpu.VMEM((per, span, 1), F32),
            pltpu.VMEM((per, span, spread), F32),
            pltpu.VMEM((4,) + rows, BF16),
            pltpu.VMEM((2,) + rows, BF16),
            pltpu.VMEM(rows, BF16),
            DMA((3,)),
            DMA((groups,)),
            DMA((groups,)),
            DMA((3, groups)),
            DMA((3, groups)),
            DMA((2, groups)),
            DMA((2, groups)),
            DMA((groups,)),
            DMA((groups,)),
            DMA((groups,)),
            DMA((groups,)),
        ],
        compiler_params=params(collective_id=2),
        name="experts",
    )(heads_all, own_tok, wo_all, weights, gains, cot_own, ids_all, up, down)


def send_home(me, own, home, ls, z_send, z_recv, h_send, h_recv):
    s, seqs, x, core = me.s, me.seqs, me.x, me.c
    per, span, _ = own.shape
    rows = span // PIECES
    lands = [(k, lax.rem(s + core, 2) + 2 * k) for k in range(seqs // 2)]

    def part(c):
        return pl.ds(c * rows, rows)

    def start(c):
        for j in range(per):
            to = me.block(j)
            there = home.at[per * s + x, part(c)]

            @pl.when(to != s)
            def _():
                k = lax.div(s, 2)
                send(own.at[j, part(c)], there, z_send.at[j, c], z_recv.at[k, c], seq=to)

            @pl.when(to == s)
            def _():
                pltpu.make_async_copy(own.at[j, part(c)], there, ls.at[c]).start()

    def pass_on(c):
        for k, source in lands:
            here = home.at[per * source + x, part(c)]

            @pl.when(source == s)
            def _():
                pltpu.make_async_copy(here, here, ls.at[c]).wait()

            @pl.when(source != s)
            def _():
                arrived(here, z_recv.at[k, c])

            send(here, here, h_send.at[0, k, c], h_recv.at[0, k, c], head=me.across)
            send(here, here, h_send.at[1, k, c], h_recv.at[1, k, c], head=me.near)

    def pass_near(c):
        for k, source in lands:
            there = home.at[per * source + 1 - x, part(c)]
            arrived(there, h_recv.at[0, k, c])
            send(there, there, h_send.at[2, k, c], h_recv.at[2, k, c], head=me.near)

    def finish():
        some = own.at[0, part(0)]
        for c in range(PIECES):
            for j in range(per):

                @pl.when(me.block(j) != s)
                def _():
                    pltpu.make_async_copy(some, some, z_send.at[j, c]).wait()

            for k in range(seqs // 2):
                source = lax.rem(s + 1 + core, 2) + 2 * k
                arrived(home.at[per * source + x, part(c)], h_recv.at[1, k, c])
                arrived(home.at[per * source + 1 - x, part(c)], h_recv.at[2, k, c])
                for n in range(3):
                    pltpu.make_async_copy(some, some, h_send.at[n, k, c]).wait()

    return start, pass_on, pass_near, finish


def home_sems(per, seqs):
    return [
        DMA((PIECES,)),
        DMA((per, PIECES)),
        DMA((seqs // 2, PIECES)),
        DMA((3, seqs // 2, PIECES)),
        DMA((3, seqs // 2, PIECES)),
    ]


def add_groups(me, parts, dp_take, seq_take, result, dp_send, dp_recv, seq_send, seq_recv):
    s, d, seqs, dps = me.s, me.d, me.seqs, me.dps
    order = [mod(s + n, seqs) for n in list(range(1, seqs)) + [0]]

    def start():
        for to in order:
            for i in range(1, dps):
                there = mod(d + i, dps)
                send(
                    parts.at[there, to], dp_take.at[i - 1, to], dp_send.at[i - 1, to], dp_recv.at[i - 1, to], dp=there
                )

    def middle():
        for n, to in enumerate(order):
            total = parts[d, to].astype(F32)
            for i in range(1, dps):
                arrived(dp_take.at[i - 1, to], dp_recv.at[i - 1, to])
                total = total + dp_take[i - 1, to].astype(F32)
            parts[d, to] = total.astype(parts.dtype)
            if n < seqs - 1:
                send(parts.at[d, to], seq_take.at[n], seq_send.at[n], seq_recv.at[n], seq=to)

    def end():
        total = parts[d, s].astype(F32)
        for n in range(seqs - 1):
            arrived(seq_take.at[n], seq_recv.at[n])
            total = total + seq_take[n].astype(F32)
        result[...] = total
        some = seq_take.at[0]
        for to in range(seqs):
            for i in range(1, dps):
                pltpu.make_async_copy(some, some, dp_send.at[i - 1, to]).wait()
        for n in range(seqs - 1):
            pltpu.make_async_copy(some, some, seq_send.at[n]).wait()

    return start, middle, end


def group_scratch(seqs, dps, shape, dtype):
    return [
        pltpu.VMEM((dps, seqs) + shape, dtype),
        pltpu.VMEM((max(1, dps - 1), seqs) + shape, dtype),
        pltpu.VMEM((seqs - 1,) + shape, dtype),
    ]


def group_sems(seqs, dps):
    return [DMA((max(1, dps - 1), seqs))] * 2 + [DMA((seqs - 1,))] * 2


PIECES = 2


def back_kernel(
    seqs, dps, heads,
    result, hidden_grad, own_tok, heads_all, wo_all, split_in, probs, attn_input_in, weights, weights_far, gains, router,
    gain_f,
    output, tokens_home, w_sum, small_sum, wo_sum, gain_sum, bias_sum,
    split, attn_input, attn_grad, hsend, grad_all, slot, low_ref, ext, made, x_acc, x_out, x_near, tg,
    wo_part, wo_near, wo_far, w_parts, w_dp, w_seq, w_total, far_parts, far_dp, far_seq, far_sum, last_parts, last_dp, last_seq, last_sum, far_out, far_in,
    wo_parts, wo_dp, wo_seq, g_parts, g_dp, g_seq, r_parts, r_dp, r_seq, r_sum, g_acc,
    bias, bias_out, bias_in, bias_take, small, gsmall,
    ls, p_sem, a_send, a_recv, n_send, n_recv, on_send, on_recv, of_send, of_recv,
    b_send, b_recv, s_send, s_recv, t_send, t_recv, fs, *sems
):
    me = Place(seqs, dps)
    h, s, d = me.h, me.s, me.d
    per, span, width = hidden_grad.shape
    blocks = seqs
    length = blocks * span
    local = heads * HEAD_DIM
    groups = seqs * dps
    shard = width // groups
    padded = w_sum.shape[0]
    buckets = 32
    size = span // PIECES
    others = [(i, j) for i in range(seqs) for j in range(dps) if i or j]
    loads = [pltpu.make_async_copy(split_in, split, ls.at[0]), pltpu.make_async_copy(attn_input_in, attn_input, ls.at[1])]
    for copy in loads:
        copy.start()
    greet(me.group_peers() + [{"head": mod(h + i, 4)} for i in range(1, 4)])
    out_home = send_home(me, result, output, *sems[0:5])
    grad_home = send_home(me, tg, tokens_home, *sems[5:10])
    w_group = add_groups(me, w_parts, w_dp, w_seq, w_total, *sems[10:14])
    wo_group = add_groups(me, wo_parts, wo_dp, wo_seq, wo_sum, *sems[14:18])
    g_group = add_groups(me, g_parts, g_dp, g_seq, gain_sum, *sems[18:22])
    r_group = add_groups(me, r_parts, r_dp, r_seq, r_sum, *sems[22:26])
    far_group = add_groups(me, far_parts, far_dp, far_seq, far_sum, *sems[26:30])
    last_group = add_groups(me, last_parts, last_dp, last_seq, last_sum, *sems[30:34])

    def by_group(whole, parts):
        low = whole.astype(BF16)
        if shard % 16:
            low = contract(squeeze_hot(shard, padded, width, groups), low, 0, 0).astype(BF16)
        for g in range(groups):
            parts[g % dps, g // dps] = low[g * padded : (g + 1) * padded, :]

    def fetch(group, head):
        turn = head % 2 if group else 1 - head % 2
        return turn, pltpu.make_async_copy(probs.at[group, head], slot.at[turn], p_sem.at[turn])

    def put(ref, grad):
        for head in range(heads):
            ref[head, :, :HEAD_DIM] = grad[:, head * HEAD_DIM : (head + 1) * HEAD_DIM]

    def block_rows(block):
        return pl.ds(pl.multiple_of(block * span, span), span)

    fetch(1, 0)[1].start()
    out_home[0](0)
    out_home[0](1)
    hsend[...] = jnp.zeros_like(hsend)
    attn_grad[...] = hidden_grad[...].astype(BF16)
    for group, (own, other) in ((1, (me.across, me.near_across)), (0, (h, me.near))):
        for j in range(per):
            rows = block_rows(me.block(j))
            put(hsend.at[group, j], contract(attn_grad[j], wo_all[other], 1, 1).astype(BF16))
            send(
                hsend.at[group, j],
                grad_all.at[group, :, rows, :],
                a_send.at[group, j],
                a_recv.at[group, j],
                head=me.near,
            )
            put(grad_all.at[group, :, rows, :], contract(attn_grad[j], wo_all[own], 1, 1).astype(BF16))
    for k, q in enumerate((me.near_across, me.near, me.across, h)):
        total = jnp.zeros((local, width), F32)
        for j in range(per):
            total = total + contract(heads_all[q, j], attn_grad[j], 0, 0)
        wo_part[k] = total.astype(BF16)
        if k < 2:
            send(wo_part.at[k], wo_near.at[k], on_send.at[k], on_recv.at[k], head=me.near)
    by_group(router[...].T, r_parts)
    r_group[0]()
    for copy in loads:
        copy.wait()
    ext[...] = jnp.zeros_like(ext)
    made[...] = jnp.zeros_like(made)

    def wo_across():
        arrived(wo_near.at[0], on_recv.at[0])
        wo_part[2] = (wo_part[2].astype(F32) + wo_near[0].astype(F32)).astype(BF16)
        send(wo_part.at[2], wo_far, of_send, of_recv, head=me.across)

    def wo_total():
        arrived(wo_near.at[1], on_recv.at[1])
        arrived(wo_far, of_recv)
        total = (wo_part[3].astype(F32) + wo_near[1].astype(F32) + wo_far[...].astype(F32)).astype(BF16)
        for g in range(groups):
            hot = spread_hot(g * shard, shard, width)
            wo_parts[g % dps, g // dps] = contract(total, hot, 1, 1).astype(BF16)
        wo_group[0]()

    def cut(c):
        return pl.ds(c * size, size)

    def x_partial():
        for core in (1 - me.c, me.c):
            for c in range(PIECES):
                for j in range(per):
                    rows = pl.ds(pl.multiple_of(me.block(j, core) * span + c * size, size), size)
                    total = x_acc[rows, :] + contract(made[rows, :], weights[...], 1, 1)
                    if core is me.c:
                        x_acc[rows, :] = total
                    else:
                        x_out[j, cut(c)] = total.astype(BF16)
                        send(x_out.at[j, cut(c)], x_near.at[j, cut(c)], n_send.at[j, c], n_recv.at[j, c], head=me.near)

    def x_total(c):
        for j in range(per):
            arrived(x_near.at[j, cut(c)], n_recv.at[j, c])
            rows = pl.ds(pl.multiple_of(me.block(j) * span + c * size, size), size)
            grad = x_acc[rows, :] + x_near[j, cut(c)].astype(F32)
            v = own_tok[j, cut(c)].astype(F32)
            inverse = lax.rsqrt(jnp.mean(v * v, axis=-1, keepdims=True) + EPS)
            r = v * inverse
            u = grad * gains[0:1, :]
            back = (u - r * jnp.mean(u * r, axis=-1, keepdims=True)) * inverse
            tg[j, cut(c)] = (hidden_grad[j, cut(c)] + back).astype(BF16)
            g_acc[0:1, :] += jnp.sum(grad * r, axis=0, keepdims=True)
        grad_home[0](c)

    def attention(group, service):
        for j in range(per):
            rows = block_rows(me.block(j, 1 - me.c))
            arrived(grad_all.at[group, :, rows, :], a_recv.at[group, j])
        for head in range(heads):
            turn, copy = fetch(group, head)
            copy.wait()
            if head < heads - 1:
                fetch(group, head + 1)[1].start()
            elif group:
                fetch(0, 0)[1].start()
            key, value = split[group, heads + head, :, :HEAD_DIM], split[group, 2 * heads + head, :, :HEAD_DIM]
            for block in range(blocks):
                rows = slice(block * span, (block + 1) * span)
                grad = grad_all[group, head, rows, :HEAD_DIM]
                wide = slot[turn, rows, :].astype(F32)
                prob_grad = contract(grad, value, 1, 1)
                delta = jnp.sum(wide * prob_grad, axis=-1, keepdims=True)
                score_grad = wide * (prob_grad - delta)
                first = (blocks - 1 - block) * span
                ext[head, :, first : first + length] += score_grad
                low = score_grad.astype(BF16)
                low_ref[rows, :] = low
                cols = slice(head * HEAD_DIM, (head + 1) * HEAD_DIM)
                made[rows, cols] = jnp.dot(low, key, preferred_element_type=F32).astype(BF16)
            for kind, (narrow, wide_ref) in enumerate(
                ((split[group, head, :, :HEAD_DIM], low_ref), (grad_all[group, head, :, :HEAD_DIM], slot.at[turn]))
            ):
                first = (kind + 1) * local + head * HEAD_DIM
                made[:, first : first + HEAD_DIM] = contract(narrow, wide_ref[...], 0, 0).T.astype(BF16)
            for act in service[head]:
                act()

    def weight_grad(first, last):
        pieces = []
        for kind in range(3):
            at = kind * local
            pieces.append(contract(attn_input[...], made[:, at + first * HEAD_DIM : at + last * HEAD_DIM], 0, 0))
        lanes = 3 * (last - first) * HEAD_DIM
        if lanes % 128:
            pieces.append(jnp.zeros((width, 128 - lanes % 128), F32))
        return jnp.concatenate(pieces, axis=1)

    def bias_rows(into):
        turn = lax.broadcasted_iota(jnp.int32, (4 * span, 128), 0)
        bucket = bucket_of(jnp.where(turn < 3 * span, turn, turn - 4 * span) - span, buckets)
        hot = (bucket == lax.broadcasted_iota(jnp.int32, (4 * span, 128), 1)).astype(F32)
        lane = lax.broadcasted_iota(jnp.int32, (1, 128), 1)
        head_row = lax.broadcasted_iota(jnp.int32, (8, 4 * span), 0)
        diagonals = jnp.zeros((8, 4 * span), F32)
        far_row = lax.broadcasted_iota(jnp.int32, (8, 128), 0)
        far = jnp.zeros((8, 128), F32)
        for head in range(heads):
            eight = jnp.zeros((8, 4 * span), F32)
            for group in range(span // 8):
                piece = ext[head, group * 8 : (group + 1) * 8, 2 * span : 5 * span]
                piece = jnp.concatenate([piece, jnp.zeros((8, span), F32)], axis=1)
                eight = eight + pltpu.roll(piece, (4 * span - 8 * group) % (4 * span), 1)
            one = jnp.zeros((8, 4 * span), F32)
            for i in range(8):
                line = jnp.broadcast_to(eight[i : i + 1, :], (8, 4 * span))
                one = one + pltpu.roll(line, (4 * span - i) % (4 * span), 1)
            diagonals = jnp.where(head_row == head, one, diagonals)
            left, right = jnp.sum(ext[head, :, : 2 * span]), jnp.sum(ext[head, :, 5 * span :])
            sides = jnp.where(lane == buckets // 2 - 1, left, jnp.where(lane == buckets - 1, right, 0.0))
            far = jnp.where(far_row == head, sides, far)
        into[...] = far + jnp.dot(diagonals, hot, preferred_element_type=F32, precision=lax.Precision.HIGHEST)

    def router_total():
        r_group[2]()
        small[0] = r_sum[...]
        for i in range(1, 4):
            send(small.at[0], small.at[i], s_send.at[i - 1], s_recv.at[i - 1], head=mod(h + i, 4))

    g_acc[...] = jnp.zeros_like(g_acc)
    g_acc[1:2, :] = gain_f[...]
    def far_weights():
        by_group(weight_grad(0, heads - 1), far_parts)
        far_group[0]()

    def far_weights():
        by_group(weight_grad(0, heads - 1), far_parts)
        far_group[0]()

    attention(1, ((wo_across,), (far_weights, r_group[1]), (wo_total,)))
    by_group(weight_grad(heads - 1, heads), last_parts)
    last_group[0]()
    out_home[1](0)
    x_acc[...] = contract(made[...], weights_far[...], 1, 1)
    far_group[1]()
    out_home[1](1)
    bias_rows(bias_out)
    to_bias = send(bias_out, bias_in, fs.at[0], fs.at[1], head=me.across)
    ext[...] = jnp.zeros_like(ext)
    attention(
        0,
        (
            (),
            (wo_group[1], last_group[1]),
            (router_total,),
        ),
    )
    x_partial()
    x_total(0)
    x_total(1)
    by_group(weight_grad(0, heads), w_parts)
    w_group[0]()
    g_rows = g_acc[...].astype(BF16)
    for g in range(groups):
        g_parts[g % dps, g // dps] = contract(g_rows, spread_hot(g * shard, shard, width), 1, 1)
    g_group[0]()
    bias_rows(bias)
    arrived(bias_in, fs.at[1])
    bias[...] += bias_in[...]
    for n, (i, j) in enumerate(others):
        send(bias, bias_take.at[n], b_send.at[n], b_recv.at[n], seq=mod(s + i, seqs), dp=mod(d + j, dps))
    out_home[2](0)
    out_home[2](1)
    grad_home[1](0)
    w_group[1]()
    grad_home[1](1)
    g_group[1]()
    far_group[2]()
    last_group[2]()
    most, last = far_sum.shape[1], last_sum.shape[1]
    far_out[:, :most] = far_sum[...].astype(BF16)
    far_out[:, most:] = last_sum[...].astype(BF16)
    to_far = send(far_out, far_in, fs.at[2], fs.at[3], head=me.across)
    g_group[2]()
    gsmall[0] = gain_sum[...]
    for i in range(1, 4):
        send(gsmall.at[0], gsmall.at[i], t_send.at[i - 1], t_recv.at[i - 1], head=mod(h + i, 4))
    wo_group[2]()
    total = bias[...]
    for n in range(len(others)):
        arrived(bias_take.at[n], b_recv.at[n])
        total = total + bias_take[n]
    bias_sum[...] = total
    grad_home[2](0)
    w_group[2]()
    arrived(far_in, fs.at[3])
    first_heads, last_head = far_in[:, :most].astype(F32), far_in[:, most:].astype(F32)
    many = (heads - 1) * HEAD_DIM
    for kind in range(3):
        at = kind * local
        into = slice(at, at + many)
        w_sum[:, into] = w_total[:, into] + first_heads[:, kind * many : (kind + 1) * many]
        into = slice(at + many, at + local)
        w_sum[:, into] = w_total[:, into] + last_head[:, kind * HEAD_DIM : (kind + 1) * HEAD_DIM]
    total, gain_total = small[0], gsmall[0]
    for i in range(1, 4):
        arrived(small.at[i], s_recv.at[i - 1])
        arrived(gsmall.at[i], t_recv.at[i - 1])
        total = total + small[i]
        gain_total = gain_total + gsmall[i]
    small_sum[...] = total
    gain_sum[...] = gain_total
    grad_home[2](1)
    out_home[3]()
    grad_home[3]()
    to_bias.wait_send()
    to_far.wait_send()
    for j in range(per):
        for group in range(2):
            pltpu.make_async_copy(hsend.at[0, 0], hsend.at[0, 0], a_send.at[group, j]).wait()
        some = x_near.at[0, cut(0)]
        for c in range(PIECES):
            pltpu.make_async_copy(some, some, n_send.at[j, c]).wait()
    for k in range(2):
        pltpu.make_async_copy(wo_far, wo_far, on_send.at[k]).wait()
    pltpu.make_async_copy(wo_far, wo_far, of_send).wait()
    for i in range(3):
        pltpu.make_async_copy(small.at[0], small.at[0], s_send.at[i]).wait()
        pltpu.make_async_copy(gsmall.at[0], gsmall.at[0], t_send.at[i]).wait()
    for n in range(len(others)):
        pltpu.make_async_copy(bias, bias, b_send.at[n]).wait()


def back_pass(
    result, hidden_grad, own_tok, heads_all, wo_all, split, probs, attn_input, weights, weights_far, gains, router, gain_f,
    seqs, dps
):
    per, span, width = hidden_grad.shape
    length = seqs * span
    heads = probs.shape[1]
    local = heads * HEAD_DIM
    groups = seqs * dps
    shard = width // groups
    padded = up_to(shard, 16)
    lanes = weights.shape[1]
    spread = router.shape[0]
    all_three = up_to(3 * local, 128)
    most, last = up_to(3 * (heads - 1) * HEAD_DIM, 128), up_to(3 * HEAD_DIM, 128)
    block = (span, width)
    return pl.pallas_call(
        functools.partial(back_kernel, seqs, dps, heads),
        out_shape=(
            jax.ShapeDtypeStruct((per * seqs,) + block, BF16),
            jax.ShapeDtypeStruct((per * seqs,) + block, BF16),
            jax.ShapeDtypeStruct((padded, 3 * local), F32),
            jax.ShapeDtypeStruct((padded, spread), F32),
            jax.ShapeDtypeStruct((local, 128), F32),
            jax.ShapeDtypeStruct((8, 128), F32),
            jax.ShapeDtypeStruct((8, 128), F32),
        ),
        in_specs=[VMEM] * 5 + [ANY] * 3 + [VMEM] * 5,
        out_specs=[ANY] * 2 + [VMEM] * 5,
        scratch_shapes=[
            pltpu.VMEM(split.shape, BF16),
            pltpu.VMEM(attn_input.shape, BF16),
            pltpu.VMEM((per,) + block, BF16),
            pltpu.VMEM((2, per, heads, span, 128), BF16),
            pltpu.VMEM((2, heads, length, 128), BF16),
            pltpu.VMEM((2, length, length), BF16),
            pltpu.VMEM((length, length), BF16),
            pltpu.VMEM((heads, span, 7 * span), F32),
            pltpu.VMEM((length, lanes), BF16),
            pltpu.VMEM((length, width), F32),
            pltpu.VMEM((per,) + block, BF16),
            pltpu.VMEM((per,) + block, BF16),
            pltpu.VMEM((per,) + block, BF16),
            pltpu.VMEM((4, local, width), BF16),
            pltpu.VMEM((2, local, width), BF16),
            pltpu.VMEM((local, width), BF16),
        ]
        + group_scratch(seqs, dps, (padded, all_three), BF16)
        + [pltpu.VMEM((padded, all_three), F32)]
        + group_scratch(seqs, dps, (padded, most), BF16)
        + [pltpu.VMEM((padded, most), F32)]
        + group_scratch(seqs, dps, (padded, last), BF16)
        + [pltpu.VMEM((padded, last), F32)]
        + [
            pltpu.VMEM((padded, most + last), BF16),
            pltpu.VMEM((padded, most + last), BF16),
        ]
        + group_scratch(seqs, dps, (local, 128), BF16)
        + group_scratch(seqs, dps, (8, 128), F32)
        + group_scratch(seqs, dps, (padded, spread), BF16)
        + [
            pltpu.VMEM((padded, spread), F32),
            pltpu.VMEM((8, width), F32),
            pltpu.VMEM((8, 128), F32),
            pltpu.VMEM((8, 128), F32),
            pltpu.VMEM((8, 128), F32),
            pltpu.VMEM((groups - 1, 8, 128), F32),
            pltpu.VMEM((4, padded, spread), F32),
            pltpu.VMEM((4, 8, 128), F32),
            DMA((2,)),
            DMA((2,)),
            DMA((2, per)),
            DMA((2, per)),
            DMA((per, PIECES)),
            DMA((per, PIECES)),
            DMA((2,)),
            DMA((2,)),
            DMA(()),
            DMA(()),
            DMA((groups - 1,)),
            DMA((groups - 1,)),
            DMA((3,)),
            DMA((3,)),
            DMA((3,)),
            DMA((3,)),
            DMA((4,)),
        ]
        + home_sems(per, seqs) * 2
        + group_sems(seqs, dps) * 6,
        compiler_params=params(collective_id=4),
        name="back",
    )(
        result, hidden_grad, own_tok, heads_all, wo_all, split, probs, attn_input, weights, weights_far, gains, router, gain_f
    )


def settle_kernel(count, *refs):
    large, (w, router, wo, gain, bias) = refs[:count], refs[count : count + 5]
    refs = refs[count + 5 :]
    large_out, (wq_out, wk_out, wv_out, wo_out, router_out, gain_a, gain_f, bias_out) = refs[:count], refs[count : count + 8]
    refs = refs[count + 8 :]
    held, wide, sems = refs[:count], refs[count : 2 * count], refs[2 * count]
    copies = []
    for n in reversed(range(count)):
        half = large[n].shape[0] // 2
        for k in range(2):
            part = pl.ds(k * half, half)
            come = pltpu.make_async_copy(large[n].at[part], held[n].at[part], sems.at[0, n, k])
            rounded = large[n].dtype == large_out[n].dtype
            source = held[n] if rounded else wide[n]
            go = pltpu.make_async_copy(source.at[part], large_out[n].at[part], sems.at[1, n, k])
            come.start()
            copies.append((come, go, None if rounded else (wide[n], held[n], slice(k * half, (k + 1) * half))))
    shard, local = wq_out.shape
    for n, ref in enumerate((wq_out, wk_out, wv_out)):
        ref[...] = w[:shard, n * local : (n + 1) * local]
    wo_out[...] = wo[:, :shard]
    spread = router.shape[1]
    at = 3 * local % 128
    turned = jnp.concatenate([router[...], jnp.zeros((128 - router.shape[0], spread), F32)], axis=0).T
    router_out[...] = turned[at : at + router_out.shape[0], :shard]
    gain_a[...] = gain[0:1, :shard]
    gain_f[...] = gain[1:2, :shard]
    bias_out[...] = bias[: bias_out.shape[0], : bias_out.shape[1]]
    for come, go, widen in copies:
        come.wait()
        if widen is not None:
            into, source, part = widen
            into[part] = source[part].astype(F32)
        go.start()
    for _, go, _ in copies:
        go.wait()


def settle(large, types, small, shapes):
    count = len(large)
    return pl.pallas_call(
        functools.partial(settle_kernel, count),
        out_shape=tuple(jax.ShapeDtypeStruct(x.shape, kind) for x, kind in zip(large, types))
        + tuple(jax.ShapeDtypeStruct(shape, F32) for shape in shapes),
        in_specs=[ANY] * count + [VMEM] * len(small),
        out_specs=[ANY] * count + [VMEM] * len(shapes),
        scratch_shapes=[pltpu.VMEM(x.shape, x.dtype) for x in large]
        + [pltpu.VMEM(x.shape if x.dtype != kind else (8, 128), kind) for x, kind in zip(large, types)]
        + [DMA((2, count, 2))],
        compiler_params=pltpu.CompilerParams(vmem_limit_bytes=60 * 2**20),
        name="settle",
    )(*large, *small)


def up_to(value, unit):
    return -(-value // unit) * unit


def body(
    tokens,
    lengths,
    expert_ids,
    attention_gain,
    query_weight,
    key_weight,
    value_weight,
    output_weight,
    position_bias,
    feedforward_gain,
    router_weight,
    expert_up,
    expert_down,
    cotangent,
):
    seqs, dps = lax.axis_size("seq"), lax.axis_size("dp")
    groups = seqs * dps
    seq_local, span, width = tokens.shape
    per = seq_local // seqs
    local_width = query_weight.shape[1]
    bucket_count, heads = position_bias.shape
    experts = router_weight.shape[1]
    shard = query_weight.shape[0]
    capacity = max(2, (5 * span + 4 * experts - 1) // (4 * experts))
    attn_input, weights, weights_far, split, probs, heads_all, own_tok, cot_own, out_weight, gains, ids_all = front(
        tokens,
        cotangent,
        query_weight,
        key_weight,
        value_weight,
        output_weight,
        router_weight.T,
        attention_gain[None, :],
        feedforward_gain[None, :],
        expert_ids.reshape(seq_local, span),
        position_bias.T,
        lengths,
        seqs,
        dps,
    )
    result, hidden_grad, router_grad, gain_two_grad, up_grad, down_grad = run_experts(
        heads_all,
        own_tok,
        out_weight,
        weights,
        gains,
        cot_own,
        ids_all,
        expert_up,
        expert_down,
        seqs,
        dps,
        per * capacity,
        capacity,
    )
    output, tokens_grad, w_sum, small_sum, wo_sum, gain_sum, bias_sum = back_pass(
        result,
        hidden_grad,
        own_tok,
        heads_all,
        out_weight,
        split,
        probs,
        attn_input,
        weights,
        weights_far,
        gains,
        router_grad,
        gain_two_grad,
        seqs,
        dps,
    )
    output, tokens_grad, up_grad, down_grad, *small = settle(
        (output, tokens_grad, up_grad, down_grad),
        (BF16, BF16, F32, F32),
        (w_sum, small_sum, wo_sum, gain_sum, bias_sum),
        ((shard, local_width),) * 3
        + ((local_width, shard), (experts, shard), (1, shard), (1, shard), (heads, bucket_count)),
    )
    return (
        output,
        tokens_grad,
        small[5][0],
        small[0],
        small[1],
        small[2],
        small[3],
        small[7].T,
        small[6][0],
        small[4].T,
        up_grad,
        down_grad,
    )


def solution(mesh):
    placed = (
        P("dp", "seq", None),
        P("dp"),
        P("dp", "seq", None),
        P(("seq", "dp")),
        P(("seq", "dp"), "head"),
        P(("seq", "dp"), "head"),
        P(("seq", "dp"), "head"),
        P("head", ("seq", "dp")),
        P(None, "head"),
        P(("seq", "dp")),
        P(("seq", "dp"), None),
        P(("seq", "dp"), None, "head"),
        P(("seq", "dp"), "head", None),
        P("dp", "seq", None),
    )
    return jax.shard_map(
        body,
        mesh=mesh,
        in_specs=placed,
        out_specs=(
            P("dp", "seq", None),
            P("dp", "seq", None),
            P(("seq", "dp")),
            P(("seq", "dp"), "head"),
            P(("seq", "dp"), "head"),
            P(("seq", "dp"), "head"),
            P("head", ("seq", "dp")),
            P(None, "head"),
            P(("seq", "dp")),
            P(("seq", "dp"), None),
            P(("seq", "dp"), None, "head"),
            P(("seq", "dp"), "head", None),
        ),
        check_vma=False,
    )
```

```python
import functools

import jax
import jax.numpy as jnp
import numpy as np
from jax import lax
from jax.experimental import pallas as pl
from jax.experimental.pallas import tpu as pltpu
from jax.sharding import PartitionSpec as P

HEAD_DIM = 64
EPS = 1e-06
bucket_edges = np.array([1, 2, 3, 4, 5, 6, 7, 8, 12, 16, 23, 32, 46, 64, 91], np.int32)
ANY = pl.BlockSpec(memory_space=pl.ANY)
VMEM = pl.BlockSpec(memory_space=pltpu.VMEM)
MESH = pl.DeviceIdType.MESH
DMA = pltpu.SemaphoreType.DMA
F32 = jnp.float32
BF16 = jnp.bfloat16


def bucket_of(offset, bucket_count):
    distance = jnp.abs(offset)
    magnitude = jnp.zeros_like(offset)
    for edge in bucket_edges:
        magnitude = magnitude + (distance >= int(edge)).astype(jnp.int32)
    return magnitude + bucket_count // 2 * (offset > 0).astype(jnp.int32)


def send(src, dst, send_sem, recv_sem, **device):
    copy = pltpu.make_async_remote_copy(
        src_ref=src,
        dst_ref=dst,
        send_sem=send_sem,
        recv_sem=recv_sem,
        device_id=device,
        device_id_type=MESH,
    )
    copy.start()
    return copy


def arrived(ref, recv_sem):
    pltpu.make_async_copy(ref, ref, recv_sem).wait()


def greet(devices):
    barrier = pltpu.get_barrier_semaphore()
    for device in devices:
        pl.semaphore_signal(barrier, inc=1, device_id=device, device_id_type=MESH)
    pl.semaphore_wait(barrier, len(devices))


def mod(value, size):
    return lax.rem(value + 4 * size, size)


class Place:
    def __init__(self, seqs, dps):
        self.h, self.s, self.d = lax.axis_index("head"), lax.axis_index("seq"), lax.axis_index("dp")
        self.seqs, self.dps = seqs, dps
        self.x, self.c = lax.div(self.h, 2), lax.rem(self.h, 2)
        self.near = self.h + 1 - 2 * self.c
        self.across = mod(self.h + 2, 4)
        self.near_across = lax.rem(self.across, 2) * -2 + self.across + 1

    def seq_peers(self):
        return [{"seq": mod(self.s + i, self.seqs)} for i in range(1, self.seqs)]

    def dp_peers(self):
        return [{"dp": mod(self.d + i, self.dps)} for i in range(1, self.dps)]

    def head_pair(self):
        return [{"head": self.near}, {"head": self.across}]

    def group_peers(self):
        return [
            {"seq": mod(self.s + i, self.seqs), "dp": mod(self.d + j, self.dps)}
            for i in range(self.seqs)
            for j in range(self.dps)
            if i or j
        ]

    def block(self, j, core=None):
        return lax.rem((self.c if core is None else core) + self.s, 2) + 2 * j


def params(**more):
    return pltpu.CompilerParams(has_side_effects=True, vmem_limit_bytes=60 * 2**20, **more)


def gather_groups(me, own, whole, z_send, z_recv, dp_send, dp_recv, far=None, far_send=None, far_recv=None):
    s, d, seqs, dps = me.s, me.d, me.seqs, me.dps

    def spread(src, source):
        for i in range(1, dps):
            send(
                src,
                whole.at[source, d],
                dp_send.at[i - 1, source],
                dp_recv.at[i - 1, source],
                dp=mod(d + i, dps),
            )

    def onward(src, source, dp):
        if far is not None:
            send(src, far.at[source, dp], far_send.at[source, dp], far_recv.at[source, dp], head=me.across)

    def start():
        for i in range(1, seqs):
            send(own, whole.at[s, d], z_send.at[i - 1], z_recv.at[i - 1], seq=mod(s + i, seqs))
        spread(own, s)
        onward(own, s, d)

    def relay(i):
        source = mod(s - i, seqs)
        here = whole.at[source, d]
        arrived(here, z_recv.at[i - 1])
        spread(here, source)
        onward(here, source, d)

    def finish():
        for i in range(1, dps):
            for source in range(seqs):
                there = mod(d - i, dps)
                arrived(whole.at[source, there], dp_recv.at[i - 1, source])
                onward(whole.at[source, there], source, there)
                pltpu.make_async_copy(own, own, dp_send.at[i - 1, source]).wait()
        for i in range(1, seqs):
            pltpu.make_async_copy(own, own, z_send.at[i - 1]).wait()

    def take_far():
        for source in range(seqs):
            for dp in range(dps):
                arrived(far.at[source, dp], far_recv.at[source, dp])

    def finish_far():
        for source in range(seqs):
            for dp in range(dps):
                pltpu.make_async_copy(own, own, far_send.at[source, dp]).wait()

    return start, relay, finish, take_far, finish_far


def gather_sems(seqs, dps):
    return [
        DMA((seqs - 1,)),
        DMA((seqs - 1,)),
        DMA((max(1, dps - 1), seqs)),
        DMA((max(1, dps - 1), seqs)),
    ]


def spread_hot(at, shard, width):
    row = lax.broadcasted_iota(jnp.int32, (128, width), 0)
    column = lax.broadcasted_iota(jnp.int32, (128, width), 1)
    return ((column == row + at) & (row < shard)).astype(BF16)


def squeeze_hot(shard, padded, rows, count):
    row = lax.broadcasted_iota(jnp.int32, (rows, count * padded), 0)
    column = lax.broadcasted_iota(jnp.int32, (rows, count * padded), 1)
    inside = lax.rem(column, padded)
    return ((lax.div(column, padded) * shard + inside == row) & (inside < shard)).astype(BF16)


def front_kernel(
    seqs, dps, heads,
    tok, cot, wq, wk, wv, wo, router, gain_a, gain_f, ids_own, table, lengths,
    attn_input_out, weights_out, far_out, split_out, probs, heads_all, own_tok, cot_own, wo_all, gains, ids_all,
    attn_input, weights, weights_far, split, tok_all, pack, pack_all, far_all, wo_pad, wo_parts, tile, tile_all, table_own, table_far,
    ext, slot, out,
    p_sem, ls, os, z_send, z_recv, h_send, h_recv, c_send, c_recv, a_send, a_recv, w_send, w_recv, i_send, i_recv,
    f_send, f_recv, t_sem, *line
):
    me = Place(seqs, dps)
    h, s, d, x, c = me.h, me.s, me.d, me.x, me.c
    blocks, span, width = tok_all.shape
    per = own_tok.shape[0]
    length = blocks * span
    shard, local = wq.shape
    groups = seqs * dps
    experts = router.shape[0]
    half = span // 2
    own_half = pl.ds(pl.multiple_of(c * half, half), half)
    other_half = pl.ds(pl.multiple_of((1 - c) * half, half), half)
    pack[...] = jnp.zeros_like(pack)
    split[...] = jnp.zeros_like(split)
    for n, ref in enumerate((wq, wk, wv)):
        pack[:shard, n * local : (n + 1) * local] = ref[...]
    same = lax.broadcasted_iota(jnp.int32, (experts, experts), 0) == lax.broadcasted_iota(jnp.int32, (experts, experts), 1)
    pack[:shard, 3 * local : 3 * local + experts] = contract(router[...], same.astype(BF16), 0, 0).astype(BF16)
    wo_pad[...] = jnp.zeros_like(wo_pad)
    wo_pad[:, :shard] = wo[...]
    tile[...] = jnp.zeros_like(tile)
    tile[0:1, :shard] = gain_a[...].astype(F32)
    tile[1:2, :shard] = gain_f[...].astype(F32)
    buckets = table.shape[1]
    table_own[...] = jnp.zeros_like(table_own)
    table_own[:heads, :buckets] = table[...].astype(F32)
    own_copies = [
        pltpu.make_async_copy(pack, pack_all.at[s, d], ls.at[0]),
        pltpu.make_async_copy(tile, tile_all.at[s, d], ls.at[1]),
        pltpu.make_async_copy(wo_pad, wo_parts.at[s, d], ls.at[2]),
        pltpu.make_async_copy(ids_own, ids_all.at[s], ls.at[3]),
        pltpu.make_async_copy(tok.at[per * s + x], tok_all.at[s], ls.at[4]),
    ]
    for copy in own_copies:
        copy.start()

    @pl.when(c == 0)
    def _():
        pltpu.make_async_copy(cot.at[per * s + x], cot_own.at[lax.div(s, 2)], ls.at[5]).start()

    greet(
        me.seq_peers()
        + [{"head": me.near} | peer for peer in me.seq_peers()]
        + me.dp_peers()
        + [{"head": mod(h + i, 4)} for i in range(1, 4)]
    )
    packs = gather_groups(me, pack, pack_all, *line[0:4], far_all, f_send, f_recv)
    tiles = gather_groups(me, tile, tile_all, *line[4:8])
    outs = gather_groups(me, wo_pad, wo_parts, *line[8:12])
    packs[0]()
    tiles[0]()
    to_table = send(table_own, table_far, t_sem.at[0], t_sem.at[1], head=me.across)
    for i in range(1, seqs):
        send(ids_own, ids_all.at[s], i_send.at[i - 1], i_recv.at[i - 1], seq=mod(s + i, seqs))
    for i in range(1, seqs):
        to = mod(s + i, seqs)
        send(tok.at[per * to + x, own_half], tok_all.at[s, own_half], z_send.at[i - 1], z_recv.at[i - 1], seq=to)

    def send_cotangent():
        for i in range(1, seqs):
            to = mod(s + i, seqs)
            target = jnp.where(lax.rem(s + to, 2) == c, h, me.near)
            j = lax.div(s, 2)
            send(
                cot.at[per * to + x, own_half],
                cot_own.at[j, own_half],
                c_send.at[i - 1],
                c_recv.at[j, c],
                head=target,
                seq=to,
            )

    def build_bias(rows):
        turn = lax.broadcasted_iota(jnp.int32, (128, 4 * span), 1)
        bucket = bucket_of(jnp.where(turn < 3 * span, turn, turn - 4 * span) - span, buckets)
        hot = (bucket == lax.broadcasted_iota(jnp.int32, (128, 4 * span), 0)).astype(BF16)
        bias_rows = jnp.dot(rows[...].astype(BF16), hot, preferred_element_type=F32)
        for head in range(heads):
            row = bias_rows[head : head + 1]
            rolled = pltpu.roll(jnp.broadcast_to(row, (span, 4 * span)), 0, 1, stride=1, stride_axis=0)
            ext[head, :, 2 * span : 5 * span] = rolled[:, : 3 * span]
            ext[head, :, : 2 * span] = jnp.broadcast_to(row[:, 0:1], (span, 2 * span))
            ext[head, :, 5 * span :] = jnp.broadcast_to(row[:, 3 * span - 1 : 3 * span], (span, 2 * span))

    def whole_weights(parts, into):
        if shard % 16:
            whole = parts[...].reshape(groups * pack.shape[0], pack.shape[1])
            hot = squeeze_hot(shard, pack.shape[0], width, groups)
            into[...] = jnp.dot(hot, whole, preferred_element_type=F32).astype(BF16)
        else:
            into[...] = parts[...].reshape(width, pack.shape[1])

    def assemble():
        whole_weights(pack_all, weights)
        row = jnp.zeros((8, width), F32)
        for g in range(groups):
            piece = tile_all[g // dps, g % dps].astype(BF16)
            row = row + jnp.dot(piece, spread_hot(g * shard, shard, width), preferred_element_type=F32)
        gains[...] = row

    def project(group, block):
        rows = pl.ds(pl.multiple_of(block * span, span), span)
        if group == 0:
            v = tok_all[block].astype(F32)
            normed = v * lax.rsqrt(jnp.mean(v * v, axis=-1, keepdims=True) + EPS) * gains[0:1, :]
            attn_input[rows, :] = normed.astype(BF16)
        which = weights if group == 0 else weights_far
        parts = jnp.dot(attn_input[rows, :], which[...], preferred_element_type=F32).astype(BF16)
        for n in range(3 * heads):
            split[group, n, rows, :HEAD_DIM] = parts[:, n * HEAD_DIM : (n + 1) * HEAD_DIM]

    build_bias(table_own)
    for i in range(1, seqs):
        packs[1](i)
        tiles[1](i)
    far_first = [i for i in range(1, seqs) if i != 2] + [2]

    def pass_own(i):
        here = tok_all.at[mod(s - i, seqs), own_half]
        arrived(here, z_recv.at[i - 1])
        send(here, here, h_send.at[i - 1], h_recv.at[i - 1], head=me.near)

    for copy in own_copies:
        copy.wait()
    packs[2]()
    tiles[2]()
    assemble()
    project(0, s)
    for i in far_first:
        pass_own(i)
    outs[0]()
    for i in far_first:
        source = mod(s - i, seqs)
        arrived(tok_all.at[source, other_half], h_recv.at[i - 1])
        project(0, source)
    kept = [
        pltpu.make_async_copy(attn_input, attn_input_out, ls.at[6]),
        pltpu.make_async_copy(split.at[0], split_out.at[0], ls.at[7]),
        pltpu.make_async_copy(weights, weights_out, ls.at[8]),
    ]
    kept += [pltpu.make_async_copy(tok_all.at[me.block(j)], own_tok.at[j], ls.at[9 + j]) for j in range(per)]
    for copy in kept:
        copy.start()
    late = [
        pltpu.make_async_copy(split.at[1], split_out.at[1], ls.at[9 + per]),
        pltpu.make_async_copy(weights_far, far_out, ls.at[10 + per]),
    ]

    def second_group():
        packs[3]()
        whole_weights(far_all, weights_far)
        arrived(table_far, t_sem.at[1])
        build_bias(table_far)

        @pl.loop(0, blocks)
        def _(block):
            project(1, block)

        for copy in late:
            copy.start()

    @pl.loop(0, 2 * blocks)
    def _(unit):
        group, block = lax.div(unit, blocks), lax.rem(unit, blocks)
        rows = pl.ds(pl.multiple_of(block * span, span), span)
        turn = lax.rem(unit, 2)

        @pl.when(unit == blocks)
        def _():
            second_group()

        @pl.when(unit >= 2)
        def _():
            pltpu.make_async_copy(slot.at[turn], slot.at[turn], p_sem.at[turn]).wait()

        window = pl.ds(pl.multiple_of((blocks - 1 - block) * span, span), length)
        valid = lax.broadcasted_iota(jnp.int32, (1, length), 1) < lengths[per * s + x]
        for head in range(heads):
            query = split[group, head, rows, :HEAD_DIM]
            key, value = split[group, heads + head, :, :HEAD_DIM], split[group, 2 * heads + head, :, :HEAD_DIM]
            scores = lax.dot_general(query, key, (((1,), (1,)), ((), ())), preferred_element_type=F32)
            scores = jnp.where(valid, scores + ext[head, :, window], -1e30)
            top = jnp.max(scores, axis=-1, keepdims=True)
            grown = jnp.exp(scores - top)
            total = jnp.sum(grown, axis=-1, keepdims=True)
            part = (grown * (1.0 / total)).astype(BF16)
            slot[turn, head] = part
            mixed = jnp.dot(part, value, preferred_element_type=F32)
            out[unit, :, head * HEAD_DIM : (head + 1) * HEAD_DIM] = mixed.astype(BF16)
        pltpu.make_async_copy(slot.at[turn], probs.at[group, :, rows, :], p_sem.at[turn]).start()
        source = jnp.where(group == 0, h, me.across)
        j = lax.div(block, 2)

        @pl.when(lax.rem(block + s, 2) == c)
        def _():
            pltpu.make_async_copy(out.at[unit], heads_all.at[source, j], os.at[group, j]).start()

        @pl.when(lax.rem(block + s, 2) != c)
        def _():
            send(out.at[unit], heads_all.at[source, j], a_send.at[group, j], a_recv.at[group, j], head=me.near)

        @pl.when(unit == 1)
        def _():
            for i in range(1, seqs):
                outs[1](i)
            send_cotangent()

        @pl.when(unit == 3)
        def _():
            outs[2]()
            total = jnp.zeros((local, width), F32)
            for g in range(groups):
                total = total + jnp.dot(
                    wo_parts[g // dps, g % dps], spread_hot(g * shard, shard, width), preferred_element_type=F32
                )
            wo_all[h] = total.astype(BF16)
            send(wo_all.at[h], wo_all.at[h], w_send.at[0], w_recv.at[0], head=me.across)
            send(wo_all.at[h], wo_all.at[h], w_send.at[1], w_recv.at[1], head=me.near)

    there = wo_all.at[me.across]
    arrived(there, w_recv.at[0])
    send(there, there, w_send.at[2], w_recv.at[2], head=me.near)
    for copy in kept + late:
        copy.wait()
    for turn in range(2):
        pltpu.make_async_copy(slot.at[turn], slot.at[turn], p_sem.at[turn]).wait()
    packs[4]()
    to_table.wait_send()
    for j in range(per):
        block = me.block(j)

        @pl.when(block == s)
        def _():
            pltpu.make_async_copy(cot_own.at[j], cot_own.at[j], ls.at[5]).wait()

        @pl.when(block != s)
        def _():
            for part in range(2):
                arrived(cot_own.at[j, pl.ds(part * half, half)], c_recv.at[j, part])

        for group in range(2):
            pltpu.make_async_copy(out.at[0], heads_all.at[h, j], os.at[group, j]).wait()
            pltpu.make_async_copy(out.at[0], out.at[0], a_send.at[group, j]).wait()
            source = me.near if group == 0 else me.near_across
            arrived(heads_all.at[source, j], a_recv.at[group, j])

    for i in range(1, seqs):
        rows = tok.at[0, pl.ds(0, half)]
        for sem in (z_send, h_send, c_send):
            pltpu.make_async_copy(rows, rows, sem.at[i - 1]).wait()
        pltpu.make_async_copy(ids_own, ids_own, i_send.at[i - 1]).wait()
        arrived(ids_all.at[mod(s - i, seqs)], i_recv.at[i - 1])
    for k in range(3):
        pltpu.make_async_copy(wo_all.at[h], wo_all.at[h], w_send.at[k]).wait()
    arrived(wo_all.at[me.near], w_recv.at[1])
    arrived(wo_all.at[me.near_across], w_recv.at[2])


def front(tokens, cot, wq, wk, wv, wo, router, gain_a, gain_f, ids, table, lengths, seqs, dps):
    seq_local, span, width = tokens.shape
    per = seq_local // seqs
    length = seqs * span
    shard, local = wq.shape
    heads = local // HEAD_DIM
    lanes = up_to(3 * local + router.shape[0], 128)
    padded = up_to(shard, 16)
    smem = pl.BlockSpec(memory_space=pltpu.SMEM)
    return pl.pallas_call(
        functools.partial(front_kernel, seqs, dps, heads),
        out_shape=(
            jax.ShapeDtypeStruct((length, width), BF16),
            jax.ShapeDtypeStruct((width, lanes), BF16),
            jax.ShapeDtypeStruct((width, lanes), BF16),
            jax.ShapeDtypeStruct((2, 3 * heads, length, 128), BF16),
            jax.ShapeDtypeStruct((2, heads, length, length), BF16),
            jax.ShapeDtypeStruct((4, per, span, local), BF16),
            jax.ShapeDtypeStruct((per, span, width), BF16),
            jax.ShapeDtypeStruct((per, span, width), BF16),
            jax.ShapeDtypeStruct((4, local, width), BF16),
            jax.ShapeDtypeStruct((8, width), F32),
            jax.ShapeDtypeStruct((seqs,) + ids.shape[:2], jnp.int32),
        ),
        in_specs=[ANY] * 2 + [VMEM] * 7 + [ANY, VMEM, smem],
        out_specs=[ANY] * 8 + [VMEM] * 2 + [ANY],
        scratch_shapes=[
            pltpu.VMEM((length, width), BF16),
            pltpu.VMEM((width, lanes), BF16),
            pltpu.VMEM((width, lanes), BF16),
            pltpu.VMEM((2, 3 * heads, length, 128), BF16),
            pltpu.VMEM((seqs, span, width), BF16),
            pltpu.VMEM((padded, lanes), BF16),
            pltpu.VMEM((seqs, dps, padded, lanes), BF16),
            pltpu.VMEM((seqs, dps, padded, lanes), BF16),
            pltpu.VMEM((local, 128), BF16),
            pltpu.VMEM((seqs, dps, local, 128), BF16),
            pltpu.VMEM((8, 128), F32),
            pltpu.VMEM((seqs, dps, 8, 128), F32),
            pltpu.VMEM((8, 128), F32),
            pltpu.VMEM((8, 128), F32),
            pltpu.VMEM((heads, span, 7 * span), F32),
            pltpu.VMEM((2, heads, span, length), BF16),
            pltpu.VMEM((2 * seqs, span, local), BF16),
            DMA((2,)),
            DMA((11 + per,)),
            DMA((2, per)),
            DMA((seqs - 1,)),
            DMA((seqs - 1,)),
            DMA((seqs - 1,)),
            DMA((seqs - 1,)),
            DMA((seqs - 1,)),
            DMA((per, 2)),
            DMA((2, per)),
            DMA((2, per)),
            DMA((3,)),
            DMA((3,)),
            DMA((seqs - 1,)),
            DMA((seqs - 1,)),
            DMA((seqs, dps)),
            DMA((seqs, dps)),
            DMA((2,)),
        ]
        + gather_sems(seqs, dps) * 3,
        compiler_params=params(collective_id=0),
        name="front",
    )(tokens, cot, wq, wk, wv, wo, router, gain_a, gain_f, ids, table, lengths)


def expert_windows(exp_local, per_expert):
    return [(e * per_expert // 16 * 16, up_to((e + 1) * per_expert, 16)) for e in range(exp_local)]


def contract(a, b, over_a, over_b):
    return lax.dot_general(a, b, (((over_a,), (over_b,)), ((), ())), preferred_element_type=F32)


AHEAD = 3
GELU_A, GELU_B = float(np.sqrt(2.0 / np.pi)), 0.044715


def experts_kernel(
    seqs, dps, per_expert, capacity, local,
    heads_all, own_tok, wo_all, weights, gains, cot_own, ids_all, up_in, down_in,
    result, hidden_grad, router_grad, gain_grad, up_out, down_out,
    up, down, up_grad, down_grad, rows, summed, place_hot, place_turned, hidden_ref, ffn_ref, router_ref, gate_ref, hot_ref, taken, near, far,
    ls, g_send, g_recv, h_send, h_recv, n_send, n_recv, x_send, x_recv, r_send, r_recv
):
    me = Place(seqs, dps)
    h, s, d = me.h, me.s, me.d
    groups, _, height, width = rows.shape
    exp_local = up.shape[0]
    windows = expert_windows(exp_local, per_expert)
    me_group = s * dps + d

    def away(n):
        return lax.div(n, dps), lax.rem(n, dps)

    def ahead(n):
        i, j = away(n)
        return mod(s + i, seqs), mod(d + j, dps)

    def behind(n):
        i, j = away(n)
        return mod(s - i, seqs), mod(d - j, dps)

    per, span, _ = own_tok.shape
    loads = [pltpu.make_async_copy(up_in, up, ls.at[1]), pltpu.make_async_copy(down_in, down, ls.at[2])]
    for copy in loads:
        copy.start()
    spots = groups * height
    first_lane = 3 * local // 128 * 128
    spread = weights.shape[1] - first_lane
    shift = 3 * local - first_lane
    experts = groups * exp_local
    router = weights[:, first_lane:]
    earlier = lax.broadcasted_iota(jnp.int32, (span, span), 0) < lax.broadcasted_iota(jnp.int32, (span, span), 1)
    earlier = earlier.astype(BF16)
    lane = lax.broadcasted_iota(jnp.int32, (span, spread), 1)
    is_expert = (lane >= shift) & (lane < shift + experts)

    def tokens_in(j):
        total = own_tok[j].astype(F32)
        for q in range(4):
            total = total + jnp.dot(heads_all[q, j], wo_all[q], preferred_element_type=F32)
        hidden_ref[j] = total
        inverse = lax.rsqrt(jnp.mean(total * total, axis=-1, keepdims=True) + EPS)
        ffn = (total * inverse * gains[1:2, :]).astype(BF16)
        ffn_ref[j] = ffn
        logits = jnp.where(is_expert, jnp.dot(ffn, router, preferred_element_type=F32), -1e30)
        grown = jnp.exp(logits - jnp.max(logits, axis=-1, keepdims=True))
        router_probs = grown / jnp.sum(grown, axis=-1, keepdims=True)
        router_ref[j] = router_probs
        ids = ids_all[me.block(j), pl.ds(per * s + me.x, 1), :]
        own = lax.broadcasted_iota(jnp.int32, (spread, span), 0) == ids + shift
        own_low = own.astype(BF16)
        before = jnp.dot(own_low, earlier, preferred_element_type=F32)
        slot = jnp.sum(jnp.where(own, before, 0.0), axis=0, keepdims=True).astype(jnp.int32)
        same = lax.broadcasted_iota(jnp.int32, (spread, spread), 0) == lax.broadcasted_iota(jnp.int32, (spread, spread), 1)
        hot = contract(own_low, same.astype(BF16), 0, 0)
        hot_ref[j] = hot
        gate = jnp.sum(router_probs * hot, axis=-1, keepdims=True)
        gate_ref[j] = gate
        group = lax.div(ids, exp_local)
        place = group * height + ((ids - group * exp_local) * per + j) * capacity + slot
        spot = lax.broadcasted_iota(jnp.int32, (spots, span), 0)
        place_hot[j] = (spot == place).astype(BF16)
        return ffn, (gate * cot_own[j].astype(F32)).astype(BF16)

    made = [tokens_in(j) for j in range(per)]
    for part in range(2):
        total = jnp.zeros((spots, width), F32)
        for j in range(per):
            total = total + jnp.dot(place_hot[j], made[j][part], preferred_element_type=F32)
        total = total.astype(BF16)
        for g in range(groups):
            rows[g, part] = total[g * height : (g + 1) * height, :]
    up_grad[...] = jnp.zeros_like(up_grad)
    down_grad[...] = jnp.zeros_like(down_grad)
    greet(me.group_peers() + me.head_pair())
    pltpu.make_async_copy(rows.at[me_group], taken.at[h, 0], ls.at[0]).start()

    def send_out(n):
        to_s, to_d = ahead(n)
        send(rows.at[to_s * dps + to_d], taken.at[h, n], g_send.at[n], g_recv.at[n], seq=to_s, dp=to_d)

    for n in range(1, min(AHEAD + 1, groups)):
        send_out(n)

    def gather_own(n):
        here = taken.at[h, n]

        @pl.when(n == 0)
        def _():
            pltpu.make_async_copy(here, here, ls.at[0]).wait()

        @pl.when(n > 0)
        def _():
            arrived(here, g_recv.at[n])

        send(here, here, h_send.at[0, n], h_recv.at[0, n], head=me.across)
        send(here, here, h_send.at[1, n], h_recv.at[1, n], head=me.near)

    def gather_across(n):
        there = taken.at[me.across, n]
        arrived(there, h_recv.at[0, n])
        send(there, there, h_send.at[2, n], h_recv.at[2, n], head=me.near)

    def compute(n):
        @pl.when(n == first_turn)
        def _():
            for copy in loads:
                copy.wait()

        arrived(taken.at[me.near, n], h_recv.at[1, n])
        arrived(taken.at[me.near_across, n], h_recv.at[2, n])
        for k in range(3):
            pltpu.make_async_copy(taken.at[h, n], taken.at[h, n], h_send.at[k, n]).wait()
        kept = []
        for e, (low, high) in enumerate(windows):
            size = high - low
            at = lax.broadcasted_iota(jnp.int32, (4 * size, width), 0)
            slot = lax.rem(at, size) + low
            inside = (slot >= e * per_expert) & (slot < (e + 1) * per_expert)

            def mine(part):
                block = jnp.concatenate([taken[q, n, part, low:high, :] for q in range(4)], axis=0)
                return jnp.where(inside, block.astype(F32), 0.0).astype(BF16)

            x, g = mine(0), mine(1)
            pre = jnp.dot(x, up[e], preferred_element_type=F32)
            square = pre * pre
            bent = jnp.tanh(GELU_A * pre * (1.0 + GELU_B * square))
            act = (0.5 * pre * (1.0 + bent)).astype(BF16)
            slope = 0.5 * (1.0 + bent) + 0.5 * pre * (1.0 - bent * bent) * (GELU_A * (1.0 + 3.0 * GELU_B * square))
            out = jnp.dot(act, down[e], preferred_element_type=F32).astype(BF16)
            act_grad = contract(g, down[e], 1, 1)
            pre_grad = (act_grad * slope).astype(BF16)
            back = contract(pre_grad, up[e], 1, 1).astype(BF16)
            kept.append((x, g, act, pre_grad, out, back))
        for q in range(4):
            for part in range(2):
                for tile in range(0, height, 16):
                    total = None
                    for (low, high), made in zip(windows, kept):
                        if low <= tile < high:
                            begin = q * (high - low) + tile - low
                            piece = made[4 + part][begin : begin + 16, :]
                            total = piece if total is None else total + piece
                    if total is not None:
                        taken[q, n, part, tile : tile + 16, :] = total
        send(taken.at[me.near_across, n], near.at[0, n], n_send.at[0, n], n_recv.at[0, n], head=me.near)
        send(taken.at[me.near, n], near.at[1, n], n_send.at[1, n], n_recv.at[1, n], head=me.near)
        for e in range(exp_local):
            x, g, act, pre_grad, _, _ = kept[e]
            up_grad[e] += contract(x, pre_grad, 0, 0)
            down_grad[e] += contract(act, g, 0, 0)

    def add_near(n):
        arrived(near.at[0, n], n_recv.at[0, n])
        both = taken[me.across, n].astype(F32) + near[0, n].astype(F32)
        taken[me.across, n] = both.astype(BF16)
        send(taken.at[me.across, n], far.at[n], x_send.at[n], x_recv.at[n], head=me.across)

    def send_back(n):
        arrived(near.at[1, n], n_recv.at[1, n])
        arrived(far.at[n], x_recv.at[n])
        total = taken[h, n].astype(F32) + near[1, n].astype(F32) + far[n].astype(F32)
        taken[h, n] = total.astype(BF16)
        to_s, to_d = behind(n)

        @pl.when(n == 0)
        def _():
            pltpu.make_async_copy(taken.at[h, n], summed.at[:, me_group], r_send.at[n]).start()

        @pl.when(n > 0)
        def _():
            send(taken.at[h, n], summed.at[:, me_group], r_send.at[n], r_recv.at[n], seq=to_s, dp=to_d)

    first_turn = 1 % groups
    gather_own(0)
    stages = (send_back, add_near, compute, gather_across, gather_own)

    @pl.loop(0, groups + len(stages) - 1)
    def _(step):
        @pl.when((step > 0) & (step + AHEAD < groups))
        def _():
            send_out(step + AHEAD)

        for j in range(per):

            @pl.when(step == 2 + j)
            def _():
                place_turned[j] = place_hot[j].astype(F32).T.astype(BF16)

        for k, stage in enumerate(stages):
            turn = step - (len(stages) - 1 - k)
            last = groups - 1 if stage is gather_own else groups

            @pl.when((turn >= 0) & (turn < last))
            def _():
                stage(lax.rem(turn + 1, groups))

    up[...] = up_grad[...].astype(BF16)
    down[...] = down_grad[...].astype(BF16)
    stores = [
        pltpu.make_async_copy(up, up_out, ls.at[1]),
        pltpu.make_async_copy(down, down_out, ls.at[2]),
    ]
    for copy in stores:
        copy.start()

    @pl.loop(0, groups)
    def _(n):
        here = taken.at[h, n]
        for k in range(2):
            pltpu.make_async_copy(here, here, n_send.at[k, n]).wait()
        pltpu.make_async_copy(here, here, x_send.at[n]).wait()
        pltpu.make_async_copy(here, here, r_send.at[n]).wait()

        @pl.when(n > 0)
        def _():
            pltpu.make_async_copy(here, here, g_send.at[n]).wait()
            from_s, from_d = ahead(n)
            arrived(summed.at[:, from_s * dps + from_d], r_recv.at[n])

    def tokens_out(j):
        hidden, gate, router_probs, hot = hidden_ref[j], gate_ref[j], router_ref[j], hot_ref[j]
        grad = cot_own[j].astype(F32)
        token_out = jnp.dot(place_turned[j], summed[0].reshape(spots, width), preferred_element_type=F32)
        input_grad = jnp.dot(place_turned[j], summed[1].reshape(spots, width), preferred_element_type=F32)
        result[j] = (hidden + gate * token_out).astype(BF16)
        gate_grad = jnp.sum(grad * token_out, axis=-1, keepdims=True)
        logit_low = (router_probs * (gate_grad * hot - gate_grad * gate)).astype(BF16)
        router_part = contract(logit_low, ffn_ref[j], 0, 0)
        input_grad = input_grad + contract(logit_low, router, 1, 1)
        inverse = lax.rsqrt(jnp.mean(hidden * hidden, axis=-1, keepdims=True) + EPS)
        r = hidden * inverse
        u = input_grad * gains[1:2, :]
        hidden_grad[j] = grad + (u - r * jnp.mean(u * r, axis=-1, keepdims=True)) * inverse
        gain_part = jnp.sum(input_grad * r, axis=0, keepdims=True)
        if j == 0:
            router_grad[...] = router_part
            gain_grad[...] = gain_part
        else:
            router_grad[...] += router_part
            gain_grad[...] += gain_part

    for j in range(per):
        tokens_out(j)
    for copy in stores:
        copy.wait()


def run_experts(
    heads_all, own_tok, wo_all, weights, gains, cot_own, ids_all, up, down, seqs, dps, per_expert, capacity
):
    per, span, width = own_tok.shape
    local = wo_all.shape[1]
    groups = seqs * dps
    height = up_to(up.shape[0] * per_expert, 16)
    spread = weights.shape[1] - 3 * local // 128 * 128
    rows = (groups, 2, height, width)
    return pl.pallas_call(
        functools.partial(experts_kernel, seqs, dps, per_expert, capacity, local),
        out_shape=(
            jax.ShapeDtypeStruct((per, span, width), BF16),
            jax.ShapeDtypeStruct((per, span, width), F32),
            jax.ShapeDtypeStruct((spread, width), F32),
            jax.ShapeDtypeStruct((1, width), F32),
            jax.ShapeDtypeStruct(up.shape, BF16),
            jax.ShapeDtypeStruct(down.shape, BF16),
        ),
        in_specs=[VMEM] * 7 + [ANY] * 2,
        out_specs=[VMEM] * 4 + [ANY] * 2,
        scratch_shapes=[
            pltpu.VMEM(up.shape, BF16),
            pltpu.VMEM(down.shape, BF16),
            pltpu.VMEM(up.shape, F32),
            pltpu.VMEM(down.shape, F32),
            pltpu.VMEM(rows, BF16),
            pltpu.VMEM((2, groups, height, width), BF16),
            pltpu.VMEM((per, groups * height, span), BF16),
            pltpu.VMEM((per, span, groups * height), BF16),
            pltpu.VMEM((per, span, width), F32),
            pltpu.VMEM((per, span, width), BF16),
            pltpu.VMEM((per, span, spread), F32),
            pltpu.VMEM((per, span, 1), F32),
            pltpu.VMEM((per, span, spread), F32),
            pltpu.VMEM((4,) + rows, BF16),
            pltpu.VMEM((2,) + rows, BF16),
            pltpu.VMEM(rows, BF16),
            DMA((3,)),
            DMA((groups,)),
            DMA((groups,)),
            DMA((3, groups)),
            DMA((3, groups)),
            DMA((2, groups)),
            DMA((2, groups)),
            DMA((groups,)),
            DMA((groups,)),
            DMA((groups,)),
            DMA((groups,)),
        ],
        compiler_params=params(collective_id=2),
        name="experts",
    )(heads_all, own_tok, wo_all, weights, gains, cot_own, ids_all, up, down)


def send_home(me, own, home, ls, z_send, z_recv, h_send, h_recv):
    s, seqs, x, core = me.s, me.seqs, me.x, me.c
    per, span, _ = own.shape
    rows = span // PIECES
    lands = [(k, lax.rem(s + core, 2) + 2 * k) for k in range(seqs // 2)]

    def part(c):
        return pl.ds(c * rows, rows)

    def start(c):
        for j in range(per):
            to = me.block(j)
            there = home.at[per * s + x, part(c)]

            @pl.when(to != s)
            def _():
                k = lax.div(s, 2)
                send(own.at[j, part(c)], there, z_send.at[j, c], z_recv.at[k, c], seq=to)

            @pl.when(to == s)
            def _():
                pltpu.make_async_copy(own.at[j, part(c)], there, ls.at[c]).start()

    def pass_on(c):
        for k, source in lands:
            here = home.at[per * source + x, part(c)]

            @pl.when(source == s)
            def _():
                pltpu.make_async_copy(here, here, ls.at[c]).wait()

            @pl.when(source != s)
            def _():
                arrived(here, z_recv.at[k, c])

            send(here, here, h_send.at[0, k, c], h_recv.at[0, k, c], head=me.across)
            send(here, here, h_send.at[1, k, c], h_recv.at[1, k, c], head=me.near)

    def pass_near(c):
        for k, source in lands:
            there = home.at[per * source + 1 - x, part(c)]
            arrived(there, h_recv.at[0, k, c])
            send(there, there, h_send.at[2, k, c], h_recv.at[2, k, c], head=me.near)

    def finish():
        some = own.at[0, part(0)]
        for c in range(PIECES):
            for j in range(per):

                @pl.when(me.block(j) != s)
                def _():
                    pltpu.make_async_copy(some, some, z_send.at[j, c]).wait()

            for k in range(seqs // 2):
                source = lax.rem(s + 1 + core, 2) + 2 * k
                arrived(home.at[per * source + x, part(c)], h_recv.at[1, k, c])
                arrived(home.at[per * source + 1 - x, part(c)], h_recv.at[2, k, c])
                for n in range(3):
                    pltpu.make_async_copy(some, some, h_send.at[n, k, c]).wait()

    return start, pass_on, pass_near, finish


def home_sems(per, seqs):
    return [
        DMA((PIECES,)),
        DMA((per, PIECES)),
        DMA((seqs // 2, PIECES)),
        DMA((3, seqs // 2, PIECES)),
        DMA((3, seqs // 2, PIECES)),
    ]


def add_groups(me, parts, dp_take, seq_take, result, dp_send, dp_recv, seq_send, seq_recv):
    s, d, seqs, dps = me.s, me.d, me.seqs, me.dps
    order = [mod(s + n, seqs) for n in list(range(1, seqs)) + [0]]

    def start():
        for to in order:
            for i in range(1, dps):
                there = mod(d + i, dps)
                send(
                    parts.at[there, to], dp_take.at[i - 1, to], dp_send.at[i - 1, to], dp_recv.at[i - 1, to], dp=there
                )

    def middle():
        for n, to in enumerate(order):
            total = parts[d, to].astype(F32)
            for i in range(1, dps):
                arrived(dp_take.at[i - 1, to], dp_recv.at[i - 1, to])
                total = total + dp_take[i - 1, to].astype(F32)
            parts[d, to] = total.astype(parts.dtype)
            if n < seqs - 1:
                send(parts.at[d, to], seq_take.at[n], seq_send.at[n], seq_recv.at[n], seq=to)

    def end():
        total = parts[d, s].astype(F32)
        for n in range(seqs - 1):
            arrived(seq_take.at[n], seq_recv.at[n])
            total = total + seq_take[n].astype(F32)
        result[...] = total
        some = seq_take.at[0]
        for to in range(seqs):
            for i in range(1, dps):
                pltpu.make_async_copy(some, some, dp_send.at[i - 1, to]).wait()
        for n in range(seqs - 1):
            pltpu.make_async_copy(some, some, seq_send.at[n]).wait()

    return start, middle, end


def group_scratch(seqs, dps, shape, dtype):
    return [
        pltpu.VMEM((dps, seqs) + shape, dtype),
        pltpu.VMEM((max(1, dps - 1), seqs) + shape, dtype),
        pltpu.VMEM((seqs - 1,) + shape, dtype),
    ]


def group_sems(seqs, dps):
    return [DMA((max(1, dps - 1), seqs))] * 2 + [DMA((seqs - 1,))] * 2


PIECES = 2


def back_kernel(
    seqs, dps, heads,
    result, hidden_grad, own_tok, heads_all, wo_all, split_in, probs, attn_input_in, weights, weights_far, gains, router,
    gain_f,
    output, tokens_home, w_sum, small_sum, wo_sum, gain_sum, bias_sum,
    split, attn_input, turned, attn_grad, hsend, grad_all, slot, low_ref, ext, made, x_acc, x_out, x_near, tg,
    wo_part, wo_near, wo_far, w_parts, w_dp, w_seq, w_total, far_parts, far_dp, far_seq, far_sum, last_parts, last_dp, last_seq, last_sum, far_out, far_in,
    wo_parts, wo_dp, wo_seq, g_parts, g_dp, g_seq, r_parts, r_dp, r_seq, r_sum, g_acc,
    bias, bias_out, bias_in, bias_take, small, gsmall,
    ls, p_sem, a_send, a_recv, n_send, n_recv, on_send, on_recv, of_send, of_recv,
    b_send, b_recv, s_send, s_recv, t_send, t_recv, fs, *sems
):
    me = Place(seqs, dps)
    h, s, d = me.h, me.s, me.d
    per, span, width = hidden_grad.shape
    blocks = seqs
    length = blocks * span
    local = heads * HEAD_DIM
    groups = seqs * dps
    shard = width // groups
    padded = w_sum.shape[0]
    buckets = 32
    size = span // PIECES
    others = [(i, j) for i in range(seqs) for j in range(dps) if i or j]
    loads = [pltpu.make_async_copy(split_in, split, ls.at[0]), pltpu.make_async_copy(attn_input_in, attn_input, ls.at[1])]
    for copy in loads:
        copy.start()
    greet(me.group_peers() + [{"head": mod(h + i, 4)} for i in range(1, 4)])
    out_home = send_home(me, result, output, *sems[0:5])
    grad_home = send_home(me, tg, tokens_home, *sems[5:10])
    w_group = add_groups(me, w_parts, w_dp, w_seq, w_total, *sems[10:14])
    wo_group = add_groups(me, wo_parts, wo_dp, wo_seq, wo_sum, *sems[14:18])
    g_group = add_groups(me, g_parts, g_dp, g_seq, gain_sum, *sems[18:22])
    r_group = add_groups(me, r_parts, r_dp, r_seq, r_sum, *sems[22:26])
    far_group = add_groups(me, far_parts, far_dp, far_seq, far_sum, *sems[26:30])
    last_group = add_groups(me, last_parts, last_dp, last_seq, last_sum, *sems[30:34])

    def by_group(whole, parts):
        low = whole.astype(BF16)
        if shard % 16:
            low = contract(squeeze_hot(shard, padded, width, groups), low, 0, 0).astype(BF16)
        for g in range(groups):
            parts[g % dps, g // dps] = low[g * padded : (g + 1) * padded, :]

    def fetch(group, head):
        turn = head % 2 if group else 1 - head % 2
        return turn, pltpu.make_async_copy(probs.at[group, head], slot.at[turn], p_sem.at[turn])

    def put(ref, grad):
        for head in range(heads):
            ref[head, :, :HEAD_DIM] = grad[:, head * HEAD_DIM : (head + 1) * HEAD_DIM]

    def block_rows(block):
        return pl.ds(pl.multiple_of(block * span, span), span)

    fetch(1, 0)[1].start()
    out_home[0](0)
    out_home[0](1)
    hsend[...] = jnp.zeros_like(hsend)
    attn_grad[...] = hidden_grad[...].astype(BF16)
    for group, (own, other) in ((1, (me.across, me.near_across)), (0, (h, me.near))):
        for j in range(per):
            rows = block_rows(me.block(j))
            put(hsend.at[group, j], contract(attn_grad[j], wo_all[other], 1, 1).astype(BF16))
            send(
                hsend.at[group, j],
                grad_all.at[group, :, rows, :],
                a_send.at[group, j],
                a_recv.at[group, j],
                head=me.near,
            )
            put(grad_all.at[group, :, rows, :], contract(attn_grad[j], wo_all[own], 1, 1).astype(BF16))
    for k, q in enumerate((me.near_across, me.near, me.across, h)):
        total = jnp.zeros((local, width), F32)
        for j in range(per):
            total = total + contract(heads_all[q, j], attn_grad[j], 0, 0)
        wo_part[k] = total.astype(BF16)
        if k < 2:
            send(wo_part.at[k], wo_near.at[k], on_send.at[k], on_recv.at[k], head=me.near)
    by_group(router[...].T, r_parts)
    r_group[0]()
    for copy in loads:
        copy.wait()
    turned[...] = attn_input[...].T
    ext[...] = jnp.zeros_like(ext)
    made[...] = jnp.zeros_like(made)

    def wo_across():
        arrived(wo_near.at[0], on_recv.at[0])
        wo_part[2] = (wo_part[2].astype(F32) + wo_near[0].astype(F32)).astype(BF16)
        send(wo_part.at[2], wo_far, of_send, of_recv, head=me.across)

    def wo_total():
        arrived(wo_near.at[1], on_recv.at[1])
        arrived(wo_far, of_recv)
        total = (wo_part[3].astype(F32) + wo_near[1].astype(F32) + wo_far[...].astype(F32)).astype(BF16)
        for g in range(groups):
            hot = spread_hot(g * shard, shard, width)
            wo_parts[g % dps, g // dps] = contract(total, hot, 1, 1).astype(BF16)
        wo_group[0]()

    def cut(c):
        return pl.ds(c * size, size)

    def x_partial():
        x_acc[...] += contract(made[...], weights[...], 1, 1)
        for c in range(PIECES):
            for j in range(per):
                rows = pl.ds(pl.multiple_of(me.block(j, 1 - me.c) * span + c * size, size), size)
                x_out[j, cut(c)] = x_acc[rows, :].astype(BF16)
                send(x_out.at[j, cut(c)], x_near.at[j, cut(c)], n_send.at[j, c], n_recv.at[j, c], head=me.near)

    def x_total(c):
        for j in range(per):
            arrived(x_near.at[j, cut(c)], n_recv.at[j, c])
            rows = pl.ds(pl.multiple_of(me.block(j) * span + c * size, size), size)
            grad = x_acc[rows, :] + x_near[j, cut(c)].astype(F32)
            v = own_tok[j, cut(c)].astype(F32)
            inverse = lax.rsqrt(jnp.mean(v * v, axis=-1, keepdims=True) + EPS)
            r = v * inverse
            u = grad * gains[0:1, :]
            back = (u - r * jnp.mean(u * r, axis=-1, keepdims=True)) * inverse
            tg[j, cut(c)] = (hidden_grad[j, cut(c)] + back).astype(BF16)
            g_acc[0:1, :] += jnp.sum(grad * r, axis=0, keepdims=True)
        grad_home[0](c)

    def attention(group, service):
        for j in range(per):
            rows = block_rows(me.block(j, 1 - me.c))
            arrived(grad_all.at[group, :, rows, :], a_recv.at[group, j])
        for head in range(heads):
            turn, copy = fetch(group, head)
            copy.wait()
            if head < heads - 1:
                fetch(group, head + 1)[1].start()
            elif group:
                fetch(0, 0)[1].start()
            key, value = split[group, heads + head, :, :HEAD_DIM], split[group, 2 * heads + head, :, :HEAD_DIM]
            for block in range(blocks):
                rows = slice(block * span, (block + 1) * span)
                grad = grad_all[group, head, rows, :HEAD_DIM]
                wide = slot[turn, rows, :].astype(F32)
                prob_grad = contract(grad, value, 1, 1)
                delta = jnp.sum(wide * prob_grad, axis=-1, keepdims=True)
                score_grad = wide * (prob_grad - delta)
                first = (blocks - 1 - block) * span
                ext[head, :, first : first + length] += score_grad
                low = score_grad.astype(BF16)
                low_ref[rows, :] = low
                cols = slice(head * HEAD_DIM, (head + 1) * HEAD_DIM)
                made[rows, cols] = jnp.dot(low, key, preferred_element_type=F32).astype(BF16)
            for kind, (narrow, wide_ref) in enumerate(
                ((split[group, head, :, :HEAD_DIM], low_ref), (grad_all[group, head, :, :HEAD_DIM], slot.at[turn]))
            ):
                first = (kind + 1) * local + head * HEAD_DIM
                made[:, first : first + HEAD_DIM] = contract(narrow, wide_ref[...], 0, 0).T.astype(BF16)
            for act in service[head]:
                act()

    def weight_grad(first, last):
        pieces = []
        for kind in range(3):
            at = kind * local
            part = made[:, at + first * HEAD_DIM : at + last * HEAD_DIM]
            pieces.append(jnp.dot(turned[...], part, preferred_element_type=F32))
        lanes = 3 * (last - first) * HEAD_DIM
        if lanes % 128:
            pieces.append(jnp.zeros((width, 128 - lanes % 128), F32))
        return jnp.concatenate(pieces, axis=1)

    def bias_rows(into):
        turn = lax.broadcasted_iota(jnp.int32, (4 * span, 128), 0)
        bucket = bucket_of(jnp.where(turn < 3 * span, turn, turn - 4 * span) - span, buckets)
        hot = (bucket == lax.broadcasted_iota(jnp.int32, (4 * span, 128), 1)).astype(F32)
        lane = lax.broadcasted_iota(jnp.int32, (1, 128), 1)
        head_row = lax.broadcasted_iota(jnp.int32, (8, 4 * span), 0)
        diagonals = jnp.zeros((8, 4 * span), F32)
        far_row = lax.broadcasted_iota(jnp.int32, (8, 128), 0)
        far = jnp.zeros((8, 128), F32)
        for head in range(heads):
            eight = jnp.zeros((8, 4 * span), F32)
            for group in range(span // 8):
                piece = ext[head, group * 8 : (group + 1) * 8, 2 * span : 5 * span]
                piece = jnp.concatenate([piece, jnp.zeros((8, span), F32)], axis=1)
                eight = eight + pltpu.roll(piece, (4 * span - 8 * group) % (4 * span), 1)
            one = jnp.zeros((8, 4 * span), F32)
            for i in range(8):
                line = jnp.broadcast_to(eight[i : i + 1, :], (8, 4 * span))
                one = one + pltpu.roll(line, (4 * span - i) % (4 * span), 1)
            diagonals = jnp.where(head_row == head, one, diagonals)
            left, right = jnp.sum(ext[head, :, : 2 * span]), jnp.sum(ext[head, :, 5 * span :])
            sides = jnp.where(lane == buckets // 2 - 1, left, jnp.where(lane == buckets - 1, right, 0.0))
            far = jnp.where(far_row == head, sides, far)
        into[...] = far + jnp.dot(diagonals, hot, preferred_element_type=F32, precision=lax.Precision.HIGHEST)

    def router_total():
        r_group[2]()
        small[0] = r_sum[...]
        for i in range(1, 4):
            send(small.at[0], small.at[i], s_send.at[i - 1], s_recv.at[i - 1], head=mod(h + i, 4))

    g_acc[...] = jnp.zeros_like(g_acc)
    g_acc[1:2, :] = gain_f[...]
    def far_weights():
        by_group(weight_grad(0, heads - 1), far_parts)
        far_group[0]()

    def far_weights():
        by_group(weight_grad(0, heads - 1), far_parts)
        far_group[0]()

    attention(1, ((wo_across,), (far_weights, r_group[1]), (wo_total,)))
    by_group(weight_grad(heads - 1, heads), last_parts)
    last_group[0]()
    out_home[1](0)
    x_acc[...] = contract(made[...], weights_far[...], 1, 1)
    far_group[1]()
    out_home[1](1)
    bias_rows(bias_out)
    to_bias = send(bias_out, bias_in, fs.at[0], fs.at[1], head=me.across)
    ext[...] = jnp.zeros_like(ext)
    attention(
        0,
        (
            (),
            (wo_group[1], last_group[1]),
            (router_total,),
        ),
    )
    x_partial()
    x_total(0)
    x_total(1)
    by_group(jnp.dot(turned[...], made[:, : w_parts.shape[-1]], preferred_element_type=F32), w_parts)
    w_group[0]()
    g_rows = g_acc[...].astype(BF16)
    for g in range(groups):
        g_parts[g % dps, g // dps] = contract(g_rows, spread_hot(g * shard, shard, width), 1, 1)
    g_group[0]()
    bias_rows(bias)
    arrived(bias_in, fs.at[1])
    bias[...] += bias_in[...]
    for n, (i, j) in enumerate(others):
        send(bias, bias_take.at[n], b_send.at[n], b_recv.at[n], seq=mod(s + i, seqs), dp=mod(d + j, dps))
    out_home[2](0)
    out_home[2](1)
    grad_home[1](0)
    w_group[1]()
    grad_home[1](1)
    g_group[1]()
    far_group[2]()
    last_group[2]()
    most, last = far_sum.shape[1], last_sum.shape[1]
    far_out[:, :most] = far_sum[...].astype(BF16)
    far_out[:, most:] = last_sum[...].astype(BF16)
    to_far = send(far_out, far_in, fs.at[2], fs.at[3], head=me.across)
    g_group[2]()
    gsmall[0] = gain_sum[...]
    for i in range(1, 4):
        send(gsmall.at[0], gsmall.at[i], t_send.at[i - 1], t_recv.at[i - 1], head=mod(h + i, 4))
    wo_group[2]()
    total = bias[...]
    for n in range(len(others)):
        arrived(bias_take.at[n], b_recv.at[n])
        total = total + bias_take[n]
    bias_sum[...] = total
    grad_home[2](0)
    grad_home[2](1)
    w_group[2]()
    arrived(far_in, fs.at[3])
    first_heads, last_head = far_in[:, :most].astype(F32), far_in[:, most:].astype(F32)
    many = (heads - 1) * HEAD_DIM
    for kind in range(3):
        at = kind * local
        into = slice(at, at + many)
        w_sum[:, into] = w_total[:, into] + first_heads[:, kind * many : (kind + 1) * many]
        into = slice(at + many, at + local)
        w_sum[:, into] = w_total[:, into] + last_head[:, kind * HEAD_DIM : (kind + 1) * HEAD_DIM]
    total, gain_total = small[0], gsmall[0]
    for i in range(1, 4):
        arrived(small.at[i], s_recv.at[i - 1])
        arrived(gsmall.at[i], t_recv.at[i - 1])
        total = total + small[i]
        gain_total = gain_total + gsmall[i]
    small_sum[...] = total
    gain_sum[...] = gain_total
    out_home[3]()
    grad_home[3]()
    to_bias.wait_send()
    to_far.wait_send()
    for j in range(per):
        for group in range(2):
            pltpu.make_async_copy(hsend.at[0, 0], hsend.at[0, 0], a_send.at[group, j]).wait()
        some = x_near.at[0, cut(0)]
        for c in range(PIECES):
            pltpu.make_async_copy(some, some, n_send.at[j, c]).wait()
    for k in range(2):
        pltpu.make_async_copy(wo_far, wo_far, on_send.at[k]).wait()
    pltpu.make_async_copy(wo_far, wo_far, of_send).wait()
    for i in range(3):
        pltpu.make_async_copy(small.at[0], small.at[0], s_send.at[i]).wait()
        pltpu.make_async_copy(gsmall.at[0], gsmall.at[0], t_send.at[i]).wait()
    for n in range(len(others)):
        pltpu.make_async_copy(bias, bias, b_send.at[n]).wait()


def back_pass(
    result, hidden_grad, own_tok, heads_all, wo_all, split, probs, attn_input, weights, weights_far, gains, router, gain_f,
    seqs, dps
):
    per, span, width = hidden_grad.shape
    length = seqs * span
    heads = probs.shape[1]
    local = heads * HEAD_DIM
    groups = seqs * dps
    shard = width // groups
    padded = up_to(shard, 16)
    lanes = weights.shape[1]
    spread = router.shape[0]
    all_three = up_to(3 * local, 128)
    most, last = up_to(3 * (heads - 1) * HEAD_DIM, 128), up_to(3 * HEAD_DIM, 128)
    block = (span, width)
    return pl.pallas_call(
        functools.partial(back_kernel, seqs, dps, heads),
        out_shape=(
            jax.ShapeDtypeStruct((per * seqs,) + block, BF16),
            jax.ShapeDtypeStruct((per * seqs,) + block, BF16),
            jax.ShapeDtypeStruct((padded, 3 * local), F32),
            jax.ShapeDtypeStruct((padded, spread), F32),
            jax.ShapeDtypeStruct((local, 128), F32),
            jax.ShapeDtypeStruct((8, 128), F32),
            jax.ShapeDtypeStruct((8, 128), F32),
        ),
        in_specs=[VMEM] * 5 + [ANY] * 3 + [VMEM] * 5,
        out_specs=[ANY] * 2 + [VMEM] * 5,
        scratch_shapes=[
            pltpu.VMEM(split.shape, BF16),
            pltpu.VMEM(attn_input.shape, BF16),
            pltpu.VMEM(attn_input.shape[::-1], BF16),
            pltpu.VMEM((per,) + block, BF16),
            pltpu.VMEM((2, per, heads, span, 128), BF16),
            pltpu.VMEM((2, heads, length, 128), BF16),
            pltpu.VMEM((2, length, length), BF16),
            pltpu.VMEM((length, length), BF16),
            pltpu.VMEM((heads, span, 7 * span), F32),
            pltpu.VMEM((length, lanes), BF16),
            pltpu.VMEM((length, width), F32),
            pltpu.VMEM((per,) + block, BF16),
            pltpu.VMEM((per,) + block, BF16),
            pltpu.VMEM((per,) + block, BF16),
            pltpu.VMEM((4, local, width), BF16),
            pltpu.VMEM((2, local, width), BF16),
            pltpu.VMEM((local, width), BF16),
        ]
        + group_scratch(seqs, dps, (padded, all_three), BF16)
        + [pltpu.VMEM((padded, all_three), F32)]
        + group_scratch(seqs, dps, (padded, most), BF16)
        + [pltpu.VMEM((padded, most), F32)]
        + group_scratch(seqs, dps, (padded, last), BF16)
        + [pltpu.VMEM((padded, last), F32)]
        + [
            pltpu.VMEM((padded, most + last), BF16),
            pltpu.VMEM((padded, most + last), BF16),
        ]
        + group_scratch(seqs, dps, (local, 128), BF16)
        + group_scratch(seqs, dps, (8, 128), F32)
        + group_scratch(seqs, dps, (padded, spread), BF16)
        + [
            pltpu.VMEM((padded, spread), F32),
            pltpu.VMEM((8, width), F32),
            pltpu.VMEM((8, 128), F32),
            pltpu.VMEM((8, 128), F32),
            pltpu.VMEM((8, 128), F32),
            pltpu.VMEM((groups - 1, 8, 128), F32),
            pltpu.VMEM((4, padded, spread), F32),
            pltpu.VMEM((4, 8, 128), F32),
            DMA((2,)),
            DMA((2,)),
            DMA((2, per)),
            DMA((2, per)),
            DMA((per, PIECES)),
            DMA((per, PIECES)),
            DMA((2,)),
            DMA((2,)),
            DMA(()),
            DMA(()),
            DMA((groups - 1,)),
            DMA((groups - 1,)),
            DMA((3,)),
            DMA((3,)),
            DMA((3,)),
            DMA((3,)),
            DMA((4,)),
        ]
        + home_sems(per, seqs) * 2
        + group_sems(seqs, dps) * 6,
        compiler_params=params(collective_id=4),
        name="back",
    )(
        result, hidden_grad, own_tok, heads_all, wo_all, split, probs, attn_input, weights, weights_far, gains, router, gain_f
    )


PARTS = 4


def settle_kernel(count, *refs):
    large, (w, router, wo, gain, bias) = refs[:count], refs[count : count + 5]
    refs = refs[count + 5 :]
    large_out, (wq_out, wk_out, wv_out, wo_out, router_out, gain_a, gain_f, bias_out) = refs[:count], refs[count : count + 8]
    refs = refs[count + 8 :]
    held, wide, sems = refs[:count], refs[count : 2 * count], refs[2 * count]
    copies = []
    for n in range(count):
        size = large[n].shape[0] // PARTS
        for k in range(PARTS):
            part = pl.ds(k * size, size)
            come = pltpu.make_async_copy(large[n].at[part], held[n].at[part], sems.at[0, n, k])
            rounded = large[n].dtype == large_out[n].dtype
            source = held[n] if rounded else wide[n]
            go = pltpu.make_async_copy(source.at[part], large_out[n].at[part], sems.at[1, n, k])
            come.start()
            copies.append((come, go, None if rounded else (wide[n], held[n], slice(k * size, (k + 1) * size))))
    shard, local = wq_out.shape
    for n, ref in enumerate((wq_out, wk_out, wv_out)):
        ref[...] = w[:shard, n * local : (n + 1) * local]
    wo_out[...] = wo[:, :shard]
    spread = router.shape[1]
    at = 3 * local % 128
    turned = jnp.concatenate([router[...], jnp.zeros((128 - router.shape[0], spread), F32)], axis=0).T
    router_out[...] = turned[at : at + router_out.shape[0], :shard]
    gain_a[...] = gain[0:1, :shard]
    gain_f[...] = gain[1:2, :shard]
    bias_out[...] = bias[: bias_out.shape[0], : bias_out.shape[1]]
    for come, go, widen in copies:
        come.wait()
        if widen is not None:
            into, source, part = widen
            into[part] = source[part].astype(F32)
        go.start()
    for _, go, _ in copies:
        go.wait()


def settle(large, types, small, shapes):
    count = len(large)
    return pl.pallas_call(
        functools.partial(settle_kernel, count),
        out_shape=tuple(jax.ShapeDtypeStruct(x.shape, kind) for x, kind in zip(large, types))
        + tuple(jax.ShapeDtypeStruct(shape, F32) for shape in shapes),
        in_specs=[ANY] * count + [VMEM] * len(small),
        out_specs=[ANY] * count + [VMEM] * len(shapes),
        scratch_shapes=[pltpu.VMEM(x.shape, x.dtype) for x in large]
        + [pltpu.VMEM(x.shape if x.dtype != kind else (8, 128), kind) for x, kind in zip(large, types)]
        + [DMA((2, count, PARTS))],
        compiler_params=pltpu.CompilerParams(vmem_limit_bytes=60 * 2**20),
        name="settle",
    )(*large, *small)


def up_to(value, unit):
    return -(-value // unit) * unit


def body(
    tokens,
    lengths,
    expert_ids,
    attention_gain,
    query_weight,
    key_weight,
    value_weight,
    output_weight,
    position_bias,
    feedforward_gain,
    router_weight,
    expert_up,
    expert_down,
    cotangent,
):
    seqs, dps = lax.axis_size("seq"), lax.axis_size("dp")
    groups = seqs * dps
    seq_local, span, width = tokens.shape
    per = seq_local // seqs
    local_width = query_weight.shape[1]
    bucket_count, heads = position_bias.shape
    experts = router_weight.shape[1]
    shard = query_weight.shape[0]
    capacity = max(2, (5 * span + 4 * experts - 1) // (4 * experts))
    attn_input, weights, weights_far, split, probs, heads_all, own_tok, cot_own, out_weight, gains, ids_all = front(
        tokens,
        cotangent,
        query_weight,
        key_weight,
        value_weight,
        output_weight,
        router_weight.T,
        attention_gain[None, :],
        feedforward_gain[None, :],
        expert_ids.reshape(seq_local, span),
        position_bias.T,
        lengths,
        seqs,
        dps,
    )
    result, hidden_grad, router_grad, gain_two_grad, up_grad, down_grad = run_experts(
        heads_all,
        own_tok,
        out_weight,
        weights,
        gains,
        cot_own,
        ids_all,
        expert_up,
        expert_down,
        seqs,
        dps,
        per * capacity,
        capacity,
    )
    output, tokens_grad, w_sum, small_sum, wo_sum, gain_sum, bias_sum = back_pass(
        result,
        hidden_grad,
        own_tok,
        heads_all,
        out_weight,
        split,
        probs,
        attn_input,
        weights,
        weights_far,
        gains,
        router_grad,
        gain_two_grad,
        seqs,
        dps,
    )
    output, tokens_grad, up_grad, down_grad, *small = settle(
        (output, tokens_grad, up_grad.reshape(-1, up_grad.shape[-1]), down_grad.reshape(-1, down_grad.shape[-1])),
        (BF16, BF16, F32, F32),
        (w_sum, small_sum, wo_sum, gain_sum, bias_sum),
        ((shard, local_width),) * 3
        + ((local_width, shard), (experts, shard), (1, shard), (1, shard), (heads, bucket_count)),
    )
    return (
        output,
        tokens_grad,
        small[5][0],
        small[0],
        small[1],
        small[2],
        small[3],
        small[7].T,
        small[6][0],
        small[4].T,
        up_grad.reshape(expert_up.shape),
        down_grad.reshape(expert_down.shape),
    )


def solution(mesh):
    placed = (
        P("dp", "seq", None),
        P("dp"),
        P("dp", "seq", None),
        P(("seq", "dp")),
        P(("seq", "dp"), "head"),
        P(("seq", "dp"), "head"),
        P(("seq", "dp"), "head"),
        P("head", ("seq", "dp")),
        P(None, "head"),
        P(("seq", "dp")),
        P(("seq", "dp"), None),
        P(("seq", "dp"), None, "head"),
        P(("seq", "dp"), "head", None),
        P("dp", "seq", None),
    )
    return jax.shard_map(
        body,
        mesh=mesh,
        in_specs=placed,
        out_specs=(
            P("dp", "seq", None),
            P("dp", "seq", None),
            P(("seq", "dp")),
            P(("seq", "dp"), "head"),
            P(("seq", "dp"), "head"),
            P(("seq", "dp"), "head"),
            P("head", ("seq", "dp")),
            P(None, "head"),
            P(("seq", "dp")),
            P(("seq", "dp"), None),
            P(("seq", "dp"), None, "head"),
            P(("seq", "dp"), "head", None),
        ),
        check_vma=False,
    )
```

```python
import functools

import jax
import jax.numpy as jnp
import numpy as np
from jax import lax
from jax.experimental import pallas as pl
from jax.experimental.pallas import tpu as pltpu
from jax.sharding import PartitionSpec as P

HEAD_DIM = 64
EPS = 1e-06
bucket_edges = np.array([1, 2, 3, 4, 5, 6, 7, 8, 12, 16, 23, 32, 46, 64, 91], np.int32)
ANY = pl.BlockSpec(memory_space=pl.ANY)
VMEM = pl.BlockSpec(memory_space=pltpu.VMEM)
MESH = pl.DeviceIdType.MESH
DMA = pltpu.SemaphoreType.DMA
F32 = jnp.float32
BF16 = jnp.bfloat16


def bucket_of(offset, bucket_count):
    distance = jnp.abs(offset)
    magnitude = jnp.zeros_like(offset)
    for edge in bucket_edges:
        magnitude = magnitude + (distance >= int(edge)).astype(jnp.int32)
    return magnitude + bucket_count // 2 * (offset > 0).astype(jnp.int32)


def send(src, dst, send_sem, recv_sem, **device):
    copy = pltpu.make_async_remote_copy(
        src_ref=src,
        dst_ref=dst,
        send_sem=send_sem,
        recv_sem=recv_sem,
        device_id=device,
        device_id_type=MESH,
    )
    copy.start()
    return copy


def arrived(ref, recv_sem):
    pltpu.make_async_copy(ref, ref, recv_sem).wait()


def greet(devices):
    barrier = pltpu.get_barrier_semaphore()
    for device in devices:
        pl.semaphore_signal(barrier, inc=1, device_id=device, device_id_type=MESH)
    pl.semaphore_wait(barrier, len(devices))


def mod(value, size):
    return lax.rem(value + 4 * size, size)


class Place:
    def __init__(self, seqs, dps):
        self.h, self.s, self.d = lax.axis_index("head"), lax.axis_index("seq"), lax.axis_index("dp")
        self.seqs, self.dps = seqs, dps
        self.x, self.c = lax.div(self.h, 2), lax.rem(self.h, 2)
        self.near = self.h + 1 - 2 * self.c
        self.across = mod(self.h + 2, 4)
        self.near_across = lax.rem(self.across, 2) * -2 + self.across + 1

    def seq_peers(self):
        return [{"seq": mod(self.s + i, self.seqs)} for i in range(1, self.seqs)]

    def dp_peers(self):
        return [{"dp": mod(self.d + i, self.dps)} for i in range(1, self.dps)]

    def head_pair(self):
        return [{"head": self.near}, {"head": self.across}]

    def group_peers(self):
        return [
            {"seq": mod(self.s + i, self.seqs), "dp": mod(self.d + j, self.dps)}
            for i in range(self.seqs)
            for j in range(self.dps)
            if i or j
        ]

    def block(self, j, core=None):
        return lax.rem((self.c if core is None else core) + self.s, 2) + 2 * j


def params(**more):
    return pltpu.CompilerParams(has_side_effects=True, vmem_limit_bytes=60 * 2**20, **more)


def gather_groups(me, own, whole, z_send, z_recv, dp_send, dp_recv, far=None, far_send=None, far_recv=None):
    s, d, seqs, dps = me.s, me.d, me.seqs, me.dps

    def spread(src, source):
        for i in range(1, dps):
            send(
                src,
                whole.at[source, d],
                dp_send.at[i - 1, source],
                dp_recv.at[i - 1, source],
                dp=mod(d + i, dps),
            )

    def onward(src, source, dp):
        if far is not None:
            send(src, far.at[source, dp], far_send.at[source, dp], far_recv.at[source, dp], head=me.across)

    def start():
        for i in range(1, seqs):
            send(own, whole.at[s, d], z_send.at[i - 1], z_recv.at[i - 1], seq=mod(s + i, seqs))
        spread(own, s)
        onward(own, s, d)

    def relay(i):
        source = mod(s - i, seqs)
        here = whole.at[source, d]
        arrived(here, z_recv.at[i - 1])
        spread(here, source)
        onward(here, source, d)

    def finish():
        for i in range(1, dps):
            for source in range(seqs):
                there = mod(d - i, dps)
                arrived(whole.at[source, there], dp_recv.at[i - 1, source])
                onward(whole.at[source, there], source, there)
                pltpu.make_async_copy(own, own, dp_send.at[i - 1, source]).wait()
        for i in range(1, seqs):
            pltpu.make_async_copy(own, own, z_send.at[i - 1]).wait()

    def take_far():
        for source in range(seqs):
            for dp in range(dps):
                arrived(far.at[source, dp], far_recv.at[source, dp])

    def finish_far():
        for source in range(seqs):
            for dp in range(dps):
                pltpu.make_async_copy(own, own, far_send.at[source, dp]).wait()

    return start, relay, finish, take_far, finish_far


def gather_sems(seqs, dps):
    return [
        DMA((seqs - 1,)),
        DMA((seqs - 1,)),
        DMA((max(1, dps - 1), seqs)),
        DMA((max(1, dps - 1), seqs)),
    ]


def spread_hot(at, shard, width):
    row = lax.broadcasted_iota(jnp.int32, (128, width), 0)
    column = lax.broadcasted_iota(jnp.int32, (128, width), 1)
    return ((column == row + at) & (row < shard)).astype(BF16)


def squeeze_hot(shard, padded, rows, count):
    row = lax.broadcasted_iota(jnp.int32, (rows, count * padded), 0)
    column = lax.broadcasted_iota(jnp.int32, (rows, count * padded), 1)
    inside = lax.rem(column, padded)
    return ((lax.div(column, padded) * shard + inside == row) & (inside < shard)).astype(BF16)


def front_kernel(
    seqs, dps, heads,
    tok, cot, wq, wk, wv, wo, router, gain_a, gain_f, ids_own, table, lengths,
    attn_input_out, weights_out, far_out, split_out, probs, heads_all, own_tok, cot_own, wo_all, gains, ids_all,
    attn_input, weights, weights_far, split, tok_all, pack, pack_all, far_all, wo_pad, wo_parts, tile, tile_all, table_own, table_far,
    ext, slot, out,
    p_sem, ls, os, z_send, z_recv, h_send, h_recv, c_send, c_recv, a_send, a_recv, w_send, w_recv, i_send, i_recv,
    f_send, f_recv, t_sem, *line
):
    me = Place(seqs, dps)
    h, s, d, x, c = me.h, me.s, me.d, me.x, me.c
    blocks, span, width = tok_all.shape
    per = own_tok.shape[0]
    length = blocks * span
    shard, local = wq.shape
    groups = seqs * dps
    experts = router.shape[0]
    half = span // 2
    own_half = pl.ds(pl.multiple_of(c * half, half), half)
    other_half = pl.ds(pl.multiple_of((1 - c) * half, half), half)
    pack[...] = jnp.zeros_like(pack)
    for n, ref in enumerate((wq, wk, wv)):
        pack[:shard, n * local : (n + 1) * local] = ref[...]
    same = lax.broadcasted_iota(jnp.int32, (experts, experts), 0) == lax.broadcasted_iota(jnp.int32, (experts, experts), 1)
    pack[:shard, 3 * local : 3 * local + experts] = contract(router[...], same.astype(BF16), 0, 0).astype(BF16)
    wo_pad[...] = jnp.zeros_like(wo_pad)
    wo_pad[:, :shard] = wo[...]
    tile[...] = jnp.zeros_like(tile)
    tile[0:1, :shard] = gain_a[...].astype(F32)
    tile[1:2, :shard] = gain_f[...].astype(F32)
    buckets = table.shape[1]
    table_own[...] = jnp.zeros_like(table_own)
    table_own[:heads, :buckets] = table[...].astype(F32)
    own_copies = [
        pltpu.make_async_copy(pack, pack_all.at[s, d], ls.at[0]),
        pltpu.make_async_copy(tile, tile_all.at[s, d], ls.at[1]),
        pltpu.make_async_copy(wo_pad, wo_parts.at[s, d], ls.at[2]),
        pltpu.make_async_copy(ids_own, ids_all.at[s], ls.at[3]),
        pltpu.make_async_copy(tok.at[per * s + x], tok_all.at[s], ls.at[4]),
    ]
    for copy in own_copies:
        copy.start()

    @pl.when(c == 0)
    def _():
        pltpu.make_async_copy(cot.at[per * s + x], cot_own.at[lax.div(s, 2)], ls.at[5]).start()

    greet(
        me.seq_peers()
        + [{"head": me.near} | peer for peer in me.seq_peers()]
        + me.dp_peers()
        + [{"head": mod(h + i, 4)} for i in range(1, 4)]
    )
    packs = gather_groups(me, pack, pack_all, *line[0:4], far_all, f_send, f_recv)
    tiles = gather_groups(me, tile, tile_all, *line[4:8])
    outs = gather_groups(me, wo_pad, wo_parts, *line[8:12])
    packs[0]()
    tiles[0]()
    to_table = send(table_own, table_far, t_sem.at[0], t_sem.at[1], head=me.across)
    for i in range(1, seqs):
        send(ids_own, ids_all.at[s], i_send.at[i - 1], i_recv.at[i - 1], seq=mod(s + i, seqs))
    for i in range(1, seqs):
        to = mod(s + i, seqs)
        send(tok.at[per * to + x, own_half], tok_all.at[s, own_half], z_send.at[i - 1], z_recv.at[i - 1], seq=to)

    def send_cotangent():
        for i in range(1, seqs):
            to = mod(s + i, seqs)
            target = jnp.where(lax.rem(s + to, 2) == c, h, me.near)
            j = lax.div(s, 2)
            send(
                cot.at[per * to + x, own_half],
                cot_own.at[j, own_half],
                c_send.at[i - 1],
                c_recv.at[j, c],
                head=target,
                seq=to,
            )

    def build_bias(rows):
        turn = lax.broadcasted_iota(jnp.int32, (128, 4 * span), 1)
        bucket = bucket_of(jnp.where(turn < 3 * span, turn, turn - 4 * span) - span, buckets)
        hot = (bucket == lax.broadcasted_iota(jnp.int32, (128, 4 * span), 0)).astype(BF16)
        bias_rows = jnp.dot(rows[...].astype(BF16), hot, preferred_element_type=F32)
        for head in range(heads):
            row = bias_rows[head : head + 1]
            rolled = pltpu.roll(jnp.broadcast_to(row, (span, 4 * span)), 0, 1, stride=1, stride_axis=0)
            ext[head, :, 2 * span : 5 * span] = rolled[:, : 3 * span]
            ext[head, :, : 2 * span] = jnp.broadcast_to(row[:, 0:1], (span, 2 * span))
            ext[head, :, 5 * span :] = jnp.broadcast_to(row[:, 3 * span - 1 : 3 * span], (span, 2 * span))

    def whole_weights(parts, into):
        if shard % 16:
            whole = parts[...].reshape(groups * pack.shape[0], pack.shape[1])
            hot = squeeze_hot(shard, pack.shape[0], width, groups)
            into[...] = jnp.dot(hot, whole, preferred_element_type=F32).astype(BF16)
        else:
            into[...] = parts[...].reshape(width, pack.shape[1])

    def assemble():
        whole_weights(pack_all, weights)
        row = jnp.zeros((8, width), F32)
        for g in range(groups):
            piece = tile_all[g // dps, g % dps].astype(BF16)
            row = row + jnp.dot(piece, spread_hot(g * shard, shard, width), preferred_element_type=F32)
        gains[...] = row

    def project(group, block):
        rows = pl.ds(pl.multiple_of(block * span, span), span)
        if group == 0:
            v = tok_all[block].astype(F32)
            normed = v * lax.rsqrt(jnp.mean(v * v, axis=-1, keepdims=True) + EPS) * gains[0:1, :]
            attn_input[rows, :] = normed.astype(BF16)
        which = weights if group == 0 else weights_far
        parts = jnp.dot(attn_input[rows, :], which[...], preferred_element_type=F32).astype(BF16)
        for n in range(3 * heads):
            split[group, n, rows, :HEAD_DIM] = parts[:, n * HEAD_DIM : (n + 1) * HEAD_DIM]

    split[...] = jnp.zeros_like(split)
    build_bias(table_own)
    for i in range(1, seqs):
        packs[1](i)
        tiles[1](i)
    far_first = [i for i in range(1, seqs) if i != 2] + [2]

    def pass_own(i):
        here = tok_all.at[mod(s - i, seqs), own_half]
        arrived(here, z_recv.at[i - 1])
        send(here, here, h_send.at[i - 1], h_recv.at[i - 1], head=me.near)

    for copy in own_copies:
        copy.wait()
    packs[2]()
    tiles[2]()
    assemble()
    project(0, s)
    for i in far_first:
        pass_own(i)
    outs[0]()
    for i in far_first:
        source = mod(s - i, seqs)
        arrived(tok_all.at[source, other_half], h_recv.at[i - 1])
        project(0, source)
    kept = [
        pltpu.make_async_copy(attn_input, attn_input_out, ls.at[6]),
        pltpu.make_async_copy(split.at[0], split_out.at[0], ls.at[7]),
        pltpu.make_async_copy(weights, weights_out, ls.at[8]),
    ]
    kept += [pltpu.make_async_copy(tok_all.at[me.block(j)], own_tok.at[j], ls.at[9 + j]) for j in range(per)]
    for copy in kept:
        copy.start()
    late = [
        pltpu.make_async_copy(split.at[1], split_out.at[1], ls.at[9 + per]),
        pltpu.make_async_copy(weights_far, far_out, ls.at[10 + per]),
    ]

    def second_group():
        packs[3]()
        whole_weights(far_all, weights_far)
        arrived(table_far, t_sem.at[1])
        build_bias(table_far)

        @pl.loop(0, blocks)
        def _(block):
            project(1, block)

        for copy in late:
            copy.start()

    @pl.loop(0, 2 * blocks)
    def _(unit):
        group, block = lax.div(unit, blocks), lax.rem(unit, blocks)
        rows = pl.ds(pl.multiple_of(block * span, span), span)
        turn = lax.rem(unit, 2)

        @pl.when(unit == blocks)
        def _():
            second_group()

        @pl.when(unit >= 2)
        def _():
            pltpu.make_async_copy(slot.at[turn], slot.at[turn], p_sem.at[turn]).wait()

        window = pl.ds(pl.multiple_of((blocks - 1 - block) * span, span), length)
        valid = lax.broadcasted_iota(jnp.int32, (1, length), 1) < lengths[per * s + x]
        for head in range(heads):
            query = split[group, head, rows, :HEAD_DIM]
            key, value = split[group, heads + head, :, :HEAD_DIM], split[group, 2 * heads + head, :, :HEAD_DIM]
            scores = lax.dot_general(query, key, (((1,), (1,)), ((), ())), preferred_element_type=F32)
            scores = jnp.where(valid, scores + ext[head, :, window], -1e30)
            top = jnp.max(scores, axis=-1, keepdims=True)
            grown = jnp.exp(scores - top)
            total = jnp.sum(grown, axis=-1, keepdims=True)
            part = (grown * (1.0 / total)).astype(BF16)
            slot[turn, head] = part
            mixed = jnp.dot(part, value, preferred_element_type=F32)
            out[unit, :, head * HEAD_DIM : (head + 1) * HEAD_DIM] = mixed.astype(BF16)
        pltpu.make_async_copy(slot.at[turn], probs.at[group, :, rows, :], p_sem.at[turn]).start()
        source = jnp.where(group == 0, h, me.across)
        j = lax.div(block, 2)

        @pl.when(lax.rem(block + s, 2) == c)
        def _():
            pltpu.make_async_copy(out.at[unit], heads_all.at[source, j], os.at[group, j]).start()

        @pl.when(lax.rem(block + s, 2) != c)
        def _():
            send(out.at[unit], heads_all.at[source, j], a_send.at[group, j], a_recv.at[group, j], head=me.near)

        @pl.when(unit == 1)
        def _():
            for i in range(1, seqs):
                outs[1](i)
            send_cotangent()

        @pl.when(unit == 3)
        def _():
            outs[2]()
            total = jnp.zeros((local, width), F32)
            for g in range(groups):
                total = total + jnp.dot(
                    wo_parts[g // dps, g % dps], spread_hot(g * shard, shard, width), preferred_element_type=F32
                )
            wo_all[h] = total.astype(BF16)
            send(wo_all.at[h], wo_all.at[h], w_send.at[0], w_recv.at[0], head=me.across)
            send(wo_all.at[h], wo_all.at[h], w_send.at[1], w_recv.at[1], head=me.near)

    there = wo_all.at[me.across]
    arrived(there, w_recv.at[0])
    send(there, there, w_send.at[2], w_recv.at[2], head=me.near)
    for copy in kept + late:
        copy.wait()
    for turn in range(2):
        pltpu.make_async_copy(slot.at[turn], slot.at[turn], p_sem.at[turn]).wait()
    packs[4]()
    to_table.wait_send()
    for j in range(per):
        block = me.block(j)

        @pl.when(block == s)
        def _():
            pltpu.make_async_copy(cot_own.at[j], cot_own.at[j], ls.at[5]).wait()

        @pl.when(block != s)
        def _():
            for part in range(2):
                arrived(cot_own.at[j, pl.ds(part * half, half)], c_recv.at[j, part])

        for group in range(2):
            pltpu.make_async_copy(out.at[0], heads_all.at[h, j], os.at[group, j]).wait()
            pltpu.make_async_copy(out.at[0], out.at[0], a_send.at[group, j]).wait()
            source = me.near if group == 0 else me.near_across
            arrived(heads_all.at[source, j], a_recv.at[group, j])

    for i in range(1, seqs):
        rows = tok.at[0, pl.ds(0, half)]
        for sem in (z_send, h_send, c_send):
            pltpu.make_async_copy(rows, rows, sem.at[i - 1]).wait()
        pltpu.make_async_copy(ids_own, ids_own, i_send.at[i - 1]).wait()
        arrived(ids_all.at[mod(s - i, seqs)], i_recv.at[i - 1])
    for k in range(3):
        pltpu.make_async_copy(wo_all.at[h], wo_all.at[h], w_send.at[k]).wait()
    arrived(wo_all.at[me.near], w_recv.at[1])
    arrived(wo_all.at[me.near_across], w_recv.at[2])


def front(tokens, cot, wq, wk, wv, wo, router, gain_a, gain_f, ids, table, lengths, seqs, dps):
    seq_local, span, width = tokens.shape
    per = seq_local // seqs
    length = seqs * span
    shard, local = wq.shape
    heads = local // HEAD_DIM
    lanes = up_to(3 * local + router.shape[0], 128)
    padded = up_to(shard, 16)
    smem = pl.BlockSpec(memory_space=pltpu.SMEM)
    return pl.pallas_call(
        functools.partial(front_kernel, seqs, dps, heads),
        out_shape=(
            jax.ShapeDtypeStruct((length, width), BF16),
            jax.ShapeDtypeStruct((width, lanes), BF16),
            jax.ShapeDtypeStruct((width, lanes), BF16),
            jax.ShapeDtypeStruct((2, 3 * heads, length, 128), BF16),
            jax.ShapeDtypeStruct((2, heads, length, length), BF16),
            jax.ShapeDtypeStruct((4, per, span, local), BF16),
            jax.ShapeDtypeStruct((per, span, width), BF16),
            jax.ShapeDtypeStruct((per, span, width), BF16),
            jax.ShapeDtypeStruct((4, local, width), BF16),
            jax.ShapeDtypeStruct((8, width), F32),
            jax.ShapeDtypeStruct((seqs,) + ids.shape[:2], jnp.int32),
        ),
        in_specs=[ANY] * 2 + [VMEM] * 7 + [ANY, VMEM, smem],
        out_specs=[ANY] * 8 + [VMEM] * 2 + [ANY],
        scratch_shapes=[
            pltpu.VMEM((length, width), BF16),
            pltpu.VMEM((width, lanes), BF16),
            pltpu.VMEM((width, lanes), BF16),
            pltpu.VMEM((2, 3 * heads, length, 128), BF16),
            pltpu.VMEM((seqs, span, width), BF16),
            pltpu.VMEM((padded, lanes), BF16),
            pltpu.VMEM((seqs, dps, padded, lanes), BF16),
            pltpu.VMEM((seqs, dps, padded, lanes), BF16),
            pltpu.VMEM((local, 128), BF16),
            pltpu.VMEM((seqs, dps, local, 128), BF16),
            pltpu.VMEM((8, 128), F32),
            pltpu.VMEM((seqs, dps, 8, 128), F32),
            pltpu.VMEM((8, 128), F32),
            pltpu.VMEM((8, 128), F32),
            pltpu.VMEM((heads, span, 7 * span), F32),
            pltpu.VMEM((2, heads, span, length), BF16),
            pltpu.VMEM((2 * seqs, span, local), BF16),
            DMA((2,)),
            DMA((11 + per,)),
            DMA((2, per)),
            DMA((seqs - 1,)),
            DMA((seqs - 1,)),
            DMA((seqs - 1,)),
            DMA((seqs - 1,)),
            DMA((seqs - 1,)),
            DMA((per, 2)),
            DMA((2, per)),
            DMA((2, per)),
            DMA((3,)),
            DMA((3,)),
            DMA((seqs - 1,)),
            DMA((seqs - 1,)),
            DMA((seqs, dps)),
            DMA((seqs, dps)),
            DMA((2,)),
        ]
        + gather_sems(seqs, dps) * 3,
        compiler_params=params(collective_id=0),
        name="front",
    )(tokens, cot, wq, wk, wv, wo, router, gain_a, gain_f, ids, table, lengths)


def expert_windows(exp_local, per_expert):
    return [(e * per_expert // 16 * 16, up_to((e + 1) * per_expert, 16)) for e in range(exp_local)]


def contract(a, b, over_a, over_b):
    return lax.dot_general(a, b, (((over_a,), (over_b,)), ((), ())), preferred_element_type=F32)


AHEAD = 3
GELU_A, GELU_B = float(np.sqrt(2.0 / np.pi)), 0.044715


def experts_kernel(
    seqs, dps, per_expert, capacity, local,
    heads_all, own_tok, wo_all, weights, gains, cot_own, ids_all, up_in, down_in,
    result, hidden_grad, router_grad, gain_grad, up_out, down_out,
    up, down, up_grad, down_grad, rows, summed, place_hot, place_turned, hidden_ref, ffn_ref, router_ref, gate_ref, hot_ref, taken, near, far,
    ls, g_send, g_recv, h_send, h_recv, n_send, n_recv, x_send, x_recv, r_send, r_recv
):
    me = Place(seqs, dps)
    h, s, d = me.h, me.s, me.d
    groups, _, height, width = rows.shape
    exp_local = up.shape[0]
    windows = expert_windows(exp_local, per_expert)
    me_group = s * dps + d

    def away(n):
        return lax.div(n, dps), lax.rem(n, dps)

    def ahead(n):
        i, j = away(n)
        return mod(s + i, seqs), mod(d + j, dps)

    def behind(n):
        i, j = away(n)
        return mod(s - i, seqs), mod(d - j, dps)

    per, span, _ = own_tok.shape
    loads = [pltpu.make_async_copy(up_in, up, ls.at[1]), pltpu.make_async_copy(down_in, down, ls.at[2])]
    for copy in loads:
        copy.start()
    spots = groups * height
    first_lane = 3 * local // 128 * 128
    spread = weights.shape[1] - first_lane
    shift = 3 * local - first_lane
    experts = groups * exp_local
    router = weights[:, first_lane:]
    earlier = lax.broadcasted_iota(jnp.int32, (span, span), 0) < lax.broadcasted_iota(jnp.int32, (span, span), 1)
    earlier = earlier.astype(BF16)
    lane = lax.broadcasted_iota(jnp.int32, (span, spread), 1)
    is_expert = (lane >= shift) & (lane < shift + experts)

    def tokens_in(j):
        total = own_tok[j].astype(F32)
        for q in range(4):
            total = total + jnp.dot(heads_all[q, j], wo_all[q], preferred_element_type=F32)
        hidden_ref[j] = total
        inverse = lax.rsqrt(jnp.mean(total * total, axis=-1, keepdims=True) + EPS)
        ffn = (total * inverse * gains[1:2, :]).astype(BF16)
        ffn_ref[j] = ffn
        logits = jnp.where(is_expert, jnp.dot(ffn, router, preferred_element_type=F32), -1e30)
        grown = jnp.exp(logits - jnp.max(logits, axis=-1, keepdims=True))
        router_probs = grown / jnp.sum(grown, axis=-1, keepdims=True)
        router_ref[j] = router_probs
        ids = ids_all[me.block(j), pl.ds(per * s + me.x, 1), :]
        own = lax.broadcasted_iota(jnp.int32, (spread, span), 0) == ids + shift
        own_low = own.astype(BF16)
        before = jnp.dot(own_low, earlier, preferred_element_type=F32)
        slot = jnp.sum(jnp.where(own, before, 0.0), axis=0, keepdims=True).astype(jnp.int32)
        same = lax.broadcasted_iota(jnp.int32, (spread, spread), 0) == lax.broadcasted_iota(jnp.int32, (spread, spread), 1)
        hot = contract(own_low, same.astype(BF16), 0, 0)
        hot_ref[j] = hot
        gate = jnp.sum(router_probs * hot, axis=-1, keepdims=True)
        gate_ref[j] = gate
        group = lax.div(ids, exp_local)
        place = group * height + ((ids - group * exp_local) * per + j) * capacity + slot
        spot = lax.broadcasted_iota(jnp.int32, (spots, span), 0)
        place_hot[j] = (spot == place).astype(BF16)
        return ffn, (gate * cot_own[j].astype(F32)).astype(BF16)

    made = [tokens_in(j) for j in range(per)]
    for part in range(2):
        total = jnp.zeros((spots, width), F32)
        for j in range(per):
            total = total + jnp.dot(place_hot[j], made[j][part], preferred_element_type=F32)
        total = total.astype(BF16)
        for g in range(groups):
            rows[g, part] = total[g * height : (g + 1) * height, :]
    greet(me.group_peers() + me.head_pair())
    pltpu.make_async_copy(rows.at[me_group], taken.at[h, 0], ls.at[0]).start()

    def send_out(n):
        to_s, to_d = ahead(n)
        send(rows.at[to_s * dps + to_d], taken.at[h, n], g_send.at[n], g_recv.at[n], seq=to_s, dp=to_d)

    for n in range(1, min(AHEAD + 1, groups)):
        send_out(n)

    def gather_own(n):
        here = taken.at[h, n]

        @pl.when(n == 0)
        def _():
            pltpu.make_async_copy(here, here, ls.at[0]).wait()

        @pl.when(n > 0)
        def _():
            arrived(here, g_recv.at[n])

        send(here, here, h_send.at[0, n], h_recv.at[0, n], head=me.across)
        send(here, here, h_send.at[1, n], h_recv.at[1, n], head=me.near)

    def gather_across(n):
        there = taken.at[me.across, n]
        arrived(there, h_recv.at[0, n])
        send(there, there, h_send.at[2, n], h_recv.at[2, n], head=me.near)

    def compute(n):
        @pl.when(n == first_turn)
        def _():
            for copy in loads:
                copy.wait()

        arrived(taken.at[me.near, n], h_recv.at[1, n])
        arrived(taken.at[me.near_across, n], h_recv.at[2, n])
        for k in range(3):
            pltpu.make_async_copy(taken.at[h, n], taken.at[h, n], h_send.at[k, n]).wait()
        kept = []
        for e, (low, high) in enumerate(windows):
            size = high - low
            at = lax.broadcasted_iota(jnp.int32, (4 * size, width), 0)
            slot = lax.rem(at, size) + low
            inside = (slot >= e * per_expert) & (slot < (e + 1) * per_expert)

            def mine(part):
                block = jnp.concatenate([taken[q, n, part, low:high, :] for q in range(4)], axis=0)
                return jnp.where(inside, block.astype(F32), 0.0).astype(BF16)

            x, g = mine(0), mine(1)
            pre = jnp.dot(x, up[e], preferred_element_type=F32)
            square = pre * pre
            bent = jnp.tanh(GELU_A * pre * (1.0 + GELU_B * square))
            act = (0.5 * pre * (1.0 + bent)).astype(BF16)
            slope = 0.5 * (1.0 + bent) + 0.5 * pre * (1.0 - bent * bent) * (GELU_A * (1.0 + 3.0 * GELU_B * square))
            out = jnp.dot(act, down[e], preferred_element_type=F32).astype(BF16)
            act_grad = contract(g, down[e], 1, 1)
            pre_grad = (act_grad * slope).astype(BF16)
            back = contract(pre_grad, up[e], 1, 1).astype(BF16)
            kept.append((x, g, act, pre_grad, out, back))
        for q in range(4):
            for part in range(2):
                for tile in range(0, height, 16):
                    total = None
                    for (low, high), made in zip(windows, kept):
                        if low <= tile < high:
                            begin = q * (high - low) + tile - low
                            piece = made[4 + part][begin : begin + 16, :]
                            total = piece if total is None else total + piece
                    if total is not None:
                        taken[q, n, part, tile : tile + 16, :] = total
        send(taken.at[me.near_across, n], near.at[0, n], n_send.at[0, n], n_recv.at[0, n], head=me.near)
        send(taken.at[me.near, n], near.at[1, n], n_send.at[1, n], n_recv.at[1, n], head=me.near)
        for e in range(exp_local):
            x, g, act, pre_grad, _, _ = kept[e]
            up_grad[e] += contract(x, pre_grad, 0, 0)
            down_grad[e] += contract(act, g, 0, 0)

    def add_near(n):
        arrived(near.at[0, n], n_recv.at[0, n])
        both = taken[me.across, n].astype(F32) + near[0, n].astype(F32)
        taken[me.across, n] = both.astype(BF16)
        send(taken.at[me.across, n], far.at[n], x_send.at[n], x_recv.at[n], head=me.across)

    def send_back(n):
        arrived(near.at[1, n], n_recv.at[1, n])
        arrived(far.at[n], x_recv.at[n])
        total = taken[h, n].astype(F32) + near[1, n].astype(F32) + far[n].astype(F32)
        taken[h, n] = total.astype(BF16)
        to_s, to_d = behind(n)

        @pl.when(n == 0)
        def _():
            pltpu.make_async_copy(taken.at[h, n], summed.at[:, me_group], r_send.at[n]).start()

        @pl.when(n > 0)
        def _():
            send(taken.at[h, n], summed.at[:, me_group], r_send.at[n], r_recv.at[n], seq=to_s, dp=to_d)

    first_turn = 1 % groups
    gather_own(0)
    up_grad[...] = jnp.zeros_like(up_grad)
    down_grad[...] = jnp.zeros_like(down_grad)
    stages = (send_back, add_near, compute, gather_across, gather_own)

    @pl.loop(0, groups + len(stages) - 1)
    def _(step):
        @pl.when((step > 0) & (step + AHEAD < groups))
        def _():
            send_out(step + AHEAD)

        for j in range(per):

            @pl.when(step == 2 + j)
            def _():
                place_turned[j] = place_hot[j].astype(F32).T.astype(BF16)

        for k, stage in enumerate(stages):
            turn = step - (len(stages) - 1 - k)
            last = groups - 1 if stage is gather_own else groups

            @pl.when((turn >= 0) & (turn < last))
            def _():
                stage(lax.rem(turn + 1, groups))

    up[...] = up_grad[...].astype(BF16)
    down[...] = down_grad[...].astype(BF16)
    stores = [
        pltpu.make_async_copy(up, up_out, ls.at[1]),
        pltpu.make_async_copy(down, down_out, ls.at[2]),
    ]
    for copy in stores:
        copy.start()

    @pl.loop(0, groups)
    def _(n):
        here = taken.at[h, n]
        for k in range(2):
            pltpu.make_async_copy(here, here, n_send.at[k, n]).wait()
        pltpu.make_async_copy(here, here, x_send.at[n]).wait()
        pltpu.make_async_copy(here, here, r_send.at[n]).wait()

        @pl.when(n > 0)
        def _():
            pltpu.make_async_copy(here, here, g_send.at[n]).wait()
            from_s, from_d = ahead(n)
            arrived(summed.at[:, from_s * dps + from_d], r_recv.at[n])

    def tokens_out(j):
        hidden, gate, router_probs, hot = hidden_ref[j], gate_ref[j], router_ref[j], hot_ref[j]
        grad = cot_own[j].astype(F32)
        token_out = jnp.dot(place_turned[j], summed[0].reshape(spots, width), preferred_element_type=F32)
        input_grad = jnp.dot(place_turned[j], summed[1].reshape(spots, width), preferred_element_type=F32)
        result[j] = (hidden + gate * token_out).astype(BF16)
        gate_grad = jnp.sum(grad * token_out, axis=-1, keepdims=True)
        logit_low = (router_probs * (gate_grad * hot - gate_grad * gate)).astype(BF16)
        router_part = contract(logit_low, ffn_ref[j], 0, 0)
        input_grad = input_grad + contract(logit_low, router, 1, 1)
        inverse = lax.rsqrt(jnp.mean(hidden * hidden, axis=-1, keepdims=True) + EPS)
        r = hidden * inverse
        u = input_grad * gains[1:2, :]
        hidden_grad[j] = grad + (u - r * jnp.mean(u * r, axis=-1, keepdims=True)) * inverse
        gain_part = jnp.sum(input_grad * r, axis=0, keepdims=True)
        if j == 0:
            router_grad[...] = router_part
            gain_grad[...] = gain_part
        else:
            router_grad[...] += router_part
            gain_grad[...] += gain_part

    for j in range(per):
        tokens_out(j)
    for copy in stores:
        copy.wait()


def run_experts(
    heads_all, own_tok, wo_all, weights, gains, cot_own, ids_all, up, down, seqs, dps, per_expert, capacity
):
    per, span, width = own_tok.shape
    local = wo_all.shape[1]
    groups = seqs * dps
    height = up_to(up.shape[0] * per_expert, 16)
    spread = weights.shape[1] - 3 * local // 128 * 128
    rows = (groups, 2, height, width)
    return pl.pallas_call(
        functools.partial(experts_kernel, seqs, dps, per_expert, capacity, local),
        out_shape=(
            jax.ShapeDtypeStruct((per, span, width), BF16),
            jax.ShapeDtypeStruct((per, span, width), F32),
            jax.ShapeDtypeStruct((spread, width), F32),
            jax.ShapeDtypeStruct((1, width), F32),
            jax.ShapeDtypeStruct(up.shape, BF16),
            jax.ShapeDtypeStruct(down.shape, BF16),
        ),
        in_specs=[VMEM] * 7 + [ANY] * 2,
        out_specs=[VMEM] * 4 + [ANY] * 2,
        scratch_shapes=[
            pltpu.VMEM(up.shape, BF16),
            pltpu.VMEM(down.shape, BF16),
            pltpu.VMEM(up.shape, F32),
            pltpu.VMEM(down.shape, F32),
            pltpu.VMEM(rows, BF16),
            pltpu.VMEM((2, groups, height, width), BF16),
            pltpu.VMEM((per, groups * height, span), BF16),
            pltpu.VMEM((per, span, groups * height), BF16),
            pltpu.VMEM((per, span, width), F32),
            pltpu.VMEM((per, span, width), BF16),
            pltpu.VMEM((per, span, spread), F32),
            pltpu.VMEM((per, span, 1), F32),
            pltpu.VMEM((per, span, spread), F32),
            pltpu.VMEM((4,) + rows, BF16),
            pltpu.VMEM((2,) + rows, BF16),
            pltpu.VMEM(rows, BF16),
            DMA((3,)),
            DMA((groups,)),
            DMA((groups,)),
            DMA((3, groups)),
            DMA((3, groups)),
            DMA((2, groups)),
            DMA((2, groups)),
            DMA((groups,)),
            DMA((groups,)),
            DMA((groups,)),
            DMA((groups,)),
        ],
        compiler_params=params(collective_id=2),
        name="experts",
    )(heads_all, own_tok, wo_all, weights, gains, cot_own, ids_all, up, down)


def send_home(me, own, home, ls, z_send, z_recv, h_send, h_recv):
    s, seqs, x, core = me.s, me.seqs, me.x, me.c
    per, span, _ = own.shape
    rows = span // PIECES
    lands = [(k, lax.rem(s + core, 2) + 2 * k) for k in range(seqs // 2)]

    def part(c):
        return pl.ds(c * rows, rows)

    def start(c):
        for j in range(per):
            to = me.block(j)
            there = home.at[per * s + x, part(c)]

            @pl.when(to != s)
            def _():
                k = lax.div(s, 2)
                send(own.at[j, part(c)], there, z_send.at[j, c], z_recv.at[k, c], seq=to)

            @pl.when(to == s)
            def _():
                pltpu.make_async_copy(own.at[j, part(c)], there, ls.at[c]).start()

    def pass_on(c):
        for k, source in lands:
            here = home.at[per * source + x, part(c)]

            @pl.when(source == s)
            def _():
                pltpu.make_async_copy(here, here, ls.at[c]).wait()

            @pl.when(source != s)
            def _():
                arrived(here, z_recv.at[k, c])

            send(here, here, h_send.at[0, k, c], h_recv.at[0, k, c], head=me.across)
            send(here, here, h_send.at[1, k, c], h_recv.at[1, k, c], head=me.near)

    def pass_near(c):
        for k, source in lands:
            there = home.at[per * source + 1 - x, part(c)]
            arrived(there, h_recv.at[0, k, c])
            send(there, there, h_send.at[2, k, c], h_recv.at[2, k, c], head=me.near)

    def finish():
        some = own.at[0, part(0)]
        for c in range(PIECES):
            for j in range(per):

                @pl.when(me.block(j) != s)
                def _():
                    pltpu.make_async_copy(some, some, z_send.at[j, c]).wait()

            for k in range(seqs // 2):
                source = lax.rem(s + 1 + core, 2) + 2 * k
                arrived(home.at[per * source + x, part(c)], h_recv.at[1, k, c])
                arrived(home.at[per * source + 1 - x, part(c)], h_recv.at[2, k, c])
                for n in range(3):
                    pltpu.make_async_copy(some, some, h_send.at[n, k, c]).wait()

    return start, pass_on, pass_near, finish


def home_sems(per, seqs):
    return [
        DMA((PIECES,)),
        DMA((per, PIECES)),
        DMA((seqs // 2, PIECES)),
        DMA((3, seqs // 2, PIECES)),
        DMA((3, seqs // 2, PIECES)),
    ]


def add_groups(me, parts, dp_take, seq_take, result, dp_send, dp_recv, seq_send, seq_recv):
    s, d, seqs, dps = me.s, me.d, me.seqs, me.dps
    order = [mod(s + n, seqs) for n in list(range(1, seqs)) + [0]]

    def start():
        for to in order:
            for i in range(1, dps):
                there = mod(d + i, dps)
                send(
                    parts.at[there, to], dp_take.at[i - 1, to], dp_send.at[i - 1, to], dp_recv.at[i - 1, to], dp=there
                )

    def middle():
        for n, to in enumerate(order):
            total = parts[d, to].astype(F32)
            for i in range(1, dps):
                arrived(dp_take.at[i - 1, to], dp_recv.at[i - 1, to])
                total = total + dp_take[i - 1, to].astype(F32)
            parts[d, to] = total.astype(parts.dtype)
            if n < seqs - 1:
                send(parts.at[d, to], seq_take.at[n], seq_send.at[n], seq_recv.at[n], seq=to)

    def end():
        total = parts[d, s].astype(F32)
        for n in range(seqs - 1):
            arrived(seq_take.at[n], seq_recv.at[n])
            total = total + seq_take[n].astype(F32)
        result[...] = total
        some = seq_take.at[0]
        for to in range(seqs):
            for i in range(1, dps):
                pltpu.make_async_copy(some, some, dp_send.at[i - 1, to]).wait()
        for n in range(seqs - 1):
            pltpu.make_async_copy(some, some, seq_send.at[n]).wait()

    return start, middle, end


def group_scratch(seqs, dps, shape, dtype):
    return [
        pltpu.VMEM((dps, seqs) + shape, dtype),
        pltpu.VMEM((max(1, dps - 1), seqs) + shape, dtype),
        pltpu.VMEM((seqs - 1,) + shape, dtype),
    ]


def group_sems(seqs, dps):
    return [DMA((max(1, dps - 1), seqs))] * 2 + [DMA((seqs - 1,))] * 2


PIECES = 2


def back_kernel(
    seqs, dps, heads,
    result, hidden_grad, own_tok, heads_all, wo_all, split_in, probs, attn_input_in, weights, weights_far, gains, router,
    gain_f,
    output, tokens_home, w_sum, small_sum, wo_sum, gain_sum, bias_sum,
    split, attn_input, turned, attn_grad, hsend, grad_all, slot, low_ref, ext, made, x_acc, x_out, x_near, tg,
    wo_part, wo_near, wo_far, w_parts, w_dp, w_seq, w_total, far_parts, far_dp, far_seq, far_sum, last_parts, last_dp, last_seq, last_sum, far_out, far_in,
    wo_parts, wo_dp, wo_seq, g_parts, g_dp, g_seq, r_parts, r_dp, r_seq, r_sum, g_acc,
    bias, bias_out, bias_in, bias_take, small, gsmall,
    ls, p_sem, a_send, a_recv, n_send, n_recv, on_send, on_recv, of_send, of_recv,
    b_send, b_recv, s_send, s_recv, t_send, t_recv, fs, *sems
):
    me = Place(seqs, dps)
    h, s, d = me.h, me.s, me.d
    per, span, width = hidden_grad.shape
    blocks = seqs
    length = blocks * span
    local = heads * HEAD_DIM
    groups = seqs * dps
    shard = width // groups
    padded = w_sum.shape[0]
    buckets = 32
    size = span // PIECES
    others = [(i, j) for i in range(seqs) for j in range(dps) if i or j]
    loads = [pltpu.make_async_copy(split_in, split, ls.at[0]), pltpu.make_async_copy(attn_input_in, attn_input, ls.at[1])]
    for copy in loads:
        copy.start()
    ext[...] = jnp.zeros_like(ext)
    made[...] = jnp.zeros_like(made)
    greet(me.group_peers() + [{"head": mod(h + i, 4)} for i in range(1, 4)])
    out_home = send_home(me, result, output, *sems[0:5])
    grad_home = send_home(me, tg, tokens_home, *sems[5:10])
    w_group = add_groups(me, w_parts, w_dp, w_seq, w_total, *sems[10:14])
    wo_group = add_groups(me, wo_parts, wo_dp, wo_seq, wo_sum, *sems[14:18])
    g_group = add_groups(me, g_parts, g_dp, g_seq, gain_sum, *sems[18:22])
    r_group = add_groups(me, r_parts, r_dp, r_seq, r_sum, *sems[22:26])
    far_group = add_groups(me, far_parts, far_dp, far_seq, far_sum, *sems[26:30])
    last_group = add_groups(me, last_parts, last_dp, last_seq, last_sum, *sems[30:34])

    def by_group(whole, parts):
        low = whole.astype(BF16)
        if shard % 16:
            low = contract(squeeze_hot(shard, padded, width, groups), low, 0, 0).astype(BF16)
        for g in range(groups):
            parts[g % dps, g // dps] = low[g * padded : (g + 1) * padded, :]

    def fetch(group, head):
        turn = head % 2 if group else 1 - head % 2
        return turn, pltpu.make_async_copy(probs.at[group, head], slot.at[turn], p_sem.at[turn])

    def put(ref, grad):
        for head in range(heads):
            ref[head, :, :HEAD_DIM] = grad[:, head * HEAD_DIM : (head + 1) * HEAD_DIM]

    def block_rows(block):
        return pl.ds(pl.multiple_of(block * span, span), span)

    fetch(1, 0)[1].start()
    out_home[0](0)
    out_home[0](1)
    hsend[...] = jnp.zeros_like(hsend)
    attn_grad[...] = hidden_grad[...].astype(BF16)
    for group, (own, other) in ((1, (me.across, me.near_across)), (0, (h, me.near))):
        for j in range(per):
            rows = block_rows(me.block(j))
            put(hsend.at[group, j], contract(attn_grad[j], wo_all[other], 1, 1).astype(BF16))
            send(
                hsend.at[group, j],
                grad_all.at[group, :, rows, :],
                a_send.at[group, j],
                a_recv.at[group, j],
                head=me.near,
            )
            put(grad_all.at[group, :, rows, :], contract(attn_grad[j], wo_all[own], 1, 1).astype(BF16))
    for k, q in enumerate((me.near_across, me.near, me.across, h)):
        total = jnp.zeros((local, width), F32)
        for j in range(per):
            total = total + contract(heads_all[q, j], attn_grad[j], 0, 0)
        wo_part[k] = total.astype(BF16)
        if k < 2:
            send(wo_part.at[k], wo_near.at[k], on_send.at[k], on_recv.at[k], head=me.near)
    by_group(router[...].T, r_parts)
    r_group[0]()
    for copy in loads:
        copy.wait()
    turned[...] = attn_input[...].T

    def wo_across():
        arrived(wo_near.at[0], on_recv.at[0])
        wo_part[2] = (wo_part[2].astype(F32) + wo_near[0].astype(F32)).astype(BF16)
        send(wo_part.at[2], wo_far, of_send, of_recv, head=me.across)

    def wo_total():
        arrived(wo_near.at[1], on_recv.at[1])
        arrived(wo_far, of_recv)
        total = (wo_part[3].astype(F32) + wo_near[1].astype(F32) + wo_far[...].astype(F32)).astype(BF16)
        for g in range(groups):
            hot = spread_hot(g * shard, shard, width)
            wo_parts[g % dps, g // dps] = contract(total, hot, 1, 1).astype(BF16)
        wo_group[0]()

    def cut(c):
        return pl.ds(c * size, size)

    def x_partial():
        x_acc[...] += contract(made[...], weights[...], 1, 1)
        for c in range(PIECES):
            for j in range(per):
                rows = pl.ds(pl.multiple_of(me.block(j, 1 - me.c) * span + c * size, size), size)
                x_out[j, cut(c)] = x_acc[rows, :].astype(BF16)
                send(x_out.at[j, cut(c)], x_near.at[j, cut(c)], n_send.at[j, c], n_recv.at[j, c], head=me.near)

    def x_total(c):
        for j in range(per):
            arrived(x_near.at[j, cut(c)], n_recv.at[j, c])
            rows = pl.ds(pl.multiple_of(me.block(j) * span + c * size, size), size)
            grad = x_acc[rows, :] + x_near[j, cut(c)].astype(F32)
            v = own_tok[j, cut(c)].astype(F32)
            inverse = lax.rsqrt(jnp.mean(v * v, axis=-1, keepdims=True) + EPS)
            r = v * inverse
            u = grad * gains[0:1, :]
            back = (u - r * jnp.mean(u * r, axis=-1, keepdims=True)) * inverse
            tg[j, cut(c)] = (hidden_grad[j, cut(c)] + back).astype(BF16)
            g_acc[0:1, :] += jnp.sum(grad * r, axis=0, keepdims=True)
        grad_home[0](c)

    def attention(group, service):
        for j in range(per):
            rows = block_rows(me.block(j, 1 - me.c))
            arrived(grad_all.at[group, :, rows, :], a_recv.at[group, j])
        for head in range(heads):
            turn, copy = fetch(group, head)
            copy.wait()
            if head < heads - 1:
                fetch(group, head + 1)[1].start()
            elif group:
                fetch(0, 0)[1].start()
            key, value = split[group, heads + head, :, :HEAD_DIM], split[group, 2 * heads + head, :, :HEAD_DIM]
            for block in range(blocks):
                rows = slice(block * span, (block + 1) * span)
                grad = grad_all[group, head, rows, :HEAD_DIM]
                wide = slot[turn, rows, :].astype(F32)
                prob_grad = contract(grad, value, 1, 1)
                delta = jnp.sum(wide * prob_grad, axis=-1, keepdims=True)
                score_grad = wide * (prob_grad - delta)
                first = (blocks - 1 - block) * span
                ext[head, :, first : first + length] += score_grad
                low = score_grad.astype(BF16)
                low_ref[rows, :] = low
                cols = slice(head * HEAD_DIM, (head + 1) * HEAD_DIM)
                made[rows, cols] = jnp.dot(low, key, preferred_element_type=F32).astype(BF16)
            for kind, (narrow, wide_ref) in enumerate(
                ((split[group, head, :, :HEAD_DIM], low_ref), (grad_all[group, head, :, :HEAD_DIM], slot.at[turn]))
            ):
                first = (kind + 1) * local + head * HEAD_DIM
                made[:, first : first + HEAD_DIM] = contract(narrow, wide_ref[...], 0, 0).T.astype(BF16)
            for act in service[head]:
                act()

    def weight_grad(first, last):
        pieces = []
        for kind in range(3):
            at = kind * local
            part = made[:, at + first * HEAD_DIM : at + last * HEAD_DIM]
            pieces.append(jnp.dot(turned[...], part, preferred_element_type=F32))
        lanes = 3 * (last - first) * HEAD_DIM
        if lanes % 128:
            pieces.append(jnp.zeros((width, 128 - lanes % 128), F32))
        return jnp.concatenate(pieces, axis=1)

    def bias_rows(into):
        turn = lax.broadcasted_iota(jnp.int32, (4 * span, 128), 0)
        bucket = bucket_of(jnp.where(turn < 3 * span, turn, turn - 4 * span) - span, buckets)
        hot = (bucket == lax.broadcasted_iota(jnp.int32, (4 * span, 128), 1)).astype(F32)
        lane = lax.broadcasted_iota(jnp.int32, (1, 128), 1)
        head_row = lax.broadcasted_iota(jnp.int32, (8, 4 * span), 0)
        diagonals = jnp.zeros((8, 4 * span), F32)
        far_row = lax.broadcasted_iota(jnp.int32, (8, 128), 0)
        far = jnp.zeros((8, 128), F32)
        for head in range(heads):
            eight = jnp.zeros((8, 4 * span), F32)
            for group in range(span // 8):
                piece = ext[head, group * 8 : (group + 1) * 8, 2 * span : 5 * span]
                piece = jnp.concatenate([piece, jnp.zeros((8, span), F32)], axis=1)
                eight = eight + pltpu.roll(piece, (4 * span - 8 * group) % (4 * span), 1)
            one = jnp.zeros((8, 4 * span), F32)
            for i in range(8):
                line = jnp.broadcast_to(eight[i : i + 1, :], (8, 4 * span))
                one = one + pltpu.roll(line, (4 * span - i) % (4 * span), 1)
            diagonals = jnp.where(head_row == head, one, diagonals)
            left, right = jnp.sum(ext[head, :, : 2 * span]), jnp.sum(ext[head, :, 5 * span :])
            sides = jnp.where(lane == buckets // 2 - 1, left, jnp.where(lane == buckets - 1, right, 0.0))
            far = jnp.where(far_row == head, sides, far)
        into[...] = far + jnp.dot(diagonals, hot, preferred_element_type=F32, precision=lax.Precision.HIGHEST)

    def router_total():
        r_group[2]()
        small[0] = r_sum[...]
        for i in range(1, 4):
            send(small.at[0], small.at[i], s_send.at[i - 1], s_recv.at[i - 1], head=mod(h + i, 4))

    g_acc[...] = jnp.zeros_like(g_acc)
    g_acc[1:2, :] = gain_f[...]
    def far_weights():
        by_group(weight_grad(0, heads - 1), far_parts)
        far_group[0]()

    def far_weights():
        by_group(weight_grad(0, heads - 1), far_parts)
        far_group[0]()

    attention(1, ((wo_across,), (far_weights, r_group[1]), (wo_total,)))
    by_group(weight_grad(heads - 1, heads), last_parts)
    last_group[0]()
    out_home[1](0)
    x_acc[...] = contract(made[...], weights_far[...], 1, 1)
    far_group[1]()
    out_home[1](1)
    bias_rows(bias_out)
    to_bias = send(bias_out, bias_in, fs.at[0], fs.at[1], head=me.across)
    ext[...] = jnp.zeros_like(ext)
    attention(
        0,
        (
            (),
            (wo_group[1], last_group[1]),
            (router_total,),
        ),
    )
    x_partial()
    x_total(0)
    x_total(1)
    by_group(jnp.dot(turned[...], made[:, : w_parts.shape[-1]], preferred_element_type=F32), w_parts)
    w_group[0]()
    g_rows = g_acc[...].astype(BF16)
    for g in range(groups):
        g_parts[g % dps, g // dps] = contract(g_rows, spread_hot(g * shard, shard, width), 1, 1)
    g_group[0]()
    bias_rows(bias)
    arrived(bias_in, fs.at[1])
    bias[...] += bias_in[...]
    for n, (i, j) in enumerate(others):
        send(bias, bias_take.at[n], b_send.at[n], b_recv.at[n], seq=mod(s + i, seqs), dp=mod(d + j, dps))
    out_home[2](0)
    out_home[2](1)
    grad_home[1](0)
    w_group[1]()
    grad_home[1](1)
    g_group[1]()
    far_group[2]()
    last_group[2]()
    most, last = far_sum.shape[1], last_sum.shape[1]
    far_out[:, :most] = far_sum[...].astype(BF16)
    far_out[:, most:] = last_sum[...].astype(BF16)
    to_far = send(far_out, far_in, fs.at[2], fs.at[3], head=me.across)
    g_group[2]()
    gsmall[0] = gain_sum[...]
    for i in range(1, 4):
        send(gsmall.at[0], gsmall.at[i], t_send.at[i - 1], t_recv.at[i - 1], head=mod(h + i, 4))
    wo_group[2]()
    total = bias[...]
    for n in range(len(others)):
        arrived(bias_take.at[n], b_recv.at[n])
        total = total + bias_take[n]
    bias_sum[...] = total
    grad_home[2](0)
    grad_home[2](1)
    w_group[2]()
    arrived(far_in, fs.at[3])
    first_heads, last_head = far_in[:, :most].astype(F32), far_in[:, most:].astype(F32)
    many = (heads - 1) * HEAD_DIM
    for kind in range(3):
        at = kind * local
        into = slice(at, at + many)
        w_sum[:, into] = w_total[:, into] + first_heads[:, kind * many : (kind + 1) * many]
        into = slice(at + many, at + local)
        w_sum[:, into] = w_total[:, into] + last_head[:, kind * HEAD_DIM : (kind + 1) * HEAD_DIM]
    total, gain_total = small[0], gsmall[0]
    for i in range(1, 4):
        arrived(small.at[i], s_recv.at[i - 1])
        arrived(gsmall.at[i], t_recv.at[i - 1])
        total = total + small[i]
        gain_total = gain_total + gsmall[i]
    small_sum[...] = total
    gain_sum[...] = gain_total
    out_home[3]()
    grad_home[3]()
    to_bias.wait_send()
    to_far.wait_send()
    for j in range(per):
        for group in range(2):
            pltpu.make_async_copy(hsend.at[0, 0], hsend.at[0, 0], a_send.at[group, j]).wait()
        some = x_near.at[0, cut(0)]
        for c in range(PIECES):
            pltpu.make_async_copy(some, some, n_send.at[j, c]).wait()
    for k in range(2):
        pltpu.make_async_copy(wo_far, wo_far, on_send.at[k]).wait()
    pltpu.make_async_copy(wo_far, wo_far, of_send).wait()
    for i in range(3):
        pltpu.make_async_copy(small.at[0], small.at[0], s_send.at[i]).wait()
        pltpu.make_async_copy(gsmall.at[0], gsmall.at[0], t_send.at[i]).wait()
    for n in range(len(others)):
        pltpu.make_async_copy(bias, bias, b_send.at[n]).wait()


def back_pass(
    result, hidden_grad, own_tok, heads_all, wo_all, split, probs, attn_input, weights, weights_far, gains, router, gain_f,
    seqs, dps
):
    per, span, width = hidden_grad.shape
    length = seqs * span
    heads = probs.shape[1]
    local = heads * HEAD_DIM
    groups = seqs * dps
    shard = width // groups
    padded = up_to(shard, 16)
    lanes = weights.shape[1]
    spread = router.shape[0]
    all_three = up_to(3 * local, 128)
    most, last = up_to(3 * (heads - 1) * HEAD_DIM, 128), up_to(3 * HEAD_DIM, 128)
    block = (span, width)
    return pl.pallas_call(
        functools.partial(back_kernel, seqs, dps, heads),
        out_shape=(
            jax.ShapeDtypeStruct((per * seqs,) + block, BF16),
            jax.ShapeDtypeStruct((per * seqs,) + block, BF16),
            jax.ShapeDtypeStruct((padded, 3 * local), F32),
            jax.ShapeDtypeStruct((padded, spread), F32),
            jax.ShapeDtypeStruct((local, 128), F32),
            jax.ShapeDtypeStruct((8, 128), F32),
            jax.ShapeDtypeStruct((8, 128), F32),
        ),
        in_specs=[VMEM] * 5 + [ANY] * 3 + [VMEM] * 5,
        out_specs=[ANY] * 2 + [VMEM] * 5,
        scratch_shapes=[
            pltpu.VMEM(split.shape, BF16),
            pltpu.VMEM(attn_input.shape, BF16),
            pltpu.VMEM(attn_input.shape[::-1], BF16),
            pltpu.VMEM((per,) + block, BF16),
            pltpu.VMEM((2, per, heads, span, 128), BF16),
            pltpu.VMEM((2, heads, length, 128), BF16),
            pltpu.VMEM((2, length, length), BF16),
            pltpu.VMEM((length, length), BF16),
            pltpu.VMEM((heads, span, 7 * span), F32),
            pltpu.VMEM((length, lanes), BF16),
            pltpu.VMEM((length, width), F32),
            pltpu.VMEM((per,) + block, BF16),
            pltpu.VMEM((per,) + block, BF16),
            pltpu.VMEM((per,) + block, BF16),
            pltpu.VMEM((4, local, width), BF16),
            pltpu.VMEM((2, local, width), BF16),
            pltpu.VMEM((local, width), BF16),
        ]
        + group_scratch(seqs, dps, (padded, all_three), BF16)
        + [pltpu.VMEM((padded, all_three), F32)]
        + group_scratch(seqs, dps, (padded, most), BF16)
        + [pltpu.VMEM((padded, most), F32)]
        + group_scratch(seqs, dps, (padded, last), BF16)
        + [pltpu.VMEM((padded, last), F32)]
        + [
            pltpu.VMEM((padded, most + last), BF16),
            pltpu.VMEM((padded, most + last), BF16),
        ]
        + group_scratch(seqs, dps, (local, 128), BF16)
        + group_scratch(seqs, dps, (8, 128), F32)
        + group_scratch(seqs, dps, (padded, spread), BF16)
        + [
            pltpu.VMEM((padded, spread), F32),
            pltpu.VMEM((8, width), F32),
            pltpu.VMEM((8, 128), F32),
            pltpu.VMEM((8, 128), F32),
            pltpu.VMEM((8, 128), F32),
            pltpu.VMEM((groups - 1, 8, 128), F32),
            pltpu.VMEM((4, padded, spread), F32),
            pltpu.VMEM((4, 8, 128), F32),
            DMA((2,)),
            DMA((2,)),
            DMA((2, per)),
            DMA((2, per)),
            DMA((per, PIECES)),
            DMA((per, PIECES)),
            DMA((2,)),
            DMA((2,)),
            DMA(()),
            DMA(()),
            DMA((groups - 1,)),
            DMA((groups - 1,)),
            DMA((3,)),
            DMA((3,)),
            DMA((3,)),
            DMA((3,)),
            DMA((4,)),
        ]
        + home_sems(per, seqs) * 2
        + group_sems(seqs, dps) * 6,
        compiler_params=params(collective_id=4),
        name="back",
    )(
        result, hidden_grad, own_tok, heads_all, wo_all, split, probs, attn_input, weights, weights_far, gains, router, gain_f
    )


PARTS = 4


def settle_kernel(count, *refs):
    large, (w, router, wo, gain, bias) = refs[:count], refs[count : count + 5]
    refs = refs[count + 5 :]
    large_out, (wq_out, wk_out, wv_out, wo_out, router_out, gain_a, gain_f, bias_out) = refs[:count], refs[count : count + 8]
    refs = refs[count + 8 :]
    held, wide, sems = refs[:count], refs[count : 2 * count], refs[2 * count]
    copies = []
    for n in range(count):
        size = large[n].shape[0] // PARTS
        for k in range(PARTS):
            part = pl.ds(k * size, size)
            come = pltpu.make_async_copy(large[n].at[part], held[n].at[part], sems.at[0, n, k])
            rounded = large[n].dtype == large_out[n].dtype
            source = held[n] if rounded else wide[n]
            go = pltpu.make_async_copy(source.at[part], large_out[n].at[part], sems.at[1, n, k])
            come.start()
            copies.append((come, go, None if rounded else (wide[n], held[n], slice(k * size, (k + 1) * size))))
    shard, local = wq_out.shape
    for n, ref in enumerate((wq_out, wk_out, wv_out)):
        ref[...] = w[:shard, n * local : (n + 1) * local]
    wo_out[...] = wo[:, :shard]
    spread = router.shape[1]
    at = 3 * local % 128
    turned = jnp.concatenate([router[...], jnp.zeros((128 - router.shape[0], spread), F32)], axis=0).T
    router_out[...] = turned[at : at + router_out.shape[0], :shard]
    gain_a[...] = gain[0:1, :shard]
    gain_f[...] = gain[1:2, :shard]
    bias_out[...] = bias[: bias_out.shape[0], : bias_out.shape[1]]
    for come, go, widen in copies:
        come.wait()
        if widen is not None:
            into, source, part = widen
            into[part] = source[part].astype(F32)
        go.start()
    for _, go, _ in copies:
        go.wait()


def settle(large, types, small, shapes):
    count = len(large)
    return pl.pallas_call(
        functools.partial(settle_kernel, count),
        out_shape=tuple(jax.ShapeDtypeStruct(x.shape, kind) for x, kind in zip(large, types))
        + tuple(jax.ShapeDtypeStruct(shape, F32) for shape in shapes),
        in_specs=[ANY] * count + [VMEM] * len(small),
        out_specs=[ANY] * count + [VMEM] * len(shapes),
        scratch_shapes=[pltpu.VMEM(x.shape, x.dtype) for x in large]
        + [pltpu.VMEM(x.shape if x.dtype != kind else (8, 128), kind) for x, kind in zip(large, types)]
        + [DMA((2, count, PARTS))],
        compiler_params=pltpu.CompilerParams(vmem_limit_bytes=60 * 2**20),
        name="settle",
    )(*large, *small)


def up_to(value, unit):
    return -(-value // unit) * unit


def body(
    tokens,
    lengths,
    expert_ids,
    attention_gain,
    query_weight,
    key_weight,
    value_weight,
    output_weight,
    position_bias,
    feedforward_gain,
    router_weight,
    expert_up,
    expert_down,
    cotangent,
):
    seqs, dps = lax.axis_size("seq"), lax.axis_size("dp")
    groups = seqs * dps
    seq_local, span, width = tokens.shape
    per = seq_local // seqs
    local_width = query_weight.shape[1]
    bucket_count, heads = position_bias.shape
    experts = router_weight.shape[1]
    shard = query_weight.shape[0]
    capacity = max(2, (5 * span + 4 * experts - 1) // (4 * experts))
    attn_input, weights, weights_far, split, probs, heads_all, own_tok, cot_own, out_weight, gains, ids_all = front(
        tokens,
        cotangent,
        query_weight,
        key_weight,
        value_weight,
        output_weight,
        router_weight.T,
        attention_gain[None, :],
        feedforward_gain[None, :],
        expert_ids.reshape(seq_local, span),
        position_bias.T,
        lengths,
        seqs,
        dps,
    )
    result, hidden_grad, router_grad, gain_two_grad, up_grad, down_grad = run_experts(
        heads_all,
        own_tok,
        out_weight,
        weights,
        gains,
        cot_own,
        ids_all,
        expert_up,
        expert_down,
        seqs,
        dps,
        per * capacity,
        capacity,
    )
    output, tokens_grad, w_sum, small_sum, wo_sum, gain_sum, bias_sum = back_pass(
        result,
        hidden_grad,
        own_tok,
        heads_all,
        out_weight,
        split,
        probs,
        attn_input,
        weights,
        weights_far,
        gains,
        router_grad,
        gain_two_grad,
        seqs,
        dps,
    )
    output, tokens_grad, up_grad, down_grad, *small = settle(
        (output, tokens_grad, up_grad.reshape(-1, up_grad.shape[-1]), down_grad.reshape(-1, down_grad.shape[-1])),
        (BF16, BF16, F32, F32),
        (w_sum, small_sum, wo_sum, gain_sum, bias_sum),
        ((shard, local_width),) * 3
        + ((local_width, shard), (experts, shard), (1, shard), (1, shard), (heads, bucket_count)),
    )
    return (
        output,
        tokens_grad,
        small[5][0],
        small[0],
        small[1],
        small[2],
        small[3],
        small[7].T,
        small[6][0],
        small[4].T,
        up_grad.reshape(expert_up.shape),
        down_grad.reshape(expert_down.shape),
    )


def solution(mesh):
    placed = (
        P("dp", "seq", None),
        P("dp"),
        P("dp", "seq", None),
        P(("seq", "dp")),
        P(("seq", "dp"), "head"),
        P(("seq", "dp"), "head"),
        P(("seq", "dp"), "head"),
        P("head", ("seq", "dp")),
        P(None, "head"),
        P(("seq", "dp")),
        P(("seq", "dp"), None),
        P(("seq", "dp"), None, "head"),
        P(("seq", "dp"), "head", None),
        P("dp", "seq", None),
    )
    return jax.shard_map(
        body,
        mesh=mesh,
        in_specs=placed,
        out_specs=(
            P("dp", "seq", None),
            P("dp", "seq", None),
            P(("seq", "dp")),
            P(("seq", "dp"), "head"),
            P(("seq", "dp"), "head"),
            P(("seq", "dp"), "head"),
            P("head", ("seq", "dp")),
            P(None, "head"),
            P(("seq", "dp")),
            P(("seq", "dp"), None),
            P(("seq", "dp"), None, "head"),
            P(("seq", "dp"), "head", None),
        ),
        check_vma=False,
    )
```
